32 devices in a mesh: rep: 8 (over y, x, core), shard: 4 (over z).
Axes of the slice: x: 2, y: 2, z: 4, core: 2. Of those that a mesh axis runs over, the one named last changes fastest.
Arguments:
- hidden_in: bfloat16 [8, 1104, 1024], P('rep', 'shard'), may hold values from -6 to 6
- skip_path: bfloat16 [8, 1104, 1024], P('rep', 'shard'), may hold values from -6 to 6
- cotangent: bfloat16 [8, 1104, 1024], P('rep', 'shard'), may hold values from -6 to 6
- skip_weight: float32 [2048, 1024], P('shard')
- heads_in: float32 [1024, 3072], P('shard')
- heads_out: float32 [1024, 1024], P('shard')
- expand_weight: float32 [1024, 4096], P('shard')
- reduce_weight: float32 [4096, 1024], P('shard')
- vectors: float32 [11, 1024], P(None, 'shard'), as said below
- moments_skip: float32 [2, 2048, 1024], P(None, 'shard'), as said below
- moments_in: float32 [2, 1024, 3072], P(None, 'shard'), as said below
- moments_out: float32 [2, 1024, 1024], P(None, 'shard'), as said below
- moments_expand: float32 [2, 1024, 4096], P(None, 'shard'), as said below
- moments_reduce: float32 [2, 4096, 1024], P(None, 'shard'), as said below
- moments_vectors: float32 [2, 11, 1024], P(None, None, 'shard'), as said below
Outputs:
- block_out: bfloat16 [8, 1104, 1024], P('rep', 'shard')
- input_gradient: bfloat16 [8, 1104, 1024], P('rep', 'shard')
- skip_gradient: bfloat16 [8, 1104, 1024], P('rep', 'shard')
- gradient_skip: float32 [2048, 1024], P('shard')
- gradient_in: float32 [1024, 3072], P('shard')
- gradient_out: float32 [1024, 1024], P('shard')
- gradient_expand: float32 [1024, 4096], P('shard')
- gradient_reduce: float32 [4096, 1024], P('shard')
- gradient_vectors: float32 [11, 1024], P(None, 'shard')
- new_moments_skip: float32 [2, 2048, 1024], P(None, 'shard')
- new_moments_in: float32 [2, 1024, 3072], P(None, 'shard')
- new_moments_out: float32 [2, 1024, 1024], P(None, 'shard')
- new_moments_expand: float32 [2, 1024, 4096], P(None, 'shard')
- new_moments_reduce: float32 [2, 4096, 1024], P(None, 'shard')
- new_moments_vectors: float32 [2, 11, 1024], P(None, None, 'shard')
- new_skip_weight: float32 [2048, 1024], P('shard')
- new_heads_in: float32 [1024, 3072], P('shard')
- new_heads_out: float32 [1024, 1024], P('shard')
- new_expand_weight: float32 [1024, 4096], P('shard')
- new_reduce_weight: float32 [4096, 1024], P('shard')
- new_vectors: float32 [11, 1024], P(None, 'shard')
- norms: float32 [2, 6], replicated
The draws below stay inside these ranges and needn't reach their ends.
Inputs may be any that keep to these rules, and one draw needn't show every extreme that they name: `vectors`: gains in rows 1 and 4 are positive. `moments_skip`: root mean squares positive. `moments_in`: root mean squares positive. `moments_out`: root mean squares positive. `moments_expand`: root mean squares positive. `moments_reduce`: root mean squares positive. `moments_vectors`: root mean squares positive.
All inputs are finite; a program needn't handle non-finite values.
Results may differ from the reference program's by a relative error of at most 0.015.
The reference program's roundings to bfloat16 on the way count: a program that leaves them out, or rounds other values in their place, can miss the bound.
Values may be sent and summed in bfloat16 or wider, within the bound.
A program may use at most 320 MiB of HBM per device.

```python
import math
import jax
import jax.numpy as jnp
from jax import lax

D = 1024
HEADS = 16
HEAD_DIM = 64
FF = 4096
SEQ_LEN = 1104
SEQUENCES = 8
TOKENS = 8832


def mixed_matrix(key, row_total, column_total, fan):
    keys = jax.random.split(jax.random.fold_in(key, 11), 3)
    base = jnp.clip(jax.random.normal(keys[0], (row_total, column_total), jnp.float32), -4.0, 4.0)
    place = jnp.arange(row_total, dtype=jnp.float32)[:, None] / row_total - 0.5
    row_scale = jnp.exp(place * 1.0986 + jax.random.uniform(keys[1], (row_total, 1), jnp.float32, -1.15, 1.15))
    column_scale = jnp.exp(jax.random.uniform(keys[2], (1, column_total), jnp.float32, -1.15, 1.15))
    return base * row_scale * column_scale * (0.4236 / math.sqrt(fan))


def state_pair(key, shape):
    keys = jax.random.split(jax.random.fold_in(key, 23), 2)
    level = jnp.sqrt(jnp.float32(TOKENS))
    first_part = jax.random.normal(keys[0], shape, jnp.float32) * level
    second_part = jax.random.uniform(keys[1], shape, jnp.float32, 0.3, 3.0) * level
    return jnp.stack([first_part, second_part])


def draw_skip_weight(key, part):
    return mixed_matrix(key, 2 * D, D, 2 * D)


def draw_heads_in(key, part):
    return mixed_matrix(key, D, 3 * D, D / 2)


def draw_heads_out(key, part):
    return mixed_matrix(key, D, D, D / 16)


def draw_expand_weight(key, part):
    return mixed_matrix(key, D, FF, D)


def draw_reduce_weight(key, part):
    return mixed_matrix(key, FF, D, FF)


def draw_vectors(key, part):
    keys = jax.random.split(jax.random.fold_in(key, 31), 2)
    place = jnp.arange(D, dtype=jnp.float32)[None, :] / D - 0.5
    rising = jnp.exp(place * 1.0986)
    biases = jax.random.normal(keys[0], (11, D), jnp.float32) * 0.5
    gains = jax.random.uniform(keys[1], (11, D), jnp.float32, 0.5, 1.5)
    row_index = jnp.arange(11)[:, None]
    picked = (row_index == 1) | (row_index == 4)
    return jnp.where(picked, gains, biases) * rising


def draw_moments_skip(key, part):
    return state_pair(key, (2 * D, D))


def draw_moments_in(key, part):
    return state_pair(key, (D, 3 * D))


def draw_moments_out(key, part):
    return state_pair(key, (D, D))


def draw_moments_expand(key, part):
    return state_pair(key, (D, FF))


def draw_moments_reduce(key, part):
    return state_pair(key, (FF, D))


def draw_moments_vectors(key, part):
    return state_pair(key, (11, D))


def level_of(own_key, shape, pieces, low, largest):
    factor_of, own = 1.0, jax.random.fold_in(own_key, 6)
    for axis_at, blocks in pieces:
        steps = jnp.exp(jax.random.uniform(jax.random.fold_in(own, axis_at), (blocks,), jnp.float32, low / len(pieces), largest / len(pieces)))
        factor_of = factor_of * jnp.repeat(steps, shape[axis_at] // blocks).reshape([-1 if axis == axis_at else 1 for axis in range(len(shape))])
    return factor_of


def bell_draw(key, shape, scale, reach, shards=(), kind=jnp.bfloat16):
    array = jax.random.normal(key, shape, jnp.float32) * scale
    if len(shards) > 0:
        array = level_of(key, shape, shards, -0.22, 0.18) * array
    return jnp.clip(array, min=-reach, max=reach).astype(kind)


def setup_inputs(seed: int = 0) -> dict:
    seeds = jax.random.split(jax.random.key(seed), 16)
    hidden_in = bell_draw(seeds[0], (SEQUENCES, SEQ_LEN, D), 1.0, 6.0, ((0, 8), (1, 4)))
    skip_path = bell_draw(seeds[1], (SEQUENCES, SEQ_LEN, D), 1.0, 6.0, ((0, 8), (1, 4)))
    cotangent = bell_draw(seeds[2], (SEQUENCES, SEQ_LEN, D), 1.0, 6.0, ((0, 8), (1, 4)))
    skip_weight = draw_skip_weight(jax.random.fold_in(seeds[15], 71), 0)
    heads_in = draw_heads_in(jax.random.fold_in(seeds[15], 71), 0)
    heads_out = draw_heads_out(jax.random.fold_in(seeds[15], 71), 0)
    expand_weight = draw_expand_weight(jax.random.fold_in(seeds[15], 71), 0)
    reduce_weight = draw_reduce_weight(jax.random.fold_in(seeds[15], 71), 0)
    vectors = draw_vectors(jax.random.fold_in(seeds[15], 71), 0)
    moments_skip = draw_moments_skip(jax.random.fold_in(seeds[15], 71), 0)
    moments_in = draw_moments_in(jax.random.fold_in(seeds[15], 71), 0)
    moments_out = draw_moments_out(jax.random.fold_in(seeds[15], 71), 0)
    moments_expand = draw_moments_expand(jax.random.fold_in(seeds[15], 71), 0)
    moments_reduce = draw_moments_reduce(jax.random.fold_in(seeds[15], 71), 0)
    moments_vectors = draw_moments_vectors(jax.random.fold_in(seeds[15], 71), 0)
    return dict(hidden_in=hidden_in, skip_path=skip_path, cotangent=cotangent, skip_weight=skip_weight, heads_in=heads_in, heads_out=heads_out, expand_weight=expand_weight, reduce_weight=reduce_weight, vectors=vectors, moments_skip=moments_skip, moments_in=moments_in, moments_out=moments_out, moments_expand=moments_expand, moments_reduce=moments_reduce, moments_vectors=moments_vectors)


highest = lax.Precision.HIGHEST
step_rate = 0.3

@jax.custom_vjp
def low(v):
    return lax.optimization_barrier(v.astype(jnp.bfloat16)).astype(jnp.float32)

@jax.custom_vjp
def low_back(v):
    return v

def low_keep(v):
    return (low(v), None)

def low_pass(kept, grad):
    return (grad,)

def back_keep(v):
    return (v, None)

def back_low(kept, grad):
    return (low(grad),)
low.defvjp(low_keep, low_pass)
low_back.defvjp(back_keep, back_low)

def normalize(stream, gain_row, bias_row):
    center = stream - lax.optimization_barrier(jnp.mean(stream, -1, keepdims=True))
    spread = lax.optimization_barrier(jnp.mean(center * center, -1, keepdims=True))
    return center * lax.rsqrt(spread + 1e-05) * gain_row + bias_row

def exact_gelu(inputs):
    return jax.nn.gelu(inputs, approximate=False)

def product(left, right):
    return jnp.dot(left, right, precision=highest, preferred_element_type=jnp.float32)

def sequence_block(weights, source, skip_rows):
    skip_matrix, in_matrix, out_matrix, expand_matrix, reduce_matrix, table_rows = weights
    model_width = source.shape[1]
    token_count = source.shape[0]
    factor = 1.0 / math.sqrt(HEAD_DIM)
    joined = jnp.concatenate([source, skip_rows], -1)
    entering = low_back(product(joined, skip_matrix) + table_rows[0])
    first_in = low(normalize(entering, table_rows[1], table_rows[2]))
    triple = low_back(low(product(first_in, in_matrix)))
    queries = triple[:, :model_width].reshape(token_count, HEADS, HEAD_DIM)
    keys_all = triple[:, model_width:2 * model_width].reshape(token_count, HEADS, HEAD_DIM)
    values_all = triple[:, 2 * model_width:].reshape(token_count, HEADS, HEAD_DIM)
    scores = low_back(jnp.einsum('qhd,khd->hqk', queries, keys_all, precision=highest) * factor)
    probability = jax.nn.softmax(scores, -1)
    mixed = jnp.einsum('hqk,khd->qhd', low(probability), values_all, precision=highest)
    mixed = low_back(low(mixed.reshape(token_count, model_width)))
    middle = entering + low_back(product(mixed, out_matrix) + table_rows[3])
    second_in = low(normalize(middle, table_rows[4], table_rows[5]))
    expanded = low_back(product(second_in, expand_matrix) + table_rows[7:].reshape(-1))
    activated = low(exact_gelu(expanded))
    return middle + product(activated, reduce_matrix) + table_rows[6]

def forward(hidden, skipped, masters):
    weights = tuple((low(matrix) for matrix in masters))

    def one_sequence(carry_value, inputs_pair):
        return (carry_value, sequence_block(weights, inputs_pair[0], inputs_pair[1]))
    unused, outputs = lax.scan(jax.checkpoint(one_sequence), jnp.zeros((), jnp.float32), (hidden, skipped))
    return outputs

def lamb_update(weight, gradient, moments):
    first_moment = 0.5 * moments[0] + 0.5 * gradient
    root_square = jnp.sqrt(0.5 * moments[1] * moments[1] + 0.5 * gradient * gradient)
    direction = first_moment / (root_square + 1e-06)
    weight_norm = jnp.sqrt(jnp.sum(weight * weight))
    direction_norm = jnp.sqrt(jnp.sum(direction * direction))
    updated = weight - step_rate * (weight_norm / (direction_norm + 1e-06)) * direction
    return (jnp.stack([first_moment, root_square]), updated, weight_norm, direction_norm)

def reference(hidden_in, skip_path, cotangent, skip_weight, heads_in, heads_out, expand_weight, reduce_weight, vectors, moments_skip, moments_in, moments_out, moments_expand, moments_reduce, moments_vectors):
    masters = (skip_weight, heads_in, heads_out, expand_weight, reduce_weight, vectors)
    block_result, pullback = jax.vjp(forward, hidden_in.astype(jnp.float32), skip_path.astype(jnp.float32), masters)
    grad_hidden, grad_skipped, gradients = pullback(cotangent.astype(jnp.float32))
    states = (moments_skip, moments_in, moments_out, moments_expand, moments_reduce, moments_vectors)
    results = [lamb_update(weight, gradient, moments) for weight, gradient, moments in zip(masters, gradients, states)]
    norms = jnp.stack([jnp.stack([entry[2] for entry in results]), jnp.stack([entry[3] for entry in results])])
    return (block_result.astype(jnp.bfloat16), grad_hidden.astype(jnp.bfloat16), grad_skipped.astype(jnp.bfloat16), gradients[0], gradients[1], gradients[2], gradients[3], gradients[4], gradients[5], results[0][0], results[1][0], results[2][0], results[3][0], results[4][0], results[5][0], results[0][1], results[1][1], results[2][1], results[3][1], results[4][1], results[5][1], norms)
```

```python
import math

import jax
import jax.numpy as jnp
from jax import lax
from jax.sharding import PartitionSpec as P

HEADS = 16
HEAD_DIM = 64


step_rate = 0.3


def normalize(stream, gain_row, bias_row):
    center = stream - jnp.mean(stream, -1, keepdims=True)
    spread = jnp.mean(center * center, -1, keepdims=True)
    return center * lax.rsqrt(spread + 1e-05) * gain_row + bias_row


def exact_gelu(inputs):
    return jax.nn.gelu(inputs, approximate=False)


def matmul(left, right):
    return jnp.dot(left, right, preferred_element_type=jnp.float32)


def row_sums(matrix):
    return jnp.sum(matrix, 0, dtype=jnp.float32)


def moment_step(gradient, moments):
    first_moment = 0.5 * moments[0] + 0.5 * gradient
    root_square = jnp.sqrt(0.5 * moments[1] * moments[1] + 0.5 * gradient * gradient)
    direction = first_moment / (root_square + 1e-06)
    return (jnp.stack([first_moment, root_square]), direction)


def to_heads(rows, sequences, portion, shards):
    parts = rows.shape[1] // (HEADS * HEAD_DIM)
    width = HEADS * HEAD_DIM // shards
    blocks = rows.reshape(sequences, portion, parts, shards, width).transpose(3, 0, 1, 2, 4)
    blocks = blocks.reshape(shards, sequences * portion, parts * width)
    blocks = lax.all_to_all(blocks, "shard", 0, 0, tiled=True)
    blocks = blocks.reshape(shards, sequences, portion, parts, width).transpose(1, 0, 2, 3, 4)
    return blocks.reshape(sequences, shards * portion, parts, width // HEAD_DIM, HEAD_DIM)


def to_tokens(blocks, sequences, portion, shards):
    parts = blocks.shape[2]
    width = HEADS * HEAD_DIM // shards
    rows = blocks.reshape(sequences, shards, portion, parts, width).transpose(1, 0, 2, 3, 4)
    rows = rows.reshape(shards, sequences * portion, parts * width)
    rows = lax.all_to_all(rows, "shard", 0, 0, tiled=True)
    rows = rows.reshape(shards, sequences * portion, parts, width).transpose(1, 2, 0, 3)
    return rows.reshape(sequences * portion, parts * shards * width)


def on_device(
    hidden_in,
    skip_path,
    cotangent,
    skip_weight,
    heads_in,
    heads_out,
    expand_weight,
    reduce_weight,
    vectors,
    moments_skip,
    moments_in,
    moments_out,
    moments_expand,
    moments_reduce,
    moments_vectors,
):
    sequences, portion, model_width = hidden_in.shape
    shards = lax.axis_size("shard")
    replicas = lax.axis_size("rep")
    rep_index = lax.axis_index("rep")
    row_count = sequences * portion
    factor = 1.0 / math.sqrt(HEAD_DIM)
    masters = (skip_weight, heads_in, heads_out, expand_weight, reduce_weight, vectors)
    gathered = []
    for matrix in masters[:5]:
        height = matrix.shape[0] // replicas
        piece = lax.dynamic_slice_in_dim(matrix, rep_index * height, height, 0)
        piece = piece.astype(jnp.bfloat16)
        gathered.append(lax.all_gather(piece, ("shard", "rep"), axis=0, tiled=True))
    skip_matrix, in_matrix, out_matrix, expand_matrix, reduce_matrix = gathered
    table_low = lax.all_gather(vectors.astype(jnp.bfloat16), "shard", axis=1, tiled=True)
    table_rows = table_low.astype(jnp.float32)
    source = hidden_in.reshape(row_count, model_width)
    skip_rows = skip_path.reshape(row_count, model_width)
    joined = jnp.concatenate([source, skip_rows], 1)
    entering = matmul(joined, skip_matrix) + table_rows[0]
    normed_one, norm_back_one = jax.vjp(normalize, entering, table_rows[1], table_rows[2])
    first_in = normed_one.astype(jnp.bfloat16)
    triple = matmul(first_in, in_matrix).astype(jnp.bfloat16)
    heads = to_heads(triple, sequences, portion, shards)
    queries, keys_full, values_full = heads[:, :, 0], heads[:, :, 1], heads[:, :, 2]
    scores = (
        jnp.einsum("sqhd,skhd->shqk", queries, keys_full, preferred_element_type=jnp.float32)
        * factor
    )
    row_max = jnp.max(scores, -1)
    row_total = jnp.sum(jnp.exp(scores - row_max[..., None]), -1)
    log_total = row_max + jnp.log(row_total)
    probability = jnp.exp(scores - log_total[..., None])
    mixed = jnp.einsum(
        "shqk,skhd->sqhd",
        probability.astype(jnp.bfloat16),
        values_full,
        preferred_element_type=jnp.float32,
    )
    mixed_low = to_tokens(mixed.astype(jnp.bfloat16)[:, :, None], sequences, portion, shards)
    middle = entering + matmul(mixed_low, out_matrix) + table_rows[3]
    normed_two, norm_back_two = jax.vjp(normalize, middle, table_rows[4], table_rows[5])
    second_in = normed_two.astype(jnp.bfloat16)
    expanded = matmul(second_in, expand_matrix) + table_rows[7:].reshape(-1)
    activated, gelu_back = jax.vjp(exact_gelu, expanded)
    activated_low = activated.astype(jnp.bfloat16)
    block_result = middle + matmul(activated_low, reduce_matrix) + table_rows[6]
    block_out = block_result.astype(jnp.bfloat16).reshape(sequences, portion, model_width)
    grad_out = cotangent.reshape(row_count, model_width)
    grad_reduce = matmul(activated_low.T, grad_out)
    grad_act = matmul(grad_out, reduce_matrix.T)
    grad_inner = gelu_back(grad_act)[0].astype(jnp.bfloat16)
    grad_expand = matmul(second_in.T, grad_inner)
    grad_second = matmul(grad_inner, expand_matrix.T)
    grad_mid_norm, grad_gain_two, grad_bias_two = norm_back_two(grad_second)
    grad_middle = grad_out.astype(jnp.float32) + grad_mid_norm
    grad_middle_low = grad_middle.astype(jnp.bfloat16)
    grad_outw = matmul(mixed_low.T, grad_middle_low)
    grad_mixed = matmul(grad_middle_low, out_matrix.T).astype(jnp.bfloat16)
    grad_mixed = to_heads(grad_mixed, sequences, portion, shards)[:, :, 0]
    grad_prob = jnp.einsum(
        "sqhd,skhd->shqk", grad_mixed, values_full, preferred_element_type=jnp.float32
    )
    delta = jnp.sum(probability * grad_prob, -1)
    grad_scores = (probability * (grad_prob - delta[..., None])).astype(jnp.bfloat16)
    grad_query = (
        jnp.einsum("shqk,skhd->sqhd", grad_scores, keys_full, preferred_element_type=jnp.float32)
        * factor
    )
    grad_keys = (
        jnp.einsum("shqk,sqhd->skhd", grad_scores, queries, preferred_element_type=jnp.float32)
        * factor
    )
    grad_values = jnp.einsum(
        "shqk,sqhd->skhd",
        probability.astype(jnp.bfloat16),
        grad_mixed,
        preferred_element_type=jnp.float32,
    )
    grad_heads = jnp.stack([grad_query, grad_keys, grad_values], 2).astype(jnp.bfloat16)
    grad_triple = to_tokens(grad_heads, sequences, portion, shards)
    grad_inw = matmul(first_in.T, grad_triple)
    grad_first = matmul(grad_triple, in_matrix.T)
    grad_pre_norm, grad_gain_one, grad_bias_one = norm_back_one(grad_first)
    grad_entering = (grad_middle + grad_pre_norm).astype(jnp.bfloat16)
    grad_skipw = matmul(joined.T, grad_entering)
    grad_joined = matmul(grad_entering, skip_matrix.T)
    input_gradient = (
        grad_joined[:, :model_width].astype(jnp.bfloat16).reshape(sequences, portion, model_width)
    )
    skip_gradient = (
        grad_joined[:, model_width:].astype(jnp.bfloat16).reshape(sequences, portion, model_width)
    )
    grad_table = jnp.concatenate(
        [
            jnp.stack(
                [
                    row_sums(grad_entering),
                    grad_gain_one,
                    grad_bias_one,
                    row_sums(grad_middle_low),
                    grad_gain_two,
                    grad_bias_two,
                    row_sums(grad_out),
                ]
            ),
            row_sums(grad_inner).reshape(-1, model_width),
        ],
        0,
    )
    width = vectors.shape[1]
    grad_table = lax.psum(grad_table, ("rep", "shard"))
    vector_total = lax.dynamic_slice_in_dim(grad_table, lax.axis_index("shard") * width, width, 1)
    totals = []
    for partial in (grad_skipw, grad_inw, grad_outw, grad_expand, grad_reduce):
        piece = lax.psum_scatter(
            partial.astype(jnp.bfloat16), ("shard", "rep"), scatter_dimension=0, tiled=True
        )
        whole = lax.all_gather(piece, "rep", axis=0, tiled=True)
        totals.append(whole.astype(jnp.float32))
    totals.append(vector_total)
    states = (
        moments_skip,
        moments_in,
        moments_out,
        moments_expand,
        moments_reduce,
        moments_vectors,
    )
    steps = [moment_step(total, state) for total, state in zip(totals, states)]
    squares = jnp.stack(
        [
            jnp.stack([jnp.sum(matrix * matrix) for matrix in masters]),
            jnp.stack([jnp.sum(direction * direction) for _, direction in steps]),
        ]
    )
    norms = jnp.sqrt(lax.psum(squares, "shard"))
    ratio = norms[0] / (norms[1] + 1e-06)
    updated = [
        masters[position] - step_rate * ratio[position] * steps[position][1]
        for position in range(6)
    ]
    return (
        block_out,
        input_gradient,
        skip_gradient,
        *totals,
        *(state for state, _ in steps),
        *updated,
        norms,
    )


def solution(mesh):
    placed = (
        P("rep", "shard", None),
        P("rep", "shard", None),
        P("rep", "shard", None),
        P("shard", None),
        P("shard", None),
        P("shard", None),
        P("shard", None),
        P("shard", None),
        P(None, "shard"),
        P(None, "shard", None),
        P(None, "shard", None),
        P(None, "shard", None),
        P(None, "shard", None),
        P(None, "shard", None),
        P(None, None, "shard"),
    )
    return jax.shard_map(
        on_device,
        mesh=mesh,
        in_specs=placed,
        out_specs=(
            P("rep", "shard", None),
            P("rep", "shard", None),
            P("rep", "shard", None),
            P("shard", None),
            P("shard", None),
            P("shard", None),
            P("shard", None),
            P("shard", None),
            P(None, "shard"),
            P(None, "shard", None),
            P(None, "shard", None),
            P(None, "shard", None),
            P(None, "shard", None),
            P(None, "shard", None),
            P(None, None, "shard"),
            P("shard", None),
            P("shard", None),
            P("shard", None),
            P("shard", None),
            P("shard", None),
            P(None, "shard"),
            P(),
        ),
        check_vma=False,
    )
```

```python
import functools
import math

import jax
import jax.numpy as jnp
from jax import lax
from jax.experimental import pallas as pl
from jax.experimental.pallas import tpu as pltpu
from jax.sharding import PartitionSpec as P

MESH = pl.DeviceIdType.MESH
LOW = jnp.bfloat16
ANY = pl.BlockSpec(memory_space=pl.ANY)
SHARDS, REPLICAS = 4, 8
UNIT = 16
BLOCK = 1024


class Place:
    def __init__(self):
        self.rep = lax.axis_index("rep")
        self.shard = lax.axis_index("shard")
        self.core = lax.rem(self.rep, 2)
        self.x = lax.rem(self.rep // 2, 2)
        self.y = self.rep // 4

    def across(self, axis):
        own, step = {"core": (self.core, 1), "x": (self.x, 2), "y": (self.y, 4)}[axis]
        return (self.rep + step - 2 * step * own, self.shard)

    def along(self, offset):
        return (self.rep, lax.rem(self.shard + offset, SHARDS))

    def source(self, offset):
        return lax.rem(self.shard + SHARDS - offset, SHARDS)

    def partners(self):
        return [self.across("core"), self.across("x"), self.across("y")] + [
            self.along(offset) for offset in range(1, SHARDS)
        ]


def greet(place):
    barrier = pltpu.get_barrier_semaphore()
    partners = place.partners()
    for partner in partners:
        pl.semaphore_signal(barrier, inc=1, device_id=partner, device_id_type=MESH)
    pl.semaphore_wait(barrier, len(partners))


def chunk_list(shapes):
    chunks = []
    for index, (rows, columns) in enumerate(shapes):
        for group in range(rows // SHARDS // 256):
            for part in range(columns // BLOCK):
                chunks.append((index, group, part))
    return chunks


def folded(matrix):
    rows, columns = matrix.shape
    groups = rows // (SHARDS * 256)
    return matrix.reshape(SHARDS, groups, 2, 2, 2, 2, UNIT, columns)


class Ring:
    def __init__(self, send_sems, recv_sems):
        self.send_sems, self.recv_sems = send_sems, recv_sems
        self.open = []

    def send(self, source, target, device, slot):
        copy = pltpu.make_async_remote_copy(
            src_ref=source,
            dst_ref=target,
            send_sem=self.send_sems.at[slot],
            recv_sem=self.recv_sems.at[slot],
            device_id=device,
            device_id_type=MESH,
        )
        copy.start()
        return copy


def gather_kernel(chunks, *refs):
    count = 5
    masters = refs[:count]
    wholes = refs[count : 2 * count]
    wide, own, load_sems, keep_sems, send_sems, recv_sems = refs[2 * count :]
    place = Place()
    s, k, x, y = place.shard, place.core, place.x, place.y
    total = len(chunks)
    ring = Ring(send_sems, recv_sems)

    def load(at):
        index, group, part = chunks[at]
        return pltpu.make_async_copy(
            masters[index].at[group, :, :, :, :, :, pl.ds(part * BLOCK, BLOCK)],
            wide.at[at % 2],
            load_sems.at[at % 2],
        )

    def whole(at, *where):
        index, group, part = chunks[at]
        shard, rest = where[0], where[1:]
        rest = rest + (slice(None),) * (5 - len(rest))
        return wholes[index].at[(shard, group) + rest + (pl.ds(part * BLOCK, BLOCK),)]

    sent = []
    arrivals = {}

    def go(at, name, position, source, target, device):
        slot = at * 18 + position
        copy = ring.send(source, target, device, slot)
        sent.append(copy)
        arrivals.setdefault((at, name), []).append(copy)

    def arrived(at, name):
        for copy in arrivals[(at, name)]:
            copy.wait_recv()

    load(0).start()
    load(1).start()
    greet(place)
    kept = []

    def stage_cast(at):
        load(at).wait()

        @pl.loop(0, 16)
        def _(row):
            a, b = row // 8, lax.rem(row // 4, 2)
            c, d = lax.rem(row // 2, 2), lax.rem(row, 2)
            own[at, a, b, c, d] = wide[at % 2, a, b, c, d].astype(LOW)

        if at + 2 < total:
            load(at + 2).start()
        copy = pltpu.make_async_copy(own.at[at], whole(at, s), keep_sems.at[at])
        copy.start()
        kept.append(copy)

    def stage_z(at):
        for offset in range(1, SHARDS):
            go(
                at,
                "z",
                offset - 1,
                own.at[at, k, :, y, x],
                whole(at, s, k, slice(None), y, x),
                place.along(offset),
            )

    def stage_first(at):
        arrived(at, "z")
        for offset in range(1, SHARDS):
            e = place.source(offset)
            ref = whole(at, e, k, 0, y, x)
            go(at, "first", 3 + 2 * (offset - 1), ref, ref, place.across("x"))
            ref = whole(at, e, k, 1, y, x)
            go(at, "first", 4 + 2 * (offset - 1), ref, ref, place.across("y"))

    def stage_second(at):
        arrived(at, "first")
        for offset in range(1, SHARDS):
            e = place.source(offset)
            ref = whole(at, e, k, 0, y)
            go(at, "second", 9 + 2 * (offset - 1), ref, ref, place.across("y"))
            ref = whole(at, e, k, 1, slice(None), x)
            go(at, "second", 10 + 2 * (offset - 1), ref, ref, place.across("x"))

    def stage_core(at):
        arrived(at, "second")
        for offset in range(1, SHARDS):
            e = place.source(offset)
            ref = whole(at, e, k)
            go(at, "core", 15 + offset - 1, ref, ref, place.across("core"))

    def stage_end(at):
        arrived(at, "core")

    stages = (stage_z, stage_first, stage_second, stage_core, stage_end)
    lead = 4
    for at in range(min(lead, total)):
        stage_cast(at)
        stage_z(at)
    for step in range(total + 4):
        for position in range(1, 5):
            at = step - (position - 1)
            if 0 <= at < total:
                stages[position](at)
        if step + lead < total:
            stage_cast(step + lead)
            stage_z(step + lead)
    for copy in sent:
        copy.wait_send()
    for copy in kept:
        copy.wait()


def gather_weights(masters):
    shapes = [(matrix.shape[0] * SHARDS, matrix.shape[1]) for matrix in masters]
    chunks = chunk_list(shapes)
    total = len(chunks)
    own = [
        matrix.reshape(matrix.shape[0] // 256, 2, 2, 2, 2, UNIT, matrix.shape[1])
        for matrix in masters
    ]
    outs = pl.pallas_call(
        functools.partial(gather_kernel, chunks),
        out_shape=[
            jax.ShapeDtypeStruct((SHARDS, r // SHARDS // 256, 2, 2, 2, 2, UNIT, c), LOW)
            for r, c in shapes
        ],
        in_specs=[ANY] * 5,
        out_specs=[ANY] * 5,
        scratch_shapes=[
            pltpu.VMEM((2, 2, 2, 2, 2, UNIT, BLOCK), jnp.float32),
            pltpu.VMEM((total, 2, 2, 2, 2, UNIT, BLOCK), LOW),
            pltpu.SemaphoreType.DMA((2,)),
            pltpu.SemaphoreType.DMA((total,)),
            pltpu.SemaphoreType.DMA((total * 18,)),
            pltpu.SemaphoreType.DMA((total * 18,)),
        ],
        compiler_params=pltpu.CompilerParams(
            collective_id=1, has_side_effects=True, vmem_limit_bytes=40 * 2**20
        ),
        name="gather_weights",
    )(*own)
    return [out.reshape(shape) for out, shape in zip(outs, shapes)]


def add_into(target, source, height):
    @pl.loop(0, height)
    def _(row):
        target[row] = (target[row].astype(jnp.float32) + source[row].astype(jnp.float32)).astype(
            LOW
        )


def reduce_kernel(chunks, *refs):
    count = 5
    partials = refs[:count]
    table = refs[count]
    sums = refs[count + 1 : 2 * count + 1]
    table_sum = refs[2 * count + 1]
    (
        mine,
        from_core,
        from_first,
        from_second,
        final,
        from_z,
        done,
        table_own,
        table_in,
        table_z,
        load_sems,
        keep_sems,
        send_sems,
        recv_sems,
        table_send,
        table_recv,
    ) = refs[2 * count + 2 :]
    place = Place()
    s, k, x, y = place.shard, place.core, place.x, place.y
    total = len(chunks)
    ring = Ring(send_sems, recv_sems)
    depth = 2

    def part_of(at, shard_slice, core):
        index, group, part = chunks[at]
        return partials[index].at[shard_slice, group, core, :, :, :, :, pl.ds(part * BLOCK, BLOCK)]

    def load(at):
        return pltpu.make_async_copy(
            part_of(at, slice(None), k), mine.at[at % 3], load_sems.at[at % 3]
        )

    copies = {}

    def go(at, name, position, source, target, device):
        slot = at * 14 + position
        copies.setdefault((at, name), []).append(ring.send(source, target, device, slot))

    def arrived(at, name):
        for copy in copies[(at, name)]:
            copy.wait_recv()

    def left(at, name):
        for copy in copies.pop((at, name), []):
            copy.wait_send()

    def stage_core(at):
        go(
            at,
            "core",
            0,
            part_of(at, slice(None), 1 - k),
            from_core.at[at % depth],
            place.across("core"),
        )

    def stage_first(at):
        slot = at % 3
        load(at).wait()
        arrived(at, "core")
        left(at, "core")

        @pl.loop(0, SHARDS)
        def _(shard):
            for h in range(2):
                for i in range(2):
                    for j in range(2):
                        mine[slot, shard, h, i, j] = (
                            mine[slot, shard, h, i, j].astype(jnp.float32)
                            + from_core[at % depth, shard, h, i, j].astype(jnp.float32)
                        ).astype(LOW)

        go(
            at,
            "first",
            1,
            mine.at[slot, :, 0, :, 1 - x],
            from_first.at[at % depth, 0],
            place.across("x"),
        )
        go(
            at,
            "first",
            2,
            mine.at[slot, :, 1, 1 - y],
            from_first.at[at % depth, 1],
            place.across("y"),
        )

    def stage_second(at):
        slot = at % 3
        arrived(at, "first")
        left(at, "first")

        @pl.loop(0, SHARDS)
        def _(shard):
            for i in range(2):
                mine[slot, shard, 0, i, x] = (
                    mine[slot, shard, 0, i, x].astype(jnp.float32)
                    + from_first[at % depth, 0, shard, i].astype(jnp.float32)
                ).astype(LOW)
                mine[slot, shard, 1, y, i] = (
                    mine[slot, shard, 1, y, i].astype(jnp.float32)
                    + from_first[at % depth, 1, shard, i].astype(jnp.float32)
                ).astype(LOW)

        go(
            at,
            "second",
            3,
            mine.at[slot, :, 0, 1 - y, x],
            from_second.at[at % depth, 0],
            place.across("y"),
        )
        go(
            at,
            "second",
            4,
            mine.at[slot, :, 1, y, 1 - x],
            from_second.at[at % depth, 1],
            place.across("x"),
        )

    def stage_z(at):
        slot = at % 3
        arrived(at, "second")
        left(at, "second")

        @pl.loop(0, SHARDS)
        def _(shard):
            for h in range(2):
                final[at % depth, shard, h] = (
                    mine[slot, shard, h, y, x].astype(jnp.float32)
                    + from_second[at % depth, h, shard].astype(jnp.float32)
                ).astype(LOW)

        if at + 3 < total:
            load(at + 3).start()
        for offset in range(1, SHARDS):
            target = lax.rem(s + offset, SHARDS)
            go(
                at,
                "z",
                5 + offset - 1,
                final.at[at % depth, target],
                from_z.at[at % depth, offset - 1],
                place.along(offset),
            )

    def done_at(at, *where):
        index, group, part = chunks[at]
        rest = where + (slice(None),) * (5 - len(where))
        return done.at[(at,) + rest]

    def stage_back(at):
        arrived(at, "z")
        left(at, "z")
        for h in range(2):
            value = final[at % depth, s, h].astype(jnp.float32)
            for offset in range(1, SHARDS):
                value = value + from_z[at % depth, offset - 1, h].astype(jnp.float32)
            done[at, k, h, y, x] = value.astype(LOW)
        ref = done_at(at, k, 0, y, x)
        go(at, "back", 8, ref, ref, place.across("y"))
        ref = done_at(at, k, 1, y, x)
        go(at, "back", 9, ref, ref, place.across("x"))

    def stage_wide(at):
        arrived(at, "back")
        ref = done_at(at, k, 0, slice(None), x)
        go(at, "wide", 10, ref, ref, place.across("x"))
        ref = done_at(at, k, 1, y)
        go(at, "wide", 11, ref, ref, place.across("y"))

    def stage_twin(at):
        arrived(at, "wide")
        ref = done_at(at, k)
        go(at, "twin", 12, ref, ref, place.across("core"))

    kept = []

    def stage_keep(at):
        arrived(at, "twin")
        index, group, part = chunks[at]
        copy = pltpu.make_async_copy(
            done.at[at],
            sums[index].at[group, :, :, :, :, :, pl.ds(part * BLOCK, BLOCK)],
            keep_sems.at[at],
        )
        copy.start()
        kept.append(copy)

    for at in range(min(3, total)):
        load(at).start()
    table_copy = pltpu.make_async_copy(table, table_own.at[0], table_send.at[0])
    table_copy.start()
    greet(place)
    table_copy.wait()

    def table_step(position, axis):
        copy = pltpu.make_async_remote_copy(
            src_ref=table_own.at[position],
            dst_ref=table_in.at[position],
            send_sem=table_send.at[1 + position],
            recv_sem=table_recv.at[position],
            device_id=place.across(axis),
            device_id_type=MESH,
        )
        copy.start()
        return copy

    table_copies = []

    def table_sum_step(position, axis):
        if position:
            table_copies[-1].wait_recv()
            table_own[position] = table_own[position - 1] + table_in[position - 1]
        if axis:
            table_copies.append(table_step(position, axis))

    def table_along():
        for offset in range(1, SHARDS):
            target = lax.rem(s + offset, SHARDS)
            copy = pltpu.make_async_remote_copy(
                src_ref=table_own.at[3, target],
                dst_ref=table_z.at[offset - 1],
                send_sem=table_send.at[3 + offset],
                recv_sem=table_recv.at[2 + offset],
                device_id=place.along(offset),
                device_id_type=MESH,
            )
            copy.start()
            table_copies.append(copy)

    def table_end():
        for copy in table_copies[3:]:
            copy.wait_recv()
        value = table_own[3, s]
        for offset in range(1, SHARDS):
            value = value + table_z[offset - 1]
        table_sum[...] = value

    stages = (
        stage_core,
        stage_first,
        stage_second,
        stage_z,
        stage_back,
        stage_wide,
        stage_twin,
        stage_keep,
    )
    for step in range(total + len(stages) - 1):
        for position in reversed(range(len(stages))):
            at = step - position
            if 0 <= at < total:
                stages[position](at)
        if step == 1:
            table_sum_step(0, "core")
        if step == 2:
            table_sum_step(1, "x")
        if step == 3:
            table_sum_step(2, "y")
        if step == 4:
            table_sum_step(3, None)
            table_along()
        if step == 5:
            table_end()
    for key in sorted(copies):
        for copy in copies[key]:
            copy.wait_send()
    for copy in table_copies:
        copy.wait_send()
    for copy in kept:
        copy.wait()


def reduce_gradients(partials, table):
    shapes = [matrix.shape for matrix in partials]
    chunks = chunk_list(shapes)
    total = len(chunks)
    width = table.shape[1] // SHARDS
    split = jnp.pad(table, ((0, 16 - table.shape[0]), (0, 0)))
    split = split.reshape(16, SHARDS, width).transpose(1, 0, 2)
    piece = (UNIT, BLOCK)
    outs = pl.pallas_call(
        functools.partial(reduce_kernel, chunks),
        out_shape=[
            jax.ShapeDtypeStruct((r // SHARDS // 256, 2, 2, 2, 2, UNIT, c), LOW) for r, c in shapes
        ]
        + [jax.ShapeDtypeStruct((16, width), jnp.float32)],
        in_specs=[ANY] * 6,
        out_specs=[ANY] * 5 + [pl.BlockSpec(memory_space=pltpu.VMEM)],
        scratch_shapes=[
            pltpu.VMEM((3, SHARDS, 2, 2, 2) + piece, LOW),
            pltpu.VMEM((2, SHARDS, 2, 2, 2) + piece, LOW),
            pltpu.VMEM((2, 2, SHARDS, 2) + piece, LOW),
            pltpu.VMEM((2, 2, SHARDS) + piece, LOW),
            pltpu.VMEM((2, SHARDS, 2) + piece, LOW),
            pltpu.VMEM((2, SHARDS - 1, 2) + piece, LOW),
            pltpu.VMEM((total, 2, 2, 2, 2) + piece, LOW),
            pltpu.VMEM((4, SHARDS, 16, width), jnp.float32),
            pltpu.VMEM((3, SHARDS, 16, width), jnp.float32),
            pltpu.VMEM((SHARDS - 1, 16, width), jnp.float32),
            pltpu.SemaphoreType.DMA((3,)),
            pltpu.SemaphoreType.DMA((total,)),
            pltpu.SemaphoreType.DMA((total * 14,)),
            pltpu.SemaphoreType.DMA((total * 14,)),
            pltpu.SemaphoreType.DMA((7,)),
            pltpu.SemaphoreType.DMA((6,)),
        ],
        compiler_params=pltpu.CompilerParams(
            collective_id=2, has_side_effects=True, vmem_limit_bytes=40 * 2**20
        ),
        name="reduce_gradients",
    )(*[folded(matrix) for matrix in partials], split)
    sums = [
        out.reshape(shape[0] // SHARDS, shape[1]) for out, shape in zip(outs[:5], shapes)
    ]
    return sums, outs[5][: table.shape[0]]


HEADS = 16
HEAD_DIM = 64


step_rate = 0.3


def normalize(stream, gain_row, bias_row):
    center = stream - jnp.mean(stream, -1, keepdims=True)
    spread = jnp.mean(center * center, -1, keepdims=True)
    return center * lax.rsqrt(spread + 1e-05) * gain_row + bias_row


def exact_gelu(inputs):
    return jax.nn.gelu(inputs, approximate=False)


def matmul(left, right):
    return jnp.dot(left, right, preferred_element_type=jnp.float32)


def row_sums(matrix):
    return jnp.sum(matrix, 0, dtype=jnp.float32)


def moment_step(gradient, moments):
    first_moment = 0.5 * moments[0] + 0.5 * gradient
    root_square = jnp.sqrt(0.5 * moments[1] * moments[1] + 0.5 * gradient * gradient)
    direction = first_moment / (root_square + 1e-06)
    return (jnp.stack([first_moment, root_square]), direction)


def to_heads(rows, sequences, portion, shards):
    parts = rows.shape[1] // (HEADS * HEAD_DIM)
    width = HEADS * HEAD_DIM // shards
    blocks = rows.reshape(sequences, portion, parts, shards, width).transpose(3, 0, 1, 2, 4)
    blocks = blocks.reshape(shards, sequences * portion, parts * width)
    blocks = lax.all_to_all(blocks, "shard", 0, 0, tiled=True)
    blocks = blocks.reshape(shards, sequences, portion, parts, width).transpose(1, 0, 2, 3, 4)
    return blocks.reshape(sequences, shards * portion, parts, width // HEAD_DIM, HEAD_DIM)


def to_tokens(blocks, sequences, portion, shards):
    parts = blocks.shape[2]
    width = HEADS * HEAD_DIM // shards
    rows = blocks.reshape(sequences, shards, portion, parts, width).transpose(1, 0, 2, 3, 4)
    rows = rows.reshape(shards, sequences * portion, parts * width)
    rows = lax.all_to_all(rows, "shard", 0, 0, tiled=True)
    rows = rows.reshape(shards, sequences * portion, parts, width).transpose(1, 2, 0, 3)
    return rows.reshape(sequences * portion, parts * shards * width)


def fits(shards, replicas, masters):
    return (
        shards == SHARDS
        and replicas == REPLICAS
        and all(m.shape[0] % 256 == 0 and m.shape[1] % BLOCK == 0 for m in masters)
    )


def gather_plain(masters):
    replicas, rep_index = lax.axis_size("rep"), lax.axis_index("rep")
    gathered = []
    for matrix in masters:
        height = matrix.shape[0] // replicas
        piece = lax.dynamic_slice_in_dim(matrix, rep_index * height, height, 0)
        gathered.append(lax.all_gather(piece.astype(LOW), ("shard", "rep"), axis=0, tiled=True))
    return gathered


def reduce_plain(partials, table):
    width = table.shape[1] // lax.axis_size("shard")
    table = lax.psum(table, ("rep", "shard"))
    table = lax.dynamic_slice_in_dim(table, lax.axis_index("shard") * width, width, 1)
    sums = []
    for partial in partials:
        piece = lax.psum_scatter(partial, ("shard", "rep"), scatter_dimension=0, tiled=True)
        sums.append(lax.all_gather(piece, "rep", axis=0, tiled=True))
    return sums, table


def on_device(
    hidden_in,
    skip_path,
    cotangent,
    skip_weight,
    heads_in,
    heads_out,
    expand_weight,
    reduce_weight,
    vectors,
    moments_skip,
    moments_in,
    moments_out,
    moments_expand,
    moments_reduce,
    moments_vectors,
):
    sequences, portion, model_width = hidden_in.shape
    shards = lax.axis_size("shard")
    replicas = lax.axis_size("rep")
    row_count = sequences * portion
    factor = 1.0 / math.sqrt(HEAD_DIM)
    masters = (skip_weight, heads_in, heads_out, expand_weight, reduce_weight, vectors)
    fast = fits(shards, replicas, masters[:5])
    gathered = gather_weights(masters[:5]) if fast else gather_plain(masters[:5])
    skip_matrix, in_matrix, out_matrix, expand_matrix, reduce_matrix = gathered
    table_low = lax.all_gather(vectors.astype(jnp.bfloat16), "shard", axis=1, tiled=True)
    table_rows = table_low.astype(jnp.float32)
    source = hidden_in.reshape(row_count, model_width)
    skip_rows = skip_path.reshape(row_count, model_width)
    joined = jnp.concatenate([source, skip_rows], 1)
    entering = matmul(joined, skip_matrix) + table_rows[0]
    normed_one, norm_back_one = jax.vjp(normalize, entering, table_rows[1], table_rows[2])
    first_in = normed_one.astype(jnp.bfloat16)
    triple = matmul(first_in, in_matrix).astype(jnp.bfloat16)
    heads = to_heads(triple, sequences, portion, shards)
    queries, keys_full, values_full = heads[:, :, 0], heads[:, :, 1], heads[:, :, 2]
    scores = (
        jnp.einsum("sqhd,skhd->shqk", queries, keys_full, preferred_element_type=jnp.float32)
        * factor
    )
    row_max = jnp.max(scores, -1)
    row_total = jnp.sum(jnp.exp(scores - row_max[..., None]), -1)
    log_total = row_max + jnp.log(row_total)
    probability = jnp.exp(scores - log_total[..., None])
    mixed = jnp.einsum(
        "shqk,skhd->sqhd",
        probability.astype(jnp.bfloat16),
        values_full,
        preferred_element_type=jnp.float32,
    )
    mixed_low = to_tokens(mixed.astype(jnp.bfloat16)[:, :, None], sequences, portion, shards)
    middle = entering + matmul(mixed_low, out_matrix) + table_rows[3]
    normed_two, norm_back_two = jax.vjp(normalize, middle, table_rows[4], table_rows[5])
    second_in = normed_two.astype(jnp.bfloat16)
    expanded = matmul(second_in, expand_matrix) + table_rows[7:].reshape(-1)
    activated, gelu_back = jax.vjp(exact_gelu, expanded)
    activated_low = activated.astype(jnp.bfloat16)
    block_result = middle + matmul(activated_low, reduce_matrix) + table_rows[6]
    block_out = block_result.astype(jnp.bfloat16).reshape(sequences, portion, model_width)
    grad_out = cotangent.reshape(row_count, model_width)
    grad_reduce = matmul(activated_low.T, grad_out)
    grad_act = matmul(grad_out, reduce_matrix.T)
    grad_inner = gelu_back(grad_act)[0].astype(jnp.bfloat16)
    grad_expand = matmul(second_in.T, grad_inner)
    grad_second = matmul(grad_inner, expand_matrix.T)
    grad_mid_norm, grad_gain_two, grad_bias_two = norm_back_two(grad_second)
    grad_middle = grad_out.astype(jnp.float32) + grad_mid_norm
    grad_middle_low = grad_middle.astype(jnp.bfloat16)
    grad_outw = matmul(mixed_low.T, grad_middle_low)
    grad_mixed = matmul(grad_middle_low, out_matrix.T).astype(jnp.bfloat16)
    grad_mixed = to_heads(grad_mixed, sequences, portion, shards)[:, :, 0]
    grad_prob = jnp.einsum(
        "sqhd,skhd->shqk", grad_mixed, values_full, preferred_element_type=jnp.float32
    )
    delta = jnp.sum(probability * grad_prob, -1)
    grad_scores = (probability * (grad_prob - delta[..., None])).astype(jnp.bfloat16)
    grad_query = (
        jnp.einsum("shqk,skhd->sqhd", grad_scores, keys_full, preferred_element_type=jnp.float32)
        * factor
    )
    grad_keys = (
        jnp.einsum("shqk,sqhd->skhd", grad_scores, queries, preferred_element_type=jnp.float32)
        * factor
    )
    grad_values = jnp.einsum(
        "shqk,sqhd->skhd",
        probability.astype(jnp.bfloat16),
        grad_mixed,
        preferred_element_type=jnp.float32,
    )
    grad_heads = jnp.stack([grad_query, grad_keys, grad_values], 2).astype(jnp.bfloat16)
    grad_triple = to_tokens(grad_heads, sequences, portion, shards)
    grad_inw = matmul(first_in.T, grad_triple)
    grad_first = matmul(grad_triple, in_matrix.T)
    grad_pre_norm, grad_gain_one, grad_bias_one = norm_back_one(grad_first)
    grad_entering = (grad_middle + grad_pre_norm).astype(jnp.bfloat16)
    grad_skipw = matmul(joined.T, grad_entering)
    grad_joined = matmul(grad_entering, skip_matrix.T)
    input_gradient = (
        grad_joined[:, :model_width].astype(jnp.bfloat16).reshape(sequences, portion, model_width)
    )
    skip_gradient = (
        grad_joined[:, model_width:].astype(jnp.bfloat16).reshape(sequences, portion, model_width)
    )
    grad_table = jnp.concatenate(
        [
            jnp.stack(
                [
                    row_sums(grad_entering),
                    grad_gain_one,
                    grad_bias_one,
                    row_sums(grad_middle_low),
                    grad_gain_two,
                    grad_bias_two,
                    row_sums(grad_out),
                ]
            ),
            row_sums(grad_inner).reshape(-1, model_width),
        ],
        0,
    )
    partials = [
        partial.astype(LOW)
        for partial in (grad_skipw, grad_inw, grad_outw, grad_expand, grad_reduce)
    ]
    reduce = reduce_gradients if fast else reduce_plain
    lows, vector_total = reduce(partials, grad_table)
    totals = [low.astype(jnp.float32) for low in lows]
    totals.append(vector_total)
    states = (
        moments_skip,
        moments_in,
        moments_out,
        moments_expand,
        moments_reduce,
        moments_vectors,
    )
    steps = [moment_step(total, state) for total, state in zip(totals, states)]
    squares = jnp.stack(
        [
            jnp.stack([jnp.sum(matrix * matrix) for matrix in masters]),
            jnp.stack([jnp.sum(direction * direction) for _, direction in steps]),
        ]
    )
    norms = jnp.sqrt(lax.psum(squares, "shard"))
    ratio = norms[0] / (norms[1] + 1e-06)
    updated = [
        masters[position] - step_rate * ratio[position] * steps[position][1]
        for position in range(6)
    ]
    return (
        block_out,
        input_gradient,
        skip_gradient,
        *totals,
        *(state for state, _ in steps),
        *updated,
        norms,
    )


def solution(mesh):
    placed = (
        P("rep", "shard", None),
        P("rep", "shard", None),
        P("rep", "shard", None),
        P("shard", None),
        P("shard", None),
        P("shard", None),
        P("shard", None),
        P("shard", None),
        P(None, "shard"),
        P(None, "shard", None),
        P(None, "shard", None),
        P(None, "shard", None),
        P(None, "shard", None),
        P(None, "shard", None),
        P(None, None, "shard"),
    )
    return jax.shard_map(
        on_device,
        mesh=mesh,
        in_specs=placed,
        out_specs=(
            P("rep", "shard", None),
            P("rep", "shard", None),
            P("rep", "shard", None),
            P("shard", None),
            P("shard", None),
            P("shard", None),
            P("shard", None),
            P("shard", None),
            P(None, "shard"),
            P(None, "shard", None),
            P(None, "shard", None),
            P(None, "shard", None),
            P(None, "shard", None),
            P(None, "shard", None),
            P(None, None, "shard"),
            P("shard", None),
            P("shard", None),
            P("shard", None),
            P("shard", None),
            P("shard", None),
            P(None, "shard"),
            P(),
        ),
        check_vma=False,
    )
```

```python
import functools
import math

import jax
import jax.numpy as jnp
from jax import lax
from jax.experimental import pallas as pl
from jax.experimental.pallas import tpu as pltpu
from jax.sharding import PartitionSpec as P

HEADS = 16
HEAD_DIM = 64
MESH = pl.DeviceIdType.MESH
LOW = jnp.bfloat16
ANY = pl.BlockSpec(memory_space=pl.ANY)
SHARDS, REPLICAS = 4, 8
UNIT = 16
BLOCK = 1024


class Place:
    def __init__(self):
        self.rep = lax.axis_index("rep")
        self.shard = lax.axis_index("shard")
        self.core = lax.rem(self.rep, 2)
        self.x = lax.rem(self.rep // 2, 2)
        self.y = self.rep // 4

    def across(self, axis):
        own, step = {"core": (self.core, 1), "x": (self.x, 2), "y": (self.y, 4)}[axis]
        return (self.rep + step - 2 * step * own, self.shard)

    def along(self, offset):
        return (self.rep, lax.rem(self.shard + offset, SHARDS))

    def source(self, offset):
        return lax.rem(self.shard + SHARDS - offset, SHARDS)

    def partners(self):
        return [self.across("core"), self.across("x"), self.across("y")] + [
            self.along(offset) for offset in range(1, SHARDS)
        ]


def greet(place):
    barrier = pltpu.get_barrier_semaphore()
    partners = place.partners()
    for partner in partners:
        pl.semaphore_signal(barrier, inc=1, device_id=partner, device_id_type=MESH)
    pl.semaphore_wait(barrier, len(partners))


def chunk_list(shapes):
    chunks = []
    for index, (rows, columns) in enumerate(shapes):
        for group in range(rows // SHARDS // 256):
            for part in range(columns // BLOCK):
                chunks.append((index, group, part))
    return chunks


def folded(matrix):
    rows, columns = matrix.shape
    groups = rows // (SHARDS * 256)
    return matrix.reshape(SHARDS, groups, 2, 2, 2, 2, UNIT, columns)


class Ring:
    def __init__(self, send_sems, recv_sems):
        self.send_sems, self.recv_sems = send_sems, recv_sems
        self.open = []

    def send(self, source, target, device, slot):
        copy = pltpu.make_async_remote_copy(
            src_ref=source,
            dst_ref=target,
            send_sem=self.send_sems.at[slot],
            recv_sem=self.recv_sems.at[slot],
            device_id=device,
            device_id_type=MESH,
        )
        copy.start()
        return copy


def gather_kernel(chunks, *refs):
    count = 5
    masters = refs[:count]
    wholes = refs[count : 2 * count]
    wide, own, load_sems, keep_sems, send_sems, recv_sems = refs[2 * count :]
    place = Place()
    s, k, x, y = place.shard, place.core, place.x, place.y
    total = len(chunks)
    ring = Ring(send_sems, recv_sems)

    def load(at):
        index, group, part = chunks[at]
        return pltpu.make_async_copy(
            masters[index].at[group, :, :, :, :, :, pl.ds(part * BLOCK, BLOCK)],
            wide.at[at % 2],
            load_sems.at[at % 2],
        )

    def whole(at, *where):
        index, group, part = chunks[at]
        shard, rest = where[0], where[1:]
        rest = rest + (slice(None),) * (5 - len(rest))
        return wholes[index].at[(shard, group) + rest + (pl.ds(part * BLOCK, BLOCK),)]

    sent = []
    arrivals = {}

    def go(at, name, position, source, target, device):
        slot = at * 18 + position
        copy = ring.send(source, target, device, slot)
        sent.append(copy)
        arrivals.setdefault((at, name), []).append(copy)

    def arrived(at, name):
        for copy in arrivals[(at, name)]:
            copy.wait_recv()

    load(0).start()
    load(1).start()
    greet(place)
    kept = []

    def stage_cast(at):
        load(at).wait()

        @pl.loop(0, 16)
        def _(row):
            a, b = row // 8, lax.rem(row // 4, 2)
            c, d = lax.rem(row // 2, 2), lax.rem(row, 2)
            own[at, a, b, c, d] = wide[at % 2, a, b, c, d].astype(LOW)

        if at + 2 < total:
            load(at + 2).start()
        copy = pltpu.make_async_copy(own.at[at], whole(at, s), keep_sems.at[at])
        copy.start()
        kept.append(copy)

    def stage_z(at):
        for offset in range(1, SHARDS):
            go(
                at,
                "z",
                offset - 1,
                own.at[at, k, :, y, x],
                whole(at, s, k, slice(None), y, x),
                place.along(offset),
            )

    def stage_first(at):
        arrived(at, "z")
        for offset in range(1, SHARDS):
            e = place.source(offset)
            ref = whole(at, e, k, 0, y, x)
            go(at, "first", 3 + 2 * (offset - 1), ref, ref, place.across("x"))
            ref = whole(at, e, k, 1, y, x)
            go(at, "first", 4 + 2 * (offset - 1), ref, ref, place.across("y"))

    def stage_second(at):
        arrived(at, "first")
        for offset in range(1, SHARDS):
            e = place.source(offset)
            ref = whole(at, e, k, 0, y)
            go(at, "second", 9 + 2 * (offset - 1), ref, ref, place.across("y"))
            ref = whole(at, e, k, 1, slice(None), x)
            go(at, "second", 10 + 2 * (offset - 1), ref, ref, place.across("x"))

    def stage_core(at):
        arrived(at, "second")
        for offset in range(1, SHARDS):
            e = place.source(offset)
            ref = whole(at, e, k)
            go(at, "core", 15 + offset - 1, ref, ref, place.across("core"))

    def stage_end(at):
        arrived(at, "core")

    stages = (stage_z, stage_first, stage_second, stage_core, stage_end)
    lead = 4
    for at in range(min(lead, total)):
        stage_cast(at)
        stage_z(at)
    for step in range(total + 4):
        for position in range(1, 5):
            at = step - (position - 1)
            if 0 <= at < total:
                stages[position](at)
        if step + lead < total:
            stage_cast(step + lead)
            stage_z(step + lead)
    for copy in sent:
        copy.wait_send()
    for copy in kept:
        copy.wait()


def gather_weights(masters):
    shapes = [(matrix.shape[0] * SHARDS, matrix.shape[1]) for matrix in masters]
    chunks = chunk_list(shapes)
    total = len(chunks)
    own = [
        matrix.reshape(matrix.shape[0] // 256, 2, 2, 2, 2, UNIT, matrix.shape[1])
        for matrix in masters
    ]
    outs = pl.pallas_call(
        functools.partial(gather_kernel, chunks),
        out_shape=[
            jax.ShapeDtypeStruct((SHARDS, r // SHARDS // 256, 2, 2, 2, 2, UNIT, c), LOW)
            for r, c in shapes
        ],
        in_specs=[ANY] * 5,
        out_specs=[ANY] * 5,
        scratch_shapes=[
            pltpu.VMEM((2, 2, 2, 2, 2, UNIT, BLOCK), jnp.float32),
            pltpu.VMEM((total, 2, 2, 2, 2, UNIT, BLOCK), LOW),
            pltpu.SemaphoreType.DMA((2,)),
            pltpu.SemaphoreType.DMA((total,)),
            pltpu.SemaphoreType.DMA((total * 18,)),
            pltpu.SemaphoreType.DMA((total * 18,)),
        ],
        compiler_params=pltpu.CompilerParams(
            collective_id=1, has_side_effects=True, vmem_limit_bytes=40 * 2**20
        ),
        name="gather_weights",
    )(*own)
    return [out.reshape(shape) for out, shape in zip(outs, shapes)]


def add_into(target, source, height):
    @pl.loop(0, height)
    def _(row):
        target[row] = (target[row].astype(jnp.float32) + source[row].astype(jnp.float32)).astype(
            LOW
        )


def reduce_kernel(chunks, *refs):
    count = 5
    partials = refs[:count]
    table = refs[count]
    sums = refs[count + 1 : 2 * count + 1]
    table_sum = refs[2 * count + 1]
    (
        mine,
        from_core,
        from_first,
        from_second,
        final,
        from_z,
        done,
        table_own,
        table_in,
        table_z,
        load_sems,
        keep_sems,
        send_sems,
        recv_sems,
        table_send,
        table_recv,
    ) = refs[2 * count + 2 :]
    place = Place()
    s, k, x, y = place.shard, place.core, place.x, place.y
    total = len(chunks)
    ring = Ring(send_sems, recv_sems)
    depth = 2

    def part_of(at, shard_slice, core):
        index, group, part = chunks[at]
        return partials[index].at[shard_slice, group, core, :, :, :, :, pl.ds(part * BLOCK, BLOCK)]

    def load(at):
        return pltpu.make_async_copy(
            part_of(at, slice(None), k), mine.at[at % 3], load_sems.at[at % 3]
        )

    copies = {}

    def go(at, name, position, source, target, device):
        slot = at * 14 + position
        copies.setdefault((at, name), []).append(ring.send(source, target, device, slot))

    def arrived(at, name):
        for copy in copies[(at, name)]:
            copy.wait_recv()

    def left(at, name):
        for copy in copies.pop((at, name), []):
            copy.wait_send()

    def stage_core(at):
        go(
            at,
            "core",
            0,
            part_of(at, slice(None), 1 - k),
            from_core.at[at % depth],
            place.across("core"),
        )

    def stage_first(at):
        slot = at % 3
        load(at).wait()
        arrived(at, "core")
        left(at, "core")

        @pl.loop(0, SHARDS)
        def _(shard):
            for h in range(2):
                for i in range(2):
                    for j in range(2):
                        mine[slot, shard, h, i, j] = (
                            mine[slot, shard, h, i, j].astype(jnp.float32)
                            + from_core[at % depth, shard, h, i, j].astype(jnp.float32)
                        ).astype(LOW)

        go(
            at,
            "first",
            1,
            mine.at[slot, :, 0, :, 1 - x],
            from_first.at[at % depth, 0],
            place.across("x"),
        )
        go(
            at,
            "first",
            2,
            mine.at[slot, :, 1, 1 - y],
            from_first.at[at % depth, 1],
            place.across("y"),
        )

    def stage_second(at):
        slot = at % 3
        arrived(at, "first")
        left(at, "first")

        @pl.loop(0, SHARDS)
        def _(shard):
            for i in range(2):
                mine[slot, shard, 0, i, x] = (
                    mine[slot, shard, 0, i, x].astype(jnp.float32)
                    + from_first[at % depth, 0, shard, i].astype(jnp.float32)
                ).astype(LOW)
                mine[slot, shard, 1, y, i] = (
                    mine[slot, shard, 1, y, i].astype(jnp.float32)
                    + from_first[at % depth, 1, shard, i].astype(jnp.float32)
                ).astype(LOW)

        go(
            at,
            "second",
            3,
            mine.at[slot, :, 0, 1 - y, x],
            from_second.at[at % depth, 0],
            place.across("y"),
        )
        go(
            at,
            "second",
            4,
            mine.at[slot, :, 1, y, 1 - x],
            from_second.at[at % depth, 1],
            place.across("x"),
        )

    def stage_z(at):
        slot = at % 3
        arrived(at, "second")
        left(at, "second")

        @pl.loop(0, SHARDS)
        def _(shard):
            for h in range(2):
                final[at % depth, shard, h] = (
                    mine[slot, shard, h, y, x].astype(jnp.float32)
                    + from_second[at % depth, h, shard].astype(jnp.float32)
                ).astype(LOW)

        if at + 3 < total:
            load(at + 3).start()
        for offset in range(1, SHARDS):
            target = lax.rem(s + offset, SHARDS)
            go(
                at,
                "z",
                5 + offset - 1,
                final.at[at % depth, target],
                from_z.at[at % depth, offset - 1],
                place.along(offset),
            )

    def done_at(at, *where):
        index, group, part = chunks[at]
        rest = where + (slice(None),) * (5 - len(where))
        return done.at[(at,) + rest]

    def stage_back(at):
        arrived(at, "z")
        left(at, "z")
        for h in range(2):
            value = final[at % depth, s, h].astype(jnp.float32)
            for offset in range(1, SHARDS):
                value = value + from_z[at % depth, offset - 1, h].astype(jnp.float32)
            done[at, k, h, y, x] = value.astype(LOW)
        ref = done_at(at, k, 0, y, x)
        go(at, "back", 8, ref, ref, place.across("y"))
        ref = done_at(at, k, 1, y, x)
        go(at, "back", 9, ref, ref, place.across("x"))

    def stage_wide(at):
        arrived(at, "back")
        ref = done_at(at, k, 0, slice(None), x)
        go(at, "wide", 10, ref, ref, place.across("x"))
        ref = done_at(at, k, 1, y)
        go(at, "wide", 11, ref, ref, place.across("y"))

    def stage_twin(at):
        arrived(at, "wide")
        ref = done_at(at, k)
        go(at, "twin", 12, ref, ref, place.across("core"))

    kept = []

    def stage_keep(at):
        arrived(at, "twin")
        index, group, part = chunks[at]
        copy = pltpu.make_async_copy(
            done.at[at],
            sums[index].at[group, :, :, :, :, :, pl.ds(part * BLOCK, BLOCK)],
            keep_sems.at[at],
        )
        copy.start()
        kept.append(copy)

    for at in range(min(3, total)):
        load(at).start()
    table_copy = pltpu.make_async_copy(table, table_own.at[0], table_send.at[0])
    table_copy.start()
    greet(place)
    table_copy.wait()

    def table_step(position, axis):
        copy = pltpu.make_async_remote_copy(
            src_ref=table_own.at[position],
            dst_ref=table_in.at[position],
            send_sem=table_send.at[1 + position],
            recv_sem=table_recv.at[position],
            device_id=place.across(axis),
            device_id_type=MESH,
        )
        copy.start()
        return copy

    table_copies = []

    def table_sum_step(position, axis):
        if position:
            table_copies[-1].wait_recv()
            table_own[position] = table_own[position - 1] + table_in[position - 1]
        if axis:
            table_copies.append(table_step(position, axis))

    def table_along():
        for offset in range(1, SHARDS):
            target = lax.rem(s + offset, SHARDS)
            copy = pltpu.make_async_remote_copy(
                src_ref=table_own.at[3, target],
                dst_ref=table_z.at[offset - 1],
                send_sem=table_send.at[3 + offset],
                recv_sem=table_recv.at[2 + offset],
                device_id=place.along(offset),
                device_id_type=MESH,
            )
            copy.start()
            table_copies.append(copy)

    def table_end():
        for copy in table_copies[3:]:
            copy.wait_recv()
        value = table_own[3, s]
        for offset in range(1, SHARDS):
            value = value + table_z[offset - 1]
        table_sum[...] = value

    stages = (
        stage_core,
        stage_first,
        stage_second,
        stage_z,
        stage_back,
        stage_wide,
        stage_twin,
        stage_keep,
    )
    for step in range(total + len(stages) - 1):
        for position in reversed(range(len(stages))):
            at = step - position
            if 0 <= at < total:
                stages[position](at)
        if step == 1:
            table_sum_step(0, "core")
        if step == 2:
            table_sum_step(1, "x")
        if step == 3:
            table_sum_step(2, "y")
        if step == 4:
            table_sum_step(3, None)
            table_along()
        if step == 5:
            table_end()
    for key in sorted(copies):
        for copy in copies[key]:
            copy.wait_send()
    for copy in table_copies:
        copy.wait_send()
    for copy in kept:
        copy.wait()


def reduce_gradients(partials, table):
    shapes = [matrix.shape for matrix in partials]
    chunks = chunk_list(shapes)
    total = len(chunks)
    width = table.shape[1] // SHARDS
    split = jnp.pad(table, ((0, 16 - table.shape[0]), (0, 0)))
    split = split.reshape(16, SHARDS, width).transpose(1, 0, 2)
    piece = (UNIT, BLOCK)
    outs = pl.pallas_call(
        functools.partial(reduce_kernel, chunks),
        out_shape=[
            jax.ShapeDtypeStruct((r // SHARDS // 256, 2, 2, 2, 2, UNIT, c), LOW) for r, c in shapes
        ]
        + [jax.ShapeDtypeStruct((16, width), jnp.float32)],
        in_specs=[ANY] * 6,
        out_specs=[ANY] * 5 + [pl.BlockSpec(memory_space=pltpu.VMEM)],
        scratch_shapes=[
            pltpu.VMEM((3, SHARDS, 2, 2, 2) + piece, LOW),
            pltpu.VMEM((2, SHARDS, 2, 2, 2) + piece, LOW),
            pltpu.VMEM((2, 2, SHARDS, 2) + piece, LOW),
            pltpu.VMEM((2, 2, SHARDS) + piece, LOW),
            pltpu.VMEM((2, SHARDS, 2) + piece, LOW),
            pltpu.VMEM((2, SHARDS - 1, 2) + piece, LOW),
            pltpu.VMEM((total, 2, 2, 2, 2) + piece, LOW),
            pltpu.VMEM((4, SHARDS, 16, width), jnp.float32),
            pltpu.VMEM((3, SHARDS, 16, width), jnp.float32),
            pltpu.VMEM((SHARDS - 1, 16, width), jnp.float32),
            pltpu.SemaphoreType.DMA((3,)),
            pltpu.SemaphoreType.DMA((total,)),
            pltpu.SemaphoreType.DMA((total * 14,)),
            pltpu.SemaphoreType.DMA((total * 14,)),
            pltpu.SemaphoreType.DMA((7,)),
            pltpu.SemaphoreType.DMA((6,)),
        ],
        compiler_params=pltpu.CompilerParams(
            collective_id=2, has_side_effects=True, vmem_limit_bytes=40 * 2**20
        ),
        name="reduce_gradients",
    )(*[folded(matrix) for matrix in partials], split)
    sums = [
        out.reshape(shape[0] // SHARDS, shape[1]) for out, shape in zip(outs[:5], shapes)
    ]
    return sums, outs[5][: table.shape[0]]


step_rate = 0.3


def normalize(stream, gain_row, bias_row):
    center = stream - jnp.mean(stream, -1, keepdims=True)
    spread = jnp.mean(center * center, -1, keepdims=True)
    return center * lax.rsqrt(spread + 1e-05) * gain_row + bias_row


def exact_gelu(inputs):
    return jax.nn.gelu(inputs, approximate=False)


def matmul(left, right):
    return jnp.dot(left, right, preferred_element_type=jnp.float32)


def row_sums(matrix):
    return jnp.sum(matrix, 0, dtype=jnp.float32)


def moment_step(gradient, moments):
    first_moment = 0.5 * moments[0] + 0.5 * gradient
    root_square = jnp.sqrt(0.5 * moments[1] * moments[1] + 0.5 * gradient * gradient)
    direction = first_moment / (root_square + 1e-06)
    return (jnp.stack([first_moment, root_square]), direction)


def to_heads(rows, sequences, portion, shards):
    parts = rows.shape[1] // (HEADS * HEAD_DIM)
    width = HEADS * HEAD_DIM // shards
    blocks = rows.reshape(sequences, portion, parts, shards, width).transpose(3, 0, 1, 2, 4)
    blocks = blocks.reshape(shards, sequences * portion, parts * width)
    blocks = lax.all_to_all(blocks, "shard", 0, 0, tiled=True)
    blocks = blocks.reshape(shards, sequences, portion, parts, width).transpose(1, 0, 2, 3, 4)
    return blocks.reshape(sequences, shards * portion, parts, width // HEAD_DIM, HEAD_DIM)


def to_tokens(blocks, sequences, portion, shards):
    parts = blocks.shape[2]
    width = HEADS * HEAD_DIM // shards
    rows = blocks.reshape(sequences, shards, portion, parts, width).transpose(1, 0, 2, 3, 4)
    rows = rows.reshape(shards, sequences * portion, parts * width)
    rows = lax.all_to_all(rows, "shard", 0, 0, tiled=True)
    rows = rows.reshape(shards, sequences * portion, parts, width).transpose(1, 2, 0, 3)
    return rows.reshape(sequences * portion, parts * shards * width)


def weight_tile(whole, shard, group, start, width):
    return whole[shard, group, :, :, :, :, :, pl.ds(start, width)].reshape(256, width)


def product(left, whole, start, width):
    groups = whole.shape[1]
    total = None
    for shard in range(SHARDS):
        for group in range(groups):
            first = (shard * groups + group) * 256
            term = jnp.dot(
                left[:, first : first + 256],
                weight_tile(whole, shard, group, start, width),
                preferred_element_type=jnp.float32,
            )
            total = term if total is None else total + term
    return total


def contract(left, right, left_axis, right_axis):
    return lax.dot_general(
        left, right, (((left_axis,), (right_axis,)), ((), ())), preferred_element_type=jnp.float32
    )


def norm_rows(source, gain, bias, target, rows):
    @pl.loop(0, rows // 32)
    def _(block):
        where = pl.ds(pl.multiple_of(block * 32, 32), 32)
        stream = source[where, :]
        center = stream - jnp.mean(stream, -1, keepdims=True)
        spread = jnp.mean(center * center, -1, keepdims=True)
        target[where, :] = (center * lax.rsqrt(spread + 1e-05) * gain + bias).astype(LOW)


def forward_kernel(chunks, portion, *refs):
    joined, vectors = refs[0:2]
    masters = refs[2:7]
    keeps = refs[7:12]
    (entering, first_in, heads, log_total, mixed, middle, second_in, expanded, activated, out) = (
        refs[12:22]
    )
    wholes = refs[22:27]
    (
        wide,
        table_own,
        table_all,
        table,
        outgoing,
        answer,
        load_sems,
        keep_sems,
        send_sems,
        recv_sems,
        more_send,
        more_recv,
    ) = refs[27:]
    place = Place()
    s, k, x, y = place.shard, place.core, place.x, place.y
    total = len(chunks)
    rows = entering.shape[0]
    width = entering.shape[1]
    own = width // SHARDS
    factor = 1.0 / math.sqrt(HEAD_DIM)

    def load(at):
        index, group, part = chunks[at]
        return pltpu.make_async_copy(
            masters[index].at[group, :, :, :, :, :, pl.ds(part * BLOCK, BLOCK)],
            wide.at[at % 2],
            load_sems.at[at % 2],
        )

    def whole(at, shard, *rest):
        index, group, part = chunks[at]
        rest = rest + (slice(None),) * (5 - len(rest))
        return wholes[index].at[(shard, group) + rest + (pl.ds(part * BLOCK, BLOCK),)]

    sent = []
    arrivals = {}

    def go(at, name, position, ref, device):
        slot = at * 18 + position
        copy = pltpu.make_async_remote_copy(
            src_ref=ref,
            dst_ref=ref,
            send_sem=send_sems.at[slot],
            recv_sem=recv_sems.at[slot],
            device_id=device,
            device_id_type=MESH,
        )
        copy.start()
        sent.append(copy)
        arrivals.setdefault((at, name), []).append(copy)

    def arrived(at, name):
        for copy in arrivals[(at, name)]:
            copy.wait_recv()

    def extra(slot, source, target, device):
        copy = pltpu.make_async_remote_copy(
            src_ref=source,
            dst_ref=target,
            send_sem=more_send.at[slot],
            recv_sem=more_recv.at[slot],
            device_id=device,
            device_id_type=MESH,
        )
        copy.start()
        sent.append(copy)
        return copy

    kept = []

    def stage_cast(at):
        index, group, part = chunks[at]
        load(at).wait()

        @pl.loop(0, 16)
        def _(row):
            a, b = row // 8, lax.rem(row // 4, 2)
            c, d = lax.rem(row // 2, 2), lax.rem(row, 2)
            wholes[index][s, group, a, b, c, d, :, part * BLOCK : (part + 1) * BLOCK] = wide[
                at % 2, a, b, c, d
            ].astype(LOW)

        if at + 2 < total:
            load(at + 2).start()

    def stage_z(at):
        for offset in range(1, SHARDS):
            go(at, "z", offset - 1, whole(at, s, k, slice(None), y, x), place.along(offset))

    def stage_first(at):
        arrived(at, "z")
        for offset in range(1, SHARDS):
            e = place.source(offset)
            go(at, "first", 3 + 2 * (offset - 1), whole(at, e, k, 0, y, x), place.across("x"))
            go(at, "first", 4 + 2 * (offset - 1), whole(at, e, k, 1, y, x), place.across("y"))

    def stage_second(at):
        arrived(at, "first")
        for offset in range(1, SHARDS):
            e = place.source(offset)
            go(at, "second", 9 + 2 * (offset - 1), whole(at, e, k, 0, y), place.across("y"))
            ref = whole(at, e, k, 1, slice(None), x)
            go(at, "second", 10 + 2 * (offset - 1), ref, place.across("x"))

    def stage_core(at):
        arrived(at, "second")
        for offset in range(1, SHARDS):
            e = place.source(offset)
            go(at, "core", 15 + offset - 1, whole(at, e, k), place.across("core"))

    def stage_end(at):
        arrived(at, "core")
        index, group, part = chunks[at]
        copy = pltpu.make_async_copy(
            whole(at, slice(None)),
            keeps[index].at[:, group, :, :, :, :, :, pl.ds(part * BLOCK, BLOCK)],
            keep_sems.at[at],
        )
        copy.start()
        kept.append(copy)

    stages = (stage_z, stage_first, stage_second, stage_core, stage_end)
    lead = 4
    step_now = [0]

    def advance():
        step = step_now[0]
        if step >= total + 3:
            return False
        for position in range(1, 5):
            at = step - (position - 1)
            if 0 <= at < total:
                stages[position](at)
        if step + lead < total:
            stage_cast(step + lead)
            stage_z(step + lead)
        step_now[0] = step + 1
        return True

    def until(at):
        while step_now[0] - 4 < at:
            advance()

    load(0).start()
    load(1).start()
    table_own[...] = vectors[...].astype(LOW)
    table_all[0] = vectors[...].astype(LOW)
    greet(place)
    table_copies = []
    for at in range(min(lead, total)):
        stage_cast(at)
        stage_z(at)
        if at == 0:
            for offset in range(1, SHARDS):
                table_copies.append(
                    extra(offset - 1, table_own, table_all.at[offset], place.along(offset))
                )
    last = {}
    for at, (index, group, part) in enumerate(chunks):
        last[index] = at

    until(0)
    for copy in table_copies:
        copy.wait_recv()
    for offset in range(SHARDS):
        column = pl.multiple_of(place.source(offset) * own, own)
        table[:, pl.ds(column, own)] = table_all[offset].astype(jnp.float32)
    until(last[0])

    @pl.loop(0, width // 256)
    def _(part):
        start = pl.multiple_of(part * 256, 256)
        entering[:, pl.ds(start, 256)] = (
            product(joined, wholes[0], start, 256) + table[0:1, pl.ds(start, 256)]
        )

    norm_rows(entering, table[1:2, :], table[2:3, :], first_in, rows)
    until(last[1])
    live = lax.broadcasted_iota(jnp.int32, (rows, own), 0) < portion
    for kind in range(3):

        @pl.loop(0, SHARDS)
        def _(target):
            start = pl.multiple_of(kind * width + target * own, own)
            outgoing[target, :, kind * own : (kind + 1) * own] = jnp.where(
                live, product(first_in, wholes[1], start, own), 0.0
            ).astype(LOW)

    head_copies = []
    for offset in range(1, SHARDS):
        target = lax.rem(s + offset, SHARDS)
        head_copies.append(
            extra(
                2 + offset,
                outgoing.at[target],
                heads.at[pl.ds(offset * rows, rows), :],
                place.along(offset),
            )
        )

    @pl.loop(0, rows // 32)
    def _(block):
        where = pl.ds(pl.multiple_of(block * 32, 32), 32)
        heads[where, :] = outgoing[s, where, :]

    advance()
    advance()
    for copy in head_copies:
        copy.wait_recv()

    everyone = SHARDS * rows
    tile = 384
    lane = lax.broadcasted_iota(jnp.int32, (tile, 128), 1)
    key_row = lax.broadcasted_iota(jnp.int32, (everyone, tile), 0)
    for pair in range(own // 128):

        @pl.loop(0, everyone // tile)
        def _(block):
            start = pl.multiple_of(block * tile, 128)
            where = pl.ds(start, tile)
            query = heads[where, pair * 128 : (pair + 1) * 128]
            keys = heads[:, own + pair * 128 : own + (pair + 1) * 128]
            values = heads[:, 2 * own + pair * 128 : 2 * own + (pair + 1) * 128]
            parts = []
            for half in range(2):
                inside = (lane // 64) == half
                picked = jnp.where(inside, query.astype(jnp.float32) * factor, 0.0).astype(LOW)
                scores = contract(keys, picked, 1, 1)
                scores = jnp.where(lax.rem(key_row, rows) < portion, scores, -1e30)
                top = jnp.max(scores, 0, keepdims=True)
                weight = jnp.exp(scores - top)
                weight_sum = jnp.sum(weight, 0, keepdims=True)
                log_total[2 * pair + half : 2 * pair + half + 1, pl.ds(start, tile)] = (
                    top + jnp.log(weight_sum)
                )
                weight = (weight * (1.0 / weight_sum)).astype(LOW)
                summed = contract(values, weight, 0, 0)
                parts.append(summed[half * 64 : (half + 1) * 64])
            both = jnp.concatenate(parts, 0)
            answer[where, pair * 128 : (pair + 1) * 128] = both.T.astype(LOW)

        advance()

    answer_copies = []
    column = pl.multiple_of(s * own, own)
    for offset in range(1, SHARDS):
        answer_copies.append(
            extra(
                5 + offset,
                answer.at[pl.ds(offset * rows, rows), :],
                mixed.at[:, pl.ds(column, own)],
                (place.rep, place.source(offset)),
            )
        )
    mixed[:, pl.ds(column, own)] = answer[0:rows, :]
    until(last[2])
    for copy in answer_copies:
        copy.wait_recv()

    @pl.loop(0, width // 256)
    def _(part):
        start = pl.multiple_of(part * 256, 256)
        where = pl.ds(start, 256)
        middle[:, where] = (
            entering[:, where] + product(mixed, wholes[2], start, 256) + table[3:4, where]
        )

    norm_rows(middle, table[4:5, :], table[5:6, :], second_in, rows)
    per_row = width // 256
    for part in range(expanded.shape[1] // BLOCK):
        until(last[2] + 1 + part)

        @pl.loop(0, BLOCK // 256)
        def _(piece):
            start = pl.multiple_of(part * BLOCK + piece * 256, 256)
            bias_at = pl.multiple_of(piece * 256, 256)
            value = (
                product(second_in, wholes[3], start, 256)
                + table[7 + part : 8 + part, pl.ds(bias_at, 256)]
            )
            expanded[:, pl.ds(start, 256)] = value
            activated[:, pl.ds(start, 256)] = (
                value * (0.5 + 0.5 * lax.erf(value * math.sqrt(0.5)))
            ).astype(LOW)

    until(last[4])

    @pl.loop(0, width // 256)
    def _(part):
        start = pl.multiple_of(part * 256, 256)
        where = pl.ds(start, 256)
        out[:, where] = (
            middle[:, where] + product(activated, wholes[4], start, 256) + table[6:7, where]
        ).astype(LOW)

    for copy in sent:
        copy.wait_send()
    for copy in kept:
        copy.wait()


def forward_pass(joined, vectors, masters, portion):
    shapes = [(matrix.shape[0] * SHARDS, matrix.shape[1]) for matrix in masters]
    chunks = chunk_list(shapes)
    total = len(chunks)
    rows = joined.shape[0]
    width = joined.shape[1] // 2
    own = width // SHARDS
    hidden = shapes[3][1]
    everyone = SHARDS * rows
    split = [
        matrix.reshape(matrix.shape[0] // 256, 2, 2, 2, 2, UNIT, matrix.shape[1])
        for matrix in masters
    ]
    folds = [(SHARDS, r // SHARDS // 256, 2, 2, 2, 2, UNIT, c) for r, c in shapes]
    inner = pl.BlockSpec(memory_space=pltpu.VMEM)
    table = jnp.pad(vectors, ((0, 16 - vectors.shape[0]), (0, 0)))
    outs = pl.pallas_call(
        functools.partial(forward_kernel, chunks, portion),
        out_shape=[jax.ShapeDtypeStruct(fold, LOW) for fold in folds]
        + [
            jax.ShapeDtypeStruct((rows, width), jnp.float32),
            jax.ShapeDtypeStruct((rows, width), LOW),
            jax.ShapeDtypeStruct((everyone, 3 * own), LOW),
            jax.ShapeDtypeStruct((8, everyone), jnp.float32),
            jax.ShapeDtypeStruct((rows, width), LOW),
            jax.ShapeDtypeStruct((rows, width), jnp.float32),
            jax.ShapeDtypeStruct((rows, width), LOW),
            jax.ShapeDtypeStruct((rows, hidden), jnp.float32),
            jax.ShapeDtypeStruct((rows, hidden), LOW),
            jax.ShapeDtypeStruct((rows, width), LOW),
        ],
        in_specs=[inner] * 2 + [ANY] * 5,
        out_specs=[ANY] * 5 + [inner] * 10,
        scratch_shapes=[pltpu.VMEM(fold, LOW) for fold in folds]
        + [
            pltpu.VMEM((2, 2, 2, 2, 2, UNIT, BLOCK), jnp.float32),
            pltpu.VMEM((16, own), LOW),
            pltpu.VMEM((SHARDS, 16, own), LOW),
            pltpu.VMEM((16, width), jnp.float32),
            pltpu.VMEM((SHARDS, rows, 3 * own), LOW),
            pltpu.VMEM((everyone, own), LOW),
            pltpu.SemaphoreType.DMA((2,)),
            pltpu.SemaphoreType.DMA((total,)),
            pltpu.SemaphoreType.DMA((total * 18,)),
            pltpu.SemaphoreType.DMA((total * 18,)),
            pltpu.SemaphoreType.DMA((9,)),
            pltpu.SemaphoreType.DMA((9,)),
        ],
        compiler_params=pltpu.CompilerParams(
            collective_id=1, has_side_effects=True, vmem_limit_bytes=60 * 2**20
        ),
        name="forward_pass",
    )(joined, table, *split)
    weights = [out.reshape(shape) for out, shape in zip(outs[:5], shapes)]
    return weights, outs[5:]


def fits(shards, replicas, masters):
    return (
        shards == SHARDS
        and replicas == REPLICAS
        and all(m.shape[0] % 256 == 0 and m.shape[1] % BLOCK == 0 for m in masters)
    )


def gather_plain(masters):
    replicas, rep_index = lax.axis_size("rep"), lax.axis_index("rep")
    gathered = []
    for matrix in masters:
        height = matrix.shape[0] // replicas
        piece = lax.dynamic_slice_in_dim(matrix, rep_index * height, height, 0)
        gathered.append(lax.all_gather(piece.astype(LOW), ("shard", "rep"), axis=0, tiled=True))
    return gathered


def reduce_plain(partials, table):
    width = table.shape[1] // lax.axis_size("shard")
    table = lax.psum(table, ("rep", "shard"))
    table = lax.dynamic_slice_in_dim(table, lax.axis_index("shard") * width, width, 1)
    sums = []
    for partial in partials:
        piece = lax.psum_scatter(partial, ("shard", "rep"), scatter_dimension=0, tiled=True)
        sums.append(lax.all_gather(piece, "rep", axis=0, tiled=True))
    return sums, table


def on_device(
    hidden_in,
    skip_path,
    cotangent,
    skip_weight,
    heads_in,
    heads_out,
    expand_weight,
    reduce_weight,
    vectors,
    moments_skip,
    moments_in,
    moments_out,
    moments_expand,
    moments_reduce,
    moments_vectors,
):
    sequences, portion, model_width = hidden_in.shape
    shards = lax.axis_size("shard")
    replicas = lax.axis_size("rep")
    row_count = sequences * portion
    factor = 1.0 / math.sqrt(HEAD_DIM)
    masters = (skip_weight, heads_in, heads_out, expand_weight, reduce_weight, vectors)
    fast = sequences == 1 and fits(shards, replicas, masters[:5])
    joined = jnp.concatenate(
        [hidden_in.reshape(row_count, model_width), skip_path.reshape(row_count, model_width)], 1
    )
    if fast:
        padded = -(-portion // 32) * 32
        gathered, kept = forward_pass(
            jnp.pad(joined, ((0, padded - portion), (0, 0))), vectors, masters[:5], portion
        )
        entering, first_in, heads, log_total = kept[:4]
        mixed_low, middle, second_in, expanded, activated_low, block_out = [
            rows[:portion] for rows in kept[4:]
        ]
        entering, first_in = entering[:portion], first_in[:portion]
        block_out = block_out.reshape(sequences, portion, model_width)
        own = HEADS * HEAD_DIM // shards
        heads = heads.reshape(shards, padded, 3 * own)[:, :portion]
        order = lax.rem(lax.axis_index("shard") + shards - jnp.arange(shards), shards)
        heads = jnp.zeros_like(heads).at[order].set(heads)
        heads = heads.reshape(1, shards * portion, 3, own // HEAD_DIM, HEAD_DIM)
        queries, keys_full, values_full = heads[:, :, 0], heads[:, :, 1], heads[:, :, 2]
        log_total = log_total[: own // HEAD_DIM].reshape(-1, shards, padded)[:, :, :portion]
        log_total = jnp.zeros_like(log_total).at[:, order].set(log_total)
        log_total = log_total.reshape(1, -1, shards * portion)
        scores = (
            jnp.einsum("sqhd,skhd->shqk", queries, keys_full, preferred_element_type=jnp.float32)
            * factor
        )
        probability = jnp.exp(scores - log_total[..., None])
        table_low = lax.all_gather(vectors.astype(LOW), "shard", axis=1, tiled=True)
        table_rows = table_low.astype(jnp.float32)
        norm_back_one = jax.vjp(normalize, entering, table_rows[1], table_rows[2])[1]
        norm_back_two = jax.vjp(normalize, middle, table_rows[4], table_rows[5])[1]
        gelu_back = jax.vjp(exact_gelu, expanded)[1]
        skip_matrix, in_matrix, out_matrix, expand_matrix, reduce_matrix = gathered
    else:
        gathered = gather_plain(masters[:5])
        skip_matrix, in_matrix, out_matrix, expand_matrix, reduce_matrix = gathered
        table_low = lax.all_gather(vectors.astype(jnp.bfloat16), "shard", axis=1, tiled=True)
        table_rows = table_low.astype(jnp.float32)
        source = hidden_in.reshape(row_count, model_width)
        skip_rows = skip_path.reshape(row_count, model_width)
        joined = jnp.concatenate([source, skip_rows], 1)
        entering = matmul(joined, skip_matrix) + table_rows[0]
        normed_one, norm_back_one = jax.vjp(normalize, entering, table_rows[1], table_rows[2])
        first_in = normed_one.astype(jnp.bfloat16)
        triple = matmul(first_in, in_matrix).astype(jnp.bfloat16)
        heads = to_heads(triple, sequences, portion, shards)
        queries, keys_full, values_full = heads[:, :, 0], heads[:, :, 1], heads[:, :, 2]
        scores = (
            jnp.einsum("sqhd,skhd->shqk", queries, keys_full, preferred_element_type=jnp.float32)
            * factor
        )
        row_max = jnp.max(scores, -1)
        row_total = jnp.sum(jnp.exp(scores - row_max[..., None]), -1)
        log_total = row_max + jnp.log(row_total)
        probability = jnp.exp(scores - log_total[..., None])
        mixed = jnp.einsum(
            "shqk,skhd->sqhd",
            probability.astype(jnp.bfloat16),
            values_full,
            preferred_element_type=jnp.float32,
        )
        mixed_low = to_tokens(mixed.astype(jnp.bfloat16)[:, :, None], sequences, portion, shards)
        middle = entering + matmul(mixed_low, out_matrix) + table_rows[3]
        normed_two, norm_back_two = jax.vjp(normalize, middle, table_rows[4], table_rows[5])
        second_in = normed_two.astype(jnp.bfloat16)
        expanded = matmul(second_in, expand_matrix) + table_rows[7:].reshape(-1)
        activated, gelu_back = jax.vjp(exact_gelu, expanded)
        activated_low = activated.astype(jnp.bfloat16)
        block_result = middle + matmul(activated_low, reduce_matrix) + table_rows[6]
        block_out = block_result.astype(jnp.bfloat16).reshape(sequences, portion, model_width)
    grad_out = cotangent.reshape(row_count, model_width)
    grad_reduce = matmul(activated_low.T, grad_out)
    grad_act = matmul(grad_out, reduce_matrix.T)
    grad_inner = gelu_back(grad_act)[0].astype(jnp.bfloat16)
    grad_expand = matmul(second_in.T, grad_inner)
    grad_second = matmul(grad_inner, expand_matrix.T)
    grad_mid_norm, grad_gain_two, grad_bias_two = norm_back_two(grad_second)
    grad_middle = grad_out.astype(jnp.float32) + grad_mid_norm
    grad_middle_low = grad_middle.astype(jnp.bfloat16)
    grad_outw = matmul(mixed_low.T, grad_middle_low)
    grad_mixed = matmul(grad_middle_low, out_matrix.T).astype(jnp.bfloat16)
    grad_mixed = to_heads(grad_mixed, sequences, portion, shards)[:, :, 0]
    grad_prob = jnp.einsum(
        "sqhd,skhd->shqk", grad_mixed, values_full, preferred_element_type=jnp.float32
    )
    delta = jnp.sum(probability * grad_prob, -1)
    grad_scores = (probability * (grad_prob - delta[..., None])).astype(jnp.bfloat16)
    grad_query = (
        jnp.einsum("shqk,skhd->sqhd", grad_scores, keys_full, preferred_element_type=jnp.float32)
        * factor
    )
    grad_keys = (
        jnp.einsum("shqk,sqhd->skhd", grad_scores, queries, preferred_element_type=jnp.float32)
        * factor
    )
    grad_values = jnp.einsum(
        "shqk,sqhd->skhd",
        probability.astype(jnp.bfloat16),
        grad_mixed,
        preferred_element_type=jnp.float32,
    )
    grad_heads = jnp.stack([grad_query, grad_keys, grad_values], 2).astype(jnp.bfloat16)
    grad_triple = to_tokens(grad_heads, sequences, portion, shards)
    grad_inw = matmul(first_in.T, grad_triple)
    grad_first = matmul(grad_triple, in_matrix.T)
    grad_pre_norm, grad_gain_one, grad_bias_one = norm_back_one(grad_first)
    grad_entering = (grad_middle + grad_pre_norm).astype(jnp.bfloat16)
    grad_skipw = matmul(joined.T, grad_entering)
    grad_joined = matmul(grad_entering, skip_matrix.T)
    input_gradient = (
        grad_joined[:, :model_width].astype(jnp.bfloat16).reshape(sequences, portion, model_width)
    )
    skip_gradient = (
        grad_joined[:, model_width:].astype(jnp.bfloat16).reshape(sequences, portion, model_width)
    )
    grad_table = jnp.concatenate(
        [
            jnp.stack(
                [
                    row_sums(grad_entering),
                    grad_gain_one,
                    grad_bias_one,
                    row_sums(grad_middle_low),
                    grad_gain_two,
                    grad_bias_two,
                    row_sums(grad_out),
                ]
            ),
            row_sums(grad_inner).reshape(-1, model_width),
        ],
        0,
    )
    partials = [
        partial.astype(LOW)
        for partial in (grad_skipw, grad_inw, grad_outw, grad_expand, grad_reduce)
    ]
    reduce = reduce_gradients if fast else reduce_plain
    lows, vector_total = reduce(partials, grad_table)
    totals = [low.astype(jnp.float32) for low in lows]
    totals.append(vector_total)
    states = (
        moments_skip,
        moments_in,
        moments_out,
        moments_expand,
        moments_reduce,
        moments_vectors,
    )
    steps = [moment_step(total, state) for total, state in zip(totals, states)]
    squares = jnp.stack(
        [
            jnp.stack([jnp.sum(matrix * matrix) for matrix in masters]),
            jnp.stack([jnp.sum(direction * direction) for _, direction in steps]),
        ]
    )
    norms = jnp.sqrt(lax.psum(squares, "shard"))
    ratio = norms[0] / (norms[1] + 1e-06)
    updated = [
        masters[position] - step_rate * ratio[position] * steps[position][1]
        for position in range(6)
    ]
    return (
        block_out,
        input_gradient,
        skip_gradient,
        *totals,
        *(state for state, _ in steps),
        *updated,
        norms,
    )


def solution(mesh):
    placed = (
        P("rep", "shard", None),
        P("rep", "shard", None),
        P("rep", "shard", None),
        P("shard", None),
        P("shard", None),
        P("shard", None),
        P("shard", None),
        P("shard", None),
        P(None, "shard"),
        P(None, "shard", None),
        P(None, "shard", None),
        P(None, "shard", None),
        P(None, "shard", None),
        P(None, "shard", None),
        P(None, None, "shard"),
    )
    return jax.shard_map(
        on_device,
        mesh=mesh,
        in_specs=placed,
        out_specs=(
            P("rep", "shard", None),
            P("rep", "shard", None),
            P("rep", "shard", None),
            P("shard", None),
            P("shard", None),
            P("shard", None),
            P("shard", None),
            P("shard", None),
            P(None, "shard"),
            P(None, "shard", None),
            P(None, "shard", None),
            P(None, "shard", None),
            P(None, "shard", None),
            P(None, "shard", None),
            P(None, None, "shard"),
            P("shard", None),
            P("shard", None),
            P("shard", None),
            P("shard", None),
            P("shard", None),
            P(None, "shard"),
            P(),
        ),
        check_vma=False,
    )
```

```python
import functools
import math

import jax
import jax.numpy as jnp
from jax import lax
from jax.experimental import pallas as pl
from jax.experimental.pallas import tpu as pltpu
from jax.sharding import PartitionSpec as P

HEADS = 16
HEAD_DIM = 64
MESH = pl.DeviceIdType.MESH
LOW = jnp.bfloat16
ANY = pl.BlockSpec(memory_space=pl.ANY)
SHARDS, REPLICAS = 4, 8
UNIT = 16
BLOCK = 1024


class Place:
    def __init__(self):
        self.rep = lax.axis_index("rep")
        self.shard = lax.axis_index("shard")
        self.core = lax.rem(self.rep, 2)
        self.x = lax.rem(self.rep // 2, 2)
        self.y = self.rep // 4

    def across(self, axis):
        own, step = {"core": (self.core, 1), "x": (self.x, 2), "y": (self.y, 4)}[axis]
        return (self.rep + step - 2 * step * own, self.shard)

    def along(self, offset):
        return (self.rep, lax.rem(self.shard + offset, SHARDS))

    def source(self, offset):
        return lax.rem(self.shard + SHARDS - offset, SHARDS)

    def partners(self):
        return [self.across("core"), self.across("x"), self.across("y")] + [
            self.along(offset) for offset in range(1, SHARDS)
        ]


def greet(place):
    barrier = pltpu.get_barrier_semaphore()
    partners = place.partners()
    for partner in partners:
        pl.semaphore_signal(barrier, inc=1, device_id=partner, device_id_type=MESH)
    pl.semaphore_wait(barrier, len(partners))


def chunk_list(shapes):
    chunks = []
    for index, (rows, columns) in enumerate(shapes):
        for group in range(rows // SHARDS // 256):
            for part in range(columns // BLOCK):
                chunks.append((index, group, part))
    return chunks


step_rate = 0.3


def normalize(stream, gain_row, bias_row):
    center = stream - jnp.mean(stream, -1, keepdims=True)
    spread = jnp.mean(center * center, -1, keepdims=True)
    return center * lax.rsqrt(spread + 1e-05) * gain_row + bias_row


def exact_gelu(inputs):
    return jax.nn.gelu(inputs, approximate=False)


def matmul(left, right):
    return jnp.dot(left, right, preferred_element_type=jnp.float32)


def row_sums(matrix):
    return jnp.sum(matrix, 0, dtype=jnp.float32)


def moment_step(gradient, moments):
    first_moment = 0.5 * moments[0] + 0.5 * gradient
    root_square = jnp.sqrt(0.5 * moments[1] * moments[1] + 0.5 * gradient * gradient)
    direction = first_moment / (root_square + 1e-06)
    return (jnp.stack([first_moment, root_square]), direction)


def to_heads(rows, sequences, portion, shards):
    parts = rows.shape[1] // (HEADS * HEAD_DIM)
    width = HEADS * HEAD_DIM // shards
    blocks = rows.reshape(sequences, portion, parts, shards, width).transpose(3, 0, 1, 2, 4)
    blocks = blocks.reshape(shards, sequences * portion, parts * width)
    blocks = lax.all_to_all(blocks, "shard", 0, 0, tiled=True)
    blocks = blocks.reshape(shards, sequences, portion, parts, width).transpose(1, 0, 2, 3, 4)
    return blocks.reshape(sequences, shards * portion, parts, width // HEAD_DIM, HEAD_DIM)


def to_tokens(blocks, sequences, portion, shards):
    parts = blocks.shape[2]
    width = HEADS * HEAD_DIM // shards
    rows = blocks.reshape(sequences, shards, portion, parts, width).transpose(1, 0, 2, 3, 4)
    rows = rows.reshape(shards, sequences * portion, parts * width)
    rows = lax.all_to_all(rows, "shard", 0, 0, tiled=True)
    rows = rows.reshape(shards, sequences * portion, parts, width).transpose(1, 2, 0, 3)
    return rows.reshape(sequences * portion, parts * shards * width)


def weight_tile(whole, shard, group, start, width):
    return whole[shard, group, :, :, :, :, :, pl.ds(start, width)].reshape(256, width)


def product(left, whole, start, width):
    groups = whole.shape[1]
    total = None
    for shard in range(SHARDS):
        for group in range(groups):
            first = (shard * groups + group) * 256
            term = jnp.dot(
                left[:, first : first + 256],
                weight_tile(whole, shard, group, start, width),
                preferred_element_type=jnp.float32,
            )
            total = term if total is None else total + term
    return total


def contract(left, right, left_axis, right_axis):
    return lax.dot_general(
        left, right, (((left_axis,), (right_axis,)), ((), ())), preferred_element_type=jnp.float32
    )


def norm_rows(source, gain, bias, target, rows):
    @pl.loop(0, rows // 32)
    def _(block):
        where = pl.ds(pl.multiple_of(block * 32, 32), 32)
        stream = source[where, :]
        center = stream - jnp.mean(stream, -1, keepdims=True)
        spread = jnp.mean(center * center, -1, keepdims=True)
        target[where, :] = (center * lax.rsqrt(spread + 1e-05) * gain + bias).astype(LOW)


def forward_kernel(chunks, portion, *refs):
    joined, vectors = refs[0:2]
    masters = refs[2:7]
    keeps = refs[7:12]
    (
        entering,
        first_in,
        heads,
        log_total,
        mixed,
        middle,
        second_in,
        expanded,
        activated,
        out,
        table,
    ) = refs[12:23]
    wholes = refs[23:28]
    (
        wide,
        table_own,
        table_all,
        outgoing,
        answer,
        load_sems,
        keep_sems,
        send_sems,
        recv_sems,
        more_send,
        more_recv,
    ) = refs[28:]
    place = Place()
    s, k, x, y = place.shard, place.core, place.x, place.y
    total = len(chunks)
    rows = entering.shape[0]
    width = entering.shape[1]
    own = width // SHARDS
    factor = 1.0 / math.sqrt(HEAD_DIM)

    def load(at):
        index, group, part = chunks[at]
        return pltpu.make_async_copy(
            masters[index].at[group, :, :, :, :, :, pl.ds(part * BLOCK, BLOCK)],
            wide.at[at % 2],
            load_sems.at[at % 2],
        )

    def whole(at, shard, *rest):
        index, group, part = chunks[at]
        rest = rest + (slice(None),) * (5 - len(rest))
        return wholes[index].at[(shard, group) + rest + (pl.ds(part * BLOCK, BLOCK),)]

    sent = []
    arrivals = {}

    def go(at, name, position, ref, device):
        slot = at * 18 + position
        copy = pltpu.make_async_remote_copy(
            src_ref=ref,
            dst_ref=ref,
            send_sem=send_sems.at[slot],
            recv_sem=recv_sems.at[slot],
            device_id=device,
            device_id_type=MESH,
        )
        copy.start()
        sent.append(copy)
        arrivals.setdefault((at, name), []).append(copy)

    def arrived(at, name):
        for copy in arrivals[(at, name)]:
            copy.wait_recv()

    def extra(slot, source, target, device):
        copy = pltpu.make_async_remote_copy(
            src_ref=source,
            dst_ref=target,
            send_sem=more_send.at[slot],
            recv_sem=more_recv.at[slot],
            device_id=device,
            device_id_type=MESH,
        )
        copy.start()
        sent.append(copy)
        return copy

    kept = []

    def stage_cast(at):
        index, group, part = chunks[at]
        load(at).wait()

        @pl.loop(0, 16)
        def _(row):
            a, b = row // 8, lax.rem(row // 4, 2)
            c, d = lax.rem(row // 2, 2), lax.rem(row, 2)
            wholes[index][s, group, a, b, c, d, :, part * BLOCK : (part + 1) * BLOCK] = wide[
                at % 2, a, b, c, d
            ].astype(LOW)

        if at + 2 < total:
            load(at + 2).start()

    def stage_z(at):
        for offset in range(1, SHARDS):
            go(at, "z", offset - 1, whole(at, s, k, slice(None), y, x), place.along(offset))

    def stage_first(at):
        arrived(at, "z")
        for offset in range(1, SHARDS):
            e = place.source(offset)
            go(at, "first", 3 + 2 * (offset - 1), whole(at, e, k, 0, y, x), place.across("x"))
            go(at, "first", 4 + 2 * (offset - 1), whole(at, e, k, 1, y, x), place.across("y"))

    def stage_second(at):
        arrived(at, "first")
        for offset in range(1, SHARDS):
            e = place.source(offset)
            go(at, "second", 9 + 2 * (offset - 1), whole(at, e, k, 0, y), place.across("y"))
            ref = whole(at, e, k, 1, slice(None), x)
            go(at, "second", 10 + 2 * (offset - 1), ref, place.across("x"))

    def stage_core(at):
        arrived(at, "second")
        for offset in range(1, SHARDS):
            e = place.source(offset)
            go(at, "core", 15 + offset - 1, whole(at, e, k), place.across("core"))

    def stage_end(at):
        arrived(at, "core")
        index, group, part = chunks[at]
        copy = pltpu.make_async_copy(
            whole(at, slice(None)),
            keeps[index].at[:, group, :, :, :, :, :, pl.ds(part * BLOCK, BLOCK)],
            keep_sems.at[at],
        )
        copy.start()
        kept.append(copy)

    stages = (stage_z, stage_first, stage_second, stage_core, stage_end)
    lead = 4
    step_now = [0]

    def advance():
        step = step_now[0]
        if step >= total + 3:
            return False
        for position in range(1, 5):
            at = step - (position - 1)
            if 0 <= at < total:
                stages[position](at)
        if step + lead < total:
            stage_cast(step + lead)
            stage_z(step + lead)
        step_now[0] = step + 1
        return True

    def until(at):
        while step_now[0] - 4 < at:
            advance()

    load(0).start()
    load(1).start()
    table_own[...] = vectors[...].astype(LOW)
    table_all[0] = vectors[...].astype(LOW)
    greet(place)
    table_copies = []
    for at in range(min(lead, total)):
        stage_cast(at)
        stage_z(at)
        if at == 0:
            for offset in range(1, SHARDS):
                table_copies.append(
                    extra(offset - 1, table_own, table_all.at[offset], place.along(offset))
                )
    last = {}
    for at, (index, group, part) in enumerate(chunks):
        last[index] = at

    until(0)
    for copy in table_copies:
        copy.wait_recv()
    for offset in range(SHARDS):
        column = pl.multiple_of(place.source(offset) * own, own)
        table[:, pl.ds(column, own)] = table_all[offset].astype(jnp.float32)
    until(last[0])

    @pl.loop(0, width // 256)
    def _(part):
        start = pl.multiple_of(part * 256, 256)
        entering[:, pl.ds(start, 256)] = (
            product(joined, wholes[0], start, 256) + table[0:1, pl.ds(start, 256)]
        )

    norm_rows(entering, table[1:2, :], table[2:3, :], first_in, rows)
    until(last[1])
    live = lax.broadcasted_iota(jnp.int32, (rows, own), 0) < portion
    for kind in range(3):

        @pl.loop(0, SHARDS)
        def _(target):
            start = pl.multiple_of(kind * width + target * own, own)
            outgoing[target, :, kind * own : (kind + 1) * own] = jnp.where(
                live, product(first_in, wholes[1], start, own), 0.0
            ).astype(LOW)

    head_copies = []
    for offset in range(1, SHARDS):
        target = lax.rem(s + offset, SHARDS)
        head_copies.append(
            extra(
                2 + offset,
                outgoing.at[target],
                heads.at[pl.ds(offset * rows, rows), :],
                place.along(offset),
            )
        )

    @pl.loop(0, rows // 32)
    def _(block):
        where = pl.ds(pl.multiple_of(block * 32, 32), 32)
        heads[where, :] = outgoing[s, where, :]

    advance()
    advance()
    for copy in head_copies:
        copy.wait_recv()

    everyone = SHARDS * rows
    tile = 384
    lane = lax.broadcasted_iota(jnp.int32, (tile, 128), 1)
    key_row = lax.broadcasted_iota(jnp.int32, (everyone, tile), 0)
    for pair in range(own // 128):

        @pl.loop(0, everyone // tile)
        def _(block):
            start = pl.multiple_of(block * tile, 128)
            where = pl.ds(start, tile)
            query = heads[where, pair * 128 : (pair + 1) * 128]
            keys = heads[:, own + pair * 128 : own + (pair + 1) * 128]
            values = heads[:, 2 * own + pair * 128 : 2 * own + (pair + 1) * 128]
            parts = []
            for half in range(2):
                inside = (lane // 64) == half
                picked = jnp.where(inside, query.astype(jnp.float32) * factor, 0.0).astype(LOW)
                scores = contract(keys, picked, 1, 1)
                scores = jnp.where(lax.rem(key_row, rows) < portion, scores, -1e30)
                top = jnp.max(scores, 0, keepdims=True)
                weight = jnp.exp(scores - top)
                weight_sum = jnp.sum(weight, 0, keepdims=True)
                log_total[2 * pair + half : 2 * pair + half + 1, pl.ds(start, tile)] = (
                    top + jnp.log(weight_sum)
                )
                weight = (weight * (1.0 / weight_sum)).astype(LOW)
                summed = contract(values, weight, 0, 0)
                parts.append(summed[half * 64 : (half + 1) * 64])
            both = jnp.concatenate(parts, 0)
            answer[where, pair * 128 : (pair + 1) * 128] = both.T.astype(LOW)

        advance()

    answer_copies = []
    column = pl.multiple_of(s * own, own)
    for offset in range(1, SHARDS):
        answer_copies.append(
            extra(
                5 + offset,
                answer.at[pl.ds(offset * rows, rows), :],
                mixed.at[:, pl.ds(column, own)],
                (place.rep, place.source(offset)),
            )
        )
    mixed[:, pl.ds(column, own)] = answer[0:rows, :]
    until(last[2])
    for copy in answer_copies:
        copy.wait_recv()

    @pl.loop(0, width // 256)
    def _(part):
        start = pl.multiple_of(part * 256, 256)
        where = pl.ds(start, 256)
        middle[:, where] = (
            entering[:, where] + product(mixed, wholes[2], start, 256) + table[3:4, where]
        )

    norm_rows(middle, table[4:5, :], table[5:6, :], second_in, rows)
    per_row = width // 256
    for part in range(expanded.shape[1] // BLOCK):
        until(last[2] + 1 + part)

        @pl.loop(0, BLOCK // 256)
        def _(piece):
            start = pl.multiple_of(part * BLOCK + piece * 256, 256)
            bias_at = pl.multiple_of(piece * 256, 256)
            value = (
                product(second_in, wholes[3], start, 256)
                + table[7 + part : 8 + part, pl.ds(bias_at, 256)]
            )
            expanded[:, pl.ds(start, 256)] = value
            activated[:, pl.ds(start, 256)] = (
                value * (0.5 + 0.5 * lax.erf(value * math.sqrt(0.5)))
            ).astype(LOW)

    until(last[4])

    @pl.loop(0, width // 256)
    def _(part):
        start = pl.multiple_of(part * 256, 256)
        where = pl.ds(start, 256)
        out[:, where] = (
            middle[:, where] + product(activated, wholes[4], start, 256) + table[6:7, where]
        ).astype(LOW)

    for copy in sent:
        copy.wait_send()
    for copy in kept:
        copy.wait()


def forward_pass(joined, vectors, masters, portion):
    shapes = [(matrix.shape[0] * SHARDS, matrix.shape[1]) for matrix in masters]
    chunks = chunk_list(shapes)
    total = len(chunks)
    rows = joined.shape[0]
    width = joined.shape[1] // 2
    own = width // SHARDS
    hidden = shapes[3][1]
    everyone = SHARDS * rows
    split = [
        matrix.reshape(matrix.shape[0] // 256, 2, 2, 2, 2, UNIT, matrix.shape[1])
        for matrix in masters
    ]
    folds = [(SHARDS, r // SHARDS // 256, 2, 2, 2, 2, UNIT, c) for r, c in shapes]
    inner = pl.BlockSpec(memory_space=pltpu.VMEM)
    table = jnp.pad(vectors, ((0, 16 - vectors.shape[0]), (0, 0)))
    outs = pl.pallas_call(
        functools.partial(forward_kernel, chunks, portion),
        out_shape=[jax.ShapeDtypeStruct(fold, LOW) for fold in folds]
        + [
            jax.ShapeDtypeStruct((rows, width), jnp.float32),
            jax.ShapeDtypeStruct((rows, width), LOW),
            jax.ShapeDtypeStruct((everyone, 3 * own), LOW),
            jax.ShapeDtypeStruct((8, everyone), jnp.float32),
            jax.ShapeDtypeStruct((rows, width), LOW),
            jax.ShapeDtypeStruct((rows, width), jnp.float32),
            jax.ShapeDtypeStruct((rows, width), LOW),
            jax.ShapeDtypeStruct((rows, hidden), jnp.float32),
            jax.ShapeDtypeStruct((rows, hidden), LOW),
            jax.ShapeDtypeStruct((rows, width), LOW),
            jax.ShapeDtypeStruct((16, width), jnp.float32),
        ],
        in_specs=[inner] * 2 + [ANY] * 5,
        out_specs=[ANY] * 5 + [inner] * 11,
        scratch_shapes=[pltpu.VMEM(fold, LOW) for fold in folds]
        + [
            pltpu.VMEM((2, 2, 2, 2, 2, UNIT, BLOCK), jnp.float32),
            pltpu.VMEM((16, own), LOW),
            pltpu.VMEM((SHARDS, 16, own), LOW),
            pltpu.VMEM((SHARDS, rows, 3 * own), LOW),
            pltpu.VMEM((everyone, own), LOW),
            pltpu.SemaphoreType.DMA((2,)),
            pltpu.SemaphoreType.DMA((total,)),
            pltpu.SemaphoreType.DMA((total * 18,)),
            pltpu.SemaphoreType.DMA((total * 18,)),
            pltpu.SemaphoreType.DMA((9,)),
            pltpu.SemaphoreType.DMA((9,)),
        ],
        compiler_params=pltpu.CompilerParams(
            collective_id=1, has_side_effects=True, vmem_limit_bytes=60 * 2**20
        ),
        name="forward_pass",
    )(joined, table, *split)
    weights = [out.reshape(shape) for out, shape in zip(outs[:5], shapes)]
    return weights, outs[5:]


def norm_back(source, gain, incoming, residual, wide_out, low_out, rows):
    columns = source.shape[1]

    def body(block, carry):
        where = pl.ds(pl.multiple_of(block * 32, 32), 32)
        stream = source[where, :]
        center = stream - jnp.mean(stream, -1, keepdims=True)
        spread = jnp.mean(center * center, -1, keepdims=True)
        scale = lax.rsqrt(spread + 1e-05)
        hat = center * scale
        grad = incoming[where, :]
        scaled = grad * gain
        slope = scale * (
            scaled
            - jnp.mean(scaled, -1, keepdims=True)
            - hat * jnp.mean(scaled * hat, -1, keepdims=True)
        )
        value = residual[where, :].astype(jnp.float32) + slope
        low = value.astype(LOW)
        if wide_out is not None:
            wide_out[where, :] = value
        low_out[where, :] = low
        terms = (grad * hat, grad, low.astype(jnp.float32))
        return tuple(kept + jnp.sum(term, 0, keepdims=True) for kept, term in zip(carry, terms))

    zero = jnp.zeros((1, columns), jnp.float32)
    return lax.fori_loop(0, rows // 32, body, (zero, zero, zero))


def backward_kernel(chunks, portion, *refs):
    (
        cotangent,
        joined,
        vectors,
        entering,
        first_in,
        heads,
        log_total,
        mixed,
        middle,
        second_in,
        expanded,
        activated,
    ) = refs[:12]
    weights = refs[12:17]
    masters = refs[17:22]
    states = refs[22:27]
    own_vectors, own_states = refs[27:29]
    sums = refs[29:34]
    table_sum, norms, grad_joined = refs[34:37]
    (
        ring,
        theirs,
        mine,
        from_core,
        from_first,
        from_second,
        final,
        from_z,
        ready,
        state_in,
        master_in,
        squares,
        square_in,
        square_z,
        table_own,
        table_in,
        table_z,
        grad_inner,
        grad_second,
        grad_middle,
        grad_middle_low,
        outgoing,
        grad_mixed,
        grad_key,
        grad_value,
        grad_heads,
        grad_triple,
        grad_entering,
        ring_sems,
        state_sems,
        ready_sems,
        send_sems,
        recv_sems,
        more_send,
        more_recv,
    ) = refs[37:]
    place = Place()
    s, k, x, y = place.shard, place.core, place.x, place.y
    rows, width = entering.shape
    own = width // SHARDS
    factor = 1.0 / math.sqrt(HEAD_DIM)
    depth = ring.shape[0]

    def tiles(index):
        parts = weights[index].shape[7] // BLOCK
        return weights[index].shape[1], parts, SHARDS * weights[index].shape[1] * parts

    def fetch(index, at):
        groups, parts, _ = tiles(index)
        shard, rest = at // (groups * parts), lax.rem(at, groups * parts)
        group, part = rest // parts, lax.rem(rest, parts)
        start = pl.multiple_of(part * BLOCK, BLOCK)
        return pltpu.make_async_copy(
            weights[index].at[shard, group, :, :, :, :, :, pl.ds(start, BLOCK)],
            ring.at[lax.rem(at, depth)],
            ring_sems.at[lax.rem(at, depth)],
        )

    def prime(index):
        @pl.loop(0, min(depth, tiles(index)[2]))
        def _(at):
            fetch(index, at).start()

    def take(index, at):
        fetch(index, at).wait()
        return ring[lax.rem(at, depth)].reshape(256, BLOCK)

    def give(index, at):
        @pl.when(at + depth < tiles(index)[2])
        def _():
            fetch(index, at + depth).start()

    copies = {}

    def go(at, name, position, source, target, device):
        slot = at * 14 + position
        copy = pltpu.make_async_remote_copy(
            src_ref=source,
            dst_ref=target,
            send_sem=send_sems.at[slot],
            recv_sem=recv_sems.at[slot],
            device_id=device,
            device_id_type=MESH,
        )
        copy.start()
        copies.setdefault((at, name), []).append(copy)

    sent = []

    def extra(slot, source, target, device):
        copy = pltpu.make_async_remote_copy(
            src_ref=source,
            dst_ref=target,
            send_sem=more_send.at[slot],
            recv_sem=more_recv.at[slot],
            device_id=device,
            device_id_type=MESH,
        )
        copy.start()
        sent.append(copy)
        return copy

    def arrived(at, name):
        for copy in copies[(at, name)]:
            copy.wait_recv()

    def left(at, name):
        for copy in copies.pop((at, name), []):
            copy.wait_send()

    def gradient_half(at, core):
        index, group, part = chunks[at]
        lefts = (joined, first_in, mixed, second_in, activated)[index]
        pitch = lefts.shape[1] // SHARDS
        columns = [
            lefts[:, pl.ds(pl.multiple_of(shard * pitch + group * 256 + core * 128, 128), 128)]
            for shard in range(SHARDS)
        ]
        if index == 0:
            right = grad_entering[...]
        elif index == 1:
            right = jnp.concatenate(
                [grad_triple[shard, :, part * own : (part + 1) * own] for shard in range(SHARDS)],
                1,
            )
        elif index == 2:
            right = grad_middle_low[...]
        elif index == 3:
            right = grad_inner[:, part * BLOCK : (part + 1) * BLOCK]
        else:
            right = cotangent[...]
        return contract(jnp.concatenate(columns, 1), right, 0, 0)

    def stage_core(at):
        slot = at % 2
        value = gradient_half(at, 1 - k).astype(LOW)
        theirs[slot] = value.reshape(SHARDS, 2, 2, 2, UNIT, BLOCK)
        go(at, "core", 0, theirs.at[slot], from_core.at[slot], place.across("core"))

    def stage_first(at):
        slot = at % 3
        value = gradient_half(at, k).reshape(SHARDS, 2, 2, 2, UNIT, BLOCK)
        arrived(at, "core")
        left(at, "core")
        mine[slot] = (value + from_core[at % 2].astype(jnp.float32)).astype(LOW)
        target = from_first.at[at % 2]
        go(at, "first", 1, mine.at[slot, :, 0, :, 1 - x], target.at[0], place.across("x"))
        go(at, "first", 2, mine.at[slot, :, 1, 1 - y], target.at[1], place.across("y"))

    def stage_second(at):
        slot = at % 3
        arrived(at, "first")
        left(at, "first")

        @pl.loop(0, SHARDS)
        def _(shard):
            for i in range(2):
                mine[slot, shard, 0, i, x] = (
                    mine[slot, shard, 0, i, x].astype(jnp.float32)
                    + from_first[at % 2, 0, shard, i].astype(jnp.float32)
                ).astype(LOW)
                mine[slot, shard, 1, y, i] = (
                    mine[slot, shard, 1, y, i].astype(jnp.float32)
                    + from_first[at % 2, 1, shard, i].astype(jnp.float32)
                ).astype(LOW)

        target = from_second.at[at % 2]
        go(at, "second", 3, mine.at[slot, :, 0, 1 - y, x], target.at[0], place.across("y"))
        go(at, "second", 4, mine.at[slot, :, 1, y, 1 - x], target.at[1], place.across("x"))

    def piece_loads(at):
        index, group, part = chunks[at]
        slot = at % 2
        where = pl.ds(part * BLOCK, BLOCK)
        return (
            pltpu.make_async_copy(
                states[index].at[:, group, k, :, y, x, :, where],
                state_in.at[slot],
                state_sems.at[slot, 0],
            ),
            pltpu.make_async_copy(
                masters[index].at[group, k, :, y, x, :, where],
                master_in.at[slot],
                state_sems.at[slot, 1],
            ),
        )

    def stage_z(at):
        slot = at % 3
        arrived(at, "second")
        left(at, "second")

        @pl.loop(0, SHARDS)
        def _(shard):
            for h in range(2):
                final[at % 2, shard, h] = (
                    mine[slot, shard, h, y, x].astype(jnp.float32)
                    + from_second[at % 2, h, shard].astype(jnp.float32)
                ).astype(LOW)

        for copy in piece_loads(at):
            copy.start()
        for offset in range(1, SHARDS):
            target = lax.rem(s + offset, SHARDS)
            go(
                at,
                "z",
                5 + offset - 1,
                final.at[at % 2, target],
                from_z.at[at % 2, offset - 1],
                place.along(offset),
            )

    def summed(at, *where):
        index, group, part = chunks[at]
        rest = where + (slice(None),) * (5 - len(where))
        return sums[index].at[(group,) + rest + (pl.ds(part * BLOCK, BLOCK),)]

    def own_piece(at):
        return pltpu.make_async_copy(
            ready.at[at % 2], summed(at, k, slice(None), y, x), ready_sems.at[at % 2]
        )

    def direction_of(gradient, first, second):
        moment = 0.5 * first + 0.5 * gradient
        root = jnp.sqrt(0.5 * second * second + 0.5 * gradient * gradient)
        return moment / (root + 1e-06)

    def lanes(square):
        total = jnp.sum(square, 0, keepdims=True)
        parts = [total[:, i * 128 : (i + 1) * 128] for i in range(total.shape[1] // 128)]
        return sum(parts[1:], parts[0])

    def stage_back(at):
        index = chunks[at][0]
        slot = at % 2
        for copy in piece_loads(at):
            copy.wait()
        arrived(at, "z")
        left(at, "z")
        for h in range(2):
            value = final[slot, s, h].astype(jnp.float32)
            for offset in range(1, SHARDS):
                value = value + from_z[slot, offset - 1, h].astype(jnp.float32)
            low = value.astype(LOW)
            ready[slot, h] = low
            direction = direction_of(
                low.astype(jnp.float32), state_in[slot, 0, h], state_in[slot, 1, h]
            )
            master = master_in[slot, h]
            squares[0, index : index + 1, :] += lanes(master * master)
            squares[0, 8 + index : 9 + index, :] += lanes(direction * direction)
        own_piece(at).start()
        target = summed(at, k, 0, y, x)
        go(at, "back", 8, ready.at[slot, 0], target, place.across("y"))
        target = summed(at, k, 1, y, x)
        go(at, "back", 9, ready.at[slot, 1], target, place.across("x"))

    def stage_wide(at):
        own_piece(at).wait()
        arrived(at, "back")
        left(at, "back")
        ref = summed(at, k, 0, slice(None), x)
        go(at, "wide", 10, ref, ref, place.across("x"))
        ref = summed(at, k, 1, y)
        go(at, "wide", 11, ref, ref, place.across("y"))

    def stage_twin(at):
        arrived(at, "wide")
        ref = summed(at, k)
        go(at, "twin", 12, ref, ref, place.across("core"))

    def stage_end(at):
        arrived(at, "twin")

    stages = (
        stage_core,
        stage_first,
        stage_second,
        stage_z,
        stage_back,
        stage_wide,
        stage_twin,
        stage_end,
    )
    ages = {}
    upcoming = [0]

    def tick(start=False):
        for at in sorted(ages):
            stages[ages[at]](at)
            ages[at] += 1
            if ages[at] == len(stages):
                del ages[at]
        if start:
            at = upcoming[0]
            stages[0](at)
            ages[at] = 1
            upcoming[0] = at + 1

    prime(4)
    squares[...] = jnp.zeros_like(squares)
    table_own[...] = jnp.zeros_like(table_own)
    greet(place)
    tick(True)

    def put_row(row, value):
        for shard in range(SHARDS):
            table_own[0, shard, row : row + 1, :] = value[:, shard * own : (shard + 1) * own]

    put_row(6, jnp.sum(cotangent[...].astype(jnp.float32), 0, keepdims=True))

    groups = tiles(4)[0]
    for quarter in range(SHARDS):

        @pl.loop(0, groups)
        def _(group):
            at = quarter * groups + group
            act = contract(cotangent[...], take(4, at), 1, 1)
            give(4, at)
            where = pl.ds(pl.multiple_of(at * 256, 256), 256)
            value = expanded[:, where]
            slope = 0.5 + 0.5 * lax.erf(value * math.sqrt(0.5))
            slope = slope + value * jnp.exp(-0.5 * value * value) * (1.0 / math.sqrt(2.0 * math.pi))
            low = (act * slope).astype(LOW)
            grad_inner[:, where] = low
            table_own[0, group, 7 + quarter : 8 + quarter, :] = jnp.sum(
                low.astype(jnp.float32), 0, keepdims=True
            )

        if quarter % 2:
            tick(True)
    prime(3)
    parts = tiles(3)[1]

    @pl.loop(0, SHARDS)
    def _(shard):
        where = pl.ds(pl.multiple_of(shard * 256, 256), 256)
        total = None
        for part in range(parts):
            at = shard * parts + part
            term = contract(grad_inner[:, part * BLOCK : (part + 1) * BLOCK], take(3, at), 1, 1)
            give(3, at)
            total = term if total is None else total + term
        grad_second[:, where] = total

    prime(2)
    tick(True)
    gain_sum, bias_sum, low_sum = norm_back(
        middle, vectors[4:5, :], grad_second, cotangent, grad_middle, grad_middle_low, rows
    )
    put_row(4, gain_sum)
    put_row(5, bias_sum)
    put_row(3, low_sum)

    @pl.loop(0, SHARDS)
    def _(shard):
        outgoing[shard, :, 0:own] = contract(grad_middle_low[...], take(2, shard), 1, 1).astype(LOW)

    prime(1)
    mixed_copies = []
    for offset in range(1, SHARDS):
        mixed_copies.append(
            extra(
                offset - 1,
                outgoing.at[lax.rem(s + offset, SHARDS), :, pl.ds(0, own)],
                grad_mixed.at[pl.ds(offset * rows, rows), :],
                place.along(offset),
            )
        )

    @pl.loop(0, rows // 32)
    def _(block):
        where = pl.ds(pl.multiple_of(block * 32, 32), 32)
        grad_mixed[where, :] = outgoing[s, where, 0:own]

    tick(True)
    for copy in mixed_copies:
        copy.wait_recv()

    everyone = SHARDS * rows
    tile = 384
    lane = lax.broadcasted_iota(jnp.int32, (tile, 128), 1)
    key_row = lax.broadcasted_iota(jnp.int32, (everyone, tile), 0)
    for pair in range(own // 128):
        grad_key[...] = jnp.zeros_like(grad_key)
        grad_value[...] = jnp.zeros_like(grad_value)
        low, high = pair * 128, (pair + 1) * 128

        @pl.loop(0, everyone // tile)
        def _(block):
            start = pl.multiple_of(block * tile, 128)
            where = pl.ds(start, tile)
            query = heads[where, low:high]
            keys = heads[:, own + low : own + high]
            values = heads[:, 2 * own + low : 2 * own + high]
            incoming = grad_mixed[where, low:high]
            parts = []
            for half in range(2):
                inside = (lane // 64) == half
                picked = jnp.where(inside, query.astype(jnp.float32) * factor, 0.0).astype(LOW)
                grads = jnp.where(inside, incoming.astype(jnp.float32), 0.0).astype(LOW)
                scores = contract(keys, picked, 1, 1)
                scores = jnp.where(lax.rem(key_row, rows) < portion, scores, -1e30)
                at = 2 * pair + half
                weight = jnp.exp(scores - log_total[at : at + 1, pl.ds(start, tile)])
                slope = contract(values, grads, 1, 1)
                delta = jnp.sum(weight * slope, 0, keepdims=True)
                grad_scores = (weight * (slope - delta)).astype(LOW)
                grad_key[...] += jnp.dot(
                    grad_scores, picked, preferred_element_type=jnp.float32
                )
                grad_value[...] += jnp.dot(
                    weight.astype(LOW), grads, preferred_element_type=jnp.float32
                )
                turned = contract(keys, grad_scores, 0, 0)
                parts.append(turned[half * 64 : (half + 1) * 64])
            both = jnp.concatenate(parts, 0) * factor
            grad_heads[where, low:high] = both.T.astype(LOW)

        grad_heads[:, own + low : own + high] = grad_key[...].astype(LOW)
        grad_heads[:, 2 * own + low : 2 * own + high] = grad_value[...].astype(LOW)
        tick(True)

    triple_copies = []
    for offset in range(1, SHARDS):
        triple_copies.append(
            extra(
                2 + offset,
                grad_heads.at[pl.ds(offset * rows, rows), :],
                grad_triple.at[s],
                (place.rep, place.source(offset)),
            )
        )

    @pl.loop(0, rows // 32)
    def _(block):
        where = pl.ds(pl.multiple_of(block * 32, 32), 32)
        grad_triple[s, where, :] = grad_heads[where, :]

    tick(True)
    tick(True)
    for copy in triple_copies:
        copy.wait_recv()
    parts_in = tiles(1)[1]

    @pl.loop(0, SHARDS)
    def _(shard):
        where = pl.ds(pl.multiple_of(shard * 256, 256), 256)
        total = None
        for part in range(parts_in):
            at = shard * parts_in + part
            left_side = jnp.concatenate(
                [grad_triple[g, :, part * own : (part + 1) * own] for g in range(SHARDS)], 1
            )
            term = contract(left_side, take(1, at), 1, 1)
            give(1, at)
            total = term if total is None else total + term
        grad_second[:, where] = total

    prime(0)
    gain_sum, bias_sum, low_sum = norm_back(
        entering, vectors[1:2, :], grad_second, grad_middle, None, grad_entering, rows
    )
    put_row(1, gain_sum)
    put_row(2, bias_sum)
    put_row(0, low_sum)
    table_copies = []

    def table_step(position, axis):
        if position:
            table_copies[-1].wait_recv()
            table_own[position] = table_own[position - 1] + table_in[position - 1]
        if axis:
            table_copies.append(
                extra(
                    6 + position,
                    table_own.at[position],
                    table_in.at[position],
                    place.across(axis),
                )
            )

    table_step(0, "core")
    tick(True)
    table_step(1, "x")

    @pl.loop(0, tiles(0)[2])
    def _(at):
        where = pl.ds(pl.multiple_of(at * 256, 256), 256)
        grad_joined[:, where] = contract(grad_entering[...], take(0, at), 1, 1).astype(LOW)
        give(0, at)

    table_step(2, "y")
    tick(True)
    table_step(3, None)
    for offset in range(1, SHARDS):
        table_copies.append(
            extra(
                8 + offset,
                table_own.at[3, lax.rem(s + offset, SHARDS)],
                table_z.at[offset - 1],
                place.along(offset),
            )
        )
    tick(True)
    for copy in table_copies[3:]:
        copy.wait_recv()
    value = table_own[3, s]
    for offset in range(1, SHARDS):
        value = value + table_z[offset - 1]
    table_sum[...] = value
    direction = direction_of(value, own_states[0], own_states[1])
    share = 1.0 / REPLICAS
    squares[0, 5:6, :] = share * lanes(own_vectors[...] * own_vectors[...])
    squares[0, 13:14, :] = share * lanes(direction * direction)
    while upcoming[0] < len(chunks):
        tick(True)
    square_copies = []
    square_axes = ("core", "x", "y")
    position = 0
    while ages or position < 4:
        if ages:
            tick()
        waiting = [at for at in ages if ages[at] <= 4]
        if not waiting and position < 4:
            if position:
                square_copies[-1].wait_recv()
                squares[position] = squares[position - 1] + square_in[position - 1]
            if position < 3:
                square_copies.append(
                    extra(
                        12 + position,
                        squares.at[position],
                        square_in.at[position],
                        place.across(square_axes[position]),
                    )
                )
            position += 1
    for offset in range(1, SHARDS):
        square_copies.append(
            extra(14 + offset, squares.at[3], square_z.at[offset], place.along(offset))
        )
    square_z[0] = squares[3]
    for copy in square_copies[3:]:
        copy.wait_recv()
    value = square_z[s]
    for shard in range(1, SHARDS):
        value = value + square_z[lax.rem(s + SHARDS - shard, SHARDS)]
    norms[...] = jnp.sqrt(jnp.sum(value, 1, keepdims=True)) + jnp.zeros_like(value)
    for key in sorted(copies):
        for copy in copies[key]:
            copy.wait_send()
    for copy in sent:
        copy.wait_send()


def backward_pass(cotangent, joined, table, kept, weights, masters, states, vectors, vector_states, portion):
    entering, first_in, heads, log_total, mixed, middle, second_in, expanded, activated = kept[:9]
    shapes = [(matrix.shape[0] * SHARDS, matrix.shape[1]) for matrix in masters]
    order = chunk_list(shapes)
    chunks = [chunk for index in (4, 3, 2, 1, 0) for chunk in order if chunk[0] == index]
    total = len(chunks)
    rows, width = entering.shape
    own = width // SHARDS
    hidden = expanded.shape[1]
    everyone = SHARDS * rows
    piece = (UNIT, BLOCK)
    inner = pl.BlockSpec(memory_space=pltpu.VMEM)
    folds = [(SHARDS, r // SHARDS // 256, 2, 2, 2, 2, UNIT, c) for r, c in shapes]
    extra_rows = 16 - vectors.shape[0]
    own_vectors = jnp.pad(vectors, ((0, extra_rows), (0, 0)))
    own_states = jnp.pad(vector_states, ((0, 0), (0, extra_rows), (0, 0)))
    outs = pl.pallas_call(
        functools.partial(backward_kernel, chunks, portion),
        out_shape=[jax.ShapeDtypeStruct(fold[1:], LOW) for fold in folds]
        + [
            jax.ShapeDtypeStruct((16, own), jnp.float32),
            jax.ShapeDtypeStruct((16, 128), jnp.float32),
            jax.ShapeDtypeStruct((rows, 2 * width), LOW),
        ],
        in_specs=[inner] * 12 + [ANY] * 15 + [inner] * 2,
        out_specs=[ANY] * 5 + [inner] * 3,
        scratch_shapes=[
            pltpu.VMEM((8, 2, 2, 2, 2) + piece, LOW),
            pltpu.VMEM((2, SHARDS, 2, 2, 2) + piece, LOW),
            pltpu.VMEM((3, SHARDS, 2, 2, 2) + piece, LOW),
            pltpu.VMEM((2, SHARDS, 2, 2, 2) + piece, LOW),
            pltpu.VMEM((2, 2, SHARDS, 2) + piece, LOW),
            pltpu.VMEM((2, 2, SHARDS) + piece, LOW),
            pltpu.VMEM((2, SHARDS, 2) + piece, LOW),
            pltpu.VMEM((2, SHARDS - 1, 2) + piece, LOW),
            pltpu.VMEM((2, 2) + piece, LOW),
            pltpu.VMEM((2, 2, 2) + piece, jnp.float32),
            pltpu.VMEM((2, 2) + piece, jnp.float32),
            pltpu.VMEM((4, 16, 128), jnp.float32),
            pltpu.VMEM((3, 16, 128), jnp.float32),
            pltpu.VMEM((SHARDS, 16, 128), jnp.float32),
            pltpu.VMEM((4, SHARDS, 16, own), jnp.float32),
            pltpu.VMEM((3, SHARDS, 16, own), jnp.float32),
            pltpu.VMEM((SHARDS - 1, 16, own), jnp.float32),
            pltpu.VMEM((rows, hidden), LOW),
            pltpu.VMEM((rows, width), jnp.float32),
            pltpu.VMEM((rows, width), jnp.float32),
            pltpu.VMEM((rows, width), LOW),
            pltpu.VMEM((SHARDS, rows, own), LOW),
            pltpu.VMEM((everyone, own), LOW),
            pltpu.VMEM((everyone, 128), jnp.float32),
            pltpu.VMEM((everyone, 128), jnp.float32),
            pltpu.VMEM((everyone, 3 * own), LOW),
            pltpu.VMEM((SHARDS, rows, 3 * own), LOW),
            pltpu.VMEM((rows, width), LOW),
            pltpu.SemaphoreType.DMA((8,)),
            pltpu.SemaphoreType.DMA((2, 2)),
            pltpu.SemaphoreType.DMA((2,)),
            pltpu.SemaphoreType.DMA((total * 14,)),
            pltpu.SemaphoreType.DMA((total * 14,)),
            pltpu.SemaphoreType.DMA((18,)),
            pltpu.SemaphoreType.DMA((18,)),
        ],
        compiler_params=pltpu.CompilerParams(
            collective_id=2, has_side_effects=True, vmem_limit_bytes=60 * 2**20
        ),
        name="backward_pass",
    )(
        cotangent,
        joined,
        table,
        entering,
        first_in,
        heads,
        log_total,
        mixed,
        middle,
        second_in,
        expanded,
        activated,
        *[matrix.reshape(fold) for matrix, fold in zip(weights, folds)],
        *[matrix.reshape(fold[1:]) for matrix, fold in zip(masters, folds)],
        *[state.reshape((2,) + fold[1:]) for state, fold in zip(states, folds)],
        own_vectors,
        own_states,
    )
    lows = [low.reshape(r // SHARDS, c) for low, (r, c) in zip(outs[:5], shapes)]
    return lows, outs[5][: vectors.shape[0]], outs[6], outs[7]


def update_kernel(position, norms, gradient, state, master, wide, new_state, new_master):
    grad = gradient[...].astype(jnp.float32)
    moment = 0.5 * state[0] + 0.5 * grad
    root = jnp.sqrt(0.5 * state[1] * state[1] + 0.5 * grad * grad)
    wide[...] = grad
    new_state[0] = moment
    new_state[1] = root
    ratio = norms[position : position + 1, 0:1] / (
        norms[8 + position : 9 + position, 0:1] + 1e-06
    )
    new_master[...] = master[...] - (step_rate * ratio) * (moment / (root + 1e-06))


def update_weight(position, norms, gradient, state, master):
    rows, columns = master.shape
    block = 256 if columns <= BLOCK else 64
    plain = pl.BlockSpec((block, columns), lambda i: (i, 0))
    paired = pl.BlockSpec((2, block, columns), lambda i: (0, i, 0))
    return pl.pallas_call(
        functools.partial(update_kernel, position),
        grid=(rows // block,),
        out_shape=[
            jax.ShapeDtypeStruct(master.shape, jnp.float32),
            jax.ShapeDtypeStruct(state.shape, jnp.float32),
            jax.ShapeDtypeStruct(master.shape, jnp.float32),
        ],
        in_specs=[pl.BlockSpec((16, 128), lambda i: (0, 0)), plain, paired, plain],
        out_specs=[plain, paired, plain],
        name="update_weight",
    )(norms, gradient, state, master)


def fits(masters):
    return (
        lax.axis_size("shard") == SHARDS
        and lax.axis_size("rep") == REPLICAS
        and all(m.shape[0] % 256 == 0 and m.shape[1] % BLOCK == 0 for m in masters)
        and masters[0].shape[1] == HEADS * HEAD_DIM == BLOCK
    )


def plain_device(
    hidden_in,
    skip_path,
    cotangent,
    skip_weight,
    heads_in,
    heads_out,
    expand_weight,
    reduce_weight,
    vectors,
    moments_skip,
    moments_in,
    moments_out,
    moments_expand,
    moments_reduce,
    moments_vectors,
):
    sequences, portion, model_width = hidden_in.shape
    shards = lax.axis_size("shard")
    replicas = lax.axis_size("rep")
    rep_index = lax.axis_index("rep")
    row_count = sequences * portion
    factor = 1.0 / math.sqrt(HEAD_DIM)
    masters = (skip_weight, heads_in, heads_out, expand_weight, reduce_weight, vectors)
    gathered = []
    for matrix in masters[:5]:
        height = matrix.shape[0] // replicas
        piece = lax.dynamic_slice_in_dim(matrix, rep_index * height, height, 0)
        piece = piece.astype(jnp.bfloat16)
        gathered.append(lax.all_gather(piece, ("shard", "rep"), axis=0, tiled=True))
    skip_matrix, in_matrix, out_matrix, expand_matrix, reduce_matrix = gathered
    table_low = lax.all_gather(vectors.astype(jnp.bfloat16), "shard", axis=1, tiled=True)
    table_rows = table_low.astype(jnp.float32)
    source = hidden_in.reshape(row_count, model_width)
    skip_rows = skip_path.reshape(row_count, model_width)
    joined = jnp.concatenate([source, skip_rows], 1)
    entering = matmul(joined, skip_matrix) + table_rows[0]
    normed_one, norm_back_one = jax.vjp(normalize, entering, table_rows[1], table_rows[2])
    first_in = normed_one.astype(jnp.bfloat16)
    triple = matmul(first_in, in_matrix).astype(jnp.bfloat16)
    heads = to_heads(triple, sequences, portion, shards)
    queries, keys_full, values_full = heads[:, :, 0], heads[:, :, 1], heads[:, :, 2]
    scores = (
        jnp.einsum("sqhd,skhd->shqk", queries, keys_full, preferred_element_type=jnp.float32)
        * factor
    )
    row_max = jnp.max(scores, -1)
    row_total = jnp.sum(jnp.exp(scores - row_max[..., None]), -1)
    log_total = row_max + jnp.log(row_total)
    probability = jnp.exp(scores - log_total[..., None])
    mixed = jnp.einsum(
        "shqk,skhd->sqhd",
        probability.astype(jnp.bfloat16),
        values_full,
        preferred_element_type=jnp.float32,
    )
    mixed_low = to_tokens(mixed.astype(jnp.bfloat16)[:, :, None], sequences, portion, shards)
    middle = entering + matmul(mixed_low, out_matrix) + table_rows[3]
    normed_two, norm_back_two = jax.vjp(normalize, middle, table_rows[4], table_rows[5])
    second_in = normed_two.astype(jnp.bfloat16)
    expanded = matmul(second_in, expand_matrix) + table_rows[7:].reshape(-1)
    activated, gelu_back = jax.vjp(exact_gelu, expanded)
    activated_low = activated.astype(jnp.bfloat16)
    block_result = middle + matmul(activated_low, reduce_matrix) + table_rows[6]
    block_out = block_result.astype(jnp.bfloat16).reshape(sequences, portion, model_width)
    grad_out = cotangent.reshape(row_count, model_width)
    grad_reduce = matmul(activated_low.T, grad_out)
    grad_act = matmul(grad_out, reduce_matrix.T)
    grad_inner = gelu_back(grad_act)[0].astype(jnp.bfloat16)
    grad_expand = matmul(second_in.T, grad_inner)
    grad_second = matmul(grad_inner, expand_matrix.T)
    grad_mid_norm, grad_gain_two, grad_bias_two = norm_back_two(grad_second)
    grad_middle = grad_out.astype(jnp.float32) + grad_mid_norm
    grad_middle_low = grad_middle.astype(jnp.bfloat16)
    grad_outw = matmul(mixed_low.T, grad_middle_low)
    grad_mixed = matmul(grad_middle_low, out_matrix.T).astype(jnp.bfloat16)
    grad_mixed = to_heads(grad_mixed, sequences, portion, shards)[:, :, 0]
    grad_prob = jnp.einsum(
        "sqhd,skhd->shqk", grad_mixed, values_full, preferred_element_type=jnp.float32
    )
    delta = jnp.sum(probability * grad_prob, -1)
    grad_scores = (probability * (grad_prob - delta[..., None])).astype(jnp.bfloat16)
    grad_query = (
        jnp.einsum("shqk,skhd->sqhd", grad_scores, keys_full, preferred_element_type=jnp.float32)
        * factor
    )
    grad_keys = (
        jnp.einsum("shqk,sqhd->skhd", grad_scores, queries, preferred_element_type=jnp.float32)
        * factor
    )
    grad_values = jnp.einsum(
        "shqk,sqhd->skhd",
        probability.astype(jnp.bfloat16),
        grad_mixed,
        preferred_element_type=jnp.float32,
    )
    grad_heads = jnp.stack([grad_query, grad_keys, grad_values], 2).astype(jnp.bfloat16)
    grad_triple = to_tokens(grad_heads, sequences, portion, shards)
    grad_inw = matmul(first_in.T, grad_triple)
    grad_first = matmul(grad_triple, in_matrix.T)
    grad_pre_norm, grad_gain_one, grad_bias_one = norm_back_one(grad_first)
    grad_entering = (grad_middle + grad_pre_norm).astype(jnp.bfloat16)
    grad_skipw = matmul(joined.T, grad_entering)
    grad_joined = matmul(grad_entering, skip_matrix.T)
    input_gradient = (
        grad_joined[:, :model_width].astype(jnp.bfloat16).reshape(sequences, portion, model_width)
    )
    skip_gradient = (
        grad_joined[:, model_width:].astype(jnp.bfloat16).reshape(sequences, portion, model_width)
    )
    grad_table = jnp.concatenate(
        [
            jnp.stack(
                [
                    row_sums(grad_entering),
                    grad_gain_one,
                    grad_bias_one,
                    row_sums(grad_middle_low),
                    grad_gain_two,
                    grad_bias_two,
                    row_sums(grad_out),
                ]
            ),
            row_sums(grad_inner).reshape(-1, model_width),
        ],
        0,
    )
    width = vectors.shape[1]
    grad_table = lax.psum(grad_table, ("rep", "shard"))
    vector_total = lax.dynamic_slice_in_dim(grad_table, lax.axis_index("shard") * width, width, 1)
    totals = []
    for partial in (grad_skipw, grad_inw, grad_outw, grad_expand, grad_reduce):
        piece = lax.psum_scatter(
            partial.astype(jnp.bfloat16), ("shard", "rep"), scatter_dimension=0, tiled=True
        )
        whole = lax.all_gather(piece, "rep", axis=0, tiled=True)
        totals.append(whole.astype(jnp.float32))
    totals.append(vector_total)
    states = (
        moments_skip,
        moments_in,
        moments_out,
        moments_expand,
        moments_reduce,
        moments_vectors,
    )
    steps = [moment_step(total, state) for total, state in zip(totals, states)]
    squares = jnp.stack(
        [
            jnp.stack([jnp.sum(matrix * matrix) for matrix in masters]),
            jnp.stack([jnp.sum(direction * direction) for _, direction in steps]),
        ]
    )
    norms = jnp.sqrt(lax.psum(squares, "shard"))
    ratio = norms[0] / (norms[1] + 1e-06)
    updated = [
        masters[position] - step_rate * ratio[position] * steps[position][1]
        for position in range(6)
    ]
    return (
        block_out,
        input_gradient,
        skip_gradient,
        *totals,
        *(state for state, _ in steps),
        *updated,
        norms,
    )


def on_device(
    hidden_in,
    skip_path,
    cotangent,
    skip_weight,
    heads_in,
    heads_out,
    expand_weight,
    reduce_weight,
    vectors,
    moments_skip,
    moments_in,
    moments_out,
    moments_expand,
    moments_reduce,
    moments_vectors,
):
    sequences, portion, model_width = hidden_in.shape
    masters = (skip_weight, heads_in, heads_out, expand_weight, reduce_weight)
    states = (moments_skip, moments_in, moments_out, moments_expand, moments_reduce)
    if not (sequences == 1 and fits(masters)):
        return plain_device(
            hidden_in, skip_path, cotangent, *masters, vectors, *states, moments_vectors
        )
    more = -portion % 32
    joined = jnp.concatenate([hidden_in[0], skip_path[0]], 1)
    joined = jnp.pad(joined, ((0, more), (0, 0)))
    incoming = jnp.pad(cotangent[0], ((0, more), (0, 0)))
    weights, kept = forward_pass(joined, vectors, masters, portion)
    block_out, table = kept[9], kept[10]
    lows, vector_total, norms, grad_joined = backward_pass(
        incoming, joined, table, kept, weights, masters, states, vectors, moments_vectors, portion
    )
    steps = [
        update_weight(position, norms, lows[position], states[position], masters[position])
        for position in range(5)
    ]
    vector_state, direction = moment_step(vector_total, moments_vectors)
    ratio = norms[5, 0] / (norms[13, 0] + 1e-06)
    return (
        block_out[None, :portion],
        grad_joined[None, :portion, :model_width],
        grad_joined[None, :portion, model_width:],
        *(step[0] for step in steps),
        vector_total,
        *(step[1] for step in steps),
        vector_state,
        *(step[2] for step in steps),
        vectors - step_rate * ratio * direction,
        jnp.stack([norms[:6, 0], norms[8:14, 0]]),
    )


def solution(mesh):
    placed = (
        P("rep", "shard", None),
        P("rep", "shard", None),
        P("rep", "shard", None),
        P("shard", None),
        P("shard", None),
        P("shard", None),
        P("shard", None),
        P("shard", None),
        P(None, "shard"),
        P(None, "shard", None),
        P(None, "shard", None),
        P(None, "shard", None),
        P(None, "shard", None),
        P(None, "shard", None),
        P(None, None, "shard"),
    )
    return jax.shard_map(
        on_device,
        mesh=mesh,
        in_specs=placed,
        out_specs=(
            P("rep", "shard", None),
            P("rep", "shard", None),
            P("rep", "shard", None),
            P("shard", None),
            P("shard", None),
            P("shard", None),
            P("shard", None),
            P("shard", None),
            P(None, "shard"),
            P(None, "shard", None),
            P(None, "shard", None),
            P(None, "shard", None),
            P(None, "shard", None),
            P(None, "shard", None),
            P(None, None, "shard"),
            P("shard", None),
            P("shard", None),
            P("shard", None),
            P("shard", None),
            P("shard", None),
            P(None, "shard"),
            P(),
        ),
        check_vma=False,
    )
```

```python
import functools
import math

import jax
import jax.numpy as jnp
from jax import lax
from jax.experimental import pallas as pl
from jax.experimental.pallas import tpu as pltpu
from jax.sharding import PartitionSpec as P

HEADS = 16
HEAD_DIM = 64
MESH = pl.DeviceIdType.MESH
LOW = jnp.bfloat16
ANY = pl.BlockSpec(memory_space=pl.ANY)
SHARDS, REPLICAS = 4, 8
UNIT = 16
BLOCK = 1024


class Place:
    def __init__(self):
        self.rep = lax.axis_index("rep")
        self.shard = lax.axis_index("shard")
        self.core = lax.rem(self.rep, 2)
        self.x = lax.rem(self.rep // 2, 2)
        self.y = self.rep // 4

    def across(self, axis):
        own, step = {"core": (self.core, 1), "x": (self.x, 2), "y": (self.y, 4)}[axis]
        return (self.rep + step - 2 * step * own, self.shard)

    def along(self, offset):
        return (self.rep, lax.rem(self.shard + offset, SHARDS))

    def source(self, offset):
        return lax.rem(self.shard + SHARDS - offset, SHARDS)

    def partners(self):
        return [self.across("core"), self.across("x"), self.across("y")] + [
            self.along(offset) for offset in range(1, SHARDS)
        ]


def greet(place):
    barrier = pltpu.get_barrier_semaphore()
    partners = place.partners()
    for partner in partners:
        pl.semaphore_signal(barrier, inc=1, device_id=partner, device_id_type=MESH)
    pl.semaphore_wait(barrier, len(partners))


def chunk_list(shapes):
    chunks = []
    for index, (rows, columns) in enumerate(shapes):
        for group in range(rows // SHARDS // 256):
            for part in range(columns // BLOCK):
                chunks.append((index, group, part))
    return chunks


class Plan:
    def __init__(self, latency=1.5):
        self.now, self.latency = 0.0, latency
        self.free = {}
        self.agents = []

    def transfer(self, link, length):
        self.free[link] = max(self.now, self.free.get(link, 0.0)) + length
        return self.free[link] + self.latency

    def backlog(self, link):
        return self.free.get(link, 0.0) - self.now

    def add(self, steps):
        agent = [steps, 0.0, None]
        self.agents.append(agent)
        self.resume(agent)

    def resume(self, agent):
        try:
            agent[1], agent[2] = next(agent[0])
        except StopIteration:
            self.agents.remove(agent)

    def ready(self):
        return [a for a in self.agents if a[2] is None or a[2]()]

    def pump(self):
        while True:
            able = [agent for agent in self.ready() if agent[1] <= self.now]
            if not able:
                return
            self.resume(able[0])

    def spend(self, length):
        self.now += length
        self.pump()

    def until(self, moment):
        self.pump()
        while self.now < moment:
            times = [agent[1] for agent in self.ready() if agent[1] > self.now]
            self.now = min(times + [moment])
            self.pump()

    def finish(self, test):
        self.pump()
        while not test():
            times = [agent[1] for agent in self.ready()]
            self.now = max(self.now, min(times))
            self.pump()


step_rate = 0.3


def normalize(stream, gain_row, bias_row):
    center = stream - jnp.mean(stream, -1, keepdims=True)
    spread = jnp.mean(center * center, -1, keepdims=True)
    return center * lax.rsqrt(spread + 1e-05) * gain_row + bias_row


def exact_gelu(inputs):
    return jax.nn.gelu(inputs, approximate=False)


def matmul(left, right):
    return jnp.dot(left, right, preferred_element_type=jnp.float32)


def row_sums(matrix):
    return jnp.sum(matrix, 0, dtype=jnp.float32)


def moment_step(gradient, moments):
    first_moment = 0.5 * moments[0] + 0.5 * gradient
    root_square = jnp.sqrt(0.5 * moments[1] * moments[1] + 0.5 * gradient * gradient)
    direction = first_moment / (root_square + 1e-06)
    return (jnp.stack([first_moment, root_square]), direction)


def to_heads(rows, sequences, portion, shards):
    parts = rows.shape[1] // (HEADS * HEAD_DIM)
    width = HEADS * HEAD_DIM // shards
    blocks = rows.reshape(sequences, portion, parts, shards, width).transpose(3, 0, 1, 2, 4)
    blocks = blocks.reshape(shards, sequences * portion, parts * width)
    blocks = lax.all_to_all(blocks, "shard", 0, 0, tiled=True)
    blocks = blocks.reshape(shards, sequences, portion, parts, width).transpose(1, 0, 2, 3, 4)
    return blocks.reshape(sequences, shards * portion, parts, width // HEAD_DIM, HEAD_DIM)


def to_tokens(blocks, sequences, portion, shards):
    parts = blocks.shape[2]
    width = HEADS * HEAD_DIM // shards
    rows = blocks.reshape(sequences, shards, portion, parts, width).transpose(1, 0, 2, 3, 4)
    rows = rows.reshape(shards, sequences * portion, parts * width)
    rows = lax.all_to_all(rows, "shard", 0, 0, tiled=True)
    rows = rows.reshape(shards, sequences * portion, parts, width).transpose(1, 2, 0, 3)
    return rows.reshape(sequences * portion, parts * shards * width)


SLOTS = 19
LINK_RATE = 45e3
Z_BACKLOG = 5.0


def weight_tile(whole, shard, group, start, width):
    return whole[shard, group, :, :, :, :, :, pl.ds(start, width)].reshape(256, width)


def product(left, whole, start, width):
    groups = whole.shape[1]
    total = None
    for shard in range(SHARDS):
        for group in range(groups):
            first = (shard * groups + group) * 256
            term = jnp.dot(
                left[:, first : first + 256],
                weight_tile(whole, shard, group, start, width),
                preferred_element_type=jnp.float32,
            )
            total = term if total is None else total + term
    return total


def contract(left, right, left_axis, right_axis):
    return lax.dot_general(
        left, right, (((left_axis,), (right_axis,)), ((), ())), preferred_element_type=jnp.float32
    )


def norm_rows(source, gain, bias, target, rows):
    @pl.loop(0, rows // 32)
    def _(block):
        where = pl.ds(pl.multiple_of(block * 32, 32), 32)
        stream = source[where, :]
        center = stream - jnp.mean(stream, -1, keepdims=True)
        spread = jnp.mean(center * center, -1, keepdims=True)
        target[where, :] = (center * lax.rsqrt(spread + 1e-05) * gain + bias).astype(LOW)


def forward_kernel(chunks, portion, *refs):
    joined, vectors = refs[0:2]
    masters = refs[2:7]
    keeps = refs[7:12]
    (
        entering,
        first_in,
        heads,
        log_total,
        mixed,
        middle,
        second_in,
        slope,
        activated,
        out,
        table,
    ) = refs[12:23]
    wholes = refs[23:28]
    (
        wide,
        table_own,
        table_all,
        outgoing,
        answer,
        load_sems,
        keep_sems,
        send_sems,
        recv_sems,
        more_send,
        more_recv,
    ) = refs[28:]
    place = Place()
    s, k, x, y = place.shard, place.core, place.x, place.y
    total = len(chunks)
    rows = entering.shape[0]
    width = entering.shape[1]
    own = width // SHARDS
    pairs = own // 128
    factor = 1.0 / math.sqrt(HEAD_DIM)

    def load(at):
        index, group, part = chunks[at]
        return pltpu.make_async_copy(
            masters[index].at[group, :, :, :, :, :, pl.ds(part * BLOCK, BLOCK)],
            wide.at[at % 2],
            load_sems.at[at % 2],
        )

    def whole(at, shard, *rest):
        index, group, part = chunks[at]
        rest = rest + (slice(None),) * (5 - len(rest))
        return wholes[index].at[(shard, group) + rest + (pl.ds(part * BLOCK, BLOCK),)]

    sent = []
    far = []
    arrivals = {}

    def relay_copy(at):
        up = s == SHARDS - 2
        ref = whole(at, place.source(2), k, slice(None), y, x)
        target = jnp.where(up, SHARDS - 1, 0)
        return pltpu.make_async_remote_copy(
            src_ref=ref,
            dst_ref=ref,
            send_sem=send_sems.at[at * SLOTS + SLOTS - 1],
            recv_sem=recv_sems.at[at * SLOTS + jnp.where(up, SHARDS - 2, 0)],
            device_id=(place.rep, target),
            device_id_type=MESH,
        )

    def go(at, name, position, ref, device):
        slot = at * SLOTS + position
        copy = pltpu.make_async_remote_copy(
            src_ref=ref,
            dst_ref=ref,
            send_sem=send_sems.at[slot],
            recv_sem=recv_sems.at[slot],
            device_id=device,
            device_id_type=MESH,
        )
        copy.start()
        sent.append(copy)
        arrivals.setdefault((at, name), []).append(copy)

    def arrived(at, name):
        for copy in arrivals[(at, name)]:
            copy.wait_recv()

    def extra(slot, source, target, device):
        copy = pltpu.make_async_remote_copy(
            src_ref=source,
            dst_ref=target,
            send_sem=more_send.at[slot],
            recv_sem=more_recv.at[slot],
            device_id=device,
            device_id_type=MESH,
        )
        copy.start()
        sent.append(copy)
        return copy

    kept = []

    def stage_cast(at):
        index, group, part = chunks[at]
        load(at).wait()

        @pl.loop(0, 16)
        def _(row):
            a, b = row // 8, lax.rem(row // 4, 2)
            c, d = lax.rem(row // 2, 2), lax.rem(row, 2)
            wholes[index][s, group, a, b, c, d, :, part * BLOCK : (part + 1) * BLOCK] = wide[
                at % 2, a, b, c, d
            ].astype(LOW)

        if at + 2 < total:
            load(at + 2).start()

    def stage_z(at):
        for offset in range(1, SHARDS):
            ref = whole(at, s, k, slice(None), y, x)
            slot = at * SLOTS + offset - 1
            target = lax.rem(s + offset, SHARDS)
            copy = pltpu.make_async_remote_copy(
                src_ref=ref,
                dst_ref=ref,
                send_sem=send_sems.at[slot],
                recv_sem=recv_sems.at[slot],
                device_id=(place.rep, target),
                device_id_type=MESH,
            )
            arrivals[(at, "z", offset)] = copy
            if offset == 2:
                copy.start()
                sent.append(copy)
            else:
                near = s != (0 if offset == SHARDS - 1 else SHARDS - 1)
                far.append((near, copy))

                @pl.when(near)
                def _(copy=copy):
                    copy.start()

    def stage_relay(at):
        arrivals[(at, "z", 2)].wait_recv()
        inner = (s > 0) & (s < SHARDS - 1)
        copy = relay_copy(at)
        far.append((inner, copy))

        @pl.when(inner)
        def _():
            copy.start()

    def stage_first(at):
        arrivals[(at, "z", 1)].wait_recv()
        arrivals[(at, "z", 3)].wait_recv()
        for offset in range(1, SHARDS):
            e = place.source(offset)
            go(at, "first", 3 + 2 * (offset - 1), whole(at, e, k, 0, y, x), place.across("x"))
            go(at, "first", 4 + 2 * (offset - 1), whole(at, e, k, 1, y, x), place.across("y"))

    def stage_second(at):
        arrived(at, "first")
        for offset in range(1, SHARDS):
            e = place.source(offset)
            go(at, "second", 9 + 2 * (offset - 1), whole(at, e, k, 0, y), place.across("y"))
            ref = whole(at, e, k, 1, slice(None), x)
            go(at, "second", 10 + 2 * (offset - 1), ref, place.across("x"))

    def stage_core(at):
        arrived(at, "second")
        for offset in range(1, SHARDS):
            e = place.source(offset)
            go(at, "core", 15 + offset - 1, whole(at, e, k), place.across("core"))

    def stage_end(at):
        arrived(at, "core")
        index, group, part = chunks[at]
        copy = pltpu.make_async_copy(
            whole(at, slice(None)),
            keeps[index].at[:, group, :, :, :, :, :, pl.ds(part * BLOCK, BLOCK)],
            keep_sems.at[at],
        )
        copy.start()
        kept.append(copy)

    plan = Plan()
    done = [0] * total
    unit = UNIT * BLOCK * 2 / LINK_RATE

    def chunk_steps(at):
        yield 0.0, lambda: (at == 0 or done[at - 1] >= 1) and plan.backlog("z") < Z_BACKLOG
        stage_cast(at)
        plan.now += 0.6
        stage_z(at)
        start = plan.transfer("z", 6 * unit)
        done[at] = 1
        yield start - 2 * unit, None
        stage_relay(at)
        yield start + 1.0, None
        stage_first(at)
        moment = max(plan.transfer("x", 3 * unit), plan.transfer("y", 3 * unit))
        yield moment, None
        stage_second(at)
        moment = max(plan.transfer("x", 6 * unit), plan.transfer("y", 6 * unit))
        yield moment, None
        stage_core(at)
        plan.now += 0.2
        yield plan.transfer("core", 24 * unit / 6), None
        stage_end(at)
        done[at] = 2

    def until(at):
        plan.finish(lambda: done[at] == 2)

    def arrive(copies, moment):
        plan.until(moment)
        for copy in copies:
            copy.wait_recv()

    load(0).start()
    load(1).start()
    table_own[...] = vectors[...].astype(LOW)
    table_all[0] = vectors[...].astype(LOW)
    greet(place)
    table_copies = []
    for offset in range(1, SHARDS):
        table_copies.append(extra(offset - 1, table_own, table_all.at[offset], place.along(offset)))
    for at in range(total):
        plan.add(chunk_steps(at))
    last = {}
    for at, (index, group, part) in enumerate(chunks):
        last[index] = at

    until(0)
    for copy in table_copies:
        copy.wait_recv()
    for offset in range(SHARDS):
        column = pl.multiple_of(place.source(offset) * own, own)
        table[:, pl.ds(column, own)] = table_all[offset].astype(jnp.float32)
    until(last[0])

    @pl.loop(0, width // 256)
    def _(part):
        start = pl.multiple_of(part * 256, 256)
        entering[:, pl.ds(start, 256)] = (
            product(joined, wholes[0], start, 256) + table[0:1, pl.ds(start, 256)]
        )

    plan.spend(2.5)
    norm_rows(entering, table[1:2, :], table[2:3, :], first_in, rows)
    plan.spend(2.0)
    until(last[1])
    live = lax.broadcasted_iota(jnp.int32, (rows, own), 0) < portion
    for kind in range(3):

        @pl.loop(0, SHARDS)
        def _(target):
            start = pl.multiple_of(kind * width + target * own, own)
            value = jnp.where(live, product(first_in, wholes[1], start, own), 0.0).astype(LOW)
            for pair in range(pairs):
                first = (3 * pair + kind) * 128
                outgoing[target, :, first : first + 128] = value[:, pair * 128 : (pair + 1) * 128]

        plan.spend(1.5)

    head_copies = []
    moments = []
    for pair in range(pairs):
        moments.append(plan.transfer("z", 4 * rows * 384 * 2 / LINK_RATE))
        for offset in range(1, SHARDS):
            target = lax.rem(s + offset, SHARDS)
            columns = pl.ds(pair * 384, 384)
            head_copies.append(
                extra(
                    3 * pair + 2 + offset,
                    outgoing.at[target, :, columns],
                    heads.at[pl.ds(offset * rows, rows), columns],
                    place.along(offset),
                )
            )

    @pl.loop(0, rows // 32)
    def _(block):
        where = pl.ds(pl.multiple_of(block * 32, 32), 32)
        heads[where, :] = outgoing[s, where, :]

    plan.spend(0.5)
    everyone = SHARDS * rows
    tile = 384
    lane = lax.broadcasted_iota(jnp.int32, (tile, 128), 1)
    key_row = lax.rem(lax.broadcasted_iota(jnp.int32, (everyone, 1), 0), rows)
    key_bias = jnp.where(key_row < portion, 0.0, -1e30)
    answer_copies = []
    column = pl.multiple_of(s * own, own)
    for pair in range(pairs):
        arrive(head_copies[3 * pair : 3 * pair + 3], moments[pair])
        base = pair * 384

        for block in range(everyone // tile):
            start = block * tile
            where = slice(start, start + tile)
            query = heads[where, base : base + 128]
            keys = heads[:, base + 128 : base + 256]
            values = heads[:, base + 256 : base + 384]
            parts = []
            for half in range(2):
                inside = (lane // 64) == half
                picked = jnp.where(inside, query.astype(jnp.float32) * factor, 0.0).astype(LOW)
                scores = contract(keys, picked, 1, 1)
                scores = scores + key_bias
                top = jnp.max(scores, 0, keepdims=True)
                weight = jnp.exp(scores - top)
                weight_sum = jnp.sum(weight, 0, keepdims=True)
                log_total[2 * pair + half : 2 * pair + half + 1, where] = (
                    top + jnp.log(weight_sum)
                )
                weight = (weight * (1.0 / weight_sum)).astype(LOW)
                summed = contract(values, weight, 0, 0)
                parts.append(summed[half * 64 : (half + 1) * 64])
            both = jnp.concatenate(parts, 0)
            answer[where, pair * 128 : (pair + 1) * 128] = both.T.astype(LOW)
            plan.spend(2.0)

        answer_moment = plan.transfer("z", 4 * rows * 128 * 2 / LINK_RATE)
        columns = pl.ds(pair * 128, 128)
        for offset in range(1, SHARDS):
            answer_copies.append(
                extra(
                    3 * (pairs + pair) + 2 + offset,
                    answer.at[pl.ds(offset * rows, rows), columns],
                    mixed.at[:, pl.ds(column + pair * 128, 128)],
                    (place.rep, place.source(offset)),
                )
            )

    mixed[:, pl.ds(column, own)] = answer[0:rows, :]
    until(last[2])
    arrive(answer_copies, answer_moment)

    @pl.loop(0, width // 256)
    def _(part):
        start = pl.multiple_of(part * 256, 256)
        where = pl.ds(start, 256)
        middle[:, where] = (
            entering[:, where] + product(mixed, wholes[2], start, 256) + table[3:4, where]
        )

    plan.spend(1.5)
    norm_rows(middle, table[4:5, :], table[5:6, :], second_in, rows)
    plan.spend(2.0)
    per_row = width // 256
    for part in range(slope.shape[1] // BLOCK):
        until(last[2] + 1 + part)

        @pl.loop(0, BLOCK // 256)
        def _(piece):
            start = pl.multiple_of(part * BLOCK + piece * 256, 256)
            bias_at = pl.multiple_of(piece * 256, 256)
            value = (
                product(second_in, wholes[3], start, 256)
                + table[7 + part : 8 + part, pl.ds(bias_at, 256)]
            )
            below = 0.5 + 0.5 * lax.erf(value * math.sqrt(0.5))
            bell = jnp.exp(-0.5 * value * value) * (1.0 / math.sqrt(2.0 * math.pi))
            slope[:, pl.ds(start, 256)] = below + value * bell
            activated[:, pl.ds(start, 256)] = (value * below).astype(LOW)

        plan.spend(4.0)

    until(last[4])

    @pl.loop(0, width // 256)
    def _(part):
        start = pl.multiple_of(part * 256, 256)
        where = pl.ds(start, 256)
        out[:, where] = (
            middle[:, where] + product(activated, wholes[4], start, 256) + table[6:7, where]
        ).astype(LOW)

    for copy in sent:
        copy.wait_send()
    for used, copy in far:

        @pl.when(used)
        def _(copy=copy):
            copy.wait_send()

    for copy in kept:
        copy.wait()


def forward_pass(joined, vectors, masters, portion):
    shapes = [(matrix.shape[0] * SHARDS, matrix.shape[1]) for matrix in masters]
    chunks = chunk_list(shapes)
    total = len(chunks)
    rows = joined.shape[0]
    width = joined.shape[1] // 2
    own = width // SHARDS
    hidden = shapes[3][1]
    everyone = SHARDS * rows
    split = [
        matrix.reshape(matrix.shape[0] // 256, 2, 2, 2, 2, UNIT, matrix.shape[1])
        for matrix in masters
    ]
    folds = [(SHARDS, r // SHARDS // 256, 2, 2, 2, 2, UNIT, c) for r, c in shapes]
    inner = pl.BlockSpec(memory_space=pltpu.VMEM)
    table = jnp.pad(vectors, ((0, 16 - vectors.shape[0]), (0, 0)))
    outs = pl.pallas_call(
        functools.partial(forward_kernel, chunks, portion),
        out_shape=[jax.ShapeDtypeStruct(fold, LOW) for fold in folds]
        + [
            jax.ShapeDtypeStruct((rows, width), jnp.float32),
            jax.ShapeDtypeStruct((rows, width), LOW),
            jax.ShapeDtypeStruct((everyone, 3 * own), LOW),
            jax.ShapeDtypeStruct((8, everyone), jnp.float32),
            jax.ShapeDtypeStruct((rows, width), LOW),
            jax.ShapeDtypeStruct((rows, width), jnp.float32),
            jax.ShapeDtypeStruct((rows, width), LOW),
            jax.ShapeDtypeStruct((rows, hidden), jnp.float32),
            jax.ShapeDtypeStruct((rows, hidden), LOW),
            jax.ShapeDtypeStruct((rows, width), LOW),
            jax.ShapeDtypeStruct((16, width), jnp.float32),
        ],
        in_specs=[inner] * 2 + [ANY] * 5,
        out_specs=[ANY] * 5 + [inner] * 11,
        scratch_shapes=[pltpu.VMEM(fold, LOW) for fold in folds]
        + [
            pltpu.VMEM((2, 2, 2, 2, 2, UNIT, BLOCK), jnp.float32),
            pltpu.VMEM((16, own), LOW),
            pltpu.VMEM((SHARDS, 16, own), LOW),
            pltpu.VMEM((SHARDS, rows, 3 * own), LOW),
            pltpu.VMEM((everyone, own), LOW),
            pltpu.SemaphoreType.DMA((2,)),
            pltpu.SemaphoreType.DMA((total,)),
            pltpu.SemaphoreType.DMA((total * SLOTS,)),
            pltpu.SemaphoreType.DMA((total * SLOTS,)),
            pltpu.SemaphoreType.DMA((3 + 6 * (own // 128),)),
            pltpu.SemaphoreType.DMA((3 + 6 * (own // 128),)),
        ],
        compiler_params=pltpu.CompilerParams(
            collective_id=1, has_side_effects=True, vmem_limit_bytes=60 * 2**20
        ),
        name="forward_pass",
    )(joined, table, *split)
    weights = [out.reshape(shape) for out, shape in zip(outs[:5], shapes)]
    return weights, outs[5:]


def norm_back(source, gain, incoming, residual, wide_out, low_out, rows):
    columns = source.shape[1]

    def body(block, carry):
        where = pl.ds(pl.multiple_of(block * 32, 32), 32)
        stream = source[where, :]
        center = stream - jnp.mean(stream, -1, keepdims=True)
        spread = jnp.mean(center * center, -1, keepdims=True)
        scale = lax.rsqrt(spread + 1e-05)
        hat = center * scale
        grad = incoming[where, :]
        scaled = grad * gain
        slope = scale * (
            scaled
            - jnp.mean(scaled, -1, keepdims=True)
            - hat * jnp.mean(scaled * hat, -1, keepdims=True)
        )
        value = residual[where, :].astype(jnp.float32) + slope
        low = value.astype(LOW)
        if wide_out is not None:
            wide_out[where, :] = value
        low_out[where, :] = low
        terms = (grad * hat, grad, low.astype(jnp.float32))
        return tuple(kept + jnp.sum(term, 0, keepdims=True) for kept, term in zip(carry, terms))

    zero = jnp.zeros((1, columns), jnp.float32)
    return lax.fori_loop(0, rows // 32, body, (zero, zero, zero))


def backward_kernel(chunks, portion, *refs):
    (
        cotangent,
        vectors,
        log_total,
        activated,
    ) = refs[:4]
    outside = refs[4:12]
    weights = refs[12:17]
    masters = refs[17:22]
    states = refs[22:27]
    own_vectors, own_states = refs[27:29]
    sums = refs[29:34]
    table_sum, norms, grad_joined = refs[34:37]
    (
        ring,
        theirs,
        mine,
        from_core,
        from_first,
        from_second,
        final,
        from_z,
        ready,
        state_in,
        master_in,
        squares,
        square_in,
        square_z,
        table_own,
        table_in,
        table_z,
        grad_inner,
        grad_second,
        grad_middle,
        grad_middle_low,
        outgoing,
        grad_mixed,
        grad_key,
        grad_value,
        grad_heads,
        grad_triple,
        grad_entering,
        second_in,
        slope,
        middle,
        mixed,
        heads,
        first_in,
        entering,
        joined,
        load_sems,
        ring_sems,
        state_sems,
        ready_sems,
        send_sems,
        recv_sems,
        more_send,
        more_recv,
    ) = refs[37:]
    place = Place()
    s, k, x, y = place.shard, place.core, place.x, place.y
    rows, width = entering.shape
    own = width // SHARDS
    factor = 1.0 / math.sqrt(HEAD_DIM)
    depth = ring.shape[0]

    inside = (second_in, slope, middle, mixed, heads, first_in, entering, joined)
    loads = [
        pltpu.make_async_copy(source, target, load_sems.at[position])
        for position, (source, target) in enumerate(zip(outside, inside))
    ]
    names = ["second_in", "slope", "middle", "mixed", "heads", "first_in", "entering", "joined"]
    waiting_for = dict(zip(names, loads))

    def need(name):
        if name in waiting_for:
            waiting_for.pop(name).wait()

    def tiles(index):
        parts = weights[index].shape[7] // BLOCK
        return weights[index].shape[1], parts, SHARDS * weights[index].shape[1] * parts

    def fetch(index, at):
        groups, parts, _ = tiles(index)
        shard, rest = at // (groups * parts), lax.rem(at, groups * parts)
        group, part = rest // parts, lax.rem(rest, parts)
        start = pl.multiple_of(part * BLOCK, BLOCK)
        return pltpu.make_async_copy(
            weights[index].at[shard, group, :, :, :, :, :, pl.ds(start, BLOCK)],
            ring.at[lax.rem(at, depth)],
            ring_sems.at[lax.rem(at, depth)],
        )

    def prime(index):
        @pl.loop(0, min(depth, tiles(index)[2]))
        def _(at):
            fetch(index, at).start()

    def take(index, at):
        fetch(index, at).wait()
        return ring[lax.rem(at, depth)].reshape(256, BLOCK)

    def give(index, at):
        @pl.when(at + depth < tiles(index)[2])
        def _():
            fetch(index, at + depth).start()

    copies = {}

    def go(at, name, position, source, target, device):
        slot = at * 14 + position
        copy = pltpu.make_async_remote_copy(
            src_ref=source,
            dst_ref=target,
            send_sem=send_sems.at[slot],
            recv_sem=recv_sems.at[slot],
            device_id=device,
            device_id_type=MESH,
        )
        copy.start()
        copies.setdefault((at, name), []).append(copy)

    sent = []
    more = 18

    def extra(slot, source, target, device):
        copy = pltpu.make_async_remote_copy(
            src_ref=source,
            dst_ref=target,
            send_sem=more_send.at[slot],
            recv_sem=more_recv.at[slot],
            device_id=device,
            device_id_type=MESH,
        )
        copy.start()
        sent.append(copy)
        return copy

    def arrived(at, name):
        for copy in copies[(at, name)]:
            copy.wait_recv()

    def left(at, name):
        for copy in copies.pop((at, name), []):
            copy.wait_send()

    pairs = own // 128

    def triple_part(part):
        return jnp.concatenate(
            [
                grad_triple[shard, :, (3 * pair + part) * 128 : (3 * pair + part + 1) * 128]
                for shard in range(SHARDS)
                for pair in range(pairs)
            ],
            1,
        )

    def gradient_half(at, core):
        index, group, part = chunks[at]
        if index < 4:
            need(("joined", "first_in", "mixed", "second_in")[index])
        lefts = (joined, first_in, mixed, second_in, activated)[index]
        pitch = lefts.shape[1] // SHARDS
        columns = [
            lefts[:, pl.ds(pl.multiple_of(shard * pitch + group * 256 + core * 128, 128), 128)]
            for shard in range(SHARDS)
        ]
        if index == 0:
            right = grad_entering[...]
        elif index == 1:
            right = triple_part(part)
        elif index == 2:
            right = grad_middle_low[...]
        elif index == 3:
            right = grad_inner[:, part * BLOCK : (part + 1) * BLOCK]
        else:
            right = cotangent[...]
        return contract(jnp.concatenate(columns, 1), right, 0, 0)

    def stage_core(at):
        slot = at % 2
        value = gradient_half(at, 1 - k).astype(LOW)
        theirs[slot] = value.reshape(SHARDS, 2, 2, 2, UNIT, BLOCK)
        go(at, "core", 0, theirs.at[slot], from_core.at[slot], place.across("core"))

    def stage_first(at):
        slot = at % 3
        value = gradient_half(at, k).reshape(SHARDS, 2, 2, 2, UNIT, BLOCK)
        arrived(at, "core")
        left(at, "core")
        mine[slot] = (value + from_core[at % 2].astype(jnp.float32)).astype(LOW)
        target = from_first.at[at % 2]
        go(at, "first", 1, mine.at[slot, :, 0, :, 1 - x], target.at[0], place.across("x"))
        go(at, "first", 2, mine.at[slot, :, 1, 1 - y], target.at[1], place.across("y"))

    def stage_second(at):
        slot = at % 3
        arrived(at, "first")
        left(at, "first")

        @pl.loop(0, SHARDS)
        def _(shard):
            for i in range(2):
                mine[slot, shard, 0, i, x] = (
                    mine[slot, shard, 0, i, x].astype(jnp.float32)
                    + from_first[at % 2, 0, shard, i].astype(jnp.float32)
                ).astype(LOW)
                mine[slot, shard, 1, y, i] = (
                    mine[slot, shard, 1, y, i].astype(jnp.float32)
                    + from_first[at % 2, 1, shard, i].astype(jnp.float32)
                ).astype(LOW)

        target = from_second.at[at % 2]
        go(at, "second", 3, mine.at[slot, :, 0, 1 - y, x], target.at[0], place.across("y"))
        go(at, "second", 4, mine.at[slot, :, 1, y, 1 - x], target.at[1], place.across("x"))

    def piece_loads(at):
        index, group, part = chunks[at]
        slot = at % 2
        where = pl.ds(part * BLOCK, BLOCK)
        return (
            pltpu.make_async_copy(
                states[index].at[:, group, k, :, y, x, :, where],
                state_in.at[slot],
                state_sems.at[slot, 0],
            ),
            pltpu.make_async_copy(
                masters[index].at[group, k, :, y, x, :, where],
                master_in.at[slot],
                state_sems.at[slot, 1],
            ),
        )

    def stage_z(at):
        slot = at % 3
        arrived(at, "second")
        left(at, "second")

        @pl.loop(0, SHARDS)
        def _(shard):
            for h in range(2):
                final[at % 2, shard, h] = (
                    mine[slot, shard, h, y, x].astype(jnp.float32)
                    + from_second[at % 2, h, shard].astype(jnp.float32)
                ).astype(LOW)

        for copy in piece_loads(at):
            copy.start()
        for offset in range(1, SHARDS):
            target = lax.rem(s + offset, SHARDS)
            go(
                at,
                "z",
                5 + offset - 1,
                final.at[at % 2, target],
                from_z.at[at % 2, offset - 1],
                place.along(offset),
            )

    def summed(at, *where):
        index, group, part = chunks[at]
        rest = where + (slice(None),) * (5 - len(where))
        return sums[index].at[(group,) + rest + (pl.ds(part * BLOCK, BLOCK),)]

    def own_piece(at):
        return pltpu.make_async_copy(
            ready.at[at % 2], summed(at, k, slice(None), y, x), ready_sems.at[at % 2]
        )

    def direction_of(gradient, first, second):
        moment = 0.5 * first + 0.5 * gradient
        root = jnp.sqrt(0.5 * second * second + 0.5 * gradient * gradient)
        return moment / (root + 1e-06)

    def lanes(square):
        total = jnp.sum(square, 0, keepdims=True)
        parts = [total[:, i * 128 : (i + 1) * 128] for i in range(total.shape[1] // 128)]
        return sum(parts[1:], parts[0])

    def stage_back(at):
        index = chunks[at][0]
        slot = at % 2
        for copy in piece_loads(at):
            copy.wait()
        arrived(at, "z")
        left(at, "z")
        for h in range(2):
            value = final[slot, s, h].astype(jnp.float32)
            for offset in range(1, SHARDS):
                value = value + from_z[slot, offset - 1, h].astype(jnp.float32)
            low = value.astype(LOW)
            ready[slot, h] = low
            direction = direction_of(
                low.astype(jnp.float32), state_in[slot, 0, h], state_in[slot, 1, h]
            )
            master = master_in[slot, h]
            squares[0, index : index + 1, :] += lanes(master * master)
            squares[0, 8 + index : 9 + index, :] += lanes(direction * direction)
        own_piece(at).start()
        target = summed(at, k, 0, y, x)
        go(at, "back", 8, ready.at[slot, 0], target, place.across("y"))
        target = summed(at, k, 1, y, x)
        go(at, "back", 9, ready.at[slot, 1], target, place.across("x"))

    def stage_wide(at):
        own_piece(at).wait()
        arrived(at, "back")
        left(at, "back")
        ref = summed(at, k, 0, slice(None), x)
        go(at, "wide", 10, ref, ref, place.across("x"))
        ref = summed(at, k, 1, y)
        go(at, "wide", 11, ref, ref, place.across("y"))

    def stage_twin(at):
        arrived(at, "wide")
        ref = summed(at, k)
        go(at, "twin", 12, ref, ref, place.across("core"))

    def stage_end(at):
        arrived(at, "twin")

    stages = (
        stage_core,
        stage_first,
        stage_second,
        stage_z,
        stage_back,
        stage_wide,
        stage_twin,
        stage_end,
    )
    plan = Plan()
    total = len(chunks)
    at_stage = [0] * total
    allowed = [0]
    unit = UNIT * BLOCK * 2 / LINK_RATE
    costs = (0.8, 1.8, 0.6, 0.4, 0.4, 0.2, 0.1, 0.0)
    lengths = (
        (("core", 32 * unit / 6),),
        (("x", 8 * unit), ("y", 8 * unit)),
        (("x", 4 * unit), ("y", 4 * unit)),
        (("z", 8 * unit),),
        (("x", unit), ("y", unit)),
        (("x", 2 * unit), ("y", 2 * unit)),
        (("core", 8 * unit / 6),),
        (),
    )

    def chunk_steps(at):
        moment = 0.0
        for number, stage in enumerate(stages):
            def free(number=number):
                if number == 0 and at >= allowed[0]:
                    return False
                return at == 0 or at_stage[at - 1] >= min(number + 2, len(stages))

            yield moment, free
            stage(at)
            plan.now += costs[number]
            at_stage[at] = number + 1
            moment = max([plan.transfer(link, length) for link, length in lengths[number]] + [0.0])

    for at in range(total):
        plan.add(chunk_steps(at))

    def allow(index):
        allowed[0] = sum(1 for chunk in chunks if chunk[0] >= index)
        plan.pump()

    def arrive(copies, moment):
        plan.until(moment)
        for copy in copies:
            copy.wait_recv()

    prime(4)
    for copy in loads:
        copy.start()
    squares[...] = jnp.zeros_like(squares)
    table_own[...] = jnp.zeros_like(table_own)
    greet(place)
    allow(4)

    def put_row(row, value):
        for shard in range(SHARDS):
            table_own[0, shard, row : row + 1, :] = value[:, shard * own : (shard + 1) * own]

    put_row(6, jnp.sum(cotangent[...].astype(jnp.float32), 0, keepdims=True))

    groups = tiles(4)[0]
    need("slope")
    for quarter in range(SHARDS):

        @pl.loop(0, groups)
        def _(group):
            at = quarter * groups + group
            act = contract(cotangent[...], take(4, at), 1, 1)
            give(4, at)
            where = pl.ds(pl.multiple_of(at * 256, 256), 256)
            low = (act * slope[:, where]).astype(LOW)
            grad_inner[:, where] = low
            table_own[0, group, 7 + quarter : 8 + quarter, :] = jnp.sum(
                low.astype(jnp.float32), 0, keepdims=True
            )

        plan.spend(1.5)
    prime(3)
    allow(3)
    parts = tiles(3)[1]

    @pl.loop(0, SHARDS)
    def _(shard):
        where = pl.ds(pl.multiple_of(shard * 256, 256), 256)
        total = None
        for part in range(parts):
            at = shard * parts + part
            term = contract(grad_inner[:, part * BLOCK : (part + 1) * BLOCK], take(3, at), 1, 1)
            give(3, at)
            total = term if total is None else total + term
        grad_second[:, where] = total

    prime(2)
    plan.spend(3.0)
    need("middle")
    gain_sum, bias_sum, low_sum = norm_back(
        middle, vectors[4:5, :], grad_second, cotangent, grad_middle, grad_middle_low, rows
    )
    put_row(4, gain_sum)
    put_row(5, bias_sum)
    put_row(3, low_sum)
    plan.spend(3.0)
    allow(2)

    @pl.loop(0, SHARDS)
    def _(shard):
        outgoing[shard, :, 0:own] = contract(grad_middle_low[...], take(2, shard), 1, 1).astype(LOW)

    prime(1)
    plan.spend(1.0)
    mixed_copies = []
    moments = []
    for pair in range(pairs):
        moments.append(plan.transfer("z", 4 * rows * 128 * 2 / LINK_RATE))
        columns = pl.ds(pair * 128, 128)
        for offset in range(1, SHARDS):
            mixed_copies.append(
                extra(
                    more + 3 * pair + offset - 1,
                    outgoing.at[lax.rem(s + offset, SHARDS), :, columns],
                    grad_mixed.at[pl.ds(offset * rows, rows), columns],
                    place.along(offset),
                )
            )

    @pl.loop(0, rows // 32)
    def _(block):
        where = pl.ds(pl.multiple_of(block * 32, 32), 32)
        grad_mixed[where, :] = outgoing[s, where, 0:own]

    plan.spend(0.5)
    need("heads")
    everyone = SHARDS * rows
    tile = 384
    lane = lax.broadcasted_iota(jnp.int32, (tile, 128), 1)
    key_row = lax.rem(lax.broadcasted_iota(jnp.int32, (everyone, 128), 0), rows)
    live = key_row < portion
    triple_copies = []
    for pair in range(pairs):
        arrive(mixed_copies[3 * pair : 3 * pair + 3], moments[pair])
        base = pair * 384
        grad_key[...] = jnp.zeros_like(grad_key)
        grad_value[...] = jnp.zeros_like(grad_value)
        low, high = pair * 128, (pair + 1) * 128

        for block in range(everyone // tile):
            start = block * tile
            where = slice(start, start + tile)
            query = heads[where, base : base + 128]
            keys = heads[:, base + 128 : base + 256]
            values = heads[:, base + 256 : base + 384]
            incoming = grad_mixed[where, low:high]
            parts = []
            for half in range(2):
                inside = (lane // 64) == half
                picked = jnp.where(inside, query.astype(jnp.float32) * factor, 0.0).astype(LOW)
                grads = jnp.where(inside, incoming.astype(jnp.float32), 0.0).astype(LOW)
                scores = contract(keys, picked, 1, 1)
                at = 2 * pair + half
                below = scores - log_total[at : at + 1, where]
                weight = jnp.exp(jnp.minimum(below, 0.0))
                into = contract(values, grads, 1, 1)
                delta = jnp.sum(weight * into, 0, keepdims=True)
                grad_scores = (weight * (into - delta)).astype(LOW)
                grad_key[...] += jnp.dot(
                    grad_scores, picked, preferred_element_type=jnp.float32
                )
                grad_value[...] += jnp.dot(
                    weight.astype(LOW), grads, preferred_element_type=jnp.float32
                )
                turned = contract(keys, grad_scores, 0, 0)
                parts.append(turned[half * 64 : (half + 1) * 64])
            both = jnp.concatenate(parts, 0) * factor
            grad_heads[where, base : base + 128] = both.T.astype(LOW)
            plan.spend(4.0)

        grad_heads[:, base + 128 : base + 256] = jnp.where(live, grad_key[...], 0.0).astype(LOW)
        grad_heads[:, base + 256 : base + 384] = jnp.where(live, grad_value[...], 0.0).astype(LOW)
        columns = pl.ds(base, 384)
        triple_moment = plan.transfer("z", 4 * rows * 384 * 2 / LINK_RATE)
        for offset in range(1, SHARDS):
            triple_copies.append(
                extra(
                    more + 3 * (pairs + pair) + offset - 1,
                    grad_heads.at[pl.ds(offset * rows, rows), columns],
                    grad_triple.at[s, :, columns],
                    (place.rep, place.source(offset)),
                )
            )
        plan.pump()

    @pl.loop(0, rows // 32)
    def _(block):
        where = pl.ds(pl.multiple_of(block * 32, 32), 32)
        grad_triple[s, where, :] = grad_heads[where, :]

    arrive(triple_copies, triple_moment)
    allow(1)
    parts_in = tiles(1)[1]

    @pl.loop(0, SHARDS)
    def _(shard):
        where = pl.ds(pl.multiple_of(shard * 256, 256), 256)
        total = None
        for part in range(parts_in):
            at = shard * parts_in + part
            term = contract(triple_part(part), take(1, at), 1, 1)
            give(1, at)
            total = term if total is None else total + term
        grad_second[:, where] = total

    prime(0)
    need("entering")
    plan.spend(3.0)
    gain_sum, bias_sum, low_sum = norm_back(
        entering, vectors[1:2, :], grad_second, grad_middle, None, grad_entering, rows
    )
    put_row(1, gain_sum)
    put_row(2, bias_sum)
    put_row(0, low_sum)
    plan.spend(3.0)
    allow(0)
    table_copies = []

    def table_step(position, axis):
        if position:
            table_copies[-1].wait_recv()
            table_own[position] = table_own[position - 1] + table_in[position - 1]
        if axis:
            table_copies.append(
                extra(
                    6 + position,
                    table_own.at[position],
                    table_in.at[position],
                    place.across(axis),
                )
            )

    @pl.loop(0, tiles(0)[2])
    def _(at):
        where = pl.ds(pl.multiple_of(at * 256, 256), 256)
        grad_joined[:, where] = contract(grad_entering[...], take(0, at), 1, 1).astype(LOW)
        give(0, at)

    plan.spend(1.5)

    def table_steps():
        for position, axis in enumerate(("core", "x", "y", None)):
            table_step(position, axis)
            if axis:
                yield plan.transfer(axis, 1.5), None
        for offset in range(1, SHARDS):
            table_copies.append(
                extra(
                    8 + offset,
                    table_own.at[3, lax.rem(s + offset, SHARDS)],
                    table_z.at[offset - 1],
                    place.along(offset),
                )
            )
        yield plan.transfer("z", 2.0), None
        for copy in table_copies[3:]:
            copy.wait_recv()
        value = table_own[3, s]
        for offset in range(1, SHARDS):
            value = value + table_z[offset - 1]
        table_sum[...] = value
        direction = direction_of(value, own_states[0], own_states[1])
        share = 1.0 / REPLICAS
        squares[0, 5:6, :] = share * lanes(own_vectors[...] * own_vectors[...])
        squares[0, 13:14, :] = share * lanes(direction * direction)
        table_done[0] = True

    table_done = [False]
    squares_done = [False]

    def square_steps():
        yield 0.0, lambda: table_done[0] and min(at_stage) >= 5
        hops = []
        for position, axis in enumerate(("core", "x", "y", None)):
            if position:
                hops[-1].wait_recv()
                squares[position] = squares[position - 1] + square_in[position - 1]
            if axis:
                hops.append(
                    extra(
                        12 + position,
                        squares.at[position],
                        square_in.at[position],
                        place.across(axis),
                    )
                )
                yield plan.transfer(axis, 0.5), None
        hops = []
        for offset in range(1, SHARDS):
            hops.append(
                extra(14 + offset, squares.at[3], square_z.at[offset], place.along(offset))
            )
        square_z[0] = squares[3]
        yield plan.transfer("z", 0.5), None
        for copy in hops:
            copy.wait_recv()
        value = square_z[s]
        for shard in range(1, SHARDS):
            value = value + square_z[lax.rem(s + SHARDS - shard, SHARDS)]
        norms[...] = jnp.sqrt(jnp.sum(value, 1, keepdims=True)) + jnp.zeros_like(value)
        squares_done[0] = True

    plan.add(table_steps())
    plan.add(square_steps())
    plan.finish(lambda: squares_done[0] and min(at_stage) == len(stages))
    for key in sorted(copies):
        for copy in copies[key]:
            copy.wait_send()
    for copy in sent:
        copy.wait_send()


def backward_pass(cotangent, joined, table, kept, weights, masters, states, vectors, vector_states, portion):
    entering, first_in, heads, log_total, mixed, middle, second_in, slope, activated = kept[:9]
    shapes = [(matrix.shape[0] * SHARDS, matrix.shape[1]) for matrix in masters]
    order = chunk_list(shapes)
    chunks = [chunk for index in (4, 3, 2, 1, 0) for chunk in order if chunk[0] == index]
    total = len(chunks)
    rows, width = entering.shape
    own = width // SHARDS
    hidden = slope.shape[1]
    loaded = (second_in, slope, middle, mixed, heads, first_in, entering, joined)
    everyone = SHARDS * rows
    piece = (UNIT, BLOCK)
    inner = pl.BlockSpec(memory_space=pltpu.VMEM)
    folds = [(SHARDS, r // SHARDS // 256, 2, 2, 2, 2, UNIT, c) for r, c in shapes]
    extra_rows = 16 - vectors.shape[0]
    own_vectors = jnp.pad(vectors, ((0, extra_rows), (0, 0)))
    own_states = jnp.pad(vector_states, ((0, 0), (0, extra_rows), (0, 0)))
    outs = pl.pallas_call(
        functools.partial(backward_kernel, chunks, portion),
        out_shape=[jax.ShapeDtypeStruct(fold[1:], LOW) for fold in folds]
        + [
            jax.ShapeDtypeStruct((16, own), jnp.float32),
            jax.ShapeDtypeStruct((16, 128), jnp.float32),
            jax.ShapeDtypeStruct((rows, 2 * width), LOW),
        ],
        in_specs=[inner] * 4 + [ANY] * 23 + [inner] * 2,
        out_specs=[ANY] * 5 + [inner] * 3,
        scratch_shapes=[
            pltpu.VMEM((8, 2, 2, 2, 2) + piece, LOW),
            pltpu.VMEM((2, SHARDS, 2, 2, 2) + piece, LOW),
            pltpu.VMEM((3, SHARDS, 2, 2, 2) + piece, LOW),
            pltpu.VMEM((2, SHARDS, 2, 2, 2) + piece, LOW),
            pltpu.VMEM((2, 2, SHARDS, 2) + piece, LOW),
            pltpu.VMEM((2, 2, SHARDS) + piece, LOW),
            pltpu.VMEM((2, SHARDS, 2) + piece, LOW),
            pltpu.VMEM((2, SHARDS - 1, 2) + piece, LOW),
            pltpu.VMEM((2, 2) + piece, LOW),
            pltpu.VMEM((2, 2, 2) + piece, jnp.float32),
            pltpu.VMEM((2, 2) + piece, jnp.float32),
            pltpu.VMEM((4, 16, 128), jnp.float32),
            pltpu.VMEM((3, 16, 128), jnp.float32),
            pltpu.VMEM((SHARDS, 16, 128), jnp.float32),
            pltpu.VMEM((4, SHARDS, 16, own), jnp.float32),
            pltpu.VMEM((3, SHARDS, 16, own), jnp.float32),
            pltpu.VMEM((SHARDS - 1, 16, own), jnp.float32),
            pltpu.VMEM((rows, hidden), LOW),
            pltpu.VMEM((rows, width), jnp.float32),
            pltpu.VMEM((rows, width), jnp.float32),
            pltpu.VMEM((rows, width), LOW),
            pltpu.VMEM((SHARDS, rows, own), LOW),
            pltpu.VMEM((everyone, own), LOW),
            pltpu.VMEM((everyone, 128), jnp.float32),
            pltpu.VMEM((everyone, 128), jnp.float32),
            pltpu.VMEM((everyone, 3 * own), LOW),
            pltpu.VMEM((SHARDS, rows, 3 * own), LOW),
            pltpu.VMEM((rows, width), LOW),
            *[pltpu.VMEM(array.shape, array.dtype) for array in loaded],
            pltpu.SemaphoreType.DMA((8,)),
            pltpu.SemaphoreType.DMA((8,)),
            pltpu.SemaphoreType.DMA((2, 2)),
            pltpu.SemaphoreType.DMA((2,)),
            pltpu.SemaphoreType.DMA((total * 14,)),
            pltpu.SemaphoreType.DMA((total * 14,)),
            pltpu.SemaphoreType.DMA((18 + 6 * (own // 128),)),
            pltpu.SemaphoreType.DMA((18 + 6 * (own // 128),)),
        ],
        compiler_params=pltpu.CompilerParams(
            collective_id=2, has_side_effects=True, vmem_limit_bytes=60 * 2**20
        ),
        name="backward_pass",
    )(
        cotangent,
        table,
        log_total,
        activated,
        *loaded,
        *[matrix.reshape(fold) for matrix, fold in zip(weights, folds)],
        *[matrix.reshape(fold[1:]) for matrix, fold in zip(masters, folds)],
        *[state.reshape((2,) + fold[1:]) for state, fold in zip(states, folds)],
        own_vectors,
        own_states,
    )
    lows = [low.reshape(r // SHARDS, c) for low, (r, c) in zip(outs[:5], shapes)]
    return lows, outs[5][: vectors.shape[0]], outs[6], outs[7]


def update_kernel(position, norms, gradient, state, master, wide, new_state, new_master):
    grad = gradient[...].astype(jnp.float32)
    moment = 0.5 * state[0] + 0.5 * grad
    root = jnp.sqrt(0.5 * state[1] * state[1] + 0.5 * grad * grad)
    wide[...] = grad
    new_state[0] = moment
    new_state[1] = root
    ratio = norms[position : position + 1, 0:1] / (
        norms[8 + position : 9 + position, 0:1] + 1e-06
    )
    new_master[...] = master[...] - (step_rate * ratio) * (moment / (root + 1e-06))


def update_weight(position, norms, gradient, state, master):
    rows, columns = master.shape
    block = 256 if columns <= BLOCK else 64
    plain = pl.BlockSpec((block, columns), lambda i: (i, 0))
    paired = pl.BlockSpec((2, block, columns), lambda i: (0, i, 0))
    return pl.pallas_call(
        functools.partial(update_kernel, position),
        grid=(rows // block,),
        out_shape=[
            jax.ShapeDtypeStruct(master.shape, jnp.float32),
            jax.ShapeDtypeStruct(state.shape, jnp.float32),
            jax.ShapeDtypeStruct(master.shape, jnp.float32),
        ],
        in_specs=[pl.BlockSpec((16, 128), lambda i: (0, 0)), plain, paired, plain],
        out_specs=[plain, paired, plain],
        name="update_weight",
    )(norms, gradient, state, master)


def fits(masters):
    return (
        lax.axis_size("shard") == SHARDS
        and lax.axis_size("rep") == REPLICAS
        and all(m.shape[0] % 256 == 0 and m.shape[1] % BLOCK == 0 for m in masters)
        and masters[0].shape[1] == HEADS * HEAD_DIM == BLOCK
    )


def plain_device(
    hidden_in,
    skip_path,
    cotangent,
    skip_weight,
    heads_in,
    heads_out,
    expand_weight,
    reduce_weight,
    vectors,
    moments_skip,
    moments_in,
    moments_out,
    moments_expand,
    moments_reduce,
    moments_vectors,
):
    sequences, portion, model_width = hidden_in.shape
    shards = lax.axis_size("shard")
    replicas = lax.axis_size("rep")
    rep_index = lax.axis_index("rep")
    row_count = sequences * portion
    factor = 1.0 / math.sqrt(HEAD_DIM)
    masters = (skip_weight, heads_in, heads_out, expand_weight, reduce_weight, vectors)
    gathered = []
    for matrix in masters[:5]:
        height = matrix.shape[0] // replicas
        piece = lax.dynamic_slice_in_dim(matrix, rep_index * height, height, 0)
        piece = piece.astype(jnp.bfloat16)
        gathered.append(lax.all_gather(piece, ("shard", "rep"), axis=0, tiled=True))
    skip_matrix, in_matrix, out_matrix, expand_matrix, reduce_matrix = gathered
    table_low = lax.all_gather(vectors.astype(jnp.bfloat16), "shard", axis=1, tiled=True)
    table_rows = table_low.astype(jnp.float32)
    source = hidden_in.reshape(row_count, model_width)
    skip_rows = skip_path.reshape(row_count, model_width)
    joined = jnp.concatenate([source, skip_rows], 1)
    entering = matmul(joined, skip_matrix) + table_rows[0]
    normed_one, norm_back_one = jax.vjp(normalize, entering, table_rows[1], table_rows[2])
    first_in = normed_one.astype(jnp.bfloat16)
    triple = matmul(first_in, in_matrix).astype(jnp.bfloat16)
    heads = to_heads(triple, sequences, portion, shards)
    queries, keys_full, values_full = heads[:, :, 0], heads[:, :, 1], heads[:, :, 2]
    scores = (
        jnp.einsum("sqhd,skhd->shqk", queries, keys_full, preferred_element_type=jnp.float32)
        * factor
    )
    row_max = jnp.max(scores, -1)
    row_total = jnp.sum(jnp.exp(scores - row_max[..., None]), -1)
    log_total = row_max + jnp.log(row_total)
    probability = jnp.exp(scores - log_total[..., None])
    mixed = jnp.einsum(
        "shqk,skhd->sqhd",
        probability.astype(jnp.bfloat16),
        values_full,
        preferred_element_type=jnp.float32,
    )
    mixed_low = to_tokens(mixed.astype(jnp.bfloat16)[:, :, None], sequences, portion, shards)
    middle = entering + matmul(mixed_low, out_matrix) + table_rows[3]
    normed_two, norm_back_two = jax.vjp(normalize, middle, table_rows[4], table_rows[5])
    second_in = normed_two.astype(jnp.bfloat16)
    expanded = matmul(second_in, expand_matrix) + table_rows[7:].reshape(-1)
    activated, gelu_back = jax.vjp(exact_gelu, expanded)
    activated_low = activated.astype(jnp.bfloat16)
    block_result = middle + matmul(activated_low, reduce_matrix) + table_rows[6]
    block_out = block_result.astype(jnp.bfloat16).reshape(sequences, portion, model_width)
    grad_out = cotangent.reshape(row_count, model_width)
    grad_reduce = matmul(activated_low.T, grad_out)
    grad_act = matmul(grad_out, reduce_matrix.T)
    grad_inner = gelu_back(grad_act)[0].astype(jnp.bfloat16)
    grad_expand = matmul(second_in.T, grad_inner)
    grad_second = matmul(grad_inner, expand_matrix.T)
    grad_mid_norm, grad_gain_two, grad_bias_two = norm_back_two(grad_second)
    grad_middle = grad_out.astype(jnp.float32) + grad_mid_norm
    grad_middle_low = grad_middle.astype(jnp.bfloat16)
    grad_outw = matmul(mixed_low.T, grad_middle_low)
    grad_mixed = matmul(grad_middle_low, out_matrix.T).astype(jnp.bfloat16)
    grad_mixed = to_heads(grad_mixed, sequences, portion, shards)[:, :, 0]
    grad_prob = jnp.einsum(
        "sqhd,skhd->shqk", grad_mixed, values_full, preferred_element_type=jnp.float32
    )
    delta = jnp.sum(probability * grad_prob, -1)
    grad_scores = (probability * (grad_prob - delta[..., None])).astype(jnp.bfloat16)
    grad_query = (
        jnp.einsum("shqk,skhd->sqhd", grad_scores, keys_full, preferred_element_type=jnp.float32)
        * factor
    )
    grad_keys = (
        jnp.einsum("shqk,sqhd->skhd", grad_scores, queries, preferred_element_type=jnp.float32)
        * factor
    )
    grad_values = jnp.einsum(
        "shqk,sqhd->skhd",
        probability.astype(jnp.bfloat16),
        grad_mixed,
        preferred_element_type=jnp.float32,
    )
    grad_heads = jnp.stack([grad_query, grad_keys, grad_values], 2).astype(jnp.bfloat16)
    grad_triple = to_tokens(grad_heads, sequences, portion, shards)
    grad_inw = matmul(first_in.T, grad_triple)
    grad_first = matmul(grad_triple, in_matrix.T)
    grad_pre_norm, grad_gain_one, grad_bias_one = norm_back_one(grad_first)
    grad_entering = (grad_middle + grad_pre_norm).astype(jnp.bfloat16)
    grad_skipw = matmul(joined.T, grad_entering)
    grad_joined = matmul(grad_entering, skip_matrix.T)
    input_gradient = (
        grad_joined[:, :model_width].astype(jnp.bfloat16).reshape(sequences, portion, model_width)
    )
    skip_gradient = (
        grad_joined[:, model_width:].astype(jnp.bfloat16).reshape(sequences, portion, model_width)
    )
    grad_table = jnp.concatenate(
        [
            jnp.stack(
                [
                    row_sums(grad_entering),
                    grad_gain_one,
                    grad_bias_one,
                    row_sums(grad_middle_low),
                    grad_gain_two,
                    grad_bias_two,
                    row_sums(grad_out),
                ]
            ),
            row_sums(grad_inner).reshape(-1, model_width),
        ],
        0,
    )
    width = vectors.shape[1]
    grad_table = lax.psum(grad_table, ("rep", "shard"))
    vector_total = lax.dynamic_slice_in_dim(grad_table, lax.axis_index("shard") * width, width, 1)
    totals = []
    for partial in (grad_skipw, grad_inw, grad_outw, grad_expand, grad_reduce):
        piece = lax.psum_scatter(
            partial.astype(jnp.bfloat16), ("shard", "rep"), scatter_dimension=0, tiled=True
        )
        whole = lax.all_gather(piece, "rep", axis=0, tiled=True)
        totals.append(whole.astype(jnp.float32))
    totals.append(vector_total)
    states = (
        moments_skip,
        moments_in,
        moments_out,
        moments_expand,
        moments_reduce,
        moments_vectors,
    )
    steps = [moment_step(total, state) for total, state in zip(totals, states)]
    squares = jnp.stack(
        [
            jnp.stack([jnp.sum(matrix * matrix) for matrix in masters]),
            jnp.stack([jnp.sum(direction * direction) for _, direction in steps]),
        ]
    )
    norms = jnp.sqrt(lax.psum(squares, "shard"))
    ratio = norms[0] / (norms[1] + 1e-06)
    updated = [
        masters[position] - step_rate * ratio[position] * steps[position][1]
        for position in range(6)
    ]
    return (
        block_out,
        input_gradient,
        skip_gradient,
        *totals,
        *(state for state, _ in steps),
        *updated,
        norms,
    )


def on_device(
    hidden_in,
    skip_path,
    cotangent,
    skip_weight,
    heads_in,
    heads_out,
    expand_weight,
    reduce_weight,
    vectors,
    moments_skip,
    moments_in,
    moments_out,
    moments_expand,
    moments_reduce,
    moments_vectors,
):
    sequences, portion, model_width = hidden_in.shape
    masters = (skip_weight, heads_in, heads_out, expand_weight, reduce_weight)
    states = (moments_skip, moments_in, moments_out, moments_expand, moments_reduce)
    if not (sequences == 1 and fits(masters)):
        return plain_device(
            hidden_in, skip_path, cotangent, *masters, vectors, *states, moments_vectors
        )
    more = -portion % 32
    joined = jnp.concatenate([hidden_in[0], skip_path[0]], 1)
    joined = jnp.pad(joined, ((0, more), (0, 0)))
    incoming = jnp.pad(cotangent[0], ((0, more), (0, 0)))
    weights, kept = forward_pass(joined, vectors, masters, portion)
    block_out, table = kept[9], kept[10]
    lows, vector_total, norms, grad_joined = backward_pass(
        incoming, joined, table, kept, weights, masters, states, vectors, moments_vectors, portion
    )
    steps = [
        update_weight(position, norms, lows[position], states[position], masters[position])
        for position in range(5)
    ]
    vector_state, direction = moment_step(vector_total, moments_vectors)
    ratio = norms[5, 0] / (norms[13, 0] + 1e-06)
    return (
        block_out[None, :portion],
        grad_joined[None, :portion, :model_width],
        grad_joined[None, :portion, model_width:],
        *(step[0] for step in steps),
        vector_total,
        *(step[1] for step in steps),
        vector_state,
        *(step[2] for step in steps),
        vectors - step_rate * ratio * direction,
        jnp.stack([norms[:6, 0], norms[8:14, 0]]),
    )


def solution(mesh):
    placed = (
        P("rep", "shard", None),
        P("rep", "shard", None),
        P("rep", "shard", None),
        P("shard", None),
        P("shard", None),
        P("shard", None),
        P("shard", None),
        P("shard", None),
        P(None, "shard"),
        P(None, "shard", None),
        P(None, "shard", None),
        P(None, "shard", None),
        P(None, "shard", None),
        P(None, "shard", None),
        P(None, None, "shard"),
    )
    return jax.shard_map(
        on_device,
        mesh=mesh,
        in_specs=placed,
        out_specs=(
            P("rep", "shard", None),
            P("rep", "shard", None),
            P("rep", "shard", None),
            P("shard", None),
            P("shard", None),
            P("shard", None),
            P("shard", None),
            P("shard", None),
            P(None, "shard"),
            P(None, "shard", None),
            P(None, "shard", None),
            P(None, "shard", None),
            P(None, "shard", None),
            P(None, "shard", None),
            P(None, None, "shard"),
            P("shard", None),
            P("shard", None),
            P("shard", None),
            P("shard", None),
            P("shard", None),
            P(None, "shard"),
            P(),
        ),
        check_vma=False,
    )
```

```python
import functools
import math

import jax
import jax.numpy as jnp
from jax import lax
from jax.experimental import pallas as pl
from jax.experimental.pallas import tpu as pltpu
from jax.sharding import PartitionSpec as P

HEADS = 16
HEAD_DIM = 64
MESH = pl.DeviceIdType.MESH
LOW = jnp.bfloat16
ANY = pl.BlockSpec(memory_space=pl.ANY)
SHARDS, REPLICAS = 4, 8
UNIT = 16
BLOCK = 1024


class Place:
    def __init__(self):
        self.rep = lax.axis_index("rep")
        self.shard = lax.axis_index("shard")
        self.core = lax.rem(self.rep, 2)
        self.x = lax.rem(self.rep // 2, 2)
        self.y = self.rep // 4

    def across(self, axis):
        own, step = {"core": (self.core, 1), "x": (self.x, 2), "y": (self.y, 4)}[axis]
        return (self.rep + step - 2 * step * own, self.shard)

    def along(self, offset):
        return (self.rep, lax.rem(self.shard + offset, SHARDS))

    def source(self, offset):
        return lax.rem(self.shard + SHARDS - offset, SHARDS)

    def partners(self):
        return [self.across("core"), self.across("x"), self.across("y")] + [
            self.along(offset) for offset in range(1, SHARDS)
        ]


def greet(place):
    barrier = pltpu.get_barrier_semaphore()
    partners = place.partners()
    for partner in partners:
        pl.semaphore_signal(barrier, inc=1, device_id=partner, device_id_type=MESH)
    pl.semaphore_wait(barrier, len(partners))


def chunk_list(shapes):
    chunks = []
    for index, (rows, columns) in enumerate(shapes):
        for group in range(rows // SHARDS // 256):
            for part in range(columns // BLOCK):
                chunks.append((index, group, part))
    return chunks


class Plan:
    def __init__(self, latency=1.5):
        self.now, self.latency = 0.0, latency
        self.free = {}
        self.agents = []

    def transfer(self, link, length):
        self.free[link] = max(self.now, self.free.get(link, 0.0)) + length
        return self.free[link] + self.latency

    def backlog(self, link):
        return self.free.get(link, 0.0) - self.now

    def add(self, steps):
        agent = [steps, 0.0, None]
        self.agents.append(agent)
        self.resume(agent)

    def resume(self, agent):
        try:
            agent[1], agent[2] = next(agent[0])
        except StopIteration:
            self.agents.remove(agent)

    def ready(self):
        return [a for a in self.agents if a[2] is None or a[2]()]

    def pump(self):
        while True:
            able = [agent for agent in self.ready() if agent[1] <= self.now]
            if not able:
                return
            self.resume(able[0])

    def spend(self, length):
        self.now += 0.8 * length
        self.pump()

    def until(self, moment):
        self.pump()
        while self.now < moment:
            times = [agent[1] for agent in self.ready() if agent[1] > self.now]
            self.now = min(times + [moment])
            self.pump()

    def finish(self, test):
        self.pump()
        while not test():
            times = [agent[1] for agent in self.ready()]
            self.now = max(self.now, min(times))
            self.pump()


step_rate = 0.3


def normalize(stream, gain_row, bias_row):
    center = stream - jnp.mean(stream, -1, keepdims=True)
    spread = jnp.mean(center * center, -1, keepdims=True)
    return center * lax.rsqrt(spread + 1e-05) * gain_row + bias_row


def exact_gelu(inputs):
    return jax.nn.gelu(inputs, approximate=False)


def matmul(left, right):
    return jnp.dot(left, right, preferred_element_type=jnp.float32)


def row_sums(matrix):
    return jnp.sum(matrix, 0, dtype=jnp.float32)


def moment_step(gradient, moments):
    first_moment = 0.5 * moments[0] + 0.5 * gradient
    root_square = jnp.sqrt(0.5 * moments[1] * moments[1] + 0.5 * gradient * gradient)
    direction = first_moment / (root_square + 1e-06)
    return (jnp.stack([first_moment, root_square]), direction)


def to_heads(rows, sequences, portion, shards):
    parts = rows.shape[1] // (HEADS * HEAD_DIM)
    width = HEADS * HEAD_DIM // shards
    blocks = rows.reshape(sequences, portion, parts, shards, width).transpose(3, 0, 1, 2, 4)
    blocks = blocks.reshape(shards, sequences * portion, parts * width)
    blocks = lax.all_to_all(blocks, "shard", 0, 0, tiled=True)
    blocks = blocks.reshape(shards, sequences, portion, parts, width).transpose(1, 0, 2, 3, 4)
    return blocks.reshape(sequences, shards * portion, parts, width // HEAD_DIM, HEAD_DIM)


def to_tokens(blocks, sequences, portion, shards):
    parts = blocks.shape[2]
    width = HEADS * HEAD_DIM // shards
    rows = blocks.reshape(sequences, shards, portion, parts, width).transpose(1, 0, 2, 3, 4)
    rows = rows.reshape(shards, sequences * portion, parts * width)
    rows = lax.all_to_all(rows, "shard", 0, 0, tiled=True)
    rows = rows.reshape(shards, sequences * portion, parts, width).transpose(1, 2, 0, 3)
    return rows.reshape(sequences * portion, parts * shards * width)


SLOTS = 19
LINK_RATE = 45e3
Z_BACKLOG = 5.0


def weight_tile(whole, shard, group, start, width):
    return whole[shard, group, :, :, :, :, :, pl.ds(start, width)].reshape(256, width)


def product(left, whole, start, width):
    groups = whole.shape[1]
    total = None
    for shard in range(SHARDS):
        for group in range(groups):
            first = (shard * groups + group) * 256
            term = jnp.dot(
                left[:, first : first + 256],
                weight_tile(whole, shard, group, start, width),
                preferred_element_type=jnp.float32,
            )
            total = term if total is None else total + term
    return total


def contract(left, right, left_axis, right_axis):
    return lax.dot_general(
        left, right, (((left_axis,), (right_axis,)), ((), ())), preferred_element_type=jnp.float32
    )


def norm_rows(source, gain, bias, target, rows):
    @pl.loop(0, rows // 32)
    def _(block):
        where = pl.ds(pl.multiple_of(block * 32, 32), 32)
        stream = source[where, :]
        center = stream - jnp.mean(stream, -1, keepdims=True)
        spread = jnp.mean(center * center, -1, keepdims=True)
        target[where, :] = (center * lax.rsqrt(spread + 1e-05) * gain + bias).astype(LOW)


def forward_kernel(chunks, portion, *refs):
    joined, vectors = refs[0:2]
    masters = refs[2:7]
    keeps = refs[7:12]
    (
        entering,
        first_in,
        heads,
        log_total,
        mixed,
        middle,
        second_in,
        slope,
        activated,
        out,
        table,
    ) = refs[12:23]
    wholes = refs[23:28]
    (
        wide,
        table_own,
        table_all,
        outgoing,
        answer,
        load_sems,
        keep_sems,
        send_sems,
        recv_sems,
        more_send,
        more_recv,
    ) = refs[28:]
    place = Place()
    s, k, x, y = place.shard, place.core, place.x, place.y
    total = len(chunks)
    rows = entering.shape[0]
    width = entering.shape[1]
    own = width // SHARDS
    pairs = own // 128
    factor = 1.0 / math.sqrt(HEAD_DIM)

    def load(at):
        index, group, part = chunks[at]
        return pltpu.make_async_copy(
            masters[index].at[group, :, :, :, :, :, pl.ds(part * BLOCK, BLOCK)],
            wide.at[at % 2],
            load_sems.at[at % 2],
        )

    def whole(at, shard, *rest):
        index, group, part = chunks[at]
        rest = rest + (slice(None),) * (5 - len(rest))
        return wholes[index].at[(shard, group) + rest + (pl.ds(part * BLOCK, BLOCK),)]

    sent = []
    far = []
    arrivals = {}

    def relay_copy(at):
        up = s == SHARDS - 2
        ref = whole(at, place.source(2), k, slice(None), y, x)
        target = jnp.where(up, SHARDS - 1, 0)
        return pltpu.make_async_remote_copy(
            src_ref=ref,
            dst_ref=ref,
            send_sem=send_sems.at[at * SLOTS + SLOTS - 1],
            recv_sem=recv_sems.at[at * SLOTS + jnp.where(up, SHARDS - 2, 0)],
            device_id=(place.rep, target),
            device_id_type=MESH,
        )

    def go(at, name, position, ref, device):
        slot = at * SLOTS + position
        copy = pltpu.make_async_remote_copy(
            src_ref=ref,
            dst_ref=ref,
            send_sem=send_sems.at[slot],
            recv_sem=recv_sems.at[slot],
            device_id=device,
            device_id_type=MESH,
        )
        copy.start()
        sent.append(copy)
        arrivals.setdefault((at, name), []).append(copy)

    def arrived(at, name):
        for copy in arrivals[(at, name)]:
            copy.wait_recv()

    def extra(slot, source, target, device):
        copy = pltpu.make_async_remote_copy(
            src_ref=source,
            dst_ref=target,
            send_sem=more_send.at[slot],
            recv_sem=more_recv.at[slot],
            device_id=device,
            device_id_type=MESH,
        )
        copy.start()
        sent.append(copy)
        return copy

    kept = []

    def stage_cast(at):
        index, group, part = chunks[at]
        load(at).wait()

        @pl.loop(0, 16)
        def _(row):
            a, b = row // 8, lax.rem(row // 4, 2)
            c, d = lax.rem(row // 2, 2), lax.rem(row, 2)
            wholes[index][s, group, a, b, c, d, :, part * BLOCK : (part + 1) * BLOCK] = wide[
                at % 2, a, b, c, d
            ].astype(LOW)

        if at + 2 < total:
            load(at + 2).start()

    def stage_z(at):
        for offset in range(1, SHARDS):
            ref = whole(at, s, k, slice(None), y, x)
            slot = at * SLOTS + offset - 1
            target = lax.rem(s + offset, SHARDS)
            copy = pltpu.make_async_remote_copy(
                src_ref=ref,
                dst_ref=ref,
                send_sem=send_sems.at[slot],
                recv_sem=recv_sems.at[slot],
                device_id=(place.rep, target),
                device_id_type=MESH,
            )
            arrivals[(at, "z", offset)] = copy
            if offset == 2:
                copy.start()
                sent.append(copy)
            else:
                near = s != (0 if offset == SHARDS - 1 else SHARDS - 1)
                far.append((near, copy))

                @pl.when(near)
                def _(copy=copy):
                    copy.start()

    def stage_relay(at):
        arrivals[(at, "z", 2)].wait_recv()
        inner = (s > 0) & (s < SHARDS - 1)
        copy = relay_copy(at)
        far.append((inner, copy))

        @pl.when(inner)
        def _():
            copy.start()

    def stage_first(at):
        arrivals[(at, "z", 1)].wait_recv()
        arrivals[(at, "z", 3)].wait_recv()
        for offset in range(1, SHARDS):
            e = place.source(offset)
            go(at, "first", 3 + 2 * (offset - 1), whole(at, e, k, 0, y, x), place.across("x"))
            go(at, "first", 4 + 2 * (offset - 1), whole(at, e, k, 1, y, x), place.across("y"))

    def stage_second(at):
        arrived(at, "first")
        for offset in range(1, SHARDS):
            e = place.source(offset)
            go(at, "second", 9 + 2 * (offset - 1), whole(at, e, k, 0, y), place.across("y"))
            ref = whole(at, e, k, 1, slice(None), x)
            go(at, "second", 10 + 2 * (offset - 1), ref, place.across("x"))

    def stage_core(at):
        arrived(at, "second")
        for offset in range(1, SHARDS):
            e = place.source(offset)
            go(at, "core", 15 + offset - 1, whole(at, e, k), place.across("core"))

    def stage_end(at):
        arrived(at, "core")
        index, group, part = chunks[at]
        copy = pltpu.make_async_copy(
            whole(at, slice(None)),
            keeps[index].at[:, group, :, :, :, :, :, pl.ds(part * BLOCK, BLOCK)],
            keep_sems.at[at],
        )
        copy.start()
        kept.append(copy)

    plan = Plan()
    done = [0] * total
    unit = UNIT * BLOCK * 2 / LINK_RATE

    def chunk_steps(at):
        yield 0.0, lambda: (at == 0 or done[at - 1] >= 1) and plan.backlog("z") < Z_BACKLOG
        stage_cast(at)
        plan.now += 0.6
        stage_z(at)
        start = plan.transfer("z", 6 * unit)
        done[at] = 1
        yield start - 2 * unit, None
        stage_relay(at)
        yield start + 1.0, None
        stage_first(at)
        moment = max(plan.transfer("x", 3 * unit), plan.transfer("y", 3 * unit))
        yield moment, None
        stage_second(at)
        moment = max(plan.transfer("x", 6 * unit), plan.transfer("y", 6 * unit))
        yield moment, None
        stage_core(at)
        plan.now += 0.2
        yield plan.transfer("core", 24 * unit / 6), None
        stage_end(at)
        done[at] = 2

    def until(at):
        plan.finish(lambda: done[at] == 2)

    def arrive(copies, moment):
        plan.until(moment)
        for copy in copies:
            copy.wait_recv()

    load(0).start()
    load(1).start()
    table_own[...] = vectors[...].astype(LOW)
    table_all[0] = vectors[...].astype(LOW)
    greet(place)
    table_copies = []
    for offset in range(1, SHARDS):
        table_copies.append(extra(offset - 1, table_own, table_all.at[offset], place.along(offset)))
    for at in range(total):
        plan.add(chunk_steps(at))
    last = {}
    for at, (index, group, part) in enumerate(chunks):
        last[index] = at

    until(0)
    for copy in table_copies:
        copy.wait_recv()
    for offset in range(SHARDS):
        column = pl.multiple_of(place.source(offset) * own, own)
        table[:, pl.ds(column, own)] = table_all[offset].astype(jnp.float32)
    until(last[0])

    @pl.loop(0, width // 256)
    def _(part):
        start = pl.multiple_of(part * 256, 256)
        entering[:, pl.ds(start, 256)] = (
            product(joined, wholes[0], start, 256) + table[0:1, pl.ds(start, 256)]
        )

    plan.spend(2.5)
    norm_rows(entering, table[1:2, :], table[2:3, :], first_in, rows)
    plan.spend(2.0)
    until(last[1])
    live = lax.broadcasted_iota(jnp.int32, (rows, own), 0) < portion
    for kind in range(3):

        @pl.loop(0, SHARDS)
        def _(target):
            start = pl.multiple_of(kind * width + target * own, own)
            value = jnp.where(live, product(first_in, wholes[1], start, own), 0.0).astype(LOW)
            for pair in range(pairs):
                first = (3 * pair + kind) * 128
                outgoing[target, :, first : first + 128] = value[:, pair * 128 : (pair + 1) * 128]

        plan.spend(1.5)

    head_copies = []
    moments = []
    for pair in range(pairs):
        moments.append(plan.transfer("z", 4 * rows * 384 * 2 / LINK_RATE))
        for offset in range(1, SHARDS):
            target = lax.rem(s + offset, SHARDS)
            columns = pl.ds(pair * 384, 384)
            head_copies.append(
                extra(
                    3 * pair + 2 + offset,
                    outgoing.at[target, :, columns],
                    heads.at[pl.ds(offset * rows, rows), columns],
                    place.along(offset),
                )
            )

    @pl.loop(0, rows // 32)
    def _(block):
        where = pl.ds(pl.multiple_of(block * 32, 32), 32)
        heads[where, :] = outgoing[s, where, :]

    plan.spend(0.5)
    everyone = SHARDS * rows
    tile = 384
    lane = lax.broadcasted_iota(jnp.int32, (tile, 128), 1)
    key_row = lax.rem(lax.broadcasted_iota(jnp.int32, (everyone, 1), 0), rows)
    key_bias = jnp.where(key_row < portion, 0.0, -1e30)
    answer_copies = []
    column = pl.multiple_of(s * own, own)
    for pair in range(pairs):
        arrive(head_copies[3 * pair : 3 * pair + 3], moments[pair])
        base = pair * 384

        for block in range(everyone // tile):
            start = block * tile
            where = slice(start, start + tile)
            query = heads[where, base : base + 128]
            keys = heads[:, base + 128 : base + 256]
            values = heads[:, base + 256 : base + 384]
            parts = []
            for half in range(2):
                inside = (lane // 64) == half
                picked = jnp.where(inside, query.astype(jnp.float32) * factor, 0.0).astype(LOW)
                scores = contract(keys, picked, 1, 1)
                scores = scores + key_bias
                top = jnp.max(scores, 0, keepdims=True)
                weight = jnp.exp(scores - top)
                weight_sum = jnp.sum(weight, 0, keepdims=True)
                log_total[2 * pair + half : 2 * pair + half + 1, where] = (
                    top + jnp.log(weight_sum)
                )
                weight = (weight * (1.0 / weight_sum)).astype(LOW)
                summed = contract(values, weight, 0, 0)
                parts.append(summed[half * 64 : (half + 1) * 64])
            both = jnp.concatenate(parts, 0)
            answer[where, pair * 128 : (pair + 1) * 128] = both.T.astype(LOW)
            plan.spend(2.0)

        answer_moment = plan.transfer("z", 4 * rows * 128 * 2 / LINK_RATE)
        columns = pl.ds(pair * 128, 128)
        for offset in range(1, SHARDS):
            answer_copies.append(
                extra(
                    3 * (pairs + pair) + 2 + offset,
                    answer.at[pl.ds(offset * rows, rows), columns],
                    mixed.at[:, pl.ds(column + pair * 128, 128)],
                    (place.rep, place.source(offset)),
                )
            )

    mixed[:, pl.ds(column, own)] = answer[0:rows, :]
    until(last[2])
    arrive(answer_copies, answer_moment)

    @pl.loop(0, width // 256)
    def _(part):
        start = pl.multiple_of(part * 256, 256)
        where = pl.ds(start, 256)
        middle[:, where] = (
            entering[:, where] + product(mixed, wholes[2], start, 256) + table[3:4, where]
        )

    plan.spend(1.5)
    norm_rows(middle, table[4:5, :], table[5:6, :], second_in, rows)
    plan.spend(2.0)
    per_row = width // 256
    for part in range(slope.shape[1] // BLOCK):
        until(last[2] + 1 + part)

        @pl.loop(0, BLOCK // 256)
        def _(piece):
            start = pl.multiple_of(part * BLOCK + piece * 256, 256)
            bias_at = pl.multiple_of(piece * 256, 256)
            value = (
                product(second_in, wholes[3], start, 256)
                + table[7 + part : 8 + part, pl.ds(bias_at, 256)]
            )
            below = 0.5 + 0.5 * lax.erf(value * math.sqrt(0.5))
            bell = jnp.exp(-0.5 * value * value) * (1.0 / math.sqrt(2.0 * math.pi))
            slope[:, pl.ds(start, 256)] = below + value * bell
            activated[:, pl.ds(start, 256)] = (value * below).astype(LOW)

        plan.spend(4.0)

    until(last[4])

    @pl.loop(0, width // 256)
    def _(part):
        start = pl.multiple_of(part * 256, 256)
        where = pl.ds(start, 256)
        out[:, where] = (
            middle[:, where] + product(activated, wholes[4], start, 256) + table[6:7, where]
        ).astype(LOW)

    for copy in sent:
        copy.wait_send()
    for used, copy in far:

        @pl.when(used)
        def _(copy=copy):
            copy.wait_send()

    for copy in kept:
        copy.wait()


def forward_pass(joined, vectors, masters, portion):
    shapes = [(matrix.shape[0] * SHARDS, matrix.shape[1]) for matrix in masters]
    chunks = chunk_list(shapes)
    total = len(chunks)
    rows = joined.shape[0]
    width = joined.shape[1] // 2
    own = width // SHARDS
    hidden = shapes[3][1]
    everyone = SHARDS * rows
    split = [
        matrix.reshape(matrix.shape[0] // 256, 2, 2, 2, 2, UNIT, matrix.shape[1])
        for matrix in masters
    ]
    folds = [(SHARDS, r // SHARDS // 256, 2, 2, 2, 2, UNIT, c) for r, c in shapes]
    inner = pl.BlockSpec(memory_space=pltpu.VMEM)
    table = jnp.pad(vectors, ((0, 16 - vectors.shape[0]), (0, 0)))
    outs = pl.pallas_call(
        functools.partial(forward_kernel, chunks, portion),
        out_shape=[jax.ShapeDtypeStruct(fold, LOW) for fold in folds]
        + [
            jax.ShapeDtypeStruct((rows, width), jnp.float32),
            jax.ShapeDtypeStruct((rows, width), LOW),
            jax.ShapeDtypeStruct((everyone, 3 * own), LOW),
            jax.ShapeDtypeStruct((8, everyone), jnp.float32),
            jax.ShapeDtypeStruct((rows, width), LOW),
            jax.ShapeDtypeStruct((rows, width), jnp.float32),
            jax.ShapeDtypeStruct((rows, width), LOW),
            jax.ShapeDtypeStruct((rows, hidden), jnp.float32),
            jax.ShapeDtypeStruct((rows, hidden), LOW),
            jax.ShapeDtypeStruct((rows, width), LOW),
            jax.ShapeDtypeStruct((16, width), jnp.float32),
        ],
        in_specs=[inner] * 2 + [ANY] * 5,
        out_specs=[ANY] * 5 + [inner] * 11,
        scratch_shapes=[pltpu.VMEM(fold, LOW) for fold in folds]
        + [
            pltpu.VMEM((2, 2, 2, 2, 2, UNIT, BLOCK), jnp.float32),
            pltpu.VMEM((16, own), LOW),
            pltpu.VMEM((SHARDS, 16, own), LOW),
            pltpu.VMEM((SHARDS, rows, 3 * own), LOW),
            pltpu.VMEM((everyone, own), LOW),
            pltpu.SemaphoreType.DMA((2,)),
            pltpu.SemaphoreType.DMA((total,)),
            pltpu.SemaphoreType.DMA((total * SLOTS,)),
            pltpu.SemaphoreType.DMA((total * SLOTS,)),
            pltpu.SemaphoreType.DMA((3 + 6 * (own // 128),)),
            pltpu.SemaphoreType.DMA((3 + 6 * (own // 128),)),
        ],
        compiler_params=pltpu.CompilerParams(
            collective_id=1, has_side_effects=True, vmem_limit_bytes=60 * 2**20
        ),
        name="forward_pass",
    )(joined, table, *split)
    weights = [out.reshape(shape) for out, shape in zip(outs[:5], shapes)]
    return weights, outs[5:]


def norm_back(source, gain, incoming, residual, wide_out, low_out, rows):
    columns = source.shape[1]

    def body(block, carry):
        where = pl.ds(pl.multiple_of(block * 32, 32), 32)
        stream = source[where, :]
        center = stream - jnp.mean(stream, -1, keepdims=True)
        spread = jnp.mean(center * center, -1, keepdims=True)
        scale = lax.rsqrt(spread + 1e-05)
        hat = center * scale
        grad = incoming[where, :]
        scaled = grad * gain
        slope = scale * (
            scaled
            - jnp.mean(scaled, -1, keepdims=True)
            - hat * jnp.mean(scaled * hat, -1, keepdims=True)
        )
        value = residual[where, :].astype(jnp.float32) + slope
        low = value.astype(LOW)
        if wide_out is not None:
            wide_out[where, :] = value
        low_out[where, :] = low
        terms = (grad * hat, grad, low.astype(jnp.float32))
        return tuple(kept + jnp.sum(term, 0, keepdims=True) for kept, term in zip(carry, terms))

    zero = jnp.zeros((1, columns), jnp.float32)
    return lax.fori_loop(0, rows // 32, body, (zero, zero, zero))


def backward_kernel(chunks, portion, *refs):
    (
        cotangent,
        vectors,
        log_total,
        activated,
    ) = refs[:4]
    outside = refs[4:12]
    weights = refs[12:17]
    masters = refs[17:22]
    states = refs[22:27]
    own_vectors, own_states = refs[27:29]
    sums = refs[29:34]
    table_sum, norms, grad_joined = refs[34:37]
    (
        ring,
        theirs,
        mine,
        from_core,
        from_first,
        from_second,
        final,
        from_z,
        ready,
        state_in,
        master_in,
        squares,
        square_in,
        square_z,
        table_own,
        table_in,
        table_z,
        grad_inner,
        grad_second,
        grad_middle,
        grad_middle_low,
        outgoing,
        grad_mixed,
        grad_key,
        grad_value,
        grad_heads,
        grad_triple,
        grad_entering,
        second_in,
        slope,
        middle,
        mixed,
        heads,
        first_in,
        entering,
        joined,
        load_sems,
        ring_sems,
        state_sems,
        ready_sems,
        send_sems,
        recv_sems,
        more_send,
        more_recv,
    ) = refs[37:]
    place = Place()
    s, k, x, y = place.shard, place.core, place.x, place.y
    rows, width = entering.shape
    own = width // SHARDS
    factor = 1.0 / math.sqrt(HEAD_DIM)
    depth = ring.shape[0]

    inside = (second_in, slope, middle, mixed, heads, first_in, entering, joined)
    loads = [
        pltpu.make_async_copy(source, target, load_sems.at[position])
        for position, (source, target) in enumerate(zip(outside, inside))
    ]
    names = ["second_in", "slope", "middle", "mixed", "heads", "first_in", "entering", "joined"]
    waiting_for = dict(zip(names, loads))

    def need(name):
        if name in waiting_for:
            waiting_for.pop(name).wait()

    def tiles(index):
        parts = weights[index].shape[7] // BLOCK
        return weights[index].shape[1], parts, SHARDS * weights[index].shape[1] * parts

    def fetch(index, at):
        groups, parts, _ = tiles(index)
        shard, rest = at // (groups * parts), lax.rem(at, groups * parts)
        group, part = rest // parts, lax.rem(rest, parts)
        start = pl.multiple_of(part * BLOCK, BLOCK)
        return pltpu.make_async_copy(
            weights[index].at[shard, group, :, :, :, :, :, pl.ds(start, BLOCK)],
            ring.at[lax.rem(at, depth)],
            ring_sems.at[lax.rem(at, depth)],
        )

    def prime(index):
        @pl.loop(0, min(depth, tiles(index)[2]))
        def _(at):
            fetch(index, at).start()

    def take(index, at):
        fetch(index, at).wait()
        return ring[lax.rem(at, depth)].reshape(256, BLOCK)

    def give(index, at):
        @pl.when(at + depth < tiles(index)[2])
        def _():
            fetch(index, at + depth).start()

    copies = {}

    def go(at, name, position, source, target, device):
        slot = at * 14 + position
        copy = pltpu.make_async_remote_copy(
            src_ref=source,
            dst_ref=target,
            send_sem=send_sems.at[slot],
            recv_sem=recv_sems.at[slot],
            device_id=device,
            device_id_type=MESH,
        )
        copy.start()
        copies.setdefault((at, name), []).append(copy)

    sent = []
    more = 18

    def extra(slot, source, target, device):
        copy = pltpu.make_async_remote_copy(
            src_ref=source,
            dst_ref=target,
            send_sem=more_send.at[slot],
            recv_sem=more_recv.at[slot],
            device_id=device,
            device_id_type=MESH,
        )
        copy.start()
        sent.append(copy)
        return copy

    def arrived(at, name):
        for copy in copies[(at, name)]:
            copy.wait_recv()

    def left(at, name):
        for copy in copies.pop((at, name), []):
            copy.wait_send()

    pairs = own // 128

    def triple_part(part):
        return jnp.concatenate(
            [
                grad_triple[shard, :, (3 * pair + part) * 128 : (3 * pair + part + 1) * 128]
                for shard in range(SHARDS)
                for pair in range(pairs)
            ],
            1,
        )

    def gradient_half(at, core):
        index, group, part = chunks[at]
        if index < 4:
            need(("joined", "first_in", "mixed", "second_in")[index])
        lefts = (joined, first_in, mixed, second_in, activated)[index]
        pitch = lefts.shape[1] // SHARDS
        columns = [
            lefts[:, pl.ds(pl.multiple_of(shard * pitch + group * 256 + core * 128, 128), 128)]
            for shard in range(SHARDS)
        ]
        if index == 0:
            right = grad_entering[...]
        elif index == 1:
            right = triple_part(part)
        elif index == 2:
            right = grad_middle_low[...]
        elif index == 3:
            right = grad_inner[:, part * BLOCK : (part + 1) * BLOCK]
        else:
            right = cotangent[...]
        return contract(jnp.concatenate(columns, 1), right, 0, 0)

    def stage_core(at):
        slot = at % 2
        value = gradient_half(at, 1 - k).astype(LOW)
        theirs[slot] = value.reshape(SHARDS, 2, 2, 2, UNIT, BLOCK)
        go(at, "core", 0, theirs.at[slot], from_core.at[at % 4], place.across("core"))

    def stage_first(at):
        slot = at % 5
        value = gradient_half(at, k).reshape(SHARDS, 2, 2, 2, UNIT, BLOCK)
        arrived(at, "core")
        left(at, "core")
        mine[slot] = (value + from_core[at % 4].astype(jnp.float32)).astype(LOW)
        target = from_first.at[at % 4]
        go(at, "first", 1, mine.at[slot, :, 0, :, 1 - x], target.at[0], place.across("x"))
        go(at, "first", 2, mine.at[slot, :, 1, 1 - y], target.at[1], place.across("y"))

    def stage_second(at):
        slot = at % 5
        arrived(at, "first")
        left(at, "first")

        @pl.loop(0, SHARDS)
        def _(shard):
            for i in range(2):
                mine[slot, shard, 0, i, x] = (
                    mine[slot, shard, 0, i, x].astype(jnp.float32)
                    + from_first[at % 4, 0, shard, i].astype(jnp.float32)
                ).astype(LOW)
                mine[slot, shard, 1, y, i] = (
                    mine[slot, shard, 1, y, i].astype(jnp.float32)
                    + from_first[at % 4, 1, shard, i].astype(jnp.float32)
                ).astype(LOW)

        target = from_second.at[at % 4]
        go(at, "second", 3, mine.at[slot, :, 0, 1 - y, x], target.at[0], place.across("y"))
        go(at, "second", 4, mine.at[slot, :, 1, y, 1 - x], target.at[1], place.across("x"))

    def piece_loads(at):
        index, group, part = chunks[at]
        slot = at % 2
        where = pl.ds(part * BLOCK, BLOCK)
        return (
            pltpu.make_async_copy(
                states[index].at[:, group, k, :, y, x, :, where],
                state_in.at[slot],
                state_sems.at[slot, 0],
            ),
            pltpu.make_async_copy(
                masters[index].at[group, k, :, y, x, :, where],
                master_in.at[slot],
                state_sems.at[slot, 1],
            ),
        )

    def stage_z(at):
        slot = at % 5
        arrived(at, "second")
        left(at, "second")

        @pl.loop(0, SHARDS)
        def _(shard):
            for h in range(2):
                final[at % 2, shard, h] = (
                    mine[slot, shard, h, y, x].astype(jnp.float32)
                    + from_second[at % 4, h, shard].astype(jnp.float32)
                ).astype(LOW)

        for copy in piece_loads(at):
            copy.start()
        for offset in range(1, SHARDS):
            target = lax.rem(s + offset, SHARDS)
            go(
                at,
                "z",
                5 + offset - 1,
                final.at[at % 2, target],
                from_z.at[at % 4, offset - 1],
                place.along(offset),
            )

    def summed(at, *where):
        index, group, part = chunks[at]
        rest = where + (slice(None),) * (5 - len(where))
        return sums[index].at[(group,) + rest + (pl.ds(part * BLOCK, BLOCK),)]

    def own_piece(at):
        return pltpu.make_async_copy(
            ready.at[at % 2], summed(at, k, slice(None), y, x), ready_sems.at[at % 2]
        )

    def direction_of(gradient, first, second):
        moment = 0.5 * first + 0.5 * gradient
        root = jnp.sqrt(0.5 * second * second + 0.5 * gradient * gradient)
        return moment / (root + 1e-06)

    def lanes(square):
        total = jnp.sum(square, 0, keepdims=True)
        parts = [total[:, i * 128 : (i + 1) * 128] for i in range(total.shape[1] // 128)]
        return sum(parts[1:], parts[0])

    def stage_back(at):
        index = chunks[at][0]
        slot = at % 2
        for copy in piece_loads(at):
            copy.wait()
        arrived(at, "z")
        left(at, "z")
        for h in range(2):
            value = final[slot, s, h].astype(jnp.float32)
            for offset in range(1, SHARDS):
                value = value + from_z[at % 4, offset - 1, h].astype(jnp.float32)
            low = value.astype(LOW)
            ready[slot, h] = low
            direction = direction_of(
                low.astype(jnp.float32), state_in[slot, 0, h], state_in[slot, 1, h]
            )
            master = master_in[slot, h]
            squares[0, index : index + 1, :] += lanes(master * master)
            squares[0, 8 + index : 9 + index, :] += lanes(direction * direction)
        own_piece(at).start()
        target = summed(at, k, 0, y, x)
        go(at, "back", 8, ready.at[slot, 0], target, place.across("y"))
        target = summed(at, k, 1, y, x)
        go(at, "back", 9, ready.at[slot, 1], target, place.across("x"))

    def stage_wide(at):
        own_piece(at).wait()
        arrived(at, "back")
        left(at, "back")
        ref = summed(at, k, 0, slice(None), x)
        go(at, "wide", 10, ref, ref, place.across("x"))
        ref = summed(at, k, 1, y)
        go(at, "wide", 11, ref, ref, place.across("y"))

    def stage_twin(at):
        arrived(at, "wide")
        ref = summed(at, k)
        go(at, "twin", 12, ref, ref, place.across("core"))

    def stage_end(at):
        arrived(at, "twin")

    stages = (
        stage_core,
        stage_first,
        stage_second,
        stage_z,
        stage_back,
        stage_wide,
        stage_twin,
        stage_end,
    )
    plan = Plan()
    total = len(chunks)
    at_stage = [0] * total
    allowed = [0]
    unit = UNIT * BLOCK * 2 / LINK_RATE
    costs = (0.5, 1.1, 0.4, 0.25, 0.25, 0.1, 0.1, 0.0)
    lengths = (
        (("core", 32 * unit / 6),),
        (("x", 8 * unit), ("y", 8 * unit)),
        (("x", 4 * unit), ("y", 4 * unit)),
        (("z", 8 * unit),),
        (("x", unit), ("y", unit)),
        (("x", 2 * unit), ("y", 2 * unit)),
        (("core", 8 * unit / 6),),
        (),
    )

    def chunk_steps(at):
        moment = 0.0
        for number, stage in enumerate(stages):
            def free(number=number):
                if number == 0 and at >= allowed[0]:
                    return False
                if number == 1 and at >= 5 and at_stage[at - 5] < 4:
                    return False
                if at and at_stage[at - 1] <= number:
                    return False
                return at < 2 or at_stage[at - 2] >= min(number + 2, len(stages))

            yield moment, free
            stage(at)
            plan.now += costs[number]
            at_stage[at] = number + 1
            moment = max([plan.transfer(link, length) for link, length in lengths[number]] + [0.0])

    for at in range(total):
        plan.add(chunk_steps(at))

    def allow(index):
        allowed[0] = sum(1 for chunk in chunks if chunk[0] >= index)
        plan.pump()

    def arrive(copies, moment):
        plan.until(moment)
        for copy in copies:
            copy.wait_recv()

    prime(4)
    for copy in loads:
        copy.start()
    squares[...] = jnp.zeros_like(squares)
    table_own[...] = jnp.zeros_like(table_own)
    greet(place)
    allow(4)

    def put_row(row, value):
        for shard in range(SHARDS):
            table_own[0, shard, row : row + 1, :] = value[:, shard * own : (shard + 1) * own]

    put_row(6, jnp.sum(cotangent[...].astype(jnp.float32), 0, keepdims=True))

    groups = tiles(4)[0]
    need("slope")
    for quarter in range(SHARDS):

        @pl.loop(0, groups)
        def _(group):
            at = quarter * groups + group
            act = contract(cotangent[...], take(4, at), 1, 1)
            give(4, at)
            where = pl.ds(pl.multiple_of(at * 256, 256), 256)
            low = (act * slope[:, where]).astype(LOW)
            grad_inner[:, where] = low
            table_own[0, group, 7 + quarter : 8 + quarter, :] = jnp.sum(
                low.astype(jnp.float32), 0, keepdims=True
            )

        plan.spend(1.5)
    prime(3)
    allow(3)
    parts = tiles(3)[1]

    @pl.loop(0, SHARDS)
    def _(shard):
        where = pl.ds(pl.multiple_of(shard * 256, 256), 256)
        total = None
        for part in range(parts):
            at = shard * parts + part
            term = contract(grad_inner[:, part * BLOCK : (part + 1) * BLOCK], take(3, at), 1, 1)
            give(3, at)
            total = term if total is None else total + term
        grad_second[:, where] = total

    prime(2)
    plan.spend(3.0)
    need("middle")
    gain_sum, bias_sum, low_sum = norm_back(
        middle, vectors[4:5, :], grad_second, cotangent, grad_middle, grad_middle_low, rows
    )
    put_row(4, gain_sum)
    put_row(5, bias_sum)
    put_row(3, low_sum)
    plan.spend(3.0)
    allow(2)

    @pl.loop(0, SHARDS)
    def _(shard):
        outgoing[shard, :, 0:own] = contract(grad_middle_low[...], take(2, shard), 1, 1).astype(LOW)

    prime(1)
    plan.spend(1.0)
    mixed_copies = []
    moments = []
    for pair in range(pairs):
        moments.append(plan.transfer("z", 4 * rows * 128 * 2 / LINK_RATE))
        columns = pl.ds(pair * 128, 128)
        for offset in range(1, SHARDS):
            mixed_copies.append(
                extra(
                    more + 3 * pair + offset - 1,
                    outgoing.at[lax.rem(s + offset, SHARDS), :, columns],
                    grad_mixed.at[pl.ds(offset * rows, rows), columns],
                    place.along(offset),
                )
            )

    @pl.loop(0, rows // 32)
    def _(block):
        where = pl.ds(pl.multiple_of(block * 32, 32), 32)
        grad_mixed[where, :] = outgoing[s, where, 0:own]

    plan.spend(0.5)
    need("heads")
    everyone = SHARDS * rows
    tile = 384
    lane = lax.broadcasted_iota(jnp.int32, (tile, 128), 1)
    key_row = lax.rem(lax.broadcasted_iota(jnp.int32, (everyone, 128), 0), rows)
    live = key_row < portion
    triple_copies = []
    for pair in range(pairs):
        arrive(mixed_copies[3 * pair : 3 * pair + 3], moments[pair])
        base = pair * 384
        grad_key[...] = jnp.zeros_like(grad_key)
        grad_value[...] = jnp.zeros_like(grad_value)
        low, high = pair * 128, (pair + 1) * 128

        for block in range(everyone // tile):
            start = block * tile
            where = slice(start, start + tile)
            query = heads[where, base : base + 128]
            keys = heads[:, base + 128 : base + 256]
            values = heads[:, base + 256 : base + 384]
            incoming = grad_mixed[where, low:high]
            parts = []
            for half in range(2):
                inside = (lane // 64) == half
                picked = jnp.where(inside, query.astype(jnp.float32) * factor, 0.0).astype(LOW)
                grads = jnp.where(inside, incoming.astype(jnp.float32), 0.0).astype(LOW)
                scores = contract(keys, picked, 1, 1)
                at = 2 * pair + half
                below = scores - log_total[at : at + 1, where]
                weight = jnp.exp(jnp.minimum(below, 0.0))
                into = contract(values, grads, 1, 1)
                delta = jnp.sum(weight * into, 0, keepdims=True)
                grad_scores = (weight * (into - delta)).astype(LOW)
                grad_key[...] += jnp.dot(
                    grad_scores, picked, preferred_element_type=jnp.float32
                )
                grad_value[...] += jnp.dot(
                    weight.astype(LOW), grads, preferred_element_type=jnp.float32
                )
                turned = contract(keys, grad_scores, 0, 0)
                parts.append(turned[half * 64 : (half + 1) * 64])
            both = jnp.concatenate(parts, 0) * factor
            grad_heads[where, base : base + 128] = both.T.astype(LOW)
            plan.spend(4.0)

        grad_heads[:, base + 128 : base + 256] = jnp.where(live, grad_key[...], 0.0).astype(LOW)
        grad_heads[:, base + 256 : base + 384] = jnp.where(live, grad_value[...], 0.0).astype(LOW)
        columns = pl.ds(base, 384)
        triple_moment = plan.transfer("z", 4 * rows * 384 * 2 / LINK_RATE)
        for offset in range(1, SHARDS):
            triple_copies.append(
                extra(
                    more + 3 * (pairs + pair) + offset - 1,
                    grad_heads.at[pl.ds(offset * rows, rows), columns],
                    grad_triple.at[s, :, columns],
                    (place.rep, place.source(offset)),
                )
            )
        plan.pump()

    @pl.loop(0, rows // 32)
    def _(block):
        where = pl.ds(pl.multiple_of(block * 32, 32), 32)
        grad_triple[s, where, :] = grad_heads[where, :]

    arrive(triple_copies, triple_moment)
    allow(1)
    parts_in = tiles(1)[1]

    @pl.loop(0, SHARDS)
    def _(shard):
        where = pl.ds(pl.multiple_of(shard * 256, 256), 256)
        total = None
        for part in range(parts_in):
            at = shard * parts_in + part
            term = contract(triple_part(part), take(1, at), 1, 1)
            give(1, at)
            total = term if total is None else total + term
        grad_second[:, where] = total

    prime(0)
    need("entering")
    plan.spend(3.0)
    gain_sum, bias_sum, low_sum = norm_back(
        entering, vectors[1:2, :], grad_second, grad_middle, None, grad_entering, rows
    )
    put_row(1, gain_sum)
    put_row(2, bias_sum)
    put_row(0, low_sum)
    plan.spend(3.0)
    allow(0)
    table_copies = []

    def table_step(position, axis):
        if position:
            table_copies[-1].wait_recv()
            table_own[position] = table_own[position - 1] + table_in[position - 1]
        if axis:
            table_copies.append(
                extra(
                    6 + position,
                    table_own.at[position],
                    table_in.at[position],
                    place.across(axis),
                )
            )

    @pl.loop(0, tiles(0)[2])
    def _(at):
        where = pl.ds(pl.multiple_of(at * 256, 256), 256)
        grad_joined[:, where] = contract(grad_entering[...], take(0, at), 1, 1).astype(LOW)
        give(0, at)

    plan.spend(1.5)

    def table_steps():
        for position, axis in enumerate(("core", "x", "y", None)):
            table_step(position, axis)
            if axis:
                yield plan.transfer(axis, 1.5), None
        for offset in range(1, SHARDS):
            table_copies.append(
                extra(
                    8 + offset,
                    table_own.at[3, lax.rem(s + offset, SHARDS)],
                    table_z.at[offset - 1],
                    place.along(offset),
                )
            )
        yield plan.transfer("z", 2.0), None
        for copy in table_copies[3:]:
            copy.wait_recv()
        value = table_own[3, s]
        for offset in range(1, SHARDS):
            value = value + table_z[offset - 1]
        table_sum[...] = value
        direction = direction_of(value, own_states[0], own_states[1])
        share = 1.0 / REPLICAS
        squares[0, 5:6, :] = share * lanes(own_vectors[...] * own_vectors[...])
        squares[0, 13:14, :] = share * lanes(direction * direction)
        table_done[0] = True

    table_done = [False]
    squares_done = [False]

    def square_steps():
        yield 0.0, lambda: table_done[0] and min(at_stage) >= 5
        hops = []
        for position, axis in enumerate(("core", "x", "y", None)):
            if position:
                hops[-1].wait_recv()
                squares[position] = squares[position - 1] + square_in[position - 1]
            if axis:
                hops.append(
                    extra(
                        12 + position,
                        squares.at[position],
                        square_in.at[position],
                        place.across(axis),
                    )
                )
                yield plan.transfer(axis, 0.5), None
        hops = []
        for offset in range(1, SHARDS):
            hops.append(
                extra(14 + offset, squares.at[3], square_z.at[offset], place.along(offset))
            )
        square_z[0] = squares[3]
        yield plan.transfer("z", 0.5), None
        for copy in hops:
            copy.wait_recv()
        value = square_z[s]
        for shard in range(1, SHARDS):
            value = value + square_z[lax.rem(s + SHARDS - shard, SHARDS)]
        norms[...] = jnp.sqrt(jnp.sum(value, 1, keepdims=True)) + jnp.zeros_like(value)
        squares_done[0] = True

    plan.add(table_steps())
    plan.add(square_steps())
    plan.finish(lambda: squares_done[0] and min(at_stage) == len(stages))
    for key in sorted(copies):
        for copy in copies[key]:
            copy.wait_send()
    for copy in sent:
        copy.wait_send()


def backward_pass(cotangent, joined, table, kept, weights, masters, states, vectors, vector_states, portion):
    entering, first_in, heads, log_total, mixed, middle, second_in, slope, activated = kept[:9]
    shapes = [(matrix.shape[0] * SHARDS, matrix.shape[1]) for matrix in masters]
    order = chunk_list(shapes)
    chunks = [chunk for index in (4, 3, 2, 1, 0) for chunk in order if chunk[0] == index]
    total = len(chunks)
    rows, width = entering.shape
    own = width // SHARDS
    hidden = slope.shape[1]
    loaded = (second_in, slope, middle, mixed, heads, first_in, entering, joined)
    everyone = SHARDS * rows
    piece = (UNIT, BLOCK)
    inner = pl.BlockSpec(memory_space=pltpu.VMEM)
    folds = [(SHARDS, r // SHARDS // 256, 2, 2, 2, 2, UNIT, c) for r, c in shapes]
    extra_rows = 16 - vectors.shape[0]
    own_vectors = jnp.pad(vectors, ((0, extra_rows), (0, 0)))
    own_states = jnp.pad(vector_states, ((0, 0), (0, extra_rows), (0, 0)))
    outs = pl.pallas_call(
        functools.partial(backward_kernel, chunks, portion),
        out_shape=[jax.ShapeDtypeStruct(fold[1:], LOW) for fold in folds]
        + [
            jax.ShapeDtypeStruct((16, own), jnp.float32),
            jax.ShapeDtypeStruct((16, 128), jnp.float32),
            jax.ShapeDtypeStruct((rows, 2 * width), LOW),
        ],
        in_specs=[inner] * 4 + [ANY] * 23 + [inner] * 2,
        out_specs=[ANY] * 5 + [inner] * 3,
        scratch_shapes=[
            pltpu.VMEM((8, 2, 2, 2, 2) + piece, LOW),
            pltpu.VMEM((2, SHARDS, 2, 2, 2) + piece, LOW),
            pltpu.VMEM((5, SHARDS, 2, 2, 2) + piece, LOW),
            pltpu.VMEM((4, SHARDS, 2, 2, 2) + piece, LOW),
            pltpu.VMEM((4, 2, SHARDS, 2) + piece, LOW),
            pltpu.VMEM((4, 2, SHARDS) + piece, LOW),
            pltpu.VMEM((2, SHARDS, 2) + piece, LOW),
            pltpu.VMEM((4, SHARDS - 1, 2) + piece, LOW),
            pltpu.VMEM((2, 2) + piece, LOW),
            pltpu.VMEM((2, 2, 2) + piece, jnp.float32),
            pltpu.VMEM((2, 2) + piece, jnp.float32),
            pltpu.VMEM((4, 16, 128), jnp.float32),
            pltpu.VMEM((3, 16, 128), jnp.float32),
            pltpu.VMEM((SHARDS, 16, 128), jnp.float32),
            pltpu.VMEM((4, SHARDS, 16, own), jnp.float32),
            pltpu.VMEM((3, SHARDS, 16, own), jnp.float32),
            pltpu.VMEM((SHARDS - 1, 16, own), jnp.float32),
            pltpu.VMEM((rows, hidden), LOW),
            pltpu.VMEM((rows, width), jnp.float32),
            pltpu.VMEM((rows, width), jnp.float32),
            pltpu.VMEM((rows, width), LOW),
            pltpu.VMEM((SHARDS, rows, own), LOW),
            pltpu.VMEM((everyone, own), LOW),
            pltpu.VMEM((everyone, 128), jnp.float32),
            pltpu.VMEM((everyone, 128), jnp.float32),
            pltpu.VMEM((everyone, 3 * own), LOW),
            pltpu.VMEM((SHARDS, rows, 3 * own), LOW),
            pltpu.VMEM((rows, width), LOW),
            *[pltpu.VMEM(array.shape, array.dtype) for array in loaded],
            pltpu.SemaphoreType.DMA((8,)),
            pltpu.SemaphoreType.DMA((8,)),
            pltpu.SemaphoreType.DMA((2, 2)),
            pltpu.SemaphoreType.DMA((2,)),
            pltpu.SemaphoreType.DMA((total * 14,)),
            pltpu.SemaphoreType.DMA((total * 14,)),
            pltpu.SemaphoreType.DMA((18 + 6 * (own // 128),)),
            pltpu.SemaphoreType.DMA((18 + 6 * (own // 128),)),
        ],
        compiler_params=pltpu.CompilerParams(
            collective_id=2, has_side_effects=True, vmem_limit_bytes=60 * 2**20
        ),
        name="backward_pass",
    )(
        cotangent,
        table,
        log_total,
        activated,
        *loaded,
        *[matrix.reshape(fold) for matrix, fold in zip(weights, folds)],
        *[matrix.reshape(fold[1:]) for matrix, fold in zip(masters, folds)],
        *[state.reshape((2,) + fold[1:]) for state, fold in zip(states, folds)],
        own_vectors,
        own_states,
    )
    lows = [low.reshape(r // SHARDS, c) for low, (r, c) in zip(outs[:5], shapes)]
    return lows, outs[5][: vectors.shape[0]], outs[6], outs[7]


def update_kernel(position, norms, gradient, state, master, wide, new_state, new_master):
    grad = gradient[...].astype(jnp.float32)
    moment = 0.5 * state[0] + 0.5 * grad
    root = jnp.sqrt(0.5 * state[1] * state[1] + 0.5 * grad * grad)
    wide[...] = grad
    new_state[0] = moment
    new_state[1] = root
    ratio = norms[position : position + 1, 0:1] / (
        norms[8 + position : 9 + position, 0:1] + 1e-06
    )
    new_master[...] = master[...] - (step_rate * ratio) * (moment / (root + 1e-06))


def update_weight(position, norms, gradient, state, master):
    rows, columns = master.shape
    block = 256 if columns <= BLOCK else 64
    plain = pl.BlockSpec((block, columns), lambda i: (i, 0))
    paired = pl.BlockSpec((2, block, columns), lambda i: (0, i, 0))
    return pl.pallas_call(
        functools.partial(update_kernel, position),
        grid=(rows // block,),
        out_shape=[
            jax.ShapeDtypeStruct(master.shape, jnp.float32),
            jax.ShapeDtypeStruct(state.shape, jnp.float32),
            jax.ShapeDtypeStruct(master.shape, jnp.float32),
        ],
        in_specs=[pl.BlockSpec((16, 128), lambda i: (0, 0)), plain, paired, plain],
        out_specs=[plain, paired, plain],
        name="update_weight",
    )(norms, gradient, state, master)


def fits(masters):
    return (
        lax.axis_size("shard") == SHARDS
        and lax.axis_size("rep") == REPLICAS
        and all(m.shape[0] % 256 == 0 and m.shape[1] % BLOCK == 0 for m in masters)
        and masters[0].shape[1] == HEADS * HEAD_DIM == BLOCK
    )


def plain_device(
    hidden_in,
    skip_path,
    cotangent,
    skip_weight,
    heads_in,
    heads_out,
    expand_weight,
    reduce_weight,
    vectors,
    moments_skip,
    moments_in,
    moments_out,
    moments_expand,
    moments_reduce,
    moments_vectors,
):
    sequences, portion, model_width = hidden_in.shape
    shards = lax.axis_size("shard")
    replicas = lax.axis_size("rep")
    rep_index = lax.axis_index("rep")
    row_count = sequences * portion
    factor = 1.0 / math.sqrt(HEAD_DIM)
    masters = (skip_weight, heads_in, heads_out, expand_weight, reduce_weight, vectors)
    gathered = []
    for matrix in masters[:5]:
        height = matrix.shape[0] // replicas
        piece = lax.dynamic_slice_in_dim(matrix, rep_index * height, height, 0)
        piece = piece.astype(jnp.bfloat16)
        gathered.append(lax.all_gather(piece, ("shard", "rep"), axis=0, tiled=True))
    skip_matrix, in_matrix, out_matrix, expand_matrix, reduce_matrix = gathered
    table_low = lax.all_gather(vectors.astype(jnp.bfloat16), "shard", axis=1, tiled=True)
    table_rows = table_low.astype(jnp.float32)
    source = hidden_in.reshape(row_count, model_width)
    skip_rows = skip_path.reshape(row_count, model_width)
    joined = jnp.concatenate([source, skip_rows], 1)
    entering = matmul(joined, skip_matrix) + table_rows[0]
    normed_one, norm_back_one = jax.vjp(normalize, entering, table_rows[1], table_rows[2])
    first_in = normed_one.astype(jnp.bfloat16)
    triple = matmul(first_in, in_matrix).astype(jnp.bfloat16)
    heads = to_heads(triple, sequences, portion, shards)
    queries, keys_full, values_full = heads[:, :, 0], heads[:, :, 1], heads[:, :, 2]
    scores = (
        jnp.einsum("sqhd,skhd->shqk", queries, keys_full, preferred_element_type=jnp.float32)
        * factor
    )
    row_max = jnp.max(scores, -1)
    row_total = jnp.sum(jnp.exp(scores - row_max[..., None]), -1)
    log_total = row_max + jnp.log(row_total)
    probability = jnp.exp(scores - log_total[..., None])
    mixed = jnp.einsum(
        "shqk,skhd->sqhd",
        probability.astype(jnp.bfloat16),
        values_full,
        preferred_element_type=jnp.float32,
    )
    mixed_low = to_tokens(mixed.astype(jnp.bfloat16)[:, :, None], sequences, portion, shards)
    middle = entering + matmul(mixed_low, out_matrix) + table_rows[3]
    normed_two, norm_back_two = jax.vjp(normalize, middle, table_rows[4], table_rows[5])
    second_in = normed_two.astype(jnp.bfloat16)
    expanded = matmul(second_in, expand_matrix) + table_rows[7:].reshape(-1)
    activated, gelu_back = jax.vjp(exact_gelu, expanded)
    activated_low = activated.astype(jnp.bfloat16)
    block_result = middle + matmul(activated_low, reduce_matrix) + table_rows[6]
    block_out = block_result.astype(jnp.bfloat16).reshape(sequences, portion, model_width)
    grad_out = cotangent.reshape(row_count, model_width)
    grad_reduce = matmul(activated_low.T, grad_out)
    grad_act = matmul(grad_out, reduce_matrix.T)
    grad_inner = gelu_back(grad_act)[0].astype(jnp.bfloat16)
    grad_expand = matmul(second_in.T, grad_inner)
    grad_second = matmul(grad_inner, expand_matrix.T)
    grad_mid_norm, grad_gain_two, grad_bias_two = norm_back_two(grad_second)
    grad_middle = grad_out.astype(jnp.float32) + grad_mid_norm
    grad_middle_low = grad_middle.astype(jnp.bfloat16)
    grad_outw = matmul(mixed_low.T, grad_middle_low)
    grad_mixed = matmul(grad_middle_low, out_matrix.T).astype(jnp.bfloat16)
    grad_mixed = to_heads(grad_mixed, sequences, portion, shards)[:, :, 0]
    grad_prob = jnp.einsum(
        "sqhd,skhd->shqk", grad_mixed, values_full, preferred_element_type=jnp.float32
    )
    delta = jnp.sum(probability * grad_prob, -1)
    grad_scores = (probability * (grad_prob - delta[..., None])).astype(jnp.bfloat16)
    grad_query = (
        jnp.einsum("shqk,skhd->sqhd", grad_scores, keys_full, preferred_element_type=jnp.float32)
        * factor
    )
    grad_keys = (
        jnp.einsum("shqk,sqhd->skhd", grad_scores, queries, preferred_element_type=jnp.float32)
        * factor
    )
    grad_values = jnp.einsum(
        "shqk,sqhd->skhd",
        probability.astype(jnp.bfloat16),
        grad_mixed,
        preferred_element_type=jnp.float32,
    )
    grad_heads = jnp.stack([grad_query, grad_keys, grad_values], 2).astype(jnp.bfloat16)
    grad_triple = to_tokens(grad_heads, sequences, portion, shards)
    grad_inw = matmul(first_in.T, grad_triple)
    grad_first = matmul(grad_triple, in_matrix.T)
    grad_pre_norm, grad_gain_one, grad_bias_one = norm_back_one(grad_first)
    grad_entering = (grad_middle + grad_pre_norm).astype(jnp.bfloat16)
    grad_skipw = matmul(joined.T, grad_entering)
    grad_joined = matmul(grad_entering, skip_matrix.T)
    input_gradient = (
        grad_joined[:, :model_width].astype(jnp.bfloat16).reshape(sequences, portion, model_width)
    )
    skip_gradient = (
        grad_joined[:, model_width:].astype(jnp.bfloat16).reshape(sequences, portion, model_width)
    )
    grad_table = jnp.concatenate(
        [
            jnp.stack(
                [
                    row_sums(grad_entering),
                    grad_gain_one,
                    grad_bias_one,
                    row_sums(grad_middle_low),
                    grad_gain_two,
                    grad_bias_two,
                    row_sums(grad_out),
                ]
            ),
            row_sums(grad_inner).reshape(-1, model_width),
        ],
        0,
    )
    width = vectors.shape[1]
    grad_table = lax.psum(grad_table, ("rep", "shard"))
    vector_total = lax.dynamic_slice_in_dim(grad_table, lax.axis_index("shard") * width, width, 1)
    totals = []
    for partial in (grad_skipw, grad_inw, grad_outw, grad_expand, grad_reduce):
        piece = lax.psum_scatter(
            partial.astype(jnp.bfloat16), ("shard", "rep"), scatter_dimension=0, tiled=True
        )
        whole = lax.all_gather(piece, "rep", axis=0, tiled=True)
        totals.append(whole.astype(jnp.float32))
    totals.append(vector_total)
    states = (
        moments_skip,
        moments_in,
        moments_out,
        moments_expand,
        moments_reduce,
        moments_vectors,
    )
    steps = [moment_step(total, state) for total, state in zip(totals, states)]
    squares = jnp.stack(
        [
            jnp.stack([jnp.sum(matrix * matrix) for matrix in masters]),
            jnp.stack([jnp.sum(direction * direction) for _, direction in steps]),
        ]
    )
    norms = jnp.sqrt(lax.psum(squares, "shard"))
    ratio = norms[0] / (norms[1] + 1e-06)
    updated = [
        masters[position] - step_rate * ratio[position] * steps[position][1]
        for position in range(6)
    ]
    return (
        block_out,
        input_gradient,
        skip_gradient,
        *totals,
        *(state for state, _ in steps),
        *updated,
        norms,
    )


def on_device(
    hidden_in,
    skip_path,
    cotangent,
    skip_weight,
    heads_in,
    heads_out,
    expand_weight,
    reduce_weight,
    vectors,
    moments_skip,
    moments_in,
    moments_out,
    moments_expand,
    moments_reduce,
    moments_vectors,
):
    sequences, portion, model_width = hidden_in.shape
    masters = (skip_weight, heads_in, heads_out, expand_weight, reduce_weight)
    states = (moments_skip, moments_in, moments_out, moments_expand, moments_reduce)
    if not (sequences == 1 and fits(masters)):
        return plain_device(
            hidden_in, skip_path, cotangent, *masters, vectors, *states, moments_vectors
        )
    more = -portion % 32
    joined = jnp.concatenate([hidden_in[0], skip_path[0]], 1)
    joined = jnp.pad(joined, ((0, more), (0, 0)))
    incoming = jnp.pad(cotangent[0], ((0, more), (0, 0)))
    weights, kept = forward_pass(joined, vectors, masters, portion)
    block_out, table = kept[9], kept[10]
    lows, vector_total, norms, grad_joined = backward_pass(
        incoming, joined, table, kept, weights, masters, states, vectors, moments_vectors, portion
    )
    steps = [
        update_weight(position, norms, lows[position], states[position], masters[position])
        for position in range(5)
    ]
    vector_state, direction = moment_step(vector_total, moments_vectors)
    ratio = norms[5, 0] / (norms[13, 0] + 1e-06)
    return (
        block_out[None, :portion],
        grad_joined[None, :portion, :model_width],
        grad_joined[None, :portion, model_width:],
        *(step[0] for step in steps),
        vector_total,
        *(step[1] for step in steps),
        vector_state,
        *(step[2] for step in steps),
        vectors - step_rate * ratio * direction,
        jnp.stack([norms[:6, 0], norms[8:14, 0]]),
    )


def solution(mesh):
    placed = (
        P("rep", "shard", None),
        P("rep", "shard", None),
        P("rep", "shard", None),
        P("shard", None),
        P("shard", None),
        P("shard", None),
        P("shard", None),
        P("shard", None),
        P(None, "shard"),
        P(None, "shard", None),
        P(None, "shard", None),
        P(None, "shard", None),
        P(None, "shard", None),
        P(None, "shard", None),
        P(None, None, "shard"),
    )
    return jax.shard_map(
        on_device,
        mesh=mesh,
        in_specs=placed,
        out_specs=(
            P("rep", "shard", None),
            P("rep", "shard", None),
            P("rep", "shard", None),
            P("shard", None),
            P("shard", None),
            P("shard", None),
            P("shard", None),
            P("shard", None),
            P(None, "shard"),
            P(None, "shard", None),
            P(None, "shard", None),
            P(None, "shard", None),
            P(None, "shard", None),
            P(None, "shard", None),
            P(None, None, "shard"),
            P("shard", None),
            P("shard", None),
            P("shard", None),
            P("shard", None),
            P("shard", None),
            P(None, "shard"),
            P(),
        ),
        check_vma=False,
    )
```

```python
import functools
import math

import jax
import jax.numpy as jnp
from jax import lax
from jax.experimental import pallas as pl
from jax.experimental.pallas import tpu as pltpu
from jax.sharding import PartitionSpec as P

HEADS = 16
HEAD_DIM = 64
MESH = pl.DeviceIdType.MESH
LOW = jnp.bfloat16
ANY = pl.BlockSpec(memory_space=pl.ANY)
SHARDS, REPLICAS = 4, 8
UNIT = 16
BLOCK = 1024


class Place:
    def __init__(self):
        self.rep = lax.axis_index("rep")
        self.shard = lax.axis_index("shard")
        self.core = lax.rem(self.rep, 2)
        self.x = lax.rem(self.rep // 2, 2)
        self.y = self.rep // 4

    def across(self, axis):
        own, step = {"core": (self.core, 1), "x": (self.x, 2), "y": (self.y, 4)}[axis]
        return (self.rep + step - 2 * step * own, self.shard)

    def along(self, offset):
        return (self.rep, lax.rem(self.shard + offset, SHARDS))

    def source(self, offset):
        return lax.rem(self.shard + SHARDS - offset, SHARDS)

    def partners(self):
        return [self.across("core"), self.across("x"), self.across("y")] + [
            self.along(offset) for offset in range(1, SHARDS)
        ]


def greet(place):
    barrier = pltpu.get_barrier_semaphore()
    partners = place.partners()
    for partner in partners:
        pl.semaphore_signal(barrier, inc=1, device_id=partner, device_id_type=MESH)
    pl.semaphore_wait(barrier, len(partners))


def chunk_list(shapes):
    chunks = []
    for index, (rows, columns) in enumerate(shapes):
        for group in range(rows // SHARDS // 256):
            for part in range(columns // BLOCK):
                chunks.append((index, group, part))
    return chunks


class Plan:
    def __init__(self, latency, rate, pace):
        self.now, self.latency, self.rate, self.pace = 0.0, latency, rate, pace
        self.free = {}
        self.agents = []

    def transfer(self, link, length):
        self.free[link] = max(self.now, self.free.get(link, 0.0)) + length
        return self.free[link] + self.latency

    def backlog(self, link):
        return self.free.get(link, 0.0) - self.now

    def add(self, steps):
        agent = [steps, 0.0, None]
        self.agents.append(agent)
        self.resume(agent)

    def resume(self, agent):
        try:
            agent[1], agent[2] = next(agent[0])
        except StopIteration:
            self.agents.remove(agent)

    def ready(self):
        return [a for a in self.agents if a[2] is None or a[2]()]

    def pump(self):
        while True:
            able = [agent for agent in self.ready() if agent[1] <= self.now]
            if not able:
                return
            self.resume(able[0])

    def spend(self, length):
        self.now += self.pace * length
        self.pump()

    def until(self, moment):
        self.pump()
        while self.now < moment:
            times = [agent[1] for agent in self.ready() if agent[1] > self.now]
            self.now = min(times + [moment])
            self.pump()

    def finish(self, test):
        self.pump()
        while not test():
            times = [agent[1] for agent in self.ready()]
            self.now = max(self.now, min(times))
            self.pump()


step_rate = 0.3


def normalize(stream, gain_row, bias_row):
    center = stream - jnp.mean(stream, -1, keepdims=True)
    spread = jnp.mean(center * center, -1, keepdims=True)
    return center * lax.rsqrt(spread + 1e-05) * gain_row + bias_row


def exact_gelu(inputs):
    return jax.nn.gelu(inputs, approximate=False)


def matmul(left, right):
    return jnp.dot(left, right, preferred_element_type=jnp.float32)


def row_sums(matrix):
    return jnp.sum(matrix, 0, dtype=jnp.float32)


def moment_step(gradient, moments):
    first_moment = 0.5 * moments[0] + 0.5 * gradient
    root_square = jnp.sqrt(0.5 * moments[1] * moments[1] + 0.5 * gradient * gradient)
    direction = first_moment / (root_square + 1e-06)
    return (jnp.stack([first_moment, root_square]), direction)


def to_heads(rows, sequences, portion, shards):
    parts = rows.shape[1] // (HEADS * HEAD_DIM)
    width = HEADS * HEAD_DIM // shards
    blocks = rows.reshape(sequences, portion, parts, shards, width).transpose(3, 0, 1, 2, 4)
    blocks = blocks.reshape(shards, sequences * portion, parts * width)
    blocks = lax.all_to_all(blocks, "shard", 0, 0, tiled=True)
    blocks = blocks.reshape(shards, sequences, portion, parts, width).transpose(1, 0, 2, 3, 4)
    return blocks.reshape(sequences, shards * portion, parts, width // HEAD_DIM, HEAD_DIM)


def to_tokens(blocks, sequences, portion, shards):
    parts = blocks.shape[2]
    width = HEADS * HEAD_DIM // shards
    rows = blocks.reshape(sequences, shards, portion, parts, width).transpose(1, 0, 2, 3, 4)
    rows = rows.reshape(shards, sequences * portion, parts * width)
    rows = lax.all_to_all(rows, "shard", 0, 0, tiled=True)
    rows = rows.reshape(shards, sequences * portion, parts, width).transpose(1, 2, 0, 3)
    return rows.reshape(sequences * portion, parts * shards * width)


SLOTS = 19
Z_BACKLOG = 5.0


def weight_tile(whole, shard, group, start, width):
    return whole[shard, group, :, :, :, :, :, pl.ds(start, width)].reshape(256, width)


def product(left, whole, start, width):
    groups = whole.shape[1]
    total = None
    for shard in range(SHARDS):
        for group in range(groups):
            first = (shard * groups + group) * 256
            term = jnp.dot(
                left[:, first : first + 256],
                weight_tile(whole, shard, group, start, width),
                preferred_element_type=jnp.float32,
            )
            total = term if total is None else total + term
    return total


def contract(left, right, left_axis, right_axis):
    return lax.dot_general(
        left, right, (((left_axis,), (right_axis,)), ((), ())), preferred_element_type=jnp.float32
    )


def norm_rows(source, gain, bias, target, rows):
    @pl.loop(0, rows // 32)
    def _(block):
        where = pl.ds(pl.multiple_of(block * 32, 32), 32)
        stream = source[where, :]
        center = stream - jnp.mean(stream, -1, keepdims=True)
        spread = jnp.mean(center * center, -1, keepdims=True)
        target[where, :] = (center * lax.rsqrt(spread + 1e-05) * gain + bias).astype(LOW)


def forward_kernel(chunks, portion, *refs):
    joined, vectors = refs[0:2]
    masters = refs[2:7]
    keeps = refs[7:12]
    (
        entering,
        first_in,
        heads,
        log_total,
        mixed,
        middle,
        second_in,
        slope,
        activated,
        out,
        table,
    ) = refs[12:23]
    wholes = refs[23:28]
    (
        wide,
        table_own,
        table_all,
        outgoing,
        answer,
        load_sems,
        keep_sems,
        send_sems,
        recv_sems,
        more_send,
        more_recv,
    ) = refs[28:]
    place = Place()
    s, k, x, y = place.shard, place.core, place.x, place.y
    total = len(chunks)
    rows = entering.shape[0]
    width = entering.shape[1]
    own = width // SHARDS
    pairs = own // 128
    factor = 1.0 / math.sqrt(HEAD_DIM)

    def load(at):
        index, group, part = chunks[at]
        return pltpu.make_async_copy(
            masters[index].at[group, :, :, :, :, :, pl.ds(part * BLOCK, BLOCK)],
            wide.at[at % 2],
            load_sems.at[at % 2],
        )

    def whole(at, shard, *rest):
        index, group, part = chunks[at]
        rest = rest + (slice(None),) * (5 - len(rest))
        return wholes[index].at[(shard, group) + rest + (pl.ds(part * BLOCK, BLOCK),)]

    sent = []
    far = []
    arrivals = {}

    def relay_copy(at):
        up = s == SHARDS - 2
        ref = whole(at, place.source(2), k, slice(None), y, x)
        target = jnp.where(up, SHARDS - 1, 0)
        return pltpu.make_async_remote_copy(
            src_ref=ref,
            dst_ref=ref,
            send_sem=send_sems.at[at * SLOTS + SLOTS - 1],
            recv_sem=recv_sems.at[at * SLOTS + jnp.where(up, SHARDS - 2, 0)],
            device_id=(place.rep, target),
            device_id_type=MESH,
        )

    def go(at, name, position, ref, device):
        slot = at * SLOTS + position
        copy = pltpu.make_async_remote_copy(
            src_ref=ref,
            dst_ref=ref,
            send_sem=send_sems.at[slot],
            recv_sem=recv_sems.at[slot],
            device_id=device,
            device_id_type=MESH,
        )
        copy.start()
        sent.append(copy)
        arrivals.setdefault((at, name), []).append(copy)

    def arrived(at, name):
        for copy in arrivals[(at, name)]:
            copy.wait_recv()

    def extra(slot, source, target, device):
        copy = pltpu.make_async_remote_copy(
            src_ref=source,
            dst_ref=target,
            send_sem=more_send.at[slot],
            recv_sem=more_recv.at[slot],
            device_id=device,
            device_id_type=MESH,
        )
        copy.start()
        sent.append(copy)
        return copy

    kept = []

    def stage_cast(at):
        index, group, part = chunks[at]
        load(at).wait()

        @pl.loop(0, 16)
        def _(row):
            a, b = row // 8, lax.rem(row // 4, 2)
            c, d = lax.rem(row // 2, 2), lax.rem(row, 2)
            wholes[index][s, group, a, b, c, d, :, part * BLOCK : (part + 1) * BLOCK] = wide[
                at % 2, a, b, c, d
            ].astype(LOW)

        if at + 2 < total:
            load(at + 2).start()

    def stage_z(at):
        for offset in range(1, SHARDS):
            ref = whole(at, s, k, slice(None), y, x)
            slot = at * SLOTS + offset - 1
            target = lax.rem(s + offset, SHARDS)
            copy = pltpu.make_async_remote_copy(
                src_ref=ref,
                dst_ref=ref,
                send_sem=send_sems.at[slot],
                recv_sem=recv_sems.at[slot],
                device_id=(place.rep, target),
                device_id_type=MESH,
            )
            arrivals[(at, "z", offset)] = copy
            if offset == 2:
                copy.start()
                sent.append(copy)
            else:
                near = s != (0 if offset == SHARDS - 1 else SHARDS - 1)
                far.append((near, copy))

                @pl.when(near)
                def _(copy=copy):
                    copy.start()

    def stage_relay(at):
        arrivals[(at, "z", 2)].wait_recv()
        inner = (s > 0) & (s < SHARDS - 1)
        copy = relay_copy(at)
        far.append((inner, copy))

        @pl.when(inner)
        def _():
            copy.start()

    def stage_first(at):
        arrivals[(at, "z", 1)].wait_recv()
        arrivals[(at, "z", 3)].wait_recv()
        for offset in range(1, SHARDS):
            e = place.source(offset)
            go(at, "first", 3 + 2 * (offset - 1), whole(at, e, k, 0, y, x), place.across("x"))
            go(at, "first", 4 + 2 * (offset - 1), whole(at, e, k, 1, y, x), place.across("y"))

    def stage_second(at):
        arrived(at, "first")
        for offset in range(1, SHARDS):
            e = place.source(offset)
            go(at, "second", 9 + 2 * (offset - 1), whole(at, e, k, 0, y), place.across("y"))
            ref = whole(at, e, k, 1, slice(None), x)
            go(at, "second", 10 + 2 * (offset - 1), ref, place.across("x"))

    def stage_core(at):
        arrived(at, "second")
        for offset in range(1, SHARDS):
            e = place.source(offset)
            go(at, "core", 15 + offset - 1, whole(at, e, k), place.across("core"))

    def stage_end(at):
        arrived(at, "core")
        index, group, part = chunks[at]
        copy = pltpu.make_async_copy(
            whole(at, slice(None)),
            keeps[index].at[:, group, :, :, :, :, :, pl.ds(part * BLOCK, BLOCK)],
            keep_sems.at[at],
        )
        copy.start()
        kept.append(copy)

    plan = Plan(latency=1.5, rate=45e3, pace=0.8)
    done = [0] * total
    unit = UNIT * BLOCK * 2 / plan.rate

    def chunk_steps(at):
        yield 0.0, lambda: (at == 0 or done[at - 1] >= 1) and plan.backlog("z") < Z_BACKLOG
        stage_cast(at)
        plan.now += 0.6
        stage_z(at)
        start = plan.transfer("z", 6 * unit)
        done[at] = 1
        yield start - 2 * unit, None
        stage_relay(at)
        yield start + 1.0, None
        stage_first(at)
        moment = max(plan.transfer("x", 3 * unit), plan.transfer("y", 3 * unit))
        yield moment, None
        stage_second(at)
        moment = max(plan.transfer("x", 6 * unit), plan.transfer("y", 6 * unit))
        yield moment, None
        stage_core(at)
        plan.now += 0.2
        yield plan.transfer("core", 24 * unit / 6), None
        stage_end(at)
        done[at] = 2

    def until(at):
        plan.finish(lambda: done[at] == 2)

    def arrive(copies, moment):
        plan.until(moment)
        for copy in copies:
            copy.wait_recv()

    load(0).start()
    load(1).start()
    table_own[...] = vectors[...].astype(LOW)
    table_all[0] = vectors[...].astype(LOW)
    greet(place)
    table_copies = []
    for offset in range(1, SHARDS):
        table_copies.append(extra(offset - 1, table_own, table_all.at[offset], place.along(offset)))
    for at in range(total):
        plan.add(chunk_steps(at))
    last = {}
    for at, (index, group, part) in enumerate(chunks):
        last[index] = at

    until(0)
    for copy in table_copies:
        copy.wait_recv()
    for offset in range(SHARDS):
        column = pl.multiple_of(place.source(offset) * own, own)
        table[:, pl.ds(column, own)] = table_all[offset].astype(jnp.float32)
    until(last[0])

    @pl.loop(0, width // 256)
    def _(part):
        start = pl.multiple_of(part * 256, 256)
        entering[:, pl.ds(start, 256)] = (
            product(joined, wholes[0], start, 256) + table[0:1, pl.ds(start, 256)]
        )

    plan.spend(2.5)
    norm_rows(entering, table[1:2, :], table[2:3, :], first_in, rows)
    plan.spend(2.0)
    until(last[1])
    live = lax.broadcasted_iota(jnp.int32, (rows, own), 0) < portion
    for kind in range(3):

        @pl.loop(0, SHARDS)
        def _(target):
            start = pl.multiple_of(kind * width + target * own, own)
            value = jnp.where(live, product(first_in, wholes[1], start, own), 0.0).astype(LOW)
            for pair in range(pairs):
                first = (3 * pair + kind) * 128
                outgoing[target, :, first : first + 128] = value[:, pair * 128 : (pair + 1) * 128]

        plan.spend(1.5)

    head_copies = []
    moments = []
    for pair in range(pairs):
        moments.append(plan.transfer("z", 4 * rows * 384 * 2 / plan.rate))
        for offset in range(1, SHARDS):
            target = lax.rem(s + offset, SHARDS)
            columns = pl.ds(pair * 384, 384)
            head_copies.append(
                extra(
                    3 * pair + 2 + offset,
                    outgoing.at[target, :, columns],
                    heads.at[pl.ds(offset * rows, rows), columns],
                    place.along(offset),
                )
            )

    @pl.loop(0, rows // 32)
    def _(block):
        where = pl.ds(pl.multiple_of(block * 32, 32), 32)
        heads[where, :] = outgoing[s, where, :]

    plan.spend(0.5)
    everyone = SHARDS * rows
    tile = 384
    lane = lax.broadcasted_iota(jnp.int32, (tile, 128), 1)
    key_row = lax.rem(lax.broadcasted_iota(jnp.int32, (everyone, 1), 0), rows)
    key_bias = jnp.where(key_row < portion, 0.0, -1e30)
    answer_copies = []
    column = pl.multiple_of(s * own, own)
    for pair in range(pairs):
        arrive(head_copies[3 * pair : 3 * pair + 3], moments[pair])
        base = pair * 384

        for block in range(everyone // tile):
            start = block * tile
            where = slice(start, start + tile)
            query = heads[where, base : base + 128]
            keys = heads[:, base + 128 : base + 256]
            values = heads[:, base + 256 : base + 384]
            parts = []
            for half in range(2):
                inside = (lane // 64) == half
                picked = jnp.where(inside, query.astype(jnp.float32) * factor, 0.0).astype(LOW)
                scores = contract(keys, picked, 1, 1)
                scores = scores + key_bias
                top = jnp.max(scores, 0, keepdims=True)
                weight = jnp.exp(scores - top)
                weight_sum = jnp.sum(weight, 0, keepdims=True)
                log_total[2 * pair + half : 2 * pair + half + 1, where] = (
                    top + jnp.log(weight_sum)
                )
                weight = (weight * (1.0 / weight_sum)).astype(LOW)
                summed = contract(values, weight, 0, 0)
                parts.append(summed[half * 64 : (half + 1) * 64])
            both = jnp.concatenate(parts, 0)
            answer[where, pair * 128 : (pair + 1) * 128] = both.T.astype(LOW)
            plan.spend(2.0)

        answer_moment = plan.transfer("z", 4 * rows * 128 * 2 / plan.rate)
        columns = pl.ds(pair * 128, 128)
        for offset in range(1, SHARDS):
            answer_copies.append(
                extra(
                    3 * (pairs + pair) + 2 + offset,
                    answer.at[pl.ds(offset * rows, rows), columns],
                    mixed.at[:, pl.ds(column + pair * 128, 128)],
                    (place.rep, place.source(offset)),
                )
            )

    mixed[:, pl.ds(column, own)] = answer[0:rows, :]
    until(last[2])
    arrive(answer_copies, answer_moment)

    @pl.loop(0, width // 256)
    def _(part):
        start = pl.multiple_of(part * 256, 256)
        where = pl.ds(start, 256)
        middle[:, where] = (
            entering[:, where] + product(mixed, wholes[2], start, 256) + table[3:4, where]
        )

    plan.spend(1.5)
    norm_rows(middle, table[4:5, :], table[5:6, :], second_in, rows)
    plan.spend(2.0)
    per_row = width // 256
    for part in range(slope.shape[1] // BLOCK):
        until(last[2] + 1 + part)

        @pl.loop(0, BLOCK // 256)
        def _(piece):
            start = pl.multiple_of(part * BLOCK + piece * 256, 256)
            bias_at = pl.multiple_of(piece * 256, 256)
            value = (
                product(second_in, wholes[3], start, 256)
                + table[7 + part : 8 + part, pl.ds(bias_at, 256)]
            )
            below = 0.5 + 0.5 * lax.erf(value * math.sqrt(0.5))
            bell = jnp.exp(-0.5 * value * value) * (1.0 / math.sqrt(2.0 * math.pi))
            slope[:, pl.ds(start, 256)] = below + value * bell
            activated[:, pl.ds(start, 256)] = (value * below).astype(LOW)

        plan.spend(4.0)

    until(last[4])

    @pl.loop(0, width // 256)
    def _(part):
        start = pl.multiple_of(part * 256, 256)
        where = pl.ds(start, 256)
        out[:, where] = (
            middle[:, where] + product(activated, wholes[4], start, 256) + table[6:7, where]
        ).astype(LOW)

    for copy in sent:
        copy.wait_send()
    for used, copy in far:

        @pl.when(used)
        def _(copy=copy):
            copy.wait_send()

    for copy in kept:
        copy.wait()


def forward_pass(joined, vectors, masters, portion):
    shapes = [(matrix.shape[0] * SHARDS, matrix.shape[1]) for matrix in masters]
    chunks = chunk_list(shapes)
    total = len(chunks)
    rows = joined.shape[0]
    width = joined.shape[1] // 2
    own = width // SHARDS
    hidden = shapes[3][1]
    everyone = SHARDS * rows
    split = [
        matrix.reshape(matrix.shape[0] // 256, 2, 2, 2, 2, UNIT, matrix.shape[1])
        for matrix in masters
    ]
    folds = [(SHARDS, r // SHARDS // 256, 2, 2, 2, 2, UNIT, c) for r, c in shapes]
    inner = pl.BlockSpec(memory_space=pltpu.VMEM)
    table = jnp.pad(vectors, ((0, 16 - vectors.shape[0]), (0, 0)))
    outs = pl.pallas_call(
        functools.partial(forward_kernel, chunks, portion),
        out_shape=[jax.ShapeDtypeStruct(fold, LOW) for fold in folds]
        + [
            jax.ShapeDtypeStruct((rows, width), jnp.float32),
            jax.ShapeDtypeStruct((rows, width), LOW),
            jax.ShapeDtypeStruct((everyone, 3 * own), LOW),
            jax.ShapeDtypeStruct((8, everyone), jnp.float32),
            jax.ShapeDtypeStruct((rows, width), LOW),
            jax.ShapeDtypeStruct((rows, width), jnp.float32),
            jax.ShapeDtypeStruct((rows, width), LOW),
            jax.ShapeDtypeStruct((rows, hidden), jnp.float32),
            jax.ShapeDtypeStruct((rows, hidden), LOW),
            jax.ShapeDtypeStruct((rows, width), LOW),
            jax.ShapeDtypeStruct((16, width), jnp.float32),
        ],
        in_specs=[inner] * 2 + [ANY] * 5,
        out_specs=[ANY] * 5 + [inner] * 11,
        scratch_shapes=[pltpu.VMEM(fold, LOW) for fold in folds]
        + [
            pltpu.VMEM((2, 2, 2, 2, 2, UNIT, BLOCK), jnp.float32),
            pltpu.VMEM((16, own), LOW),
            pltpu.VMEM((SHARDS, 16, own), LOW),
            pltpu.VMEM((SHARDS, rows, 3 * own), LOW),
            pltpu.VMEM((everyone, own), LOW),
            pltpu.SemaphoreType.DMA((2,)),
            pltpu.SemaphoreType.DMA((total,)),
            pltpu.SemaphoreType.DMA((total * SLOTS,)),
            pltpu.SemaphoreType.DMA((total * SLOTS,)),
            pltpu.SemaphoreType.DMA((3 + 6 * (own // 128),)),
            pltpu.SemaphoreType.DMA((3 + 6 * (own // 128),)),
        ],
        compiler_params=pltpu.CompilerParams(
            collective_id=1, has_side_effects=True, vmem_limit_bytes=60 * 2**20
        ),
        name="forward_pass",
    )(joined, table, *split)
    weights = [out.reshape(shape) for out, shape in zip(outs[:5], shapes)]
    return weights, outs[5:]


UPDATE_ROWS, UPDATE_SLOTS = 256, 3
Z_LIMIT = 1000.0


def norm_back(source, gain, incoming, residual, wide_out, low_out, rows):
    columns = source.shape[1]

    def body(block, carry):
        where = pl.ds(pl.multiple_of(block * 32, 32), 32)
        stream = source[where, :]
        center = stream - jnp.mean(stream, -1, keepdims=True)
        spread = jnp.mean(center * center, -1, keepdims=True)
        scale = lax.rsqrt(spread + 1e-05)
        hat = center * scale
        grad = incoming[where, :]
        scaled = grad * gain
        slope = scale * (
            scaled
            - jnp.mean(scaled, -1, keepdims=True)
            - hat * jnp.mean(scaled * hat, -1, keepdims=True)
        )
        value = residual[where, :].astype(jnp.float32) + slope
        low = value.astype(LOW)
        if wide_out is not None:
            wide_out[where, :] = value
        low_out[where, :] = low
        terms = (grad * hat, grad, low.astype(jnp.float32))
        return tuple(kept + jnp.sum(term, 0, keepdims=True) for kept, term in zip(carry, terms))

    zero = jnp.zeros((1, columns), jnp.float32)
    return lax.fori_loop(0, rows // 32, body, (zero, zero, zero))


def backward_kernel(chunks, portion, *refs):
    (
        cotangent,
        vectors,
        log_total,
        activated,
    ) = refs[:4]
    outside = refs[4:12]
    weights = refs[12:17]
    masters = refs[17:22]
    states = refs[22:27]
    own_vectors, own_states = refs[27:29]
    sums = refs[29:34]
    table_sum, norms, grad_joined = refs[34:37]
    (
        ring,
        theirs,
        mine,
        from_core,
        from_first,
        from_second,
        final,
        from_z,
        ready,
        state_in,
        master_in,
        squares,
        square_in,
        square_z,
        table_own,
        table_in,
        table_z,
        grad_inner,
        grad_second,
        grad_middle,
        grad_middle_low,
        outgoing,
        grad_mixed,
        grad_key,
        grad_value,
        grad_heads,
        grad_triple,
        grad_entering,
        second_in,
        slope,
        middle,
        mixed,
        heads,
        first_in,
        entering,
        joined,
        load_sems,
        ring_sems,
        state_sems,
        ready_sems,
        send_sems,
        recv_sems,
        more_send,
        more_recv,
    ) = refs[37:]
    place = Place()
    s, k, x, y = place.shard, place.core, place.x, place.y
    rows, width = entering.shape
    own = width // SHARDS
    factor = 1.0 / math.sqrt(HEAD_DIM)
    depth = ring.shape[0]

    inside = (second_in, slope, middle, mixed, heads, first_in, entering, joined)
    loads = [
        pltpu.make_async_copy(source, target, load_sems.at[position])
        for position, (source, target) in enumerate(zip(outside, inside))
    ]
    names = ["second_in", "slope", "middle", "mixed", "heads", "first_in", "entering", "joined"]
    waiting_for = dict(zip(names, loads))

    def need(name):
        if name in waiting_for:
            waiting_for.pop(name).wait()

    def tiles(index):
        parts = weights[index].shape[7] // BLOCK
        return weights[index].shape[1], parts, SHARDS * weights[index].shape[1] * parts

    def fetch(index, at):
        groups, parts, _ = tiles(index)
        shard, rest = at // (groups * parts), lax.rem(at, groups * parts)
        group, part = rest // parts, lax.rem(rest, parts)
        start = pl.multiple_of(part * BLOCK, BLOCK)
        return pltpu.make_async_copy(
            weights[index].at[shard, group, :, :, :, :, :, pl.ds(start, BLOCK)],
            ring.at[lax.rem(at, depth)],
            ring_sems.at[lax.rem(at, depth)],
        )

    def prime(index):
        @pl.loop(0, min(depth, tiles(index)[2]))
        def _(at):
            fetch(index, at).start()

    def take(index, at):
        fetch(index, at).wait()
        return ring[lax.rem(at, depth)].reshape(256, BLOCK)

    def give(index, at):
        @pl.when(at + depth < tiles(index)[2])
        def _():
            fetch(index, at + depth).start()

    copies = {}

    def go(at, name, position, source, target, device):
        slot = at * 14 + position
        copy = pltpu.make_async_remote_copy(
            src_ref=source,
            dst_ref=target,
            send_sem=send_sems.at[slot],
            recv_sem=recv_sems.at[slot],
            device_id=device,
            device_id_type=MESH,
        )
        copy.start()
        copies.setdefault((at, name), []).append(copy)

    sent = []
    more = 18

    def extra(slot, source, target, device):
        copy = pltpu.make_async_remote_copy(
            src_ref=source,
            dst_ref=target,
            send_sem=more_send.at[slot],
            recv_sem=more_recv.at[slot],
            device_id=device,
            device_id_type=MESH,
        )
        copy.start()
        sent.append(copy)
        return copy

    def arrived(at, name):
        for copy in copies[(at, name)]:
            copy.wait_recv()

    def left(at, name):
        for copy in copies.pop((at, name), []):
            copy.wait_send()

    pairs = own // 128

    def triple_part(part):
        return jnp.concatenate(
            [
                grad_triple[shard, :, (3 * pair + part) * 128 : (3 * pair + part + 1) * 128]
                for shard in range(SHARDS)
                for pair in range(pairs)
            ],
            1,
        )

    def gradient_half(at, core):
        index, group, part = chunks[at]
        if index < 4:
            need(("joined", "first_in", "mixed", "second_in")[index])
        lefts = (joined, first_in, mixed, second_in, activated)[index]
        pitch = lefts.shape[1] // SHARDS
        columns = [
            lefts[:, pl.ds(pl.multiple_of(shard * pitch + group * 256 + core * 128, 128), 128)]
            for shard in range(SHARDS)
        ]
        if index == 0:
            right = grad_entering[...]
        elif index == 1:
            right = triple_part(part)
        elif index == 2:
            right = grad_middle_low[...]
        elif index == 3:
            right = grad_inner[:, part * BLOCK : (part + 1) * BLOCK]
        else:
            right = cotangent[...]
        return contract(jnp.concatenate(columns, 1), right, 0, 0)

    def stage_core(at):
        slot = at % 2
        value = gradient_half(at, 1 - k).astype(LOW)
        theirs[slot] = value.reshape(SHARDS, 2, 2, 2, UNIT, BLOCK)
        go(at, "core", 0, theirs.at[slot], from_core.at[at % 4], place.across("core"))

    def stage_first(at):
        slot = at % 5
        value = gradient_half(at, k).reshape(SHARDS, 2, 2, 2, UNIT, BLOCK)
        arrived(at, "core")
        left(at, "core")
        mine[slot] = (value + from_core[at % 4].astype(jnp.float32)).astype(LOW)
        target = from_first.at[at % 4]
        go(at, "first", 1, mine.at[slot, :, 0, :, 1 - x], target.at[0], place.across("x"))
        go(at, "first", 2, mine.at[slot, :, 1, 1 - y], target.at[1], place.across("y"))

    def stage_second(at):
        slot = at % 5
        arrived(at, "first")
        left(at, "first")

        @pl.loop(0, SHARDS)
        def _(shard):
            for i in range(2):
                mine[slot, shard, 0, i, x] = (
                    mine[slot, shard, 0, i, x].astype(jnp.float32)
                    + from_first[at % 4, 0, shard, i].astype(jnp.float32)
                ).astype(LOW)
                mine[slot, shard, 1, y, i] = (
                    mine[slot, shard, 1, y, i].astype(jnp.float32)
                    + from_first[at % 4, 1, shard, i].astype(jnp.float32)
                ).astype(LOW)

        target = from_second.at[at % 4]
        go(at, "second", 3, mine.at[slot, :, 0, 1 - y, x], target.at[0], place.across("y"))
        go(at, "second", 4, mine.at[slot, :, 1, y, 1 - x], target.at[1], place.across("x"))

    def piece_loads(at):
        index, group, part = chunks[at]
        slot = at % 2
        where = pl.ds(part * BLOCK, BLOCK)
        return (
            pltpu.make_async_copy(
                states[index].at[:, group, k, :, y, x, :, where],
                state_in.at[slot],
                state_sems.at[slot, 0],
            ),
            pltpu.make_async_copy(
                masters[index].at[group, k, :, y, x, :, where],
                master_in.at[slot],
                state_sems.at[slot, 1],
            ),
        )

    def stage_z(at):
        slot = at % 5
        arrived(at, "second")
        left(at, "second")

        @pl.loop(0, SHARDS)
        def _(shard):
            for h in range(2):
                final[at % 2, shard, h] = (
                    mine[slot, shard, h, y, x].astype(jnp.float32)
                    + from_second[at % 4, h, shard].astype(jnp.float32)
                ).astype(LOW)

        for copy in piece_loads(at):
            copy.start()
        for offset in range(1, SHARDS):
            target = lax.rem(s + offset, SHARDS)
            go(
                at,
                "z",
                5 + offset - 1,
                final.at[at % 2, target],
                from_z.at[at % 4, offset - 1],
                place.along(offset),
            )

    def summed(at, *where):
        index, group, part = chunks[at]
        rest = where + (slice(None),) * (5 - len(where))
        return sums[index].at[(group,) + rest + (pl.ds(part * BLOCK, BLOCK),)]

    def own_piece(at):
        return pltpu.make_async_copy(
            ready.at[at % 2], summed(at, k, slice(None), y, x), ready_sems.at[at % 2]
        )

    def direction_of(gradient, first, second):
        moment = 0.5 * first + 0.5 * gradient
        root = jnp.sqrt(0.5 * second * second + 0.5 * gradient * gradient)
        return moment / (root + 1e-06)

    def lanes(square):
        total = jnp.sum(square, 0, keepdims=True)
        parts = [total[:, i * 128 : (i + 1) * 128] for i in range(total.shape[1] // 128)]
        return sum(parts[1:], parts[0])

    def stage_back(at):
        index = chunks[at][0]
        slot = at % 2
        for copy in piece_loads(at):
            copy.wait()
        arrived(at, "z")
        left(at, "z")
        for h in range(2):
            value = final[slot, s, h].astype(jnp.float32)
            for offset in range(1, SHARDS):
                value = value + from_z[at % 4, offset - 1, h].astype(jnp.float32)
            low = value.astype(LOW)
            ready[slot, h] = low
            direction = direction_of(
                low.astype(jnp.float32), state_in[slot, 0, h], state_in[slot, 1, h]
            )
            master = master_in[slot, h]
            squares[0, index : index + 1, :] += lanes(master * master)
            squares[0, 8 + index : 9 + index, :] += lanes(direction * direction)
        own_piece(at).start()
        target = summed(at, k, 0, y, x)
        go(at, "back", 8, ready.at[slot, 0], target, place.across("y"))
        target = summed(at, k, 1, y, x)
        go(at, "back", 9, ready.at[slot, 1], target, place.across("x"))

    def stage_wide(at):
        own_piece(at).wait()
        arrived(at, "back")
        left(at, "back")
        ref = summed(at, k, 0, slice(None), x)
        go(at, "wide", 10, ref, ref, place.across("x"))
        ref = summed(at, k, 1, y)
        go(at, "wide", 11, ref, ref, place.across("y"))

    def stage_twin(at):
        arrived(at, "wide")
        ref = summed(at, k)
        go(at, "twin", 12, ref, ref, place.across("core"))

    def stage_end(at):
        arrived(at, "twin")

    stages = (
        stage_core,
        stage_first,
        stage_second,
        stage_z,
        stage_back,
        stage_wide,
        stage_twin,
        stage_end,
    )
    plan = Plan(latency=1.5, rate=45e3, pace=0.8)
    total = len(chunks)
    at_stage = [0] * total
    allowed = [0]
    unit = UNIT * BLOCK * 2 / plan.rate
    costs = (0.5, 1.1, 0.4, 0.25, 0.25, 0.1, 0.1, 0.0)
    lengths = (
        (("core", 32 * unit / 6),),
        (("x", 8 * unit), ("y", 8 * unit)),
        (("x", 4 * unit), ("y", 4 * unit)),
        (("z", 8 * unit),),
        (("x", unit), ("y", unit)),
        (("x", 2 * unit), ("y", 2 * unit)),
        (("core", 8 * unit / 6),),
        (),
    )

    def chunk_steps(at):
        moment = 0.0
        for number, stage in enumerate(stages):
            def free(number=number):
                if number == 0 and at >= allowed[0]:
                    return False
                if number == 3 and plan.backlog("z") > Z_LIMIT:
                    return False
                if number == 1 and at >= 5 and at_stage[at - 5] < 4:
                    return False
                if at and at_stage[at - 1] <= number:
                    return False
                return at < 2 or at_stage[at - 2] >= min(number + 2, len(stages))

            yield moment, free
            stage(at)
            plan.now += costs[number]
            at_stage[at] = number + 1
            moment = max([plan.transfer(link, length) for link, length in lengths[number]] + [0.0])

    for at in range(total):
        plan.add(chunk_steps(at))

    def allow(index):
        allowed[0] = sum(1 for chunk in chunks if chunk[0] >= index)
        plan.pump()

    def arrive(copies, moment):
        plan.until(moment)
        for copy in copies:
            copy.wait_recv()

    prime(4)
    for copy in loads:
        copy.start()
    squares[...] = jnp.zeros_like(squares)
    table_own[...] = jnp.zeros_like(table_own)
    greet(place)
    allow(4)

    def put_row(row, value):
        for shard in range(SHARDS):
            table_own[0, shard, row : row + 1, :] = value[:, shard * own : (shard + 1) * own]

    put_row(6, jnp.sum(cotangent[...].astype(jnp.float32), 0, keepdims=True))

    groups = tiles(4)[0]
    need("slope")
    for quarter in range(SHARDS):

        @pl.loop(0, groups)
        def _(group):
            at = quarter * groups + group
            act = contract(cotangent[...], take(4, at), 1, 1)
            give(4, at)
            where = pl.ds(pl.multiple_of(at * 256, 256), 256)
            low = (act * slope[:, where]).astype(LOW)
            grad_inner[:, where] = low
            table_own[0, group, 7 + quarter : 8 + quarter, :] = jnp.sum(
                low.astype(jnp.float32), 0, keepdims=True
            )

        plan.spend(1.5)
    prime(3)
    allow(3)
    parts = tiles(3)[1]

    @pl.loop(0, SHARDS)
    def _(shard):
        where = pl.ds(pl.multiple_of(shard * 256, 256), 256)
        total = None
        for part in range(parts):
            at = shard * parts + part
            term = contract(grad_inner[:, part * BLOCK : (part + 1) * BLOCK], take(3, at), 1, 1)
            give(3, at)
            total = term if total is None else total + term
        grad_second[:, where] = total

    prime(2)
    plan.spend(3.0)
    need("middle")
    gain_sum, bias_sum, low_sum = norm_back(
        middle, vectors[4:5, :], grad_second, cotangent, grad_middle, grad_middle_low, rows
    )
    put_row(4, gain_sum)
    put_row(5, bias_sum)
    put_row(3, low_sum)
    plan.spend(3.0)
    allow(2)

    @pl.loop(0, SHARDS)
    def _(shard):
        outgoing[shard, :, 0:own] = contract(grad_middle_low[...], take(2, shard), 1, 1).astype(LOW)

    prime(1)
    plan.spend(1.0)
    mixed_copies = []
    moments = []
    for pair in range(pairs):
        moments.append(plan.transfer("z", 4 * rows * 128 * 2 / plan.rate))
        columns = pl.ds(pair * 128, 128)
        for offset in range(1, SHARDS):
            mixed_copies.append(
                extra(
                    more + 3 * pair + offset - 1,
                    outgoing.at[lax.rem(s + offset, SHARDS), :, columns],
                    grad_mixed.at[pl.ds(offset * rows, rows), columns],
                    place.along(offset),
                )
            )

    @pl.loop(0, rows // 32)
    def _(block):
        where = pl.ds(pl.multiple_of(block * 32, 32), 32)
        grad_mixed[where, :] = outgoing[s, where, 0:own]

    plan.spend(0.5)
    need("heads")
    everyone = SHARDS * rows
    tile = 384
    lane = lax.broadcasted_iota(jnp.int32, (tile, 128), 1)
    key_row = lax.rem(lax.broadcasted_iota(jnp.int32, (everyone, 128), 0), rows)
    live = key_row < portion
    triple_copies = []
    for pair in range(pairs):
        arrive(mixed_copies[3 * pair : 3 * pair + 3], moments[pair])
        base = pair * 384
        grad_key[...] = jnp.zeros_like(grad_key)
        grad_value[...] = jnp.zeros_like(grad_value)
        low, high = pair * 128, (pair + 1) * 128

        for block in range(everyone // tile):
            start = block * tile
            where = slice(start, start + tile)
            query = heads[where, base : base + 128]
            keys = heads[:, base + 128 : base + 256]
            values = heads[:, base + 256 : base + 384]
            incoming = grad_mixed[where, low:high]
            parts = []
            for half in range(2):
                inside = (lane // 64) == half
                picked = jnp.where(inside, query.astype(jnp.float32) * factor, 0.0).astype(LOW)
                grads = jnp.where(inside, incoming.astype(jnp.float32), 0.0).astype(LOW)
                scores = contract(keys, picked, 1, 1)
                at = 2 * pair + half
                below = scores - log_total[at : at + 1, where]
                weight = jnp.exp(jnp.minimum(below, 0.0))
                into = contract(values, grads, 1, 1)
                delta = jnp.sum(weight * into, 0, keepdims=True)
                grad_scores = (weight * (into - delta)).astype(LOW)
                grad_key[...] += jnp.dot(
                    grad_scores, picked, preferred_element_type=jnp.float32
                )
                grad_value[...] += jnp.dot(
                    weight.astype(LOW), grads, preferred_element_type=jnp.float32
                )
                turned = contract(keys, grad_scores, 0, 0)
                parts.append(turned[half * 64 : (half + 1) * 64])
            both = jnp.concatenate(parts, 0) * factor
            grad_heads[where, base : base + 128] = both.T.astype(LOW)
            plan.spend(4.0)

        grad_heads[:, base + 128 : base + 256] = jnp.where(live, grad_key[...], 0.0).astype(LOW)
        grad_heads[:, base + 256 : base + 384] = jnp.where(live, grad_value[...], 0.0).astype(LOW)
        columns = pl.ds(base, 384)
        triple_moment = plan.transfer("z", 4 * rows * 384 * 2 / plan.rate)
        for offset in range(1, SHARDS):
            triple_copies.append(
                extra(
                    more + 3 * (pairs + pair) + offset - 1,
                    grad_heads.at[pl.ds(offset * rows, rows), columns],
                    grad_triple.at[s, :, columns],
                    (place.rep, place.source(offset)),
                )
            )
        plan.pump()

    @pl.loop(0, rows // 32)
    def _(block):
        where = pl.ds(pl.multiple_of(block * 32, 32), 32)
        grad_triple[s, where, :] = grad_heads[where, :]

    arrive(triple_copies, triple_moment)
    allow(1)
    parts_in = tiles(1)[1]

    @pl.loop(0, SHARDS)
    def _(shard):
        where = pl.ds(pl.multiple_of(shard * 256, 256), 256)
        total = None
        for part in range(parts_in):
            at = shard * parts_in + part
            term = contract(triple_part(part), take(1, at), 1, 1)
            give(1, at)
            total = term if total is None else total + term
        grad_second[:, where] = total

    prime(0)
    need("entering")
    plan.spend(3.0)
    gain_sum, bias_sum, low_sum = norm_back(
        entering, vectors[1:2, :], grad_second, grad_middle, None, grad_entering, rows
    )
    put_row(1, gain_sum)
    put_row(2, bias_sum)
    put_row(0, low_sum)
    plan.spend(3.0)
    allow(0)
    table_copies = []

    def table_step(position, axis):
        if position:
            table_copies[-1].wait_recv()
            table_own[position] = table_own[position - 1] + table_in[position - 1]
        if axis:
            table_copies.append(
                extra(
                    6 + position,
                    table_own.at[position],
                    table_in.at[position],
                    place.across(axis),
                )
            )

    @pl.loop(0, tiles(0)[2])
    def _(at):
        where = pl.ds(pl.multiple_of(at * 256, 256), 256)
        grad_joined[:, where] = contract(grad_entering[...], take(0, at), 1, 1).astype(LOW)
        give(0, at)

    plan.spend(1.5)

    def table_steps():
        for position, axis in enumerate(("core", "x", "y", None)):
            table_step(position, axis)
            if axis:
                yield plan.transfer(axis, 1.5), None
        for offset in range(1, SHARDS):
            table_copies.append(
                extra(
                    8 + offset,
                    table_own.at[3, lax.rem(s + offset, SHARDS)],
                    table_z.at[offset - 1],
                    place.along(offset),
                )
            )
        yield plan.transfer("z", 2.0), None
        for copy in table_copies[3:]:
            copy.wait_recv()
        value = table_own[3, s]
        for offset in range(1, SHARDS):
            value = value + table_z[offset - 1]
        table_sum[...] = value
        direction = direction_of(value, own_states[0], own_states[1])
        share = 1.0 / REPLICAS
        squares[0, 5:6, :] = share * lanes(own_vectors[...] * own_vectors[...])
        squares[0, 13:14, :] = share * lanes(direction * direction)
        table_done[0] = True

    table_done = [False]
    squares_done = [False]

    def square_steps():
        yield 0.0, lambda: table_done[0] and min(at_stage) >= 5
        hops = []
        for position, axis in enumerate(("core", "x", "y", None)):
            if position:
                hops[-1].wait_recv()
                squares[position] = squares[position - 1] + square_in[position - 1]
            if axis:
                hops.append(
                    extra(
                        12 + position,
                        squares.at[position],
                        square_in.at[position],
                        place.across(axis),
                    )
                )
                yield plan.transfer(axis, 0.5), None
        hops = []
        for offset in range(1, SHARDS):
            hops.append(
                extra(14 + offset, squares.at[3], square_z.at[offset], place.along(offset))
            )
        square_z[0] = squares[3]
        yield plan.transfer("z", 0.5), None
        for copy in hops:
            copy.wait_recv()
        value = square_z[s]
        for shard in range(1, SHARDS):
            value = value + square_z[lax.rem(s + SHARDS - shard, SHARDS)]
        norms[...] = jnp.sqrt(jnp.sum(value, 1, keepdims=True)) + jnp.zeros_like(value)
        squares_done[0] = True

    plan.add(table_steps())
    plan.add(square_steps())
    plan.finish(lambda: squares_done[0] and min(at_stage) == len(stages))
    for key in sorted(copies):
        for copy in copies[key]:
            copy.wait_send()
    for copy in sent:
        copy.wait_send()


def backward_pass(cotangent, joined, table, kept, weights, masters, states, vectors, vector_states, portion):
    entering, first_in, heads, log_total, mixed, middle, second_in, slope, activated = kept[:9]
    shapes = [(matrix.shape[0] * SHARDS, matrix.shape[1]) for matrix in masters]
    order = chunk_list(shapes)
    chunks = [chunk for index in (4, 3, 2, 1, 0) for chunk in order if chunk[0] == index]
    total = len(chunks)
    rows, width = entering.shape
    own = width // SHARDS
    hidden = slope.shape[1]
    loaded = (second_in, slope, middle, mixed, heads, first_in, entering, joined)
    everyone = SHARDS * rows
    piece = (UNIT, BLOCK)
    inner = pl.BlockSpec(memory_space=pltpu.VMEM)
    folds = [(SHARDS, r // SHARDS // 256, 2, 2, 2, 2, UNIT, c) for r, c in shapes]
    extra_rows = 16 - vectors.shape[0]
    own_vectors = jnp.pad(vectors, ((0, extra_rows), (0, 0)))
    own_states = jnp.pad(vector_states, ((0, 0), (0, extra_rows), (0, 0)))
    outs = pl.pallas_call(
        functools.partial(backward_kernel, chunks, portion),
        out_shape=[jax.ShapeDtypeStruct(fold[1:], LOW) for fold in folds]
        + [
            jax.ShapeDtypeStruct((16, own), jnp.float32),
            jax.ShapeDtypeStruct((16, 128), jnp.float32),
            jax.ShapeDtypeStruct((rows, 2 * width), LOW),
        ],
        in_specs=[inner] * 4 + [ANY] * 23 + [inner] * 2,
        out_specs=[ANY] * 5 + [inner] * 3,
        scratch_shapes=[
            pltpu.VMEM((8, 2, 2, 2, 2) + piece, LOW),
            pltpu.VMEM((2, SHARDS, 2, 2, 2) + piece, LOW),
            pltpu.VMEM((5, SHARDS, 2, 2, 2) + piece, LOW),
            pltpu.VMEM((4, SHARDS, 2, 2, 2) + piece, LOW),
            pltpu.VMEM((4, 2, SHARDS, 2) + piece, LOW),
            pltpu.VMEM((4, 2, SHARDS) + piece, LOW),
            pltpu.VMEM((2, SHARDS, 2) + piece, LOW),
            pltpu.VMEM((4, SHARDS - 1, 2) + piece, LOW),
            pltpu.VMEM((2, 2) + piece, LOW),
            pltpu.VMEM((2, 2, 2) + piece, jnp.float32),
            pltpu.VMEM((2, 2) + piece, jnp.float32),
            pltpu.VMEM((4, 16, 128), jnp.float32),
            pltpu.VMEM((3, 16, 128), jnp.float32),
            pltpu.VMEM((SHARDS, 16, 128), jnp.float32),
            pltpu.VMEM((4, SHARDS, 16, own), jnp.float32),
            pltpu.VMEM((3, SHARDS, 16, own), jnp.float32),
            pltpu.VMEM((SHARDS - 1, 16, own), jnp.float32),
            pltpu.VMEM((rows, hidden), LOW),
            pltpu.VMEM((rows, width), jnp.float32),
            pltpu.VMEM((rows, width), jnp.float32),
            pltpu.VMEM((rows, width), LOW),
            pltpu.VMEM((SHARDS, rows, own), LOW),
            pltpu.VMEM((everyone, own), LOW),
            pltpu.VMEM((everyone, 128), jnp.float32),
            pltpu.VMEM((everyone, 128), jnp.float32),
            pltpu.VMEM((everyone, 3 * own), LOW),
            pltpu.VMEM((SHARDS, rows, 3 * own), LOW),
            pltpu.VMEM((rows, width), LOW),
            *[pltpu.VMEM(array.shape, array.dtype) for array in loaded],
            pltpu.SemaphoreType.DMA((8,)),
            pltpu.SemaphoreType.DMA((8,)),
            pltpu.SemaphoreType.DMA((2, 2)),
            pltpu.SemaphoreType.DMA((2,)),
            pltpu.SemaphoreType.DMA((total * 14,)),
            pltpu.SemaphoreType.DMA((total * 14,)),
            pltpu.SemaphoreType.DMA((18 + 6 * (own // 128),)),
            pltpu.SemaphoreType.DMA((18 + 6 * (own // 128),)),
        ],
        compiler_params=pltpu.CompilerParams(
            collective_id=2, has_side_effects=True, vmem_limit_bytes=60 * 2**20
        ),
        name="backward_pass",
    )(
        cotangent,
        table,
        log_total,
        activated,
        *loaded,
        *[matrix.reshape(fold) for matrix, fold in zip(weights, folds)],
        *[matrix.reshape(fold[1:]) for matrix, fold in zip(masters, folds)],
        *[state.reshape((2,) + fold[1:]) for state, fold in zip(states, folds)],
        own_vectors,
        own_states,
    )
    lows = [low.reshape(r // SHARDS, c) for low, (r, c) in zip(outs[:5], shapes)]
    return lows, outs[5][: vectors.shape[0]], outs[6], outs[7]


def update_kernel(blocks, norms, *refs):
    gradients, states, masters = refs[0:5], refs[5:10], refs[10:15]
    wides, new_states, new_masters = refs[15:20], refs[20:25], refs[25:30]
    low_in, state_in, master_in, wide_out, state_out, master_out, in_sems, out_sems = refs[30:]
    slots, height = low_in.shape[0], low_in.shape[1]

    def copies(at, arriving):
        index, row, column = blocks[at]
        slot = at % slots
        where = (pl.ds(row, height), pl.ds(column, BLOCK))
        outside = (gradients, states, masters) if arriving else (wides, new_states, new_masters)
        inside = (low_in, state_in, master_in) if arriving else (wide_out, state_out, master_out)
        sems = in_sems if arriving else out_sems
        result = []
        for number in range(3):
            far = outside[number][index].at[((slice(None),) if number == 1 else ()) + where]
            near = inside[number].at[slot]
            ends = (far, near) if arriving else (near, far)
            result.append(pltpu.make_async_copy(*ends, sems.at[slot, number]))
        return result

    def start(at, arriving):
        for copy in copies(at, arriving):
            copy.start()

    def wait(at, arriving):
        for copy in copies(at, arriving):
            copy.wait()

    total = len(blocks)
    ahead = slots - 1
    for at in range(min(ahead, total)):
        start(at, True)
    for at in range(total):
        index = blocks[at][0]
        slot = at % slots
        if at + ahead < total:
            start(at + ahead, True)
        wait(at, True)
        if at >= slots:
            wait(at - slots, False)
        ratio = step_rate * (
            norms[index : index + 1, 0:1] / (norms[8 + index : 9 + index, 0:1] + 1e-06)
        )

        @pl.loop(0, height // UNIT)
        def _(step):
            rows = pl.ds(pl.multiple_of(step * UNIT, UNIT), UNIT)
            grad = low_in[slot, rows, :].astype(jnp.float32)
            second = state_in[slot, 1, rows, :]
            moment = 0.5 * state_in[slot, 0, rows, :] + 0.5 * grad
            root = jnp.sqrt(0.5 * second * second + 0.5 * grad * grad)
            wide_out[slot, rows, :] = grad
            state_out[slot, 0, rows, :] = moment
            state_out[slot, 1, rows, :] = root
            master_out[slot, rows, :] = master_in[slot, rows, :] - ratio * (
                moment / (root + 1e-06)
            )

        start(at, False)
    for at in range(max(0, total - slots), total):
        wait(at, False)


def update_weights(norms, gradients, states, masters):
    height, slots = UPDATE_ROWS, UPDATE_SLOTS
    blocks = [
        (index, row, column)
        for index, master in enumerate(masters)
        for row in range(0, master.shape[0], height)
        for column in range(0, master.shape[1], BLOCK)
    ]
    square = (slots, height, BLOCK)
    pair = (slots, 2, height, BLOCK)
    outs = pl.pallas_call(
        functools.partial(update_kernel, blocks),
        out_shape=[jax.ShapeDtypeStruct(m.shape, jnp.float32) for m in masters]
        + [jax.ShapeDtypeStruct(state.shape, jnp.float32) for state in states]
        + [jax.ShapeDtypeStruct(m.shape, jnp.float32) for m in masters],
        in_specs=[pl.BlockSpec(memory_space=pltpu.VMEM)] + [ANY] * 15,
        out_specs=[ANY] * 15,
        scratch_shapes=[
            pltpu.VMEM(square, LOW),
            pltpu.VMEM(pair, jnp.float32),
            pltpu.VMEM(square, jnp.float32),
            pltpu.VMEM(square, jnp.float32),
            pltpu.VMEM(pair, jnp.float32),
            pltpu.VMEM(square, jnp.float32),
            pltpu.SemaphoreType.DMA((slots, 3)),
            pltpu.SemaphoreType.DMA((slots, 3)),
        ],
        compiler_params=pltpu.CompilerParams(vmem_limit_bytes=48 * 2**20),
        name="update_weights",
    )(norms, *gradients, *states, *masters)
    return outs[:5], outs[5:10], outs[10:]


def fits(masters):
    return (
        lax.axis_size("shard") == SHARDS
        and lax.axis_size("rep") == REPLICAS
        and all(m.shape[0] % 256 == 0 and m.shape[1] % BLOCK == 0 for m in masters)
        and masters[0].shape[1] == HEADS * HEAD_DIM == BLOCK
    )


def plain_device(
    hidden_in,
    skip_path,
    cotangent,
    skip_weight,
    heads_in,
    heads_out,
    expand_weight,
    reduce_weight,
    vectors,
    moments_skip,
    moments_in,
    moments_out,
    moments_expand,
    moments_reduce,
    moments_vectors,
):
    sequences, portion, model_width = hidden_in.shape
    shards = lax.axis_size("shard")
    replicas = lax.axis_size("rep")
    rep_index = lax.axis_index("rep")
    row_count = sequences * portion
    factor = 1.0 / math.sqrt(HEAD_DIM)
    masters = (skip_weight, heads_in, heads_out, expand_weight, reduce_weight, vectors)
    gathered = []
    for matrix in masters[:5]:
        height = matrix.shape[0] // replicas
        piece = lax.dynamic_slice_in_dim(matrix, rep_index * height, height, 0)
        piece = piece.astype(jnp.bfloat16)
        gathered.append(lax.all_gather(piece, ("shard", "rep"), axis=0, tiled=True))
    skip_matrix, in_matrix, out_matrix, expand_matrix, reduce_matrix = gathered
    table_low = lax.all_gather(vectors.astype(jnp.bfloat16), "shard", axis=1, tiled=True)
    table_rows = table_low.astype(jnp.float32)
    source = hidden_in.reshape(row_count, model_width)
    skip_rows = skip_path.reshape(row_count, model_width)
    joined = jnp.concatenate([source, skip_rows], 1)
    entering = matmul(joined, skip_matrix) + table_rows[0]
    normed_one, norm_back_one = jax.vjp(normalize, entering, table_rows[1], table_rows[2])
    first_in = normed_one.astype(jnp.bfloat16)
    triple = matmul(first_in, in_matrix).astype(jnp.bfloat16)
    heads = to_heads(triple, sequences, portion, shards)
    queries, keys_full, values_full = heads[:, :, 0], heads[:, :, 1], heads[:, :, 2]
    scores = (
        jnp.einsum("sqhd,skhd->shqk", queries, keys_full, preferred_element_type=jnp.float32)
        * factor
    )
    row_max = jnp.max(scores, -1)
    row_total = jnp.sum(jnp.exp(scores - row_max[..., None]), -1)
    log_total = row_max + jnp.log(row_total)
    probability = jnp.exp(scores - log_total[..., None])
    mixed = jnp.einsum(
        "shqk,skhd->sqhd",
        probability.astype(jnp.bfloat16),
        values_full,
        preferred_element_type=jnp.float32,
    )
    mixed_low = to_tokens(mixed.astype(jnp.bfloat16)[:, :, None], sequences, portion, shards)
    middle = entering + matmul(mixed_low, out_matrix) + table_rows[3]
    normed_two, norm_back_two = jax.vjp(normalize, middle, table_rows[4], table_rows[5])
    second_in = normed_two.astype(jnp.bfloat16)
    expanded = matmul(second_in, expand_matrix) + table_rows[7:].reshape(-1)
    activated, gelu_back = jax.vjp(exact_gelu, expanded)
    activated_low = activated.astype(jnp.bfloat16)
    block_result = middle + matmul(activated_low, reduce_matrix) + table_rows[6]
    block_out = block_result.astype(jnp.bfloat16).reshape(sequences, portion, model_width)
    grad_out = cotangent.reshape(row_count, model_width)
    grad_reduce = matmul(activated_low.T, grad_out)
    grad_act = matmul(grad_out, reduce_matrix.T)
    grad_inner = gelu_back(grad_act)[0].astype(jnp.bfloat16)
    grad_expand = matmul(second_in.T, grad_inner)
    grad_second = matmul(grad_inner, expand_matrix.T)
    grad_mid_norm, grad_gain_two, grad_bias_two = norm_back_two(grad_second)
    grad_middle = grad_out.astype(jnp.float32) + grad_mid_norm
    grad_middle_low = grad_middle.astype(jnp.bfloat16)
    grad_outw = matmul(mixed_low.T, grad_middle_low)
    grad_mixed = matmul(grad_middle_low, out_matrix.T).astype(jnp.bfloat16)
    grad_mixed = to_heads(grad_mixed, sequences, portion, shards)[:, :, 0]
    grad_prob = jnp.einsum(
        "sqhd,skhd->shqk", grad_mixed, values_full, preferred_element_type=jnp.float32
    )
    delta = jnp.sum(probability * grad_prob, -1)
    grad_scores = (probability * (grad_prob - delta[..., None])).astype(jnp.bfloat16)
    grad_query = (
        jnp.einsum("shqk,skhd->sqhd", grad_scores, keys_full, preferred_element_type=jnp.float32)
        * factor
    )
    grad_keys = (
        jnp.einsum("shqk,sqhd->skhd", grad_scores, queries, preferred_element_type=jnp.float32)
        * factor
    )
    grad_values = jnp.einsum(
        "shqk,sqhd->skhd",
        probability.astype(jnp.bfloat16),
        grad_mixed,
        preferred_element_type=jnp.float32,
    )
    grad_heads = jnp.stack([grad_query, grad_keys, grad_values], 2).astype(jnp.bfloat16)
    grad_triple = to_tokens(grad_heads, sequences, portion, shards)
    grad_inw = matmul(first_in.T, grad_triple)
    grad_first = matmul(grad_triple, in_matrix.T)
    grad_pre_norm, grad_gain_one, grad_bias_one = norm_back_one(grad_first)
    grad_entering = (grad_middle + grad_pre_norm).astype(jnp.bfloat16)
    grad_skipw = matmul(joined.T, grad_entering)
    grad_joined = matmul(grad_entering, skip_matrix.T)
    input_gradient = (
        grad_joined[:, :model_width].astype(jnp.bfloat16).reshape(sequences, portion, model_width)
    )
    skip_gradient = (
        grad_joined[:, model_width:].astype(jnp.bfloat16).reshape(sequences, portion, model_width)
    )
    grad_table = jnp.concatenate(
        [
            jnp.stack(
                [
                    row_sums(grad_entering),
                    grad_gain_one,
                    grad_bias_one,
                    row_sums(grad_middle_low),
                    grad_gain_two,
                    grad_bias_two,
                    row_sums(grad_out),
                ]
            ),
            row_sums(grad_inner).reshape(-1, model_width),
        ],
        0,
    )
    width = vectors.shape[1]
    grad_table = lax.psum(grad_table, ("rep", "shard"))
    vector_total = lax.dynamic_slice_in_dim(grad_table, lax.axis_index("shard") * width, width, 1)
    totals = []
    for partial in (grad_skipw, grad_inw, grad_outw, grad_expand, grad_reduce):
        piece = lax.psum_scatter(
            partial.astype(jnp.bfloat16), ("shard", "rep"), scatter_dimension=0, tiled=True
        )
        whole = lax.all_gather(piece, "rep", axis=0, tiled=True)
        totals.append(whole.astype(jnp.float32))
    totals.append(vector_total)
    states = (
        moments_skip,
        moments_in,
        moments_out,
        moments_expand,
        moments_reduce,
        moments_vectors,
    )
    steps = [moment_step(total, state) for total, state in zip(totals, states)]
    squares = jnp.stack(
        [
            jnp.stack([jnp.sum(matrix * matrix) for matrix in masters]),
            jnp.stack([jnp.sum(direction * direction) for _, direction in steps]),
        ]
    )
    norms = jnp.sqrt(lax.psum(squares, "shard"))
    ratio = norms[0] / (norms[1] + 1e-06)
    updated = [
        masters[position] - step_rate * ratio[position] * steps[position][1]
        for position in range(6)
    ]
    return (
        block_out,
        input_gradient,
        skip_gradient,
        *totals,
        *(state for state, _ in steps),
        *updated,
        norms,
    )


def on_device(
    hidden_in,
    skip_path,
    cotangent,
    skip_weight,
    heads_in,
    heads_out,
    expand_weight,
    reduce_weight,
    vectors,
    moments_skip,
    moments_in,
    moments_out,
    moments_expand,
    moments_reduce,
    moments_vectors,
):
    sequences, portion, model_width = hidden_in.shape
    masters = (skip_weight, heads_in, heads_out, expand_weight, reduce_weight)
    states = (moments_skip, moments_in, moments_out, moments_expand, moments_reduce)
    if not (sequences == 1 and fits(masters)):
        return plain_device(
            hidden_in, skip_path, cotangent, *masters, vectors, *states, moments_vectors
        )
    more = -portion % 32
    joined = jnp.concatenate([hidden_in[0], skip_path[0]], 1)
    joined = jnp.pad(joined, ((0, more), (0, 0)))
    incoming = jnp.pad(cotangent[0], ((0, more), (0, 0)))
    weights, kept = forward_pass(joined, vectors, masters, portion)
    block_out, table = kept[9], kept[10]
    lows, vector_total, norms, grad_joined = backward_pass(
        incoming, joined, table, kept, weights, masters, states, vectors, moments_vectors, portion
    )
    wides, new_states, new_masters = update_weights(norms, lows, states, masters)
    vector_state, direction = moment_step(vector_total, moments_vectors)
    ratio = norms[5, 0] / (norms[13, 0] + 1e-06)
    return (
        block_out[None, :portion],
        grad_joined[None, :portion, :model_width],
        grad_joined[None, :portion, model_width:],
        *wides,
        vector_total,
        *new_states,
        vector_state,
        *new_masters,
        vectors - step_rate * ratio * direction,
        jnp.stack([norms[:6, 0], norms[8:14, 0]]),
    )


def solution(mesh):
    placed = (
        P("rep", "shard", None),
        P("rep", "shard", None),
        P("rep", "shard", None),
        P("shard", None),
        P("shard", None),
        P("shard", None),
        P("shard", None),
        P("shard", None),
        P(None, "shard"),
        P(None, "shard", None),
        P(None, "shard", None),
        P(None, "shard", None),
        P(None, "shard", None),
        P(None, "shard", None),
        P(None, None, "shard"),
    )
    return jax.shard_map(
        on_device,
        mesh=mesh,
        in_specs=placed,
        out_specs=(
            P("rep", "shard", None),
            P("rep", "shard", None),
            P("rep", "shard", None),
            P("shard", None),
            P("shard", None),
            P("shard", None),
            P("shard", None),
            P("shard", None),
            P(None, "shard"),
            P(None, "shard", None),
            P(None, "shard", None),
            P(None, "shard", None),
            P(None, "shard", None),
            P(None, "shard", None),
            P(None, None, "shard"),
            P("shard", None),
            P("shard", None),
            P("shard", None),
            P("shard", None),
            P("shard", None),
            P(None, "shard"),
            P(),
        ),
        check_vma=False,
    )
```

```python
import functools
import math

import jax
import jax.numpy as jnp
from jax import lax
from jax.experimental import pallas as pl
from jax.experimental.pallas import tpu as pltpu
from jax.sharding import PartitionSpec as P

HEADS = 16
HEAD_DIM = 64
MESH = pl.DeviceIdType.MESH
LOW = jnp.bfloat16
ANY = pl.BlockSpec(memory_space=pl.ANY)
SHARDS, REPLICAS = 4, 8
UNIT = 16
BLOCK = 1024


class Place:
    def __init__(self):
        self.rep = lax.axis_index("rep")
        self.shard = lax.axis_index("shard")
        self.core = lax.rem(self.rep, 2)
        self.x = lax.rem(self.rep // 2, 2)
        self.y = self.rep // 4

    def across(self, axis):
        own, step = {"core": (self.core, 1), "x": (self.x, 2), "y": (self.y, 4)}[axis]
        return (self.rep + step - 2 * step * own, self.shard)

    def along(self, offset):
        return (self.rep, lax.rem(self.shard + offset, SHARDS))

    def source(self, offset):
        return lax.rem(self.shard + SHARDS - offset, SHARDS)

    def partners(self):
        return [self.across("core"), self.across("x"), self.across("y")] + [
            self.along(offset) for offset in range(1, SHARDS)
        ]


def greet(place):
    barrier = pltpu.get_barrier_semaphore()
    partners = place.partners()
    for partner in partners:
        pl.semaphore_signal(barrier, inc=1, device_id=partner, device_id_type=MESH)
    pl.semaphore_wait(barrier, len(partners))


def chunk_list(shapes):
    chunks = []
    for index, (rows, columns) in enumerate(shapes):
        for group in range(rows // SHARDS // 256):
            for part in range(columns // BLOCK):
                chunks.append((index, group, part))
    return chunks


class Plan:
    def __init__(self, latency, rate, pace):
        self.now, self.latency, self.rate, self.pace = 0.0, latency, rate, pace
        self.free = {}
        self.agents = []

    def transfer(self, link, length):
        self.free[link] = max(self.now, self.free.get(link, 0.0)) + length
        return self.free[link] + self.latency

    def backlog(self, link):
        return self.free.get(link, 0.0) - self.now

    def add(self, steps):
        agent = [steps, 0.0, None]
        self.agents.append(agent)
        self.resume(agent)

    def resume(self, agent):
        try:
            agent[1], agent[2] = next(agent[0])
        except StopIteration:
            self.agents.remove(agent)

    def ready(self):
        return [a for a in self.agents if a[2] is None or a[2]()]

    def pump(self):
        while True:
            able = [agent for agent in self.ready() if agent[1] <= self.now]
            if not able:
                return
            self.resume(able[0])

    def spend(self, length):
        self.now += self.pace * length
        self.pump()

    def until(self, moment):
        self.pump()
        while self.now < moment:
            times = [agent[1] for agent in self.ready() if agent[1] > self.now]
            self.now = min(times + [moment])
            self.pump()

    def finish(self, test):
        self.pump()
        while not test():
            times = [agent[1] for agent in self.ready()]
            self.now = max(self.now, min(times))
            self.pump()


step_rate = 0.3


def normalize(stream, gain_row, bias_row):
    center = stream - jnp.mean(stream, -1, keepdims=True)
    spread = jnp.mean(center * center, -1, keepdims=True)
    return center * lax.rsqrt(spread + 1e-05) * gain_row + bias_row


def exact_gelu(inputs):
    return jax.nn.gelu(inputs, approximate=False)


def matmul(left, right):
    return jnp.dot(left, right, preferred_element_type=jnp.float32)


def row_sums(matrix):
    return jnp.sum(matrix, 0, dtype=jnp.float32)


def moment_step(gradient, moments):
    first_moment = 0.5 * moments[0] + 0.5 * gradient
    root_square = jnp.sqrt(0.5 * moments[1] * moments[1] + 0.5 * gradient * gradient)
    direction = first_moment / (root_square + 1e-06)
    return (jnp.stack([first_moment, root_square]), direction)


def to_heads(rows, sequences, portion, shards):
    parts = rows.shape[1] // (HEADS * HEAD_DIM)
    width = HEADS * HEAD_DIM // shards
    blocks = rows.reshape(sequences, portion, parts, shards, width).transpose(3, 0, 1, 2, 4)
    blocks = blocks.reshape(shards, sequences * portion, parts * width)
    blocks = lax.all_to_all(blocks, "shard", 0, 0, tiled=True)
    blocks = blocks.reshape(shards, sequences, portion, parts, width).transpose(1, 0, 2, 3, 4)
    return blocks.reshape(sequences, shards * portion, parts, width // HEAD_DIM, HEAD_DIM)


def to_tokens(blocks, sequences, portion, shards):
    parts = blocks.shape[2]
    width = HEADS * HEAD_DIM // shards
    rows = blocks.reshape(sequences, shards, portion, parts, width).transpose(1, 0, 2, 3, 4)
    rows = rows.reshape(shards, sequences * portion, parts * width)
    rows = lax.all_to_all(rows, "shard", 0, 0, tiled=True)
    rows = rows.reshape(shards, sequences * portion, parts, width).transpose(1, 2, 0, 3)
    return rows.reshape(sequences * portion, parts * shards * width)


SLOTS = 19
Z_BACKLOG = 5.0


def weight_tile(whole, shard, group, start, width):
    return whole[shard, group, :, :, :, :, :, pl.ds(start, width)].reshape(256, width)


def product(left, whole, start, width):
    groups = whole.shape[1]
    total = None
    for shard in range(SHARDS):
        for group in range(groups):
            first = (shard * groups + group) * 256
            term = jnp.dot(
                left[:, first : first + 256],
                weight_tile(whole, shard, group, start, width),
                preferred_element_type=jnp.float32,
            )
            total = term if total is None else total + term
    return total


def contract(left, right, left_axis, right_axis):
    return lax.dot_general(
        left, right, (((left_axis,), (right_axis,)), ((), ())), preferred_element_type=jnp.float32
    )


def norm_rows(source, gain, bias, target, rows):
    @pl.loop(0, rows // 32)
    def _(block):
        where = pl.ds(pl.multiple_of(block * 32, 32), 32)
        stream = source[where, :]
        center = stream - jnp.mean(stream, -1, keepdims=True)
        spread = jnp.mean(center * center, -1, keepdims=True)
        target[where, :] = (center * lax.rsqrt(spread + 1e-05) * gain + bias).astype(LOW)


def forward_kernel(chunks, portion, *refs):
    rows_in, vectors = refs[0:2]
    masters = refs[2:7]
    keeps = refs[7:12]
    (
        entering,
        first_in,
        heads,
        log_total,
        mixed,
        middle,
        second_in,
        slope,
        activated,
        out,
        table,
    ) = refs[12:23]
    wholes = refs[23:28]
    (
        wide,
        table_own,
        table_all,
        outgoing,
        answer,
        load_sems,
        keep_sems,
        send_sems,
        recv_sems,
        more_send,
        more_recv,
        joined,
        joined_sem,
    ) = refs[28:]
    place = Place()
    s, k, x, y = place.shard, place.core, place.x, place.y
    total = len(chunks)
    rows = entering.shape[0]
    width = entering.shape[1]
    own = width // SHARDS
    pairs = own // 128
    factor = 1.0 / math.sqrt(HEAD_DIM)

    def load(at):
        index, group, part = chunks[at]
        return pltpu.make_async_copy(
            masters[index].at[group, :, :, :, :, :, pl.ds(part * BLOCK, BLOCK)],
            wide.at[at % 2],
            load_sems.at[at % 2],
        )

    def whole(at, shard, *rest):
        index, group, part = chunks[at]
        rest = rest + (slice(None),) * (5 - len(rest))
        return wholes[index].at[(shard, group) + rest + (pl.ds(part * BLOCK, BLOCK),)]

    sent = []
    far = []
    arrivals = {}

    def relay_copy(at):
        up = s == SHARDS - 2
        ref = whole(at, place.source(2), k, slice(None), y, x)
        target = jnp.where(up, SHARDS - 1, 0)
        return pltpu.make_async_remote_copy(
            src_ref=ref,
            dst_ref=ref,
            send_sem=send_sems.at[at * SLOTS + SLOTS - 1],
            recv_sem=recv_sems.at[at * SLOTS + jnp.where(up, SHARDS - 2, 0)],
            device_id=(place.rep, target),
            device_id_type=MESH,
        )

    def go(at, name, position, ref, device):
        slot = at * SLOTS + position
        copy = pltpu.make_async_remote_copy(
            src_ref=ref,
            dst_ref=ref,
            send_sem=send_sems.at[slot],
            recv_sem=recv_sems.at[slot],
            device_id=device,
            device_id_type=MESH,
        )
        copy.start()
        sent.append(copy)
        arrivals.setdefault((at, name), []).append(copy)

    def arrived(at, name):
        for copy in arrivals[(at, name)]:
            copy.wait_recv()

    def extra(slot, source, target, device):
        copy = pltpu.make_async_remote_copy(
            src_ref=source,
            dst_ref=target,
            send_sem=more_send.at[slot],
            recv_sem=more_recv.at[slot],
            device_id=device,
            device_id_type=MESH,
        )
        copy.start()
        sent.append(copy)
        return copy

    kept = []

    def stage_cast(at):
        index, group, part = chunks[at]
        load(at).wait()

        @pl.loop(0, 16)
        def _(row):
            a, b = row // 8, lax.rem(row // 4, 2)
            c, d = lax.rem(row // 2, 2), lax.rem(row, 2)
            wholes[index][s, group, a, b, c, d, :, part * BLOCK : (part + 1) * BLOCK] = wide[
                at % 2, a, b, c, d
            ].astype(LOW)

        if at + 2 < total:
            load(at + 2).start()

    def stage_z(at):
        for offset in range(1, SHARDS):
            ref = whole(at, s, k, slice(None), y, x)
            slot = at * SLOTS + offset - 1
            target = lax.rem(s + offset, SHARDS)
            copy = pltpu.make_async_remote_copy(
                src_ref=ref,
                dst_ref=ref,
                send_sem=send_sems.at[slot],
                recv_sem=recv_sems.at[slot],
                device_id=(place.rep, target),
                device_id_type=MESH,
            )
            arrivals[(at, "z", offset)] = copy
            if offset == 2:
                copy.start()
                sent.append(copy)
            else:
                near = s != (0 if offset == SHARDS - 1 else SHARDS - 1)
                far.append((near, copy))

                @pl.when(near)
                def _(copy=copy):
                    copy.start()

    def stage_relay(at):
        arrivals[(at, "z", 2)].wait_recv()
        inner = (s > 0) & (s < SHARDS - 1)
        copy = relay_copy(at)
        far.append((inner, copy))

        @pl.when(inner)
        def _():
            copy.start()

    def stage_first(at):
        arrivals[(at, "z", 1)].wait_recv()
        arrivals[(at, "z", 3)].wait_recv()
        for offset in range(1, SHARDS):
            e = place.source(offset)
            go(at, "first", 3 + 2 * (offset - 1), whole(at, e, k, 0, y, x), place.across("x"))
            go(at, "first", 4 + 2 * (offset - 1), whole(at, e, k, 1, y, x), place.across("y"))

    def stage_second(at):
        arrived(at, "first")
        for offset in range(1, SHARDS):
            e = place.source(offset)
            go(at, "second", 9 + 2 * (offset - 1), whole(at, e, k, 0, y), place.across("y"))
            ref = whole(at, e, k, 1, slice(None), x)
            go(at, "second", 10 + 2 * (offset - 1), ref, place.across("x"))

    def stage_core(at):
        arrived(at, "second")
        for offset in range(1, SHARDS):
            e = place.source(offset)
            go(at, "core", 15 + offset - 1, whole(at, e, k), place.across("core"))

    def stage_end(at):
        arrived(at, "core")
        index, group, part = chunks[at]
        copy = pltpu.make_async_copy(
            whole(at, slice(None)),
            keeps[index].at[:, group, :, :, :, :, :, pl.ds(part * BLOCK, BLOCK)],
            keep_sems.at[at],
        )
        copy.start()
        kept.append(copy)

    plan = Plan(latency=2.0, rate=45e3, pace=0.8)
    done = [0] * total
    unit = UNIT * BLOCK * 2 / plan.rate

    def chunk_steps(at):
        yield 0.0, lambda: (at == 0 or done[at - 1] >= 1) and plan.backlog("z") < Z_BACKLOG
        stage_cast(at)
        plan.now += 0.6
        stage_z(at)
        start = plan.transfer("z", 6 * unit)
        done[at] = 1
        yield start - 2 * unit, None
        stage_relay(at)
        yield start + 1.0, None
        stage_first(at)
        moment = max(plan.transfer("x", 3 * unit), plan.transfer("y", 3 * unit))
        yield moment, None
        stage_second(at)
        moment = max(plan.transfer("x", 6 * unit), plan.transfer("y", 6 * unit))
        yield moment, None
        stage_core(at)
        plan.now += 0.2
        yield plan.transfer("core", 24 * unit / 6), None
        stage_end(at)
        done[at] = 2

    def until(at):
        plan.finish(lambda: done[at] == 2)

    def arrive(copies, moment):
        plan.until(moment)
        for copy in copies:
            copy.wait_recv()

    load(0).start()
    load(1).start()
    joined_copy = pltpu.make_async_copy(
        rows_in.at[:, pl.ds(0, joined.shape[1])], joined, joined_sem.at[0]
    )
    joined_copy.start()
    table_own[...] = vectors[...].astype(LOW)
    table_all[0] = vectors[...].astype(LOW)
    greet(place)
    table_copies = []
    for offset in range(1, SHARDS):
        table_copies.append(extra(offset - 1, table_own, table_all.at[offset], place.along(offset)))
    for at in range(total):
        plan.add(chunk_steps(at))
    last = {}
    for at, (index, group, part) in enumerate(chunks):
        last[index] = at

    until(0)
    for copy in table_copies:
        copy.wait_recv()
    for offset in range(SHARDS):
        column = pl.multiple_of(place.source(offset) * own, own)
        table[:, pl.ds(column, own)] = table_all[offset].astype(jnp.float32)
    joined_copy.wait()
    until(last[0])

    @pl.loop(0, width // 256)
    def _(part):
        start = pl.multiple_of(part * 256, 256)
        entering[:, pl.ds(start, 256)] = (
            product(joined, wholes[0], start, 256) + table[0:1, pl.ds(start, 256)]
        )

    plan.spend(2.5)
    norm_rows(entering, table[1:2, :], table[2:3, :], first_in, rows)
    plan.spend(2.0)
    until(last[1])
    live = lax.broadcasted_iota(jnp.int32, (rows, own), 0) < portion
    for kind in range(3):

        @pl.loop(0, SHARDS)
        def _(target):
            start = pl.multiple_of(kind * width + target * own, own)
            value = jnp.where(live, product(first_in, wholes[1], start, own), 0.0).astype(LOW)
            for pair in range(pairs):
                first = (3 * pair + kind) * 128
                outgoing[target, :, first : first + 128] = value[:, pair * 128 : (pair + 1) * 128]

        plan.spend(1.5)

    head_copies = []
    moments = []
    for pair in range(pairs):
        moments.append(plan.transfer("z", 4 * rows * 384 * 2 / plan.rate))
        for offset in range(1, SHARDS):
            target = lax.rem(s + offset, SHARDS)
            columns = pl.ds(pair * 384, 384)
            head_copies.append(
                extra(
                    3 * pair + 2 + offset,
                    outgoing.at[target, :, columns],
                    heads.at[pl.ds(offset * rows, rows), columns],
                    place.along(offset),
                )
            )

    @pl.loop(0, rows // 32)
    def _(block):
        where = pl.ds(pl.multiple_of(block * 32, 32), 32)
        heads[where, :] = outgoing[s, where, :]

    plan.spend(0.5)
    everyone = SHARDS * rows
    tile = 384
    lane = lax.broadcasted_iota(jnp.int32, (tile, 128), 1)
    key_row = lax.rem(lax.broadcasted_iota(jnp.int32, (everyone, 1), 0), rows)
    key_bias = jnp.where(key_row < portion, 0.0, -1e30)
    answer_copies = []
    column = pl.multiple_of(s * own, own)
    for pair in range(pairs):
        arrive(head_copies[3 * pair : 3 * pair + 3], moments[pair])
        base = pair * 384

        for block in range(everyone // tile):
            start = block * tile
            where = slice(start, start + tile)
            query = heads[where, base : base + 128]
            keys = heads[:, base + 128 : base + 256]
            values = heads[:, base + 256 : base + 384]
            parts = []
            for half in range(2):
                inside = (lane // 64) == half
                picked = jnp.where(inside, query.astype(jnp.float32) * factor, 0.0).astype(LOW)
                scores = contract(keys, picked, 1, 1)
                scores = scores + key_bias
                top = jnp.max(scores, 0, keepdims=True)
                weight = jnp.exp(scores - top)
                weight_sum = jnp.sum(weight, 0, keepdims=True)
                log_total[2 * pair + half : 2 * pair + half + 1, where] = (
                    top + jnp.log(weight_sum)
                )
                weight = (weight * (1.0 / weight_sum)).astype(LOW)
                summed = contract(values, weight, 0, 0)
                parts.append(summed[half * 64 : (half + 1) * 64])
            both = jnp.concatenate(parts, 0)
            answer[where, pair * 128 : (pair + 1) * 128] = both.T.astype(LOW)
            plan.spend(2.0)

        answer_moment = plan.transfer("z", 4 * rows * 128 * 2 / plan.rate)
        columns = pl.ds(pair * 128, 128)
        for offset in range(1, SHARDS):
            answer_copies.append(
                extra(
                    3 * (pairs + pair) + 2 + offset,
                    answer.at[pl.ds(offset * rows, rows), columns],
                    mixed.at[:, pl.ds(column + pair * 128, 128)],
                    (place.rep, place.source(offset)),
                )
            )

    mixed[:, pl.ds(column, own)] = answer[0:rows, :]
    until(last[2])
    arrive(answer_copies, answer_moment)

    @pl.loop(0, width // 256)
    def _(part):
        start = pl.multiple_of(part * 256, 256)
        where = pl.ds(start, 256)
        middle[:, where] = (
            entering[:, where] + product(mixed, wholes[2], start, 256) + table[3:4, where]
        )

    plan.spend(1.5)
    norm_rows(middle, table[4:5, :], table[5:6, :], second_in, rows)
    plan.spend(2.0)
    per_row = width // 256
    for part in range(slope.shape[1] // BLOCK):
        until(last[2] + 1 + part)

        @pl.loop(0, BLOCK // 256)
        def _(piece):
            start = pl.multiple_of(part * BLOCK + piece * 256, 256)
            bias_at = pl.multiple_of(piece * 256, 256)
            value = (
                product(second_in, wholes[3], start, 256)
                + table[7 + part : 8 + part, pl.ds(bias_at, 256)]
            )
            below = 0.5 + 0.5 * lax.erf(value * math.sqrt(0.5))
            bell = jnp.exp(-0.5 * value * value) * (1.0 / math.sqrt(2.0 * math.pi))
            slope[:, pl.ds(start, 256)] = below + value * bell
            activated[:, pl.ds(start, 256)] = (value * below).astype(LOW)

        plan.spend(4.0)

    until(last[4])

    @pl.loop(0, width // 256)
    def _(part):
        start = pl.multiple_of(part * 256, 256)
        where = pl.ds(start, 256)
        out[:, where] = (
            middle[:, where] + product(activated, wholes[4], start, 256) + table[6:7, where]
        ).astype(LOW)

    for copy in sent:
        copy.wait_send()
    for used, copy in far:

        @pl.when(used)
        def _(copy=copy):
            copy.wait_send()

    for copy in kept:
        copy.wait()


def forward_pass(joined, vectors, masters, portion):
    shapes = [(matrix.shape[0] * SHARDS, matrix.shape[1]) for matrix in masters]
    chunks = chunk_list(shapes)
    total = len(chunks)
    rows = joined.shape[0]
    width = joined.shape[1] // 3
    own = width // SHARDS
    hidden = shapes[3][1]
    everyone = SHARDS * rows
    split = [
        matrix.reshape(matrix.shape[0] // 256, 2, 2, 2, 2, UNIT, matrix.shape[1])
        for matrix in masters
    ]
    folds = [(SHARDS, r // SHARDS // 256, 2, 2, 2, 2, UNIT, c) for r, c in shapes]
    inner = pl.BlockSpec(memory_space=pltpu.VMEM)
    table = jnp.pad(vectors, ((0, 16 - vectors.shape[0]), (0, 0)))
    outs = pl.pallas_call(
        functools.partial(forward_kernel, chunks, portion),
        out_shape=[jax.ShapeDtypeStruct(fold, LOW) for fold in folds]
        + [
            jax.ShapeDtypeStruct((rows, width), jnp.float32),
            jax.ShapeDtypeStruct((rows, width), LOW),
            jax.ShapeDtypeStruct((everyone, 3 * own), LOW),
            jax.ShapeDtypeStruct((8, everyone), jnp.float32),
            jax.ShapeDtypeStruct((rows, width), LOW),
            jax.ShapeDtypeStruct((rows, width), jnp.float32),
            jax.ShapeDtypeStruct((rows, width), LOW),
            jax.ShapeDtypeStruct((rows, hidden), jnp.float32),
            jax.ShapeDtypeStruct((rows, hidden), LOW),
            jax.ShapeDtypeStruct((rows, width), LOW),
            jax.ShapeDtypeStruct((16, width), jnp.float32),
        ],
        in_specs=[ANY, inner] + [ANY] * 5,
        out_specs=[ANY] * 5 + [inner] * 11,
        scratch_shapes=[pltpu.VMEM(fold, LOW) for fold in folds]
        + [
            pltpu.VMEM((2, 2, 2, 2, 2, UNIT, BLOCK), jnp.float32),
            pltpu.VMEM((16, own), LOW),
            pltpu.VMEM((SHARDS, 16, own), LOW),
            pltpu.VMEM((SHARDS, rows, 3 * own), LOW),
            pltpu.VMEM((everyone, own), LOW),
            pltpu.SemaphoreType.DMA((2,)),
            pltpu.SemaphoreType.DMA((total,)),
            pltpu.SemaphoreType.DMA((total * SLOTS,)),
            pltpu.SemaphoreType.DMA((total * SLOTS,)),
            pltpu.SemaphoreType.DMA((3 + 6 * (own // 128),)),
            pltpu.SemaphoreType.DMA((3 + 6 * (own // 128),)),
            pltpu.VMEM((rows, 2 * width), LOW),
            pltpu.SemaphoreType.DMA((1,)),
        ],
        compiler_params=pltpu.CompilerParams(
            collective_id=1, has_side_effects=True, vmem_limit_bytes=60 * 2**20
        ),
        name="forward_pass",
    )(joined, table, *split)
    weights = [out.reshape(shape) for out, shape in zip(outs[:5], shapes)]
    return weights, outs[5:]


UPDATE_ROWS, UPDATE_SLOTS = 256, 3
Z_LIMIT = 1000.0


def norm_back(source, gain, incoming, residual, wide_out, low_out, rows):
    columns = source.shape[1]

    def body(block, carry):
        where = pl.ds(pl.multiple_of(block * 32, 32), 32)
        stream = source[where, :]
        center = stream - jnp.mean(stream, -1, keepdims=True)
        spread = jnp.mean(center * center, -1, keepdims=True)
        scale = lax.rsqrt(spread + 1e-05)
        hat = center * scale
        grad = incoming[where, :]
        scaled = grad * gain
        slope = scale * (
            scaled
            - jnp.mean(scaled, -1, keepdims=True)
            - hat * jnp.mean(scaled * hat, -1, keepdims=True)
        )
        value = residual[where, :].astype(jnp.float32) + slope
        low = value.astype(LOW)
        if wide_out is not None:
            wide_out[where, :] = value
        low_out[where, :] = low
        terms = (grad * hat, grad, low.astype(jnp.float32))
        return tuple(kept + jnp.sum(term, 0, keepdims=True) for kept, term in zip(carry, terms))

    zero = jnp.zeros((1, columns), jnp.float32)
    return lax.fori_loop(0, rows // 32, body, (zero, zero, zero))


def backward_kernel(chunks, portion, *refs):
    (
        rows_in,
        vectors,
        log_total,
        activated,
    ) = refs[:4]
    outside = refs[4:12]
    weights = refs[12:17]
    masters = refs[17:22]
    states = refs[22:27]
    own_vectors, own_states = refs[27:29]
    sums = refs[29:34]
    table_sum, norms, grad_joined = refs[34:37]
    (
        ring,
        theirs,
        mine,
        from_core,
        from_first,
        from_second,
        final,
        from_z,
        ready,
        state_in,
        master_in,
        squares,
        square_in,
        square_z,
        table_own,
        table_in,
        table_z,
        grad_inner,
        grad_second,
        grad_middle,
        grad_middle_low,
        outgoing,
        grad_mixed,
        grad_key,
        grad_value,
        grad_heads,
        grad_triple,
        grad_entering,
        second_in,
        slope,
        middle,
        mixed,
        heads,
        first_in,
        entering,
        joined,
        cotangent,
        cotangent_sem,
        load_sems,
        ring_sems,
        state_sems,
        ready_sems,
        send_sems,
        recv_sems,
        more_send,
        more_recv,
    ) = refs[37:]
    place = Place()
    s, k, x, y = place.shard, place.core, place.x, place.y
    rows, width = entering.shape
    own = width // SHARDS
    factor = 1.0 / math.sqrt(HEAD_DIM)
    depth = ring.shape[0]

    inside = (second_in, slope, middle, mixed, heads, first_in, entering, joined)
    loads = [
        pltpu.make_async_copy(
            source.at[:, pl.ds(0, target.shape[1])], target, load_sems.at[position]
        )
        for position, (source, target) in enumerate(zip(outside, inside))
    ]
    names = ["second_in", "slope", "middle", "mixed", "heads", "first_in", "entering", "joined"]
    waiting_for = dict(zip(names, loads))

    def need(name):
        if name in waiting_for:
            waiting_for.pop(name).wait()

    def tiles(index):
        parts = weights[index].shape[7] // BLOCK
        return weights[index].shape[1], parts, SHARDS * weights[index].shape[1] * parts

    def fetch(index, at):
        groups, parts, _ = tiles(index)
        shard, rest = at // (groups * parts), lax.rem(at, groups * parts)
        group, part = rest // parts, lax.rem(rest, parts)
        start = pl.multiple_of(part * BLOCK, BLOCK)
        return pltpu.make_async_copy(
            weights[index].at[shard, group, :, :, :, :, :, pl.ds(start, BLOCK)],
            ring.at[lax.rem(at, depth)],
            ring_sems.at[lax.rem(at, depth)],
        )

    def prime(index):
        @pl.loop(0, min(depth, tiles(index)[2]))
        def _(at):
            fetch(index, at).start()

    def take(index, at):
        fetch(index, at).wait()
        return ring[lax.rem(at, depth)].reshape(256, BLOCK)

    def give(index, at):
        @pl.when(at + depth < tiles(index)[2])
        def _():
            fetch(index, at + depth).start()

    copies = {}

    def go(at, name, position, source, target, device):
        slot = at * 14 + position
        copy = pltpu.make_async_remote_copy(
            src_ref=source,
            dst_ref=target,
            send_sem=send_sems.at[slot],
            recv_sem=recv_sems.at[slot],
            device_id=device,
            device_id_type=MESH,
        )
        copy.start()
        copies.setdefault((at, name), []).append(copy)

    sent = []
    more = 18

    def extra(slot, source, target, device):
        copy = pltpu.make_async_remote_copy(
            src_ref=source,
            dst_ref=target,
            send_sem=more_send.at[slot],
            recv_sem=more_recv.at[slot],
            device_id=device,
            device_id_type=MESH,
        )
        copy.start()
        sent.append(copy)
        return copy

    def arrived(at, name):
        for copy in copies[(at, name)]:
            copy.wait_recv()

    def left(at, name):
        for copy in copies.pop((at, name), []):
            copy.wait_send()

    pairs = own // 128

    def triple_part(part):
        return jnp.concatenate(
            [
                grad_triple[shard, :, (3 * pair + part) * 128 : (3 * pair + part + 1) * 128]
                for shard in range(SHARDS)
                for pair in range(pairs)
            ],
            1,
        )

    def gradient_half(at, core):
        index, group, part = chunks[at]
        if index < 4:
            need(("joined", "first_in", "mixed", "second_in")[index])
        lefts = (joined, first_in, mixed, second_in, activated)[index]
        pitch = lefts.shape[1] // SHARDS
        columns = [
            lefts[:, pl.ds(pl.multiple_of(shard * pitch + group * 256 + core * 128, 128), 128)]
            for shard in range(SHARDS)
        ]
        if index == 0:
            right = grad_entering[...]
        elif index == 1:
            right = triple_part(part)
        elif index == 2:
            right = grad_middle_low[...]
        elif index == 3:
            right = grad_inner[:, part * BLOCK : (part + 1) * BLOCK]
        else:
            right = cotangent[...]
        return contract(jnp.concatenate(columns, 1), right, 0, 0)

    def stage_core(at):
        slot = at % 2
        value = gradient_half(at, 1 - k).astype(LOW)
        theirs[slot] = value.reshape(SHARDS, 2, 2, 2, UNIT, BLOCK)
        go(at, "core", 0, theirs.at[slot], from_core.at[at % 4], place.across("core"))

    def stage_first(at):
        slot = at % 5
        value = gradient_half(at, k).reshape(SHARDS, 2, 2, 2, UNIT, BLOCK)
        arrived(at, "core")
        left(at, "core")
        mine[slot] = (value + from_core[at % 4].astype(jnp.float32)).astype(LOW)
        target = from_first.at[at % 4]
        go(at, "first", 1, mine.at[slot, :, 0, :, 1 - x], target.at[0], place.across("x"))
        go(at, "first", 2, mine.at[slot, :, 1, 1 - y], target.at[1], place.across("y"))

    def stage_second(at):
        slot = at % 5
        arrived(at, "first")
        left(at, "first")

        @pl.loop(0, SHARDS)
        def _(shard):
            for i in range(2):
                mine[slot, shard, 0, i, x] = (
                    mine[slot, shard, 0, i, x].astype(jnp.float32)
                    + from_first[at % 4, 0, shard, i].astype(jnp.float32)
                ).astype(LOW)
                mine[slot, shard, 1, y, i] = (
                    mine[slot, shard, 1, y, i].astype(jnp.float32)
                    + from_first[at % 4, 1, shard, i].astype(jnp.float32)
                ).astype(LOW)

        target = from_second.at[at % 4]
        go(at, "second", 3, mine.at[slot, :, 0, 1 - y, x], target.at[0], place.across("y"))
        go(at, "second", 4, mine.at[slot, :, 1, y, 1 - x], target.at[1], place.across("x"))

    def piece_loads(at):
        index, group, part = chunks[at]
        slot = at % 2
        where = pl.ds(part * BLOCK, BLOCK)
        return (
            pltpu.make_async_copy(
                states[index].at[:, group, k, :, y, x, :, where],
                state_in.at[slot],
                state_sems.at[slot, 0],
            ),
            pltpu.make_async_copy(
                masters[index].at[group, k, :, y, x, :, where],
                master_in.at[slot],
                state_sems.at[slot, 1],
            ),
        )

    def stage_z(at):
        slot = at % 5
        arrived(at, "second")
        left(at, "second")

        @pl.loop(0, SHARDS)
        def _(shard):
            for h in range(2):
                final[at % 2, shard, h] = (
                    mine[slot, shard, h, y, x].astype(jnp.float32)
                    + from_second[at % 4, h, shard].astype(jnp.float32)
                ).astype(LOW)

        for copy in piece_loads(at):
            copy.start()
        for offset in range(1, SHARDS):
            target = lax.rem(s + offset, SHARDS)
            go(
                at,
                "z",
                5 + offset - 1,
                final.at[at % 2, target],
                from_z.at[at % 4, offset - 1],
                place.along(offset),
            )

    def summed(at, *where):
        index, group, part = chunks[at]
        rest = where + (slice(None),) * (5 - len(where))
        return sums[index].at[(group,) + rest + (pl.ds(part * BLOCK, BLOCK),)]

    def own_piece(at):
        return pltpu.make_async_copy(
            ready.at[at % 2], summed(at, k, slice(None), y, x), ready_sems.at[at % 2]
        )

    def direction_of(gradient, first, second):
        moment = 0.5 * first + 0.5 * gradient
        root = jnp.sqrt(0.5 * second * second + 0.5 * gradient * gradient)
        return moment / (root + 1e-06)

    def lanes(square):
        total = jnp.sum(square, 0, keepdims=True)
        parts = [total[:, i * 128 : (i + 1) * 128] for i in range(total.shape[1] // 128)]
        return sum(parts[1:], parts[0])

    def stage_back(at):
        index = chunks[at][0]
        slot = at % 2
        for copy in piece_loads(at):
            copy.wait()
        arrived(at, "z")
        left(at, "z")
        for h in range(2):
            value = final[slot, s, h].astype(jnp.float32)
            for offset in range(1, SHARDS):
                value = value + from_z[at % 4, offset - 1, h].astype(jnp.float32)
            low = value.astype(LOW)
            ready[slot, h] = low
            direction = direction_of(
                low.astype(jnp.float32), state_in[slot, 0, h], state_in[slot, 1, h]
            )
            master = master_in[slot, h]
            squares[0, index : index + 1, :] += lanes(master * master)
            squares[0, 8 + index : 9 + index, :] += lanes(direction * direction)
        own_piece(at).start()
        target = summed(at, k, 0, y, x)
        go(at, "back", 8, ready.at[slot, 0], target, place.across("y"))
        target = summed(at, k, 1, y, x)
        go(at, "back", 9, ready.at[slot, 1], target, place.across("x"))

    def stage_wide(at):
        own_piece(at).wait()
        arrived(at, "back")
        left(at, "back")
        ref = summed(at, k, 0, slice(None), x)
        go(at, "wide", 10, ref, ref, place.across("x"))
        ref = summed(at, k, 1, y)
        go(at, "wide", 11, ref, ref, place.across("y"))

    def stage_twin(at):
        arrived(at, "wide")
        ref = summed(at, k)
        go(at, "twin", 12, ref, ref, place.across("core"))

    def stage_end(at):
        arrived(at, "twin")

    stages = (
        stage_core,
        stage_first,
        stage_second,
        stage_z,
        stage_back,
        stage_wide,
        stage_twin,
        stage_end,
    )
    plan = Plan(latency=1.5, rate=45e3, pace=0.8)
    total = len(chunks)
    at_stage = [0] * total
    allowed = [0]
    unit = UNIT * BLOCK * 2 / plan.rate
    costs = (0.5, 1.1, 0.4, 0.25, 0.25, 0.1, 0.1, 0.0)
    lengths = (
        (("core", 32 * unit / 6),),
        (("x", 8 * unit), ("y", 8 * unit)),
        (("x", 4 * unit), ("y", 4 * unit)),
        (("z", 8 * unit),),
        (("x", unit), ("y", unit)),
        (("x", 2 * unit), ("y", 2 * unit)),
        (("core", 8 * unit / 6),),
        (),
    )

    def chunk_steps(at):
        moment = 0.0
        for number, stage in enumerate(stages):
            def free(number=number):
                if number == 0 and at >= allowed[0]:
                    return False
                if number == 3 and plan.backlog("z") > Z_LIMIT:
                    return False
                if number == 1 and at >= 5 and at_stage[at - 5] < 4:
                    return False
                if at and at_stage[at - 1] <= number:
                    return False
                return at < 2 or at_stage[at - 2] >= min(number + 2, len(stages))

            yield moment, free
            stage(at)
            plan.now += costs[number]
            at_stage[at] = number + 1
            moment = max([plan.transfer(link, length) for link, length in lengths[number]] + [0.0])

    for at in range(total):
        plan.add(chunk_steps(at))

    def allow(index):
        allowed[0] = sum(1 for chunk in chunks if chunk[0] >= index)
        plan.pump()

    def arrive(copies, moment):
        plan.until(moment)
        for copy in copies:
            copy.wait_recv()

    prime(4)
    cotangent_copy = pltpu.make_async_copy(
        rows_in.at[:, pl.ds(2 * width, width)], cotangent, cotangent_sem.at[0]
    )
    cotangent_copy.start()
    for copy in loads:
        copy.start()
    squares[...] = jnp.zeros_like(squares)
    table_own[...] = jnp.zeros_like(table_own)
    greet(place)
    cotangent_copy.wait()
    allow(4)

    def put_row(row, value):
        for shard in range(SHARDS):
            table_own[0, shard, row : row + 1, :] = value[:, shard * own : (shard + 1) * own]

    put_row(6, jnp.sum(cotangent[...].astype(jnp.float32), 0, keepdims=True))

    groups = tiles(4)[0]
    need("slope")
    for quarter in range(SHARDS):

        @pl.loop(0, groups)
        def _(group):
            at = quarter * groups + group
            act = contract(cotangent[...], take(4, at), 1, 1)
            give(4, at)
            where = pl.ds(pl.multiple_of(at * 256, 256), 256)
            low = (act * slope[:, where]).astype(LOW)
            grad_inner[:, where] = low
            table_own[0, group, 7 + quarter : 8 + quarter, :] = jnp.sum(
                low.astype(jnp.float32), 0, keepdims=True
            )

        plan.spend(1.5)
    prime(3)
    allow(3)
    parts = tiles(3)[1]

    @pl.loop(0, SHARDS)
    def _(shard):
        where = pl.ds(pl.multiple_of(shard * 256, 256), 256)
        total = None
        for part in range(parts):
            at = shard * parts + part
            term = contract(grad_inner[:, part * BLOCK : (part + 1) * BLOCK], take(3, at), 1, 1)
            give(3, at)
            total = term if total is None else total + term
        grad_second[:, where] = total

    prime(2)
    plan.spend(3.0)
    need("middle")
    gain_sum, bias_sum, low_sum = norm_back(
        middle, vectors[4:5, :], grad_second, cotangent, grad_middle, grad_middle_low, rows
    )
    put_row(4, gain_sum)
    put_row(5, bias_sum)
    put_row(3, low_sum)
    plan.spend(3.0)
    allow(2)

    @pl.loop(0, SHARDS)
    def _(shard):
        outgoing[shard, :, 0:own] = contract(grad_middle_low[...], take(2, shard), 1, 1).astype(LOW)

    prime(1)
    plan.spend(1.0)
    mixed_copies = []
    moments = []
    for pair in range(pairs):
        moments.append(plan.transfer("z", 4 * rows * 128 * 2 / plan.rate))
        columns = pl.ds(pair * 128, 128)
        for offset in range(1, SHARDS):
            mixed_copies.append(
                extra(
                    more + 3 * pair + offset - 1,
                    outgoing.at[lax.rem(s + offset, SHARDS), :, columns],
                    grad_mixed.at[pl.ds(offset * rows, rows), columns],
                    place.along(offset),
                )
            )

    @pl.loop(0, rows // 32)
    def _(block):
        where = pl.ds(pl.multiple_of(block * 32, 32), 32)
        grad_mixed[where, :] = outgoing[s, where, 0:own]

    plan.spend(0.5)
    need("heads")
    everyone = SHARDS * rows
    tile = 384
    lane = lax.broadcasted_iota(jnp.int32, (tile, 128), 1)
    key_row = lax.rem(lax.broadcasted_iota(jnp.int32, (everyone, 128), 0), rows)
    live = key_row < portion
    triple_copies = []
    for pair in range(pairs):
        arrive(mixed_copies[3 * pair : 3 * pair + 3], moments[pair])
        base = pair * 384
        grad_key[...] = jnp.zeros_like(grad_key)
        grad_value[...] = jnp.zeros_like(grad_value)
        low, high = pair * 128, (pair + 1) * 128

        for block in range(everyone // tile):
            start = block * tile
            where = slice(start, start + tile)
            query = heads[where, base : base + 128]
            keys = heads[:, base + 128 : base + 256]
            values = heads[:, base + 256 : base + 384]
            incoming = grad_mixed[where, low:high]
            parts = []
            for half in range(2):
                inside = (lane // 64) == half
                picked = jnp.where(inside, query.astype(jnp.float32) * factor, 0.0).astype(LOW)
                grads = jnp.where(inside, incoming.astype(jnp.float32), 0.0).astype(LOW)
                scores = contract(keys, picked, 1, 1)
                at = 2 * pair + half
                below = scores - log_total[at : at + 1, where]
                weight = jnp.exp(jnp.minimum(below, 0.0))
                into = contract(values, grads, 1, 1)
                delta = jnp.sum(weight * into, 0, keepdims=True)
                grad_scores = (weight * (into - delta)).astype(LOW)
                grad_key[...] += jnp.dot(
                    grad_scores, picked, preferred_element_type=jnp.float32
                )
                grad_value[...] += jnp.dot(
                    weight.astype(LOW), grads, preferred_element_type=jnp.float32
                )
                turned = contract(keys, grad_scores, 0, 0)
                parts.append(turned[half * 64 : (half + 1) * 64])
            both = jnp.concatenate(parts, 0) * factor
            grad_heads[where, base : base + 128] = both.T.astype(LOW)
            plan.spend(4.0)

        grad_heads[:, base + 128 : base + 256] = jnp.where(live, grad_key[...], 0.0).astype(LOW)
        grad_heads[:, base + 256 : base + 384] = jnp.where(live, grad_value[...], 0.0).astype(LOW)
        columns = pl.ds(base, 384)
        triple_moment = plan.transfer("z", 4 * rows * 384 * 2 / plan.rate)
        for offset in range(1, SHARDS):
            triple_copies.append(
                extra(
                    more + 3 * (pairs + pair) + offset - 1,
                    grad_heads.at[pl.ds(offset * rows, rows), columns],
                    grad_triple.at[s, :, columns],
                    (place.rep, place.source(offset)),
                )
            )
        plan.pump()

    @pl.loop(0, rows // 32)
    def _(block):
        where = pl.ds(pl.multiple_of(block * 32, 32), 32)
        grad_triple[s, where, :] = grad_heads[where, :]

    arrive(triple_copies, triple_moment)
    allow(1)
    parts_in = tiles(1)[1]

    @pl.loop(0, SHARDS)
    def _(shard):
        where = pl.ds(pl.multiple_of(shard * 256, 256), 256)
        total = None
        for part in range(parts_in):
            at = shard * parts_in + part
            term = contract(triple_part(part), take(1, at), 1, 1)
            give(1, at)
            total = term if total is None else total + term
        grad_second[:, where] = total

    prime(0)
    need("entering")
    plan.spend(3.0)
    gain_sum, bias_sum, low_sum = norm_back(
        entering, vectors[1:2, :], grad_second, grad_middle, None, grad_entering, rows
    )
    put_row(1, gain_sum)
    put_row(2, bias_sum)
    put_row(0, low_sum)
    plan.spend(3.0)
    allow(0)
    table_copies = []

    def table_step(position, axis):
        if position:
            table_copies[-1].wait_recv()
            table_own[position] = table_own[position - 1] + table_in[position - 1]
        if axis:
            table_copies.append(
                extra(
                    6 + position,
                    table_own.at[position],
                    table_in.at[position],
                    place.across(axis),
                )
            )

    @pl.loop(0, tiles(0)[2])
    def _(at):
        where = pl.ds(pl.multiple_of(at * 256, 256), 256)
        grad_joined[:, where] = contract(grad_entering[...], take(0, at), 1, 1).astype(LOW)
        give(0, at)

    plan.spend(1.5)

    def table_steps():
        for position, axis in enumerate(("core", "x", "y", None)):
            table_step(position, axis)
            if axis:
                yield plan.transfer(axis, 1.5), None
        for offset in range(1, SHARDS):
            table_copies.append(
                extra(
                    8 + offset,
                    table_own.at[3, lax.rem(s + offset, SHARDS)],
                    table_z.at[offset - 1],
                    place.along(offset),
                )
            )
        yield plan.transfer("z", 2.0), None
        for copy in table_copies[3:]:
            copy.wait_recv()
        value = table_own[3, s]
        for offset in range(1, SHARDS):
            value = value + table_z[offset - 1]
        table_sum[...] = value
        direction = direction_of(value, own_states[0], own_states[1])
        share = 1.0 / REPLICAS
        squares[0, 5:6, :] = share * lanes(own_vectors[...] * own_vectors[...])
        squares[0, 13:14, :] = share * lanes(direction * direction)
        table_done[0] = True

    table_done = [False]
    squares_done = [False]

    def square_steps():
        yield 0.0, lambda: table_done[0] and min(at_stage) >= 5
        hops = []
        for position, axis in enumerate(("core", "x", "y", None)):
            if position:
                hops[-1].wait_recv()
                squares[position] = squares[position - 1] + square_in[position - 1]
            if axis:
                hops.append(
                    extra(
                        12 + position,
                        squares.at[position],
                        square_in.at[position],
                        place.across(axis),
                    )
                )
                yield plan.transfer(axis, 0.5), None
        hops = []
        for offset in range(1, SHARDS):
            hops.append(
                extra(14 + offset, squares.at[3], square_z.at[offset], place.along(offset))
            )
        square_z[0] = squares[3]
        yield plan.transfer("z", 0.5), None
        for copy in hops:
            copy.wait_recv()
        value = square_z[s]
        for shard in range(1, SHARDS):
            value = value + square_z[lax.rem(s + SHARDS - shard, SHARDS)]
        norms[...] = jnp.sqrt(jnp.sum(value, 1, keepdims=True)) + jnp.zeros_like(value)
        squares_done[0] = True

    plan.add(table_steps())
    plan.add(square_steps())
    plan.finish(lambda: squares_done[0] and min(at_stage) == len(stages))
    for key in sorted(copies):
        for copy in copies[key]:
            copy.wait_send()
    for copy in sent:
        copy.wait_send()


def backward_pass(cotangent, joined, table, kept, weights, masters, states, vectors, vector_states, portion):
    entering, first_in, heads, log_total, mixed, middle, second_in, slope, activated = kept[:9]
    shapes = [(matrix.shape[0] * SHARDS, matrix.shape[1]) for matrix in masters]
    order = chunk_list(shapes)
    chunks = [chunk for index in (4, 3, 2, 1, 0) for chunk in order if chunk[0] == index]
    total = len(chunks)
    rows, width = entering.shape
    own = width // SHARDS
    hidden = slope.shape[1]
    loaded = (second_in, slope, middle, mixed, heads, first_in, entering, joined)
    everyone = SHARDS * rows
    piece = (UNIT, BLOCK)
    inner = pl.BlockSpec(memory_space=pltpu.VMEM)
    folds = [(SHARDS, r // SHARDS // 256, 2, 2, 2, 2, UNIT, c) for r, c in shapes]
    extra_rows = 16 - vectors.shape[0]
    own_vectors = jnp.pad(vectors, ((0, extra_rows), (0, 0)))
    own_states = jnp.pad(vector_states, ((0, 0), (0, extra_rows), (0, 0)))
    outs = pl.pallas_call(
        functools.partial(backward_kernel, chunks, portion),
        out_shape=[jax.ShapeDtypeStruct(fold[1:], LOW) for fold in folds]
        + [
            jax.ShapeDtypeStruct((16, own), jnp.float32),
            jax.ShapeDtypeStruct((16, 128), jnp.float32),
            jax.ShapeDtypeStruct((rows, 2 * width), LOW),
        ],
        in_specs=[ANY]
        + [inner] * 3
        + [ANY] * 23
        + [inner] * 2,
        out_specs=[ANY] * 5 + [inner] * 3,
        scratch_shapes=[
            pltpu.VMEM((8, 2, 2, 2, 2) + piece, LOW),
            pltpu.VMEM((2, SHARDS, 2, 2, 2) + piece, LOW),
            pltpu.VMEM((5, SHARDS, 2, 2, 2) + piece, LOW),
            pltpu.VMEM((4, SHARDS, 2, 2, 2) + piece, LOW),
            pltpu.VMEM((4, 2, SHARDS, 2) + piece, LOW),
            pltpu.VMEM((4, 2, SHARDS) + piece, LOW),
            pltpu.VMEM((2, SHARDS, 2) + piece, LOW),
            pltpu.VMEM((4, SHARDS - 1, 2) + piece, LOW),
            pltpu.VMEM((2, 2) + piece, LOW),
            pltpu.VMEM((2, 2, 2) + piece, jnp.float32),
            pltpu.VMEM((2, 2) + piece, jnp.float32),
            pltpu.VMEM((4, 16, 128), jnp.float32),
            pltpu.VMEM((3, 16, 128), jnp.float32),
            pltpu.VMEM((SHARDS, 16, 128), jnp.float32),
            pltpu.VMEM((4, SHARDS, 16, own), jnp.float32),
            pltpu.VMEM((3, SHARDS, 16, own), jnp.float32),
            pltpu.VMEM((SHARDS - 1, 16, own), jnp.float32),
            pltpu.VMEM((rows, hidden), LOW),
            pltpu.VMEM((rows, width), jnp.float32),
            pltpu.VMEM((rows, width), jnp.float32),
            pltpu.VMEM((rows, width), LOW),
            pltpu.VMEM((SHARDS, rows, own), LOW),
            pltpu.VMEM((everyone, own), LOW),
            pltpu.VMEM((everyone, 128), jnp.float32),
            pltpu.VMEM((everyone, 128), jnp.float32),
            pltpu.VMEM((everyone, 3 * own), LOW),
            pltpu.VMEM((SHARDS, rows, 3 * own), LOW),
            pltpu.VMEM((rows, width), LOW),
            *[pltpu.VMEM(array.shape, array.dtype) for array in loaded[:7]],
            pltpu.VMEM((rows, 2 * width), LOW),
            pltpu.VMEM((rows, width), LOW),
            pltpu.SemaphoreType.DMA((1,)),
            pltpu.SemaphoreType.DMA((8,)),
            pltpu.SemaphoreType.DMA((8,)),
            pltpu.SemaphoreType.DMA((2, 2)),
            pltpu.SemaphoreType.DMA((2,)),
            pltpu.SemaphoreType.DMA((total * 14,)),
            pltpu.SemaphoreType.DMA((total * 14,)),
            pltpu.SemaphoreType.DMA((18 + 6 * (own // 128),)),
            pltpu.SemaphoreType.DMA((18 + 6 * (own // 128),)),
        ],
        compiler_params=pltpu.CompilerParams(
            collective_id=2, has_side_effects=True, vmem_limit_bytes=60 * 2**20
        ),
        name="backward_pass",
    )(
        cotangent,
        table,
        log_total,
        activated,
        *loaded,
        *[matrix.reshape(fold) for matrix, fold in zip(weights, folds)],
        *[matrix.reshape(fold[1:]) for matrix, fold in zip(masters, folds)],
        *[state.reshape((2,) + fold[1:]) for state, fold in zip(states, folds)],
        own_vectors,
        own_states,
    )
    lows = [low.reshape(r // SHARDS, c) for low, (r, c) in zip(outs[:5], shapes)]
    return lows, outs[5][: vectors.shape[0]], outs[6], outs[7]


def update_kernel(blocks, norms, *refs):
    gradients, states, masters = refs[0:5], refs[5:10], refs[10:15]
    wides, new_states, new_masters = refs[15:20], refs[20:25], refs[25:30]
    low_in, state_in, master_in, wide_out, state_out, master_out, in_sems, out_sems = refs[30:]
    slots, height = low_in.shape[0], low_in.shape[1]

    def copies(at, arriving):
        index, row, column = blocks[at]
        slot = at % slots
        where = (pl.ds(row, height), pl.ds(column, BLOCK))
        outside = (gradients, states, masters) if arriving else (wides, new_states, new_masters)
        inside = (low_in, state_in, master_in) if arriving else (wide_out, state_out, master_out)
        sems = in_sems if arriving else out_sems
        result = []
        for number in range(3):
            far = outside[number][index].at[((slice(None),) if number == 1 else ()) + where]
            near = inside[number].at[slot]
            ends = (far, near) if arriving else (near, far)
            result.append(pltpu.make_async_copy(*ends, sems.at[slot, number]))
        return result

    def start(at, arriving):
        for copy in copies(at, arriving):
            copy.start()

    def wait(at, arriving):
        for copy in copies(at, arriving):
            copy.wait()

    total = len(blocks)
    ahead = slots - 1
    for at in range(min(ahead, total)):
        start(at, True)
    for at in range(total):
        index = blocks[at][0]
        slot = at % slots
        if at + ahead < total:
            start(at + ahead, True)
        wait(at, True)
        if at >= slots:
            wait(at - slots, False)
        ratio = step_rate * (
            norms[index : index + 1, 0:1] / (norms[8 + index : 9 + index, 0:1] + 1e-06)
        )

        @pl.loop(0, height // UNIT)
        def _(step):
            rows = pl.ds(pl.multiple_of(step * UNIT, UNIT), UNIT)
            grad = low_in[slot, rows, :].astype(jnp.float32)
            second = state_in[slot, 1, rows, :]
            moment = 0.5 * state_in[slot, 0, rows, :] + 0.5 * grad
            root = jnp.sqrt(0.5 * second * second + 0.5 * grad * grad)
            wide_out[slot, rows, :] = grad
            state_out[slot, 0, rows, :] = moment
            state_out[slot, 1, rows, :] = root
            master_out[slot, rows, :] = master_in[slot, rows, :] - ratio * (
                moment / (root + 1e-06)
            )

        start(at, False)
    for at in range(max(0, total - slots), total):
        wait(at, False)


def update_weights(norms, gradients, states, masters):
    height, slots = UPDATE_ROWS, UPDATE_SLOTS
    blocks = [
        (index, row, column)
        for index, master in enumerate(masters)
        for row in range(0, master.shape[0], height)
        for column in range(0, master.shape[1], BLOCK)
    ]
    square = (slots, height, BLOCK)
    pair = (slots, 2, height, BLOCK)
    outs = pl.pallas_call(
        functools.partial(update_kernel, blocks),
        out_shape=[jax.ShapeDtypeStruct(m.shape, jnp.float32) for m in masters]
        + [jax.ShapeDtypeStruct(state.shape, jnp.float32) for state in states]
        + [jax.ShapeDtypeStruct(m.shape, jnp.float32) for m in masters],
        in_specs=[pl.BlockSpec(memory_space=pltpu.VMEM)] + [ANY] * 15,
        out_specs=[ANY] * 15,
        scratch_shapes=[
            pltpu.VMEM(square, LOW),
            pltpu.VMEM(pair, jnp.float32),
            pltpu.VMEM(square, jnp.float32),
            pltpu.VMEM(square, jnp.float32),
            pltpu.VMEM(pair, jnp.float32),
            pltpu.VMEM(square, jnp.float32),
            pltpu.SemaphoreType.DMA((slots, 3)),
            pltpu.SemaphoreType.DMA((slots, 3)),
        ],
        compiler_params=pltpu.CompilerParams(vmem_limit_bytes=48 * 2**20),
        name="update_weights",
    )(norms, *gradients, *states, *masters)
    return outs[:5], outs[5:10], outs[10:]


def fits(masters):
    return (
        lax.axis_size("shard") == SHARDS
        and lax.axis_size("rep") == REPLICAS
        and all(m.shape[0] % 256 == 0 and m.shape[1] % BLOCK == 0 for m in masters)
        and masters[0].shape[1] == HEADS * HEAD_DIM == BLOCK
    )


def plain_device(
    hidden_in,
    skip_path,
    cotangent,
    skip_weight,
    heads_in,
    heads_out,
    expand_weight,
    reduce_weight,
    vectors,
    moments_skip,
    moments_in,
    moments_out,
    moments_expand,
    moments_reduce,
    moments_vectors,
):
    sequences, portion, model_width = hidden_in.shape
    shards = lax.axis_size("shard")
    replicas = lax.axis_size("rep")
    rep_index = lax.axis_index("rep")
    row_count = sequences * portion
    factor = 1.0 / math.sqrt(HEAD_DIM)
    masters = (skip_weight, heads_in, heads_out, expand_weight, reduce_weight, vectors)
    gathered = []
    for matrix in masters[:5]:
        height = matrix.shape[0] // replicas
        piece = lax.dynamic_slice_in_dim(matrix, rep_index * height, height, 0)
        piece = piece.astype(jnp.bfloat16)
        gathered.append(lax.all_gather(piece, ("shard", "rep"), axis=0, tiled=True))
    skip_matrix, in_matrix, out_matrix, expand_matrix, reduce_matrix = gathered
    table_low = lax.all_gather(vectors.astype(jnp.bfloat16), "shard", axis=1, tiled=True)
    table_rows = table_low.astype(jnp.float32)
    source = hidden_in.reshape(row_count, model_width)
    skip_rows = skip_path.reshape(row_count, model_width)
    joined = jnp.concatenate([source, skip_rows], 1)
    entering = matmul(joined, skip_matrix) + table_rows[0]
    normed_one, norm_back_one = jax.vjp(normalize, entering, table_rows[1], table_rows[2])
    first_in = normed_one.astype(jnp.bfloat16)
    triple = matmul(first_in, in_matrix).astype(jnp.bfloat16)
    heads = to_heads(triple, sequences, portion, shards)
    queries, keys_full, values_full = heads[:, :, 0], heads[:, :, 1], heads[:, :, 2]
    scores = (
        jnp.einsum("sqhd,skhd->shqk", queries, keys_full, preferred_element_type=jnp.float32)
        * factor
    )
    row_max = jnp.max(scores, -1)
    row_total = jnp.sum(jnp.exp(scores - row_max[..., None]), -1)
    log_total = row_max + jnp.log(row_total)
    probability = jnp.exp(scores - log_total[..., None])
    mixed = jnp.einsum(
        "shqk,skhd->sqhd",
        probability.astype(jnp.bfloat16),
        values_full,
        preferred_element_type=jnp.float32,
    )
    mixed_low = to_tokens(mixed.astype(jnp.bfloat16)[:, :, None], sequences, portion, shards)
    middle = entering + matmul(mixed_low, out_matrix) + table_rows[3]
    normed_two, norm_back_two = jax.vjp(normalize, middle, table_rows[4], table_rows[5])
    second_in = normed_two.astype(jnp.bfloat16)
    expanded = matmul(second_in, expand_matrix) + table_rows[7:].reshape(-1)
    activated, gelu_back = jax.vjp(exact_gelu, expanded)
    activated_low = activated.astype(jnp.bfloat16)
    block_result = middle + matmul(activated_low, reduce_matrix) + table_rows[6]
    block_out = block_result.astype(jnp.bfloat16).reshape(sequences, portion, model_width)
    grad_out = cotangent.reshape(row_count, model_width)
    grad_reduce = matmul(activated_low.T, grad_out)
    grad_act = matmul(grad_out, reduce_matrix.T)
    grad_inner = gelu_back(grad_act)[0].astype(jnp.bfloat16)
    grad_expand = matmul(second_in.T, grad_inner)
    grad_second = matmul(grad_inner, expand_matrix.T)
    grad_mid_norm, grad_gain_two, grad_bias_two = norm_back_two(grad_second)
    grad_middle = grad_out.astype(jnp.float32) + grad_mid_norm
    grad_middle_low = grad_middle.astype(jnp.bfloat16)
    grad_outw = matmul(mixed_low.T, grad_middle_low)
    grad_mixed = matmul(grad_middle_low, out_matrix.T).astype(jnp.bfloat16)
    grad_mixed = to_heads(grad_mixed, sequences, portion, shards)[:, :, 0]
    grad_prob = jnp.einsum(
        "sqhd,skhd->shqk", grad_mixed, values_full, preferred_element_type=jnp.float32
    )
    delta = jnp.sum(probability * grad_prob, -1)
    grad_scores = (probability * (grad_prob - delta[..., None])).astype(jnp.bfloat16)
    grad_query = (
        jnp.einsum("shqk,skhd->sqhd", grad_scores, keys_full, preferred_element_type=jnp.float32)
        * factor
    )
    grad_keys = (
        jnp.einsum("shqk,sqhd->skhd", grad_scores, queries, preferred_element_type=jnp.float32)
        * factor
    )
    grad_values = jnp.einsum(
        "shqk,sqhd->skhd",
        probability.astype(jnp.bfloat16),
        grad_mixed,
        preferred_element_type=jnp.float32,
    )
    grad_heads = jnp.stack([grad_query, grad_keys, grad_values], 2).astype(jnp.bfloat16)
    grad_triple = to_tokens(grad_heads, sequences, portion, shards)
    grad_inw = matmul(first_in.T, grad_triple)
    grad_first = matmul(grad_triple, in_matrix.T)
    grad_pre_norm, grad_gain_one, grad_bias_one = norm_back_one(grad_first)
    grad_entering = (grad_middle + grad_pre_norm).astype(jnp.bfloat16)
    grad_skipw = matmul(joined.T, grad_entering)
    grad_joined = matmul(grad_entering, skip_matrix.T)
    input_gradient = (
        grad_joined[:, :model_width].astype(jnp.bfloat16).reshape(sequences, portion, model_width)
    )
    skip_gradient = (
        grad_joined[:, model_width:].astype(jnp.bfloat16).reshape(sequences, portion, model_width)
    )
    grad_table = jnp.concatenate(
        [
            jnp.stack(
                [
                    row_sums(grad_entering),
                    grad_gain_one,
                    grad_bias_one,
                    row_sums(grad_middle_low),
                    grad_gain_two,
                    grad_bias_two,
                    row_sums(grad_out),
                ]
            ),
            row_sums(grad_inner).reshape(-1, model_width),
        ],
        0,
    )
    width = vectors.shape[1]
    grad_table = lax.psum(grad_table, ("rep", "shard"))
    vector_total = lax.dynamic_slice_in_dim(grad_table, lax.axis_index("shard") * width, width, 1)
    totals = []
    for partial in (grad_skipw, grad_inw, grad_outw, grad_expand, grad_reduce):
        piece = lax.psum_scatter(
            partial.astype(jnp.bfloat16), ("shard", "rep"), scatter_dimension=0, tiled=True
        )
        whole = lax.all_gather(piece, "rep", axis=0, tiled=True)
        totals.append(whole.astype(jnp.float32))
    totals.append(vector_total)
    states = (
        moments_skip,
        moments_in,
        moments_out,
        moments_expand,
        moments_reduce,
        moments_vectors,
    )
    steps = [moment_step(total, state) for total, state in zip(totals, states)]
    squares = jnp.stack(
        [
            jnp.stack([jnp.sum(matrix * matrix) for matrix in masters]),
            jnp.stack([jnp.sum(direction * direction) for _, direction in steps]),
        ]
    )
    norms = jnp.sqrt(lax.psum(squares, "shard"))
    ratio = norms[0] / (norms[1] + 1e-06)
    updated = [
        masters[position] - step_rate * ratio[position] * steps[position][1]
        for position in range(6)
    ]
    return (
        block_out,
        input_gradient,
        skip_gradient,
        *totals,
        *(state for state, _ in steps),
        *updated,
        norms,
    )


def on_device(
    hidden_in,
    skip_path,
    cotangent,
    skip_weight,
    heads_in,
    heads_out,
    expand_weight,
    reduce_weight,
    vectors,
    moments_skip,
    moments_in,
    moments_out,
    moments_expand,
    moments_reduce,
    moments_vectors,
):
    sequences, portion, model_width = hidden_in.shape
    masters = (skip_weight, heads_in, heads_out, expand_weight, reduce_weight)
    states = (moments_skip, moments_in, moments_out, moments_expand, moments_reduce)
    if not (sequences == 1 and fits(masters)):
        return plain_device(
            hidden_in, skip_path, cotangent, *masters, vectors, *states, moments_vectors
        )
    more = -portion % 32
    joined = jnp.concatenate([hidden_in[0], skip_path[0], cotangent[0]], 1)
    joined = jnp.pad(joined, ((0, more), (0, 0)))
    weights, kept = forward_pass(joined, vectors, masters, portion)
    block_out, table = kept[9], kept[10]
    lows, vector_total, norms, grad_joined = backward_pass(
        joined, joined, table, kept, weights, masters, states, vectors, moments_vectors, portion
    )
    wides, new_states, new_masters = update_weights(norms, lows, states, masters)
    vector_state, direction = moment_step(vector_total, moments_vectors)
    ratio = norms[5, 0] / (norms[13, 0] + 1e-06)
    return (
        block_out[None, :portion],
        grad_joined[None, :portion, :model_width],
        grad_joined[None, :portion, model_width:],
        *wides,
        vector_total,
        *new_states,
        vector_state,
        *new_masters,
        vectors - step_rate * ratio * direction,
        jnp.stack([norms[:6, 0], norms[8:14, 0]]),
    )


def solution(mesh):
    placed = (
        P("rep", "shard", None),
        P("rep", "shard", None),
        P("rep", "shard", None),
        P("shard", None),
        P("shard", None),
        P("shard", None),
        P("shard", None),
        P("shard", None),
        P(None, "shard"),
        P(None, "shard", None),
        P(None, "shard", None),
        P(None, "shard", None),
        P(None, "shard", None),
        P(None, "shard", None),
        P(None, None, "shard"),
    )
    return jax.shard_map(
        on_device,
        mesh=mesh,
        in_specs=placed,
        out_specs=(
            P("rep", "shard", None),
            P("rep", "shard", None),
            P("rep", "shard", None),
            P("shard", None),
            P("shard", None),
            P("shard", None),
            P("shard", None),
            P("shard", None),
            P(None, "shard"),
            P(None, "shard", None),
            P(None, "shard", None),
            P(None, "shard", None),
            P(None, "shard", None),
            P(None, "shard", None),
            P(None, None, "shard"),
            P("shard", None),
            P("shard", None),
            P("shard", None),
            P("shard", None),
            P("shard", None),
            P(None, "shard"),
            P(),
        ),
        check_vma=False,
    )
```
